32 devices in a mesh: section: 2 (over x), dp: 4 (over z), mp: 4 (over y, core).
Axes of the slice: x: 2, y: 2, z: 4, core: 2. Of those that a mesh axis runs over, the one named last changes fastest.
Arguments:
- boundary_in: bfloat16 [2, 8, 512, 768], P('section', 'dp', 'mp'), may hold values from -6 to 6
- order: int32 [4, 2], P('dp'), may hold values from 0 to 1, each once within a row
- ln1_gain: float32 [2, 768], P('section'), may hold values from 0.1 to 1.9
- ln1_bias: float32 [2, 768], P('section'), may hold values from -3 to 3
- w_qkv: bfloat16 [2, 3, 768, 768], P('section', None, None, 'mp'), may hold values from -0.21875 to 0.21875
- qkv_bias: float32 [2, 2, 768], P('section', None, 'mp'), may hold values from -0.625 to 0.625
- w_out: bfloat16 [2, 768, 768], P('section', 'mp'), may hold values from -4 to 4
- out_bias: float32 [2, 768], P('section'), may hold values from -6 to 6
- ln2_gain: float32 [2, 768], P('section'), may hold values from 0.1 to 1.9
- ln2_bias: float32 [2, 768], P('section'), may hold values from -3 to 3
- w_fc: bfloat16 [2, 768, 3072], P('section', None, 'mp'), may hold values from -0.21875 to 0.21875
- fc_bias: float32 [2, 3072], P('section', 'mp'), may hold values from -3 to 3
- w_proj: bfloat16 [2, 3072, 768], P('section', 'mp'), may hold values from -1.25 to 1.25
- proj_bias: float32 [2, 768], P('section'), may hold values from -6 to 6
Outputs:
- boundary_out: float32 [2, 8, 512, 768], P('section', 'dp', 'mp')
- ln1_gain_grad: float32 [2, 768], P('section')
- ln1_bias_grad: float32 [2, 768], P('section')
- w_qkv_grad: float32 [2, 3, 768, 768], P('section', None, None, 'mp')
- qkv_bias_grad: float32 [2, 2, 768], P('section', None, 'mp')
- w_out_grad: float32 [2, 768, 768], P('section', 'mp')
- out_bias_grad: float32 [2, 768], P('section')
- ln2_gain_grad: float32 [2, 768], P('section')
- ln2_bias_grad: float32 [2, 768], P('section')
- w_fc_grad: float32 [2, 768, 3072], P('section', None, 'mp')
- fc_bias_grad: float32 [2, 3072], P('section', 'mp')
- w_proj_grad: float32 [2, 3072, 768], P('section', 'mp')
- proj_bias_grad: float32 [2, 768], P('section')
The draws below stay inside these ranges and needn't reach their ends.
Inputs may be any that keep to these rules, and one draw needn't show every extreme that they name: Each row of order names every slot 0 to 1 once.
All inputs are finite; a program needn't handle non-finite values.
Results may differ from the reference program's by a relative error of at most 0.033.
Values may be sent and summed in bfloat16 or wider, within the bound.
A program may use at most 128 MiB of HBM per device.

```python
import math
import jax
import jax.numpy as jnp
from jax import lax

HEADS = 12
HEAD_DIM = 64
D = 768
FF = 3072
SEQ = 512
MICRO = 2
REPLICAS = 4
SEQS = 8


def block_scale(stream_key, shape, cuts, least, high):
    level, own = 1.0, jax.random.fold_in(stream_key, 6)
    for axis_at, parts in cuts:
        heights = jnp.exp(jax.random.uniform(jax.random.fold_in(own, axis_at), (parts,), jnp.float32, least / len(cuts), high / len(cuts)))
        level = level * jnp.repeat(heights, shape[axis_at] // parts).reshape([-1 if axis == axis_at else 1 for axis in range(len(shape))])
    return level


def gaussian(own_key, extent, width, most, shards=(), kind=jnp.bfloat16):
    array = width * jax.random.normal(own_key, extent, jnp.float32)
    if shards:
        array = array * block_scale(own_key, extent, shards, -0.22, 0.18)
    return jnp.clip(array, -most, most).astype(kind)


def setup_inputs(seed: int = 0) -> dict:
    key_of = jax.random.split(jax.random.key(seed), 15)
    boundary_in = gaussian(key_of[0], (2, SEQS, SEQ, D), 1.0, 6.0, ((0, 2), (1, 4), (2, 4)))
    order = jax.vmap(lambda own: jax.random.permutation(own, MICRO))(jax.random.split(key_of[1], REPLICAS)).reshape((REPLICAS, MICRO)).astype(jnp.int32)
    ln1_gain = jnp.clip(1.0 + 0.18 * jax.random.normal(key_of[2], (2, D), jnp.float32), 0.1, 1.9)
    ln1_bias = gaussian(key_of[3], (2, D), 0.5, 3.0, ((0, 2),), jnp.float32)
    w_qkv = gaussian(key_of[4], (2, 3, D, D), D ** -0.5, 0.21875, ((0, 2), (3, 4)))
    qkv_bias = gaussian(key_of[5], (2, 2, D), 0.1, 0.625, ((0, 2), (2, 4)), jnp.float32)
    w_out = gaussian(key_of[6], (2, D, D), 2 ** -0.5, 4.0, ((0, 2), (1, 4)))
    out_bias = gaussian(key_of[7], (2, D), 1.0, 6.0, ((0, 2),), jnp.float32)
    ln2_gain = jnp.clip(1.0 + 0.18 * jax.random.normal(key_of[8], (2, D), jnp.float32), 0.1, 1.9)
    ln2_bias = gaussian(key_of[9], (2, D), 0.5, 3.0, ((0, 2),), jnp.float32)
    w_fc = gaussian(key_of[10], (2, D, FF), D ** -0.5, 0.21875, ((0, 2), (2, 4)))
    fc_bias = gaussian(key_of[11], (2, FF), 0.5, 3.0, ((0, 2), (1, 4)), jnp.float32)
    w_proj = gaussian(key_of[12], (2, FF, D), 24 ** -0.5, 1.25, ((0, 2), (1, 4)))
    proj_bias = gaussian(key_of[13], (2, D), 1.0, 6.0, ((0, 2),), jnp.float32)
    return {"boundary_in": boundary_in, "order": order, "ln1_gain": ln1_gain, "ln1_bias": ln1_bias, "w_qkv": w_qkv, "qkv_bias": qkv_bias, "w_out": w_out, "out_bias": out_bias, "ln2_gain": ln2_gain, "ln2_bias": ln2_bias, "w_fc": w_fc, "fc_bias": fc_bias, "w_proj": w_proj, "proj_bias": proj_bias}


@jax.custom_vjp
def low(v):
    return lax.optimization_barrier(v.astype(jnp.bfloat16)).astype(jnp.float32)

@jax.custom_vjp
def low_back(v):
    return v

def low_keep(v):
    return (low(v), None)

def low_pass(kept, grad):
    return (grad,)

def back_keep(v):
    return (v, None)

def back_low(kept, grad):
    return (low(grad),)
low.defvjp(low_keep, low_pass)
low_back.defvjp(back_keep, back_low)
branch_scale = 0.14433756729740643
norm_eps = 1e-05
highest = lax.Precision.HIGHEST

def layer_norm(values, gain, offset):
    center = values - lax.optimization_barrier(jnp.mean(values, axis=-1, keepdims=True))
    spread = lax.optimization_barrier(jnp.mean(center * center, axis=-1, keepdims=True))
    return center * lax.rsqrt(spread + norm_eps) * gain + offset

def split_heads(values):
    return values.reshape(values.shape[0], values.shape[1], HEADS, HEAD_DIM)

def one_layer(inputs, weights):
    ln1_gain, ln1_bias, w_qkv, qkv_bias, w_out, out_bias, ln2_gain, ln2_bias, w_fc, fc_bias, w_proj, proj_bias = weights
    seq_count, length, model_width = inputs.shape
    normed = low(layer_norm(inputs, ln1_gain, ln1_bias))
    projected = jnp.einsum('bsd,cde->cbse', normed, w_qkv, precision=highest)
    queries = low_back(low(projected[0] + qkv_bias[0]))
    keys_all = low_back(low(projected[1]))
    values_all = low_back(low(projected[2] + qkv_bias[1]))
    scores = jnp.einsum('bshd,bthd->bhst', split_heads(queries), split_heads(keys_all), precision=highest)
    scores = low_back(scores * HEAD_DIM ** (-0.5))
    causal = lax.broadcasted_iota(jnp.int32, (length, length), 0) >= lax.broadcasted_iota(jnp.int32, (length, length), 1)
    attn_probs = jax.nn.softmax(jnp.where(causal, scores, -1e+30), axis=-1)
    attended = jnp.einsum('bhst,bthd->bshd', low(attn_probs), split_heads(values_all), precision=highest)
    attended = low_back(low(attended.reshape(seq_count, length, model_width)))
    attn_branch = low_back(jnp.einsum('bse,ed->bsd', attended, w_out, precision=highest) + out_bias)
    hidden = inputs + branch_scale * attn_branch
    normed_two = low(layer_norm(hidden, ln2_gain, ln2_bias))
    pre_act = low_back(jnp.einsum('bsd,df->bsf', normed_two, w_fc, precision=highest) + fc_bias)
    activation = low(jax.nn.gelu(pre_act, approximate=True))
    branch = low_back(jnp.einsum('bsf,fd->bsd', activation, w_proj, precision=highest) + proj_bias)
    return hidden + branch_scale * branch

def both_layers(inputs, weights):
    first_out = one_layer(inputs, tuple((tensor[0] for tensor in weights)))
    return one_layer(first_out, tuple((tensor[1] for tensor in weights)))

def reference(boundary_in, order, ln1_gain, ln1_bias, w_qkv, qkv_bias, w_out, out_bias, ln2_gain, ln2_bias, w_fc, fc_bias, w_proj, proj_bias):
    weights = tuple((tensor.astype(jnp.float32) for tensor in (ln1_gain, ln1_bias, w_qkv, qkv_bias, w_out, out_bias, ln2_gain, ln2_bias, w_fc, fc_bias, w_proj, proj_bias)))
    micro_count = order.shape[1]
    seq_total = boundary_in.shape[1]
    picked = (jnp.arange(order.shape[0], dtype=jnp.int32)[:, None] * micro_count + order.astype(jnp.int32)).reshape(-1).astype(jnp.int32)
    inputs = jnp.take(boundary_in[0], picked, axis=0).astype(jnp.float32)
    cotangent = boundary_in[1].astype(jnp.float32)
    group_size = math.gcd(seq_total, 4)
    shape_four = (seq_total // group_size, group_size, SEQ, D)

    def per_group(totals, pieces):
        group_in, group_cot = pieces
        group_out, pullback = jax.vjp(both_layers, group_in, weights)
        group_grad, weight_grads = pullback(group_cot)
        return (tuple((total + grad_part for total, grad_part in zip(totals, weight_grads))), (group_out, group_grad))
    zero_grads = tuple((jnp.zeros_like(tensor) for tensor in weights))
    totals, (outputs, input_grads) = lax.scan(per_group, zero_grads, (inputs.reshape(shape_four), cotangent.reshape(shape_four)))
    boundary_out = jnp.stack([input_grads.reshape(seq_total, SEQ, D), outputs.reshape(seq_total, SEQ, D)])
    return (boundary_out, totals[0], totals[1], totals[2], totals[3], totals[4], totals[5], totals[6], totals[7], totals[8], totals[9], totals[10], totals[11])
```

```python
import functools

import jax
import jax.numpy as jnp
from jax import lax
from jax.experimental import pallas as pl
from jax.experimental.pallas import tpu as pltpu
from jax.sharding import PartitionSpec as P

HEAD_DIM = 64
BRANCH_SCALE = 0.14433756729740643
NORM_EPS = 1e-05
GELU_RATE = 0.7978845608028654
GELU_CUBE = 0.044715
NEGATIVE = -1e30
BLOCK = 96
TILES = 2
MESH = pl.DeviceIdType.MESH
BF16 = jnp.bfloat16
F32 = jnp.float32


def dot_nn(a, b):
    return lax.dot_general(a, b, (((1,), (0,)), ((), ())), preferred_element_type=F32)


def dot_nt(a, b):
    return lax.dot_general(a, b, (((1,), (1,)), ((), ())), preferred_element_type=F32)


def dot_tn(a, b):
    return lax.dot_general(a, b, (((0,), (0,)), ((), ())), preferred_element_type=F32)


def normed(values):
    center = values - jnp.mean(values, axis=-1, keepdims=True)
    rate = lax.rsqrt(jnp.mean(center * center, axis=-1, keepdims=True) + NORM_EPS)
    return center * rate, rate


def norm_backward(grad, hat, rate, gain):
    scaled = grad * gain
    return rate * (
        scaled
        - jnp.mean(scaled, axis=-1, keepdims=True)
        - hat * jnp.mean(scaled * hat, axis=-1, keepdims=True)
    )


def column_sum(values):
    return jnp.sum(values.astype(F32), axis=0, keepdims=True)


def remote(src, dst, send_sem, recv_sem, device):
    return pltpu.make_async_remote_copy(
        src_ref=src,
        dst_ref=dst,
        send_sem=send_sem,
        recv_sem=recv_sem,
        device_id=device,
        device_id_type=MESH,
    )


def kernel(
    z_line,
    order_ref,
    boundary_ref,
    ln1_gain_ref,
    ln1_bias_ref,
    w_qkv_ref,
    qkv_bias_ref,
    w_out_ref,
    out_bias_ref,
    ln2_gain_ref,
    ln2_bias_ref,
    w_fc_ref,
    fc_bias_ref,
    w_proj_ref,
    proj_bias_ref,
    rows_out,
    small_out,
    qkv_out,
    out_out,
    fc_out,
    proj_out,
    raw,
    slots,
    stage,
    weights,
    bias_send,
    bias_recv,
    ends,
    results,
    rows_recv,
    n1,
    n2,
    qkv,
    probs,
    attended,
    hidden,
    act,
    slope,
    pre_grad,
    m_grad,
    r_grad,
    head_grad,
    qkv_grad,
    part,
    part_recv,
    grads,
    grads_other,
    grads_y,
    grads_pair,
    grads_mid,
    small,
    small_other,
    small_y,
    small_pair,
    small_mid,
    local_sem,
    entry_send,
    entry_recv,
    weight_y_send,
    weight_y_recv,
    weight_z_send,
    weight_z_recv,
    part_send,
    part_recv_sem,
    cross_send,
    cross_recv,
    cross_core_send,
    cross_core_recv,
    leave_send,
    leave_recv,
    grad_y_send,
    grad_y_recv,
    grad_pair_send,
    grad_pair_recv,
    grad_mid_send,
    grad_mid_recv,
):
    s, d, m = lax.axis_index("section"), lax.axis_index("dp"), lax.axis_index("mp")
    core, chip = lax.rem(m, 2), lax.div(m, 2)
    half = lax.rem(d, 2)
    sibling = (s, d, 2 * chip + 1 - core)
    across_m = 2 * (1 - chip) + core
    across = (s, d, across_m)
    other_section = (1 - s, d, m)
    pair = (s, d + 1 - 2 * half, m)
    middle = (s, 3 - d, m)
    is_first, is_second = s == 0, s == 1
    is_mid = lax.div(d + 1, 2) == 1
    is_end = lax.div(d + 1, 2) != 1

    rows = boundary_ref.shape[2]
    length, width = n1.shape
    tile = length // TILES
    piece = tile // 2
    local_width = attended.shape[2]
    heads = local_width // HEAD_DIM
    scale = HEAD_DIM ** (-0.5)
    qkv_rows = 3 * local_width
    out_at, fc_at, proj_at = qkv_rows, qkv_rows + local_width, qkv_rows + local_width + width
    weight_rows = weights.shape[1]
    blocks = weight_rows // BLOCK

    partners = [sibling, across, other_section]
    if z_line:
        partners += [pair, middle]
    barrier = pltpu.get_barrier_semaphore()
    for device in partners:
        pl.semaphore_signal(barrier, inc=1, device_id=device, device_id_type=MESH)

    loads = [
        pltpu.make_async_copy(boundary_ref.at[0], raw, local_sem.at[0]),
        pltpu.make_async_copy(w_qkv_ref.at[0], stage, local_sem.at[1]),
        pltpu.make_async_copy(
            w_out_ref.at[0], weights.at[0, pl.ds(out_at, local_width)], local_sem.at[2]
        ),
        pltpu.make_async_copy(w_fc_ref.at[0], weights.at[0, pl.ds(fc_at, width)], local_sem.at[3]),
        pltpu.make_async_copy(
            w_proj_ref.at[0], weights.at[0, pl.ds(proj_at, weight_rows - proj_at)], local_sem.at[4]
        ),
    ]
    for load in loads:
        load.start()

    bias_send[...] = jnp.zeros_like(bias_send)
    bias_send[0:1, :] = fc_bias_ref[...]
    bias_send[1:2, 0:local_width] = qkv_bias_ref[0, 0:1, :]
    bias_send[2:3, 0:local_width] = qkv_bias_ref[0, 1:2, :]

    pl.semaphore_wait(barrier, len(partners))

    def token_rows(index):
        return pl.ds(pl.multiple_of(index * rows, rows), rows)

    entry_across = remote(
        slots.at[1 - chip],
        ends.at[s, token_rows(m)],
        entry_send.at[0],
        entry_recv.at[0],
        across,
    )
    entry_sibling = remote(
        slots.at[chip], ends.at[s, token_rows(m)], entry_send.at[1], entry_recv.at[1], sibling
    )
    entry_forward = remote(
        ends.at[s, token_rows(across_m)],
        ends.at[s, token_rows(across_m)],
        entry_send.at[2],
        entry_recv.at[2],
        sibling,
    )
    bias_copy = remote(bias_send, bias_recv, entry_send.at[3], entry_recv.at[3], across)

    loads[0].wait()
    for slot in range(2):
        picked = jnp.where(is_first, order_ref[0, slot], slot).astype(F32)
        slots[slot] = (
            raw[0].astype(F32) * (1.0 - picked) + raw[1].astype(F32) * picked
        ).astype(BF16)
    entry_across.start()
    entry_sibling.start()
    bias_copy.start()
    ends[pl.ds(s, 1), token_rows(m), :] = slots[pl.ds(chip, 1)]

    def entry_finish():
        entry_across.wait_recv()
        entry_forward.start()
        entry_sibling.wait_recv()
        entry_forward.wait_recv()

    y_blocks = blocks // 2 if z_line else blocks

    def weight_block(index):
        return pl.ds(pl.multiple_of(index * BLOCK, BLOCK), BLOCK)

    def near_block(step):
        return weight_block(2 * step + half if z_line else step)

    def weight_y(step):
        return remote(
            weights.at[0, near_block(step)],
            weights.at[1, near_block(step)],
            weight_y_send.at[step],
            weight_y_recv.at[step],
            across,
        )

    def weight_z(step):
        return remote(
            weights.at[1, near_block(step)],
            weights.at[1, near_block(step)],
            weight_z_send.at[step],
            weight_z_recv.at[step],
            pair,
        )

    def weight_pass(step):
        weight_y(step).wait_recv()
        if z_line:
            weight_z(step).start()

    def weight_pass_range(first, last):
        def step_of(step, carry):
            weight_pass(step)
            return carry

        lax.fori_loop(first, last, step_of, 0)

    def weight_need(first, last):
        if z_line:
            def step_of(step, carry):
                weight_z(step).wait_recv()
                return carry

            lax.fori_loop(first, last, step_of, 0)

    per_block = blocks // y_blocks

    def steps_of(row):
        return row // BLOCK // per_block

    loads[1].wait()
    for index in range(3):
        weights[0, index * local_width : (index + 1) * local_width, :] = stage[index].T
    for load in loads[2:]:
        load.wait()

    def weight_start(step, carry):
        weight_y(step).start()
        return carry

    lax.fori_loop(0, y_blocks, weight_start, 0)

    def cross(index):
        at = pl.ds(pl.multiple_of(index * tile + core * piece, piece), piece)
        return remote(
            results.at[s, at],
            ends.at[s, at],
            cross_send.at[index],
            cross_recv.at[index],
            other_section,
        )

    def cross_core(index):
        at = pl.ds(pl.multiple_of(index * tile + core * piece, piece), piece)
        return remote(
            ends.at[1 - s, at],
            ends.at[1 - s, at],
            cross_core_send.at[index],
            cross_core_recv.at[index],
            sibling,
        )

    def cross_receive():
        for index in range(TILES):
            cross(index).wait_recv()
            cross_core(index).start()
        for index in range(TILES):
            cross_core(index).wait_recv()

    def part_copy(which, index):
        at = pl.ds(index * tile, tile)
        return remote(
            part.at[which, at],
            part_recv.at[which, at],
            part_send.at[which, index],
            part_recv_sem.at[which, index],
            sibling,
        )

    def part_sum(which, index):
        at = slice(index * tile, (index + 1) * tile)
        return part[which, at, :].astype(F32) + part_recv[which, at, :].astype(F32)

    def weight_of(slot, first, count):
        return weights[slot, first : first + count, :]

    def tile_rows(index):
        return slice(index * tile, (index + 1) * tile)

    @pl.when(is_first)
    def _():
        entry_finish()

    @pl.when(is_second)
    def _():
        weight_pass_range(0, y_blocks)
        entry_finish()
        cross_receive()

    bias_copy.wait_recv()

    for index in range(TILES):
        at = tile_rows(index)
        hat, _ = normed(ends[0, at, :].astype(F32))
        n1[at, :] = (hat * ln1_gain_ref[...] + ln1_bias_ref[...]).astype(BF16)

    causal = lax.broadcasted_iota(jnp.int32, (length, length), 0) >= lax.broadcasted_iota(
        jnp.int32, (length, length), 1
    )

    def bias_of(slot, row, count):
        source = bias_send if slot == 0 else bias_recv
        return source[row : row + 1, 0:count]

    def head_columns(kind, head):
        first = kind * local_width + head * HEAD_DIM
        return slice(first, first + HEAD_DIM)

    def attention_forward(slot):
        queries = dot_nt(n1[...], weight_of(slot, 0, local_width)) + bias_of(slot, 1, local_width)
        qkv[slot, :, 0:local_width] = (queries.astype(BF16).astype(F32) * scale).astype(BF16)
        keys = dot_nt(n1[...], weight_of(slot, local_width, local_width))
        qkv[slot, :, local_width : 2 * local_width] = keys.astype(BF16)
        values = dot_nt(n1[...], weight_of(slot, 2 * local_width, local_width))
        values = values + bias_of(slot, 2, local_width)
        qkv[slot, :, 2 * local_width :] = values.astype(BF16)
        for head in range(heads):
            scores = dot_nt(
                qkv[slot, :, head_columns(0, head)], qkv[slot, :, head_columns(1, head)]
            )
            scores = jnp.where(causal, scores, NEGATIVE)
            raised = jnp.exp(scores - jnp.max(scores, axis=-1, keepdims=True))
            shares = raised * (1.0 / jnp.sum(raised, axis=-1, keepdims=True))
            probs[slot * heads + head] = shares.astype(BF16)
            attended[slot, :, head * HEAD_DIM : (head + 1) * HEAD_DIM] = dot_nn(
                probs[slot * heads + head], qkv[slot, :, head_columns(2, head)]
            ).astype(BF16)

    def first_passes(first, last):
        @pl.when(is_first)
        def _():
            weight_pass_range(first, last)

    out_step, fc_step = steps_of(out_at), steps_of(fc_at)
    proj_step = steps_of(proj_at)
    attention_forward(0)
    first_passes(0, out_step + 1)
    weight_need(0, out_step)
    attention_forward(1)
    first_passes(out_step + 1, fc_step + 2)
    weight_need(out_step, fc_step)
    for index in range(TILES):
        at = tile_rows(index)
        part[0, at, :] = (
            dot_nn(attended[0, at, :], weight_of(0, out_at, local_width))
            + dot_nn(attended[1, at, :], weight_of(1, out_at, local_width))
        ).astype(BF16)
        part_copy(0, index).start()
    for index in range(TILES):
        at = tile_rows(index)
        part_copy(0, index).wait_recv()
        held = ends[0, at, :].astype(F32) + BRANCH_SCALE * (
            part_sum(0, index) + out_bias_ref[...]
        )
        hidden[at, :] = held
        hat, _ = normed(held)
        n2[at, :] = (hat * ln2_gain_ref[...] + ln2_bias_ref[...]).astype(BF16)

    def activate(slot):
        for index in range(TILES):
            at = tile_rows(index)
            u = dot_nn(n2[at, :], weight_of(slot, fc_at, width)) + bias_of(slot, 0, act.shape[2])
            square = u * u
            bent = jnp.tanh(GELU_RATE * (u + GELU_CUBE * u * square))
            act[slot, at, :] = (0.5 * u * (1.0 + bent)).astype(BF16)
            slope[slot, at, :] = (
                0.5 * (1.0 + bent)
                + (0.5 * GELU_RATE)
                * u
                * (1.0 - bent * bent)
                * (1.0 + (3.0 * GELU_CUBE) * square)
            ).astype(BF16)

    activate(0)
    first_passes(fc_step + 2, proj_step + 1)
    weight_need(fc_step, proj_step)
    activate(1)
    first_passes(proj_step + 1, y_blocks)
    weight_need(proj_step, y_blocks)
    for index in range(TILES):
        at = tile_rows(index)
        part[1, at, :] = (
            dot_nn(act[0, at, :], weight_of(0, proj_at, act.shape[2]))
            + dot_nn(act[1, at, :], weight_of(1, proj_at, act.shape[2]))
        ).astype(BF16)
        part_copy(1, index).start()
    for index in range(TILES):
        at = tile_rows(index)
        part_copy(1, index).wait_recv()
        results[0, at, :] = (
            hidden[at, :] + BRANCH_SCALE * (part_sum(1, index) + proj_bias_ref[...])
        ).astype(BF16)

        @pl.when(is_first)
        def _():
            cross(index).start()

    @pl.when(is_first)
    def _():
        cross_receive()

    small[...] = jnp.zeros_like(small)
    small_other[...] = jnp.zeros_like(small_other)
    proj_grad_at, fc_grad_at = 0, act.shape[2]
    out_grad_at = fc_grad_at + width
    qkv_grad_at = out_grad_at + local_width

    def grad_y(step):
        return remote(
            grads_other.at[weight_block(step)],
            grads_y.at[weight_block(step)],
            grad_y_send.at[step],
            grad_y_recv.at[step],
            across,
        )

    def put_grads(first, count, value_of):
        grads_other[first : first + count, :] = value_of(1).astype(BF16)

        def start(step, carry):
            grad_y(step).start()
            return carry

        lax.fori_loop(first // BLOCK, (first + count) // BLOCK, start, 0)
        grads[first : first + count, :] = value_of(0).astype(BF16)

    for index in range(TILES):
        at = tile_rows(index)
        m_grad[at, :] = (BRANCH_SCALE * ends[1, at, :].astype(F32)).astype(BF16)
    put_grads(proj_grad_at, act.shape[2], lambda slot: dot_tn(act[slot], m_grad[...]))
    small[5:6, :] = column_sum(m_grad[...])
    for slot in range(2):
        target = small if slot == 0 else small_other
        for index in range(TILES):
            at = tile_rows(index)
            pre_grad[slot, at, :] = (
                slope[slot, at, :].astype(F32)
                * dot_nt(m_grad[at, :], weight_of(slot, proj_at, act.shape[2]))
            ).astype(BF16)
        target[6:7, :] = column_sum(pre_grad[slot])
    for index in range(TILES):
        at = tile_rows(index)
        part[2, at, :] = (
            dot_nt(pre_grad[0, at, :], weight_of(0, fc_at, width))
            + dot_nt(pre_grad[1, at, :], weight_of(1, fc_at, width))
        ).astype(BF16)
        part_copy(2, index).start()
    put_grads(fc_grad_at, width, lambda slot: dot_tn(n2[...], pre_grad[slot]))
    for index in range(TILES):
        at = tile_rows(index)
        part_copy(2, index).wait_recv()
        n2_grad = part_sum(2, index)
        hat, rate = normed(hidden[at, :])
        small[2:3, :] += column_sum(n2_grad * hat)
        small[3:4, :] += column_sum(n2_grad)
        held = ends[1, at, :].astype(F32) + norm_backward(n2_grad, hat, rate, ln2_gain_ref[...])
        hidden[at, :] = held
        r_grad[at, :] = (BRANCH_SCALE * held).astype(BF16)
    small[4:5, :] = column_sum(r_grad[...])
    put_grads(out_grad_at, local_width, lambda slot: dot_tn(attended[slot], r_grad[...]))

    for slot in range(2):
        head_grad[slot] = dot_nt(r_grad[...], weight_of(slot, out_at, local_width)).astype(BF16)
        for head in range(heads):
            columns = slice(head * HEAD_DIM, (head + 1) * HEAD_DIM)
            shares = probs[slot * heads + head]
            qkv_grad[slot, :, head_columns(2, head)] = dot_tn(
                shares, head_grad[slot, :, columns]
            ).astype(BF16)
            share_grad = dot_nt(head_grad[slot, :, columns], qkv[slot, :, head_columns(2, head)])
            wide = shares.astype(F32)
            product = wide * share_grad
            score_grad = (
                product - wide * jnp.sum(product, axis=-1, keepdims=True)
            ).astype(BF16)
            qkv_grad[slot, :, head_columns(0, head)] = (
                dot_nn(score_grad, qkv[slot, :, head_columns(1, head)]) * scale
            ).astype(BF16)
            qkv_grad[slot, :, head_columns(1, head)] = dot_tn(
                score_grad, qkv[slot, :, head_columns(0, head)]
            ).astype(BF16)
        target = small if slot == 0 else small_other
        target[7:8, 0:local_width] = column_sum(qkv_grad[slot, :, 0:local_width])
        target[7:8, 2 * local_width : 3 * local_width] = column_sum(
            qkv_grad[slot, :, 2 * local_width :]
        )
    for index in range(TILES):
        at = tile_rows(index)
        part[3, at, :] = (
            dot_nn(qkv_grad[0, at, :], weight_of(0, 0, qkv_rows))
            + dot_nn(qkv_grad[1, at, :], weight_of(1, 0, qkv_rows))
        ).astype(BF16)
        part_copy(3, index).start()
    put_grads(qkv_grad_at, qkv_rows, lambda slot: dot_tn(qkv_grad[slot], n1[...]))
    for index in range(TILES):
        at = tile_rows(index)
        part_copy(3, index).wait_recv()
        n1_grad = part_sum(3, index)
        hat, rate = normed(ends[0, at, :].astype(F32))
        small[0:1, :] += column_sum(n1_grad * hat)
        small[1:2, :] += column_sum(n1_grad)
        results[1, at, :] = (
            hidden[at, :] + norm_backward(n1_grad, hat, rate, ln1_gain_ref[...])
        ).astype(BF16)

        @pl.when(is_second)
        def _():
            cross(index).start()

    leave = remote(
        results.at[1 - s, token_rows(across_m)], rows_recv, leave_send.at[0], leave_recv.at[0], across
    )
    leave.start()
    small_y_copy = remote(small_other, small_y, leave_send.at[1], leave_recv.at[1], across)
    small_other[0:6, :] = small[0:6, :]
    small_y_copy.start()

    def grad_pair(step, source):
        return remote(
            source.at[weight_block(step)],
            grads_pair.at[weight_block(step)],
            grad_pair_send.at[step],
            grad_pair_recv.at[step],
            pair,
        )

    def grad_mid(step):
        return remote(
            grads.at[weight_block(step)],
            grads_mid.at[weight_block(step)],
            grad_mid_send.at[step],
            grad_mid_recv.at[step],
            middle,
        )

    def add_into(target, source, step):
        at = weight_block(step)
        target[at, :] = (target[at, :].astype(F32) + source[at, :].astype(F32)).astype(BF16)

    def gather_y(step):
        grad_y(step).wait_recv()
        add_into(grads, grads_y, step)

    def send_up(step):
        gather_y(step)

        @pl.when(is_end)
        def _():
            grad_pair(step, grads).start()

        @pl.when(is_mid)
        def _():
            grad_pair(step, grads).wait_recv()
            add_into(grads, grads_pair, step)
            grad_mid(step).start()

    def send_down(step):
        @pl.when(is_mid)
        def _():
            grad_mid(step).wait_recv()
            add_into(grads_mid, grads, step)
            grad_pair(step, grads_mid).start()

    if z_line:
        send_up(0)

        def stream(step, carry):
            send_up(step)
            send_down(step - 1)
            return carry

        lax.fori_loop(1, blocks, stream, 0)
        send_down(blocks - 1)
    else:
        def stream(step, carry):
            gather_y(step)
            return carry

        lax.fori_loop(0, blocks, stream, 0)

    small_y_copy.wait_recv()
    small[...] += small_y[...]
    if z_line:
        small_up = remote(small, small_pair, leave_send.at[2], leave_recv.at[2], pair)
        small_across = remote(small, small_mid, leave_send.at[3], leave_recv.at[3], middle)
        small_down = remote(small_mid, small_pair, leave_send.at[2], leave_recv.at[2], pair)

        @pl.when(is_end)
        def _():
            small_up.start()
            small_down.wait_recv()
            small_out[...] = small_pair[...]
            small_up.wait_send()

        @pl.when(is_mid)
        def _():
            small_up.wait_recv()
            small[...] += small_pair[...]
            small_across.start()
            small_across.wait_recv()
            small_mid[...] += small[...]
            small_down.start()
            small_out[...] = small_mid[...]
            small_across.wait_send()
            small_down.wait_send()
    else:
        small_out[...] = small[...]

    leave.wait_recv()
    rows_out[pl.ds(chip, 1)] = results[pl.ds(1 - s, 1), token_rows(m), :].astype(F32)
    rows_out[pl.ds(1 - chip, 1)] = rows_recv[...].astype(F32)[None]

    def write(source):
        proj_out[...] = source[proj_grad_at : proj_grad_at + act.shape[2], :]
        fc_out[...] = source[fc_grad_at : fc_grad_at + width, :]
        out_out[...] = source[out_grad_at : out_grad_at + local_width, :]
        for index in range(3):
            first = qkv_grad_at + index * local_width
            qkv_out[index] = source[first : first + local_width, :].T

    if z_line:
        @pl.when(is_end)
        def _():
            def step_of(step, carry):
                grad_pair(step, grads_mid).wait_recv()
                return carry

            lax.fori_loop(0, blocks, step_of, 0)
            write(grads_pair)

        @pl.when(is_mid)
        def _():
            write(grads_mid)
    else:
        write(grads)

    entry_across.wait_send()
    entry_sibling.wait_send()
    entry_forward.wait_send()
    bias_copy.wait_send()
    leave.wait_send()
    small_y_copy.wait_send()

    def weights_sent(step, carry):
        weight_y(step).wait_send()
        if z_line:
            weight_z(step).wait_send()
        return carry

    lax.fori_loop(0, y_blocks, weights_sent, 0)

    def grads_sent(step, carry):
        grad_y(step).wait_send()
        if z_line:
            grad_pair(step, grads).wait_send()
        return carry

    lax.fori_loop(0, blocks, grads_sent, 0)
    if z_line:
        @pl.when(is_mid)
        def _():
            def step_of(step, carry):
                grad_mid(step).wait_send()
                return carry

            lax.fori_loop(0, blocks, step_of, 0)

    for which in range(4):
        for index in range(TILES):
            part_copy(which, index).wait_send()
    for index in range(TILES):
        cross(index).wait_send()
        cross_core(index).wait_send()


def local(
    z_line,
    boundary_in,
    order,
    ln1_gain,
    ln1_bias,
    w_qkv,
    qkv_bias,
    w_out,
    out_bias,
    ln2_gain,
    ln2_bias,
    w_fc,
    fc_bias,
    w_proj,
    proj_bias,
):
    _, micro, rows, width = boundary_in.shape
    local_width = w_qkv.shape[-1]
    local_units = w_fc.shape[-1]
    length = rows * lax.axis_size("mp")
    heads = local_width // HEAD_DIM
    weight_rows = 4 * local_width + width + local_units
    blocks = weight_rows // BLOCK
    vmem = pltpu.VMEM
    dma = pltpu.SemaphoreType.DMA
    in_vmem = pl.BlockSpec(memory_space=pltpu.VMEM)
    in_any = pl.BlockSpec(memory_space=pl.ANY)
    in_smem = pl.BlockSpec(memory_space=pltpu.SMEM)
    outs = pl.pallas_call(
        functools.partial(kernel, z_line),
        out_shape=(
            jax.ShapeDtypeStruct((micro, rows, width), F32),
            jax.ShapeDtypeStruct((8, width), F32),
            jax.ShapeDtypeStruct((3, width, local_width), BF16),
            jax.ShapeDtypeStruct((local_width, width), BF16),
            jax.ShapeDtypeStruct((width, local_units), BF16),
            jax.ShapeDtypeStruct((local_units, width), BF16),
        ),
        in_specs=[
            in_smem,
            in_any,
            in_vmem,
            in_vmem,
            in_any,
            in_vmem,
            in_any,
            in_vmem,
            in_vmem,
            in_vmem,
            in_any,
            in_vmem,
            in_any,
            in_vmem,
        ],
        out_specs=(in_vmem,) * 6,
        scratch_shapes=[
            vmem((micro, rows, width), BF16),
            vmem((micro, rows, width), BF16),
            vmem((3, width, local_width), BF16),
            vmem((2, weight_rows, width), BF16),
            vmem((8, width), F32),
            vmem((8, width), F32),
            vmem((2, length, width), BF16),
            vmem((2, length, width), BF16),
            vmem((rows, width), BF16),
            vmem((length, width), BF16),
            vmem((length, width), BF16),
            vmem((2, length, 3 * local_width), BF16),
            vmem((2 * heads, length, length), BF16),
            vmem((2, length, local_width), BF16),
            vmem((length, width), F32),
            vmem((2, length, local_units), BF16),
            vmem((2, length, local_units), BF16),
            vmem((2, length, local_units), BF16),
            vmem((length, width), BF16),
            vmem((length, width), BF16),
            vmem((2, length, local_width), BF16),
            vmem((2, length, 3 * local_width), BF16),
            vmem((4, length, width), BF16),
            vmem((4, length, width), BF16),
            vmem((weight_rows, width), BF16),
            vmem((weight_rows, width), BF16),
            vmem((weight_rows, width), BF16),
            vmem((weight_rows, width), BF16),
            vmem((weight_rows, width), BF16),
            vmem((8, width), F32),
            vmem((8, width), F32),
            vmem((8, width), F32),
            vmem((8, width), F32),
            vmem((8, width), F32),
            dma((5,)),
            dma((4,)),
            dma((4,)),
            dma((blocks,)),
            dma((blocks,)),
            dma((blocks,)),
            dma((blocks,)),
            dma((4, TILES)),
            dma((4, TILES)),
            dma((TILES,)),
            dma((TILES,)),
            dma((TILES,)),
            dma((TILES,)),
            dma((4,)),
            dma((4,)),
            dma((blocks,)),
            dma((blocks,)),
            dma((blocks,)),
            dma((blocks,)),
            dma((blocks,)),
            dma((blocks,)),
        ],
        compiler_params=pltpu.CompilerParams(
            collective_id=0, has_side_effects=True, vmem_limit_bytes=62 * 2**20
        ),
        name="two_layers",
    )(
        order,
        boundary_in,
        ln1_gain,
        ln1_bias,
        w_qkv,
        qkv_bias,
        w_out,
        out_bias,
        ln2_gain,
        ln2_bias,
        w_fc,
        fc_bias,
        w_proj,
        proj_bias,
    )
    out_rows, small, qkv_grad, out_grad, fc_grad, proj_grad = outs
    if not z_line:
        small, qkv_grad, out_grad, fc_grad, proj_grad = lax.psum(
            (small, qkv_grad, out_grad, fc_grad, proj_grad), "dp"
        )
    qkv_bias_grad = jnp.stack(
        [small[7, 0:local_width], small[7, 2 * local_width : 3 * local_width]]
    )
    return (
        out_rows[None],
        small[0:1],
        small[1:2],
        qkv_grad.astype(F32)[None],
        qkv_bias_grad[None],
        out_grad.astype(F32)[None],
        small[4:5],
        small[2:3],
        small[3:4],
        fc_grad.astype(F32)[None],
        small[6:7],
        proj_grad.astype(F32)[None],
        small[5:6],
    )


def solution(mesh):
    return jax.shard_map(
        functools.partial(local, mesh.shape["dp"] == 4),
        mesh=mesh,
        in_specs=(
            P("section", "dp", "mp", None),
            P("dp", None),
            P("section", None),
            P("section", None),
            P("section", None, None, "mp"),
            P("section", None, "mp"),
            P("section", "mp", None),
            P("section", None),
            P("section", None),
            P("section", None),
            P("section", None, "mp"),
            P("section", "mp"),
            P("section", "mp", None),
            P("section", None),
        ),
        out_specs=(
            P("section", "dp", "mp", None),
            P("section", None),
            P("section", None),
            P("section", None, None, "mp"),
            P("section", None, "mp"),
            P("section", "mp", None),
            P("section", None),
            P("section", None),
            P("section", None),
            P("section", None, "mp"),
            P("section", "mp"),
            P("section", "mp", None),
            P("section", None),
        ),
        check_vma=False,
    )
```

```python
import functools

import jax
import jax.numpy as jnp
from jax import lax
from jax.experimental import pallas as pl
from jax.experimental.pallas import tpu as pltpu
from jax.sharding import PartitionSpec as P

HEAD_DIM = 64
BRANCH_SCALE = 0.14433756729740643
NORM_EPS = 1e-05
GELU_RATE = 0.7978845608028654
GELU_CUBE = 0.044715
NEGATIVE = -1e30
BLOCK = 96
TILES = 4
MESH = pl.DeviceIdType.MESH
BF16 = jnp.bfloat16
F32 = jnp.float32


def dot_nn(a, b):
    return lax.dot_general(a, b, (((1,), (0,)), ((), ())), preferred_element_type=F32)


def dot_nt(a, b):
    return lax.dot_general(a, b, (((1,), (1,)), ((), ())), preferred_element_type=F32)


def dot_tn(a, b):
    return lax.dot_general(a, b, (((0,), (0,)), ((), ())), preferred_element_type=F32)


def normed(values):
    center = values - jnp.mean(values, axis=-1, keepdims=True)
    rate = lax.rsqrt(jnp.mean(center * center, axis=-1, keepdims=True) + NORM_EPS)
    return center * rate, rate


def norm_backward(grad, hat, rate, gain):
    scaled = grad * gain
    return rate * (
        scaled
        - jnp.mean(scaled, axis=-1, keepdims=True)
        - hat * jnp.mean(scaled * hat, axis=-1, keepdims=True)
    )


def column_sum(values):
    return jnp.sum(values.astype(F32), axis=0, keepdims=True)


def remote(src, dst, send_sem, recv_sem, device):
    return pltpu.make_async_remote_copy(
        src_ref=src,
        dst_ref=dst,
        send_sem=send_sem,
        recv_sem=recv_sem,
        device_id=device,
        device_id_type=MESH,
    )


def kernel(
    z_line,
    order_ref,
    boundary_ref,
    ln1_gain_ref,
    ln1_bias_ref,
    w_qkv_ref,
    qkv_bias_ref,
    w_out_ref,
    out_bias_ref,
    ln2_gain_ref,
    ln2_bias_ref,
    w_fc_ref,
    fc_bias_ref,
    w_proj_ref,
    proj_bias_ref,
    rows_out,
    small_out,
    grads_out,
    raw,
    slots,
    weights,
    biases,
    ends,
    results,
    rows_recv,
    n1,
    n2,
    qkv,
    probs,
    attended,
    hidden,
    act,
    slope,
    pre_grad,
    m_grad,
    r_grad,
    head_grad,
    qkv_grad,
    part,
    far_part,
    part_recv,
    grads,
    grads_other,
    grads_y,
    grads_pair,
    grads_mid,
    small,
    small_other,
    small_y,
    small_pair,
    small_mid,
    local_sem,
    entry_send,
    entry_recv,
    weight_y_send,
    weight_y_recv,
    weight_z_send,
    weight_z_recv,
    part_send,
    part_recv_sem,
    far_core_send,
    far_core_recv,
    far_send,
    far_recv,
    far_back_send,
    far_back_recv,
    share_send,
    share_recv,
    share_core_send,
    share_core_recv,
    cross_send,
    cross_recv,
    cross_core_send,
    cross_core_recv,
    leave_send,
    leave_recv,
    grad_y_send,
    grad_y_recv,
    grad_pair_send,
    grad_pair_recv,
    grad_mid_send,
    grad_mid_recv,
    grad_out_sem,
):
    s, d, m = lax.axis_index("section"), lax.axis_index("dp"), lax.axis_index("mp")
    core, chip = lax.rem(m, 2), lax.div(m, 2)
    half = lax.rem(d, 2)
    across_m = 2 * (1 - chip) + core
    sibling = (s, d, 2 * chip + 1 - core)
    across = (s, d, across_m)
    other_section = (1 - s, d, m)
    pair = (s, d + 1 - 2 * half, m)
    middle = (s, 3 - d, m)
    is_first, is_second = s == 0, s == 1
    is_mid = lax.div(d + 1, 2) == 1
    is_end = lax.div(d + 1, 2) != 1

    rows = boundary_ref.shape[2]
    length, width = n1.shape[1:]
    tile = length // TILES
    piece = tile // 2
    big = 2 * tile
    local_width = attended.shape[2]
    units = act.shape[2]
    heads = local_width // HEAD_DIM
    scale = HEAD_DIM ** (-0.5)
    qkv_rows = 3 * local_width
    out_at, fc_at, proj_at = qkv_rows, qkv_rows + local_width, qkv_rows + local_width + width
    weight_rows = weights.shape[1]
    blocks = weight_rows // BLOCK
    ends_in, ends_grad = 2 * s, 2 * (1 - s)

    def set_rows(index):
        return index * (1 - s)

    def set_weights(index):
        return index * s

    def tile_rows(index):
        return slice(index * tile, (index + 1) * tile)

    def big_rows(index):
        return slice(index * big, (index + 1) * big)

    def piece_rows(index, which):
        return pl.ds(pl.multiple_of(index * tile + which * piece, piece), piece)

    partners = [sibling, across, other_section]
    if z_line:
        partners += [pair, middle]
    barrier = pltpu.get_barrier_semaphore()
    for device in partners:
        pl.semaphore_signal(barrier, inc=1, device_id=device, device_id_type=MESH)

    loads = [
        pltpu.make_async_copy(boundary_ref.at[0], raw, local_sem.at[0]),
        pltpu.make_async_copy(
            w_qkv_ref.at[0], weights.at[0, pl.ds(0, qkv_rows)], local_sem.at[1]
        ),
        pltpu.make_async_copy(
            w_out_ref.at[0], weights.at[0, pl.ds(out_at, local_width)], local_sem.at[2]
        ),
        pltpu.make_async_copy(w_fc_ref.at[0], weights.at[0, pl.ds(fc_at, width)], local_sem.at[3]),
        pltpu.make_async_copy(
            w_proj_ref.at[0], weights.at[0, pl.ds(proj_at, units)], local_sem.at[4]
        ),
    ]
    for load in loads:
        load.start()

    biases[0] = jnp.zeros_like(biases[0])
    biases[0, 0:1, :] = fc_bias_ref[...]
    biases[0, 1:2, 0:local_width] = qkv_bias_ref[0, 0:1, :]
    biases[0, 2:3, 0:local_width] = qkv_bias_ref[0, 1:2, :]
    small[...] = jnp.zeros_like(small)
    small_other[...] = jnp.zeros_like(small_other)

    loads[0].wait()
    for slot in range(2):
        picked = jnp.where(is_first, order_ref[0, slot], slot).astype(F32)
        slots[slot] = (
            raw[0].astype(F32) * (1.0 - picked) + raw[1].astype(F32) * picked
        ).astype(BF16)

    pl.semaphore_wait(barrier, len(partners))

    def token_rows(index):
        return pl.ds(pl.multiple_of(index * rows, rows), rows)

    def entry_across(which):
        slot = 1 - chip if which == 0 else chip
        return remote(
            slots.at[slot],
            ends.at[which, token_rows(m)],
            entry_send.at[which],
            entry_recv.at[which],
            across,
        )

    def entry_sibling(which):
        slot = chip if which == 0 else 1 - chip
        return remote(
            slots.at[slot],
            ends.at[which, token_rows(m)],
            entry_send.at[2 + which],
            entry_recv.at[2 + which],
            sibling,
        )

    def entry_forward(which):
        at = token_rows(across_m)
        return remote(
            ends.at[which, at],
            ends.at[which, at],
            entry_send.at[4 + which],
            entry_recv.at[4 + which],
            sibling,
        )

    bias_copy = remote(biases.at[0], biases.at[1], entry_send.at[6], entry_recv.at[6], across)

    def entry_start(which):
        entry_across(which).start()
        entry_sibling(which).start()
        slot = chip if which == 0 else 1 - chip
        ends[which, token_rows(m), :] = slots[slot]

    def entry_finish(which):
        entry_across(which).wait_recv()
        entry_forward(which).start()
        entry_sibling(which).wait_recv()
        entry_forward(which).wait_recv()

    entry_start(0)

    @pl.when(is_first)
    def _():
        entry_start(1)

    y_blocks = blocks // 2 if z_line else blocks

    def weight_block(index):
        return pl.ds(pl.multiple_of(index * BLOCK, BLOCK), BLOCK)

    def near_block(step):
        return weight_block(2 * step + half if z_line else step)

    def weight_y(step):
        return remote(
            weights.at[0, near_block(step)],
            weights.at[1, near_block(step)],
            weight_y_send.at[step],
            weight_y_recv.at[step],
            across,
        )

    def weight_z(step):
        return remote(
            weights.at[1, near_block(step)],
            weights.at[1, near_block(step)],
            weight_z_send.at[step],
            weight_z_recv.at[step],
            pair,
        )

    def repeat(first, last, action):
        def step_of(step, carry):
            action(step)
            return carry

        lax.fori_loop(first, last, step_of, 0)

    def weight_pass(step):
        weight_y(step).wait_recv()
        if z_line:
            weight_z(step).start()

    for load in loads[1:]:
        load.wait()

    def cross(index):
        at = piece_rows(index, core)
        return remote(
            results.at[s, at],
            ends.at[2, at],
            cross_send.at[index],
            cross_recv.at[index],
            other_section,
        )

    def cross_core(index):
        at = piece_rows(index, core)
        return remote(
            ends.at[2, at],
            ends.at[2, at],
            cross_core_send.at[index],
            cross_core_recv.at[index],
            sibling,
        )

    shared = (n2, m_grad, r_grad)

    def share(which, index):
        at = piece_rows(index, core)
        return remote(
            shared[which].at[0, at],
            shared[which].at[1, at],
            share_send.at[which, index],
            share_recv.at[which, index],
            across,
        )

    def share_core(which, index):
        at = piece_rows(index, core)
        return remote(
            shared[which].at[1, at],
            shared[which].at[1, at],
            share_core_send.at[which, index],
            share_core_recv.at[which, index],
            sibling,
        )

    def share_finish(which, index):
        share(which, index).wait_recv()
        share_core(which, index).start()
        share_core(which, index).wait_recv()

    def part_copy(which, index):
        at = pl.ds(index * tile, tile)
        return remote(
            part.at[which, at],
            part_recv.at[which, at],
            part_send.at[which, index],
            part_recv_sem.at[which, index],
            sibling,
        )

    def spare_rows(which, index, core_of):
        return pl.ds(
            pl.multiple_of(which * length + index * tile + core_of * piece, piece), piece
        )

    def far_core(which, index):
        return remote(
            far_part.at[which, piece_rows(index, 1 - core)],
            grads_other.at[spare_rows(which, index, 1 - core)],
            far_core_send.at[which, index],
            far_core_recv.at[which, index],
            sibling,
        )

    def far(which, index):
        return remote(
            far_part.at[which, piece_rows(index, core)],
            weights.at[1, spare_rows(which, index, core)],
            far_send.at[which, index],
            far_recv.at[which, index],
            across,
        )

    def far_back(which, index):
        at = spare_rows(which, index, core)
        return remote(
            weights.at[1, at],
            weights.at[1, at],
            far_back_send.at[which, index],
            far_back_recv.at[which, index],
            sibling,
        )

    def far_pass(which, index):
        far_core(which, index).wait_recv()
        at = piece_rows(index, core)
        far_part[which, at, :] = (
            far_part[which, at, :].astype(F32)
            + grads_other[spare_rows(which, index, core), :].astype(F32)
        ).astype(BF16)
        far(which, index).start()

    def part_sum(which, index):
        at = tile_rows(index)
        near = part[which, at, :].astype(F32) + part_recv[which, at, :].astype(F32)
        first = which * length + index * tile
        other = weights[1, first : first + tile, :].astype(F32)
        return near + jnp.where(is_first, other, 0.0)

    def reduce_parts(which, value_of, finish, before=None, step=tile, between=None):
        spans = [slice(first, first + step) for first in range(0, length, step)]
        per = step // tile

        @pl.when(is_second)
        def _():
            for number, at in enumerate(spans):
                part[which, at, :] = (value_of(0, 0, at) + value_of(1, 1, at)).astype(BF16)
                for index in range(number * per, (number + 1) * per):
                    part_copy(which, index).start()

        @pl.when(is_first)
        def _():
            for number, at in enumerate(spans):
                for index in range(number * per, (number + 1) * per):
                    if before is not None:
                        before(index)
                far_part[which, at, :] = value_of(1, 0, at).astype(BF16)
                for index in range(number * per, (number + 1) * per):
                    far_core(which, index).start()
                    if index > 0:
                        far_pass(which, index - 1)
            part[which, spans[0], :] = value_of(0, 0, spans[0]).astype(BF16)
            far_pass(which, TILES - 1)
            for number, at in enumerate(spans):
                if number > 0:
                    part[which, at, :] = value_of(0, 0, at).astype(BF16)
                for index in range(number * per, (number + 1) * per):
                    part_copy(which, index).start()

        if between is not None:
            between()
        for index in range(TILES + 1):
            if index < TILES:
                @pl.when(is_first)
                def _():
                    far(which, index).wait_recv()
                    far_back(which, index).start()

            if index > 0:
                @pl.when(is_first)
                def _():
                    far_back(which, index - 1).wait_recv()

                part_copy(which, index - 1).wait_recv()
                finish(index - 1)

    def weight_of(shards, first, count):
        return weights[shards, first : first + count, :]

    @pl.when(is_second)
    def _():
        repeat(0, y_blocks, lambda step: weight_y(step).start())
        bias_copy.start()
        repeat(0, y_blocks, weight_pass)
        if z_line:
            repeat(0, y_blocks, lambda step: weight_z(step).wait_recv())
        bias_copy.wait_recv()

    entry_finish(0)

    def norm_one(which, source, index):
        at = tile_rows(index)
        hat, _ = normed(ends[source, at, :].astype(F32))
        n1[which, at, :] = (hat * ln1_gain_ref[...] + ln1_bias_ref[...]).astype(BF16)

    @pl.when(is_second)
    def _():
        for index in range(TILES + 1):
            if index < TILES:
                cross(index).wait_recv()
                cross_core(index).start()
            if index > 0:
                cross_core(index - 1).wait_recv()
                norm_one(0, 2, index - 1)

    @pl.when(is_first)
    def _():
        for index in range(TILES):
            norm_one(0, 0, index)

    causal = lax.broadcasted_iota(jnp.int32, (length, length), 0) >= lax.broadcasted_iota(
        jnp.int32, (length, length), 1
    )

    def bias_of(shards, row, count):
        return biases[shards, row : row + 1, 0:count]

    def head_columns(kind, head):
        first = kind * local_width + head * HEAD_DIM
        return slice(first, first + HEAD_DIM)

    def attention_forward(index):
        source, shards = set_rows(index), set_weights(index)
        queries = dot_nt(n1[source], weight_of(shards, 0, local_width))
        queries = queries + bias_of(shards, 1, local_width)
        qkv[index, :, 0:local_width] = (queries.astype(BF16).astype(F32) * scale).astype(BF16)
        keys = dot_nt(n1[source], weight_of(shards, local_width, local_width))
        qkv[index, :, local_width : 2 * local_width] = keys.astype(BF16)
        values = dot_nt(n1[source], weight_of(shards, 2 * local_width, local_width))
        values = values + bias_of(shards, 2, local_width)
        qkv[index, :, 2 * local_width :] = values.astype(BF16)
        for head in range(heads):
            scores = dot_nt(
                qkv[index, :, head_columns(0, head)], qkv[index, :, head_columns(1, head)]
            )
            scores = jnp.where(causal, scores, NEGATIVE)
            raised = jnp.exp(scores - jnp.max(scores, axis=-1, keepdims=True))
            shares = raised * (1.0 / jnp.sum(raised, axis=-1, keepdims=True))
            probs[index * heads + head] = shares.astype(BF16)
            attended[index, :, head * HEAD_DIM : (head + 1) * HEAD_DIM] = dot_nn(
                probs[index * heads + head], qkv[index, :, head_columns(2, head)]
            ).astype(BF16)

    attention_forward(0)

    @pl.when(is_first)
    def _():
        entry_finish(1)
        for index in range(TILES):
            norm_one(1, 1, index)

    attention_forward(1)

    def attention_out(index):
        at = tile_rows(index)
        held = ends[ends_in, at, :].astype(F32) + BRANCH_SCALE * (
            part_sum(0, index) + out_bias_ref[...]
        )
        hidden[at, :] = held
        hat, _ = normed(held)
        n2[0, at, :] = (hat * ln2_gain_ref[...] + ln2_bias_ref[...]).astype(BF16)

        @pl.when(is_first)
        def _():
            share(0, index).start()

    reduce_parts(
        0,
        lambda index, shards, at: dot_nn(
            attended[index, at, :], weight_of(shards, out_at, local_width)
        ),
        attention_out,
    )

    def activate(index, source, shards, at):
        u = dot_nn(n2[source, at, :], weight_of(shards, fc_at, width)) + bias_of(shards, 0, units)
        square = u * u
        bent = jnp.tanh(GELU_RATE * (u + GELU_CUBE * u * square))
        act[index, at, :] = (0.5 * u * (1.0 + bent)).astype(BF16)
        slope[index, at, :] = (
            0.5 * (1.0 + bent)
            + (0.5 * GELU_RATE) * u * (1.0 - bent * bent) * (1.0 + (3.0 * GELU_CUBE) * square)
        ).astype(BF16)

    for index in range(length // big):
        activate(0, 0, 0, big_rows(index))

    @pl.when(is_second)
    def _():
        for index in range(length // big):
            activate(1, 0, 1, big_rows(index))

    def other_activate(index):
        share_finish(0, index)
        activate(1, 1, 0, tile_rows(index))

    def layer_out(index):
        at = tile_rows(index)
        results[0, at, :] = (
            hidden[at, :] + BRANCH_SCALE * (part_sum(1, index) + proj_bias_ref[...])
        ).astype(BF16)

        @pl.when(is_first)
        def _():
            cross(index).start()

    reduce_parts(
        1,
        lambda index, shards, at: dot_nn(act[index, at, :], weight_of(shards, proj_at, units)),
        layer_out,
        before=other_activate,
    )

    def scale_grad(index):
        at = tile_rows(index)
        m_grad[0, at, :] = (BRANCH_SCALE * ends[ends_grad, at, :].astype(F32)).astype(BF16)

    @pl.when(is_first)
    def _():
        for index in range(TILES + 1):
            if index < TILES:
                cross(index).wait_recv()
                cross_core(index).start()
            if index > 0:
                cross_core(index - 1).wait_recv()
                scale_grad(index - 1)
                share(1, index - 1).start()
        for index in range(TILES):
            share_finish(1, index)

    @pl.when(is_second)
    def _():
        for index in range(TILES):
            scale_grad(index)

    proj_grad_at, fc_grad_at = 0, units
    out_grad_at = fc_grad_at + width
    qkv_grad_at = out_grad_at + local_width

    def grad_y(step):
        return remote(
            grads_other.at[weight_block(step)],
            grads_y.at[weight_block(step)],
            grad_y_send.at[step],
            grad_y_recv.at[step],
            across,
        )

    def grad_pair(step, source):
        return remote(
            source.at[weight_block(step)],
            grads_pair.at[weight_block(step)],
            grad_pair_send.at[step],
            grad_pair_recv.at[step],
            pair,
        )

    def grad_mid(step):
        return remote(
            grads.at[weight_block(step)],
            grads_mid.at[weight_block(step)],
            grad_mid_send.at[step],
            grad_mid_recv.at[step],
            middle,
        )

    def grad_out(step, source):
        at = weight_block(step)
        return pltpu.make_async_copy(source.at[at], grads_out.at[at], grad_out_sem.at[step])

    def add_into(target, source, step):
        at = weight_block(step)
        target[at, :] = (target[at, :].astype(F32) + source[at, :].astype(F32)).astype(BF16)

    def gather_y(step):
        grad_y(step).wait_recv()
        add_into(grads, grads_y, step)

    def mid_up(step):
        grad_pair(step, grads).wait_recv()
        add_into(grads, grads_pair, step)
        grad_mid(step).start()

    def mid_down(step):
        grad_mid(step).wait_recv()
        add_into(grads_mid, grads, step)
        grad_pair(step, grads_mid).start()
        grad_out(step, grads_mid).start()

    def stream_ends(first, last):
        if z_line:
            @pl.when(jnp.logical_and(is_first, is_end))
            def _():
                repeat(first, last, lambda step: grad_pair(step, grads).start())

    def stream_mids(first, last):
        if z_line:
            @pl.when(jnp.logical_and(is_first, is_mid))
            def _():
                if first == 0:
                    mid_up(0)

                def both(step):
                    mid_up(step)
                    mid_down(step - 1)

                repeat(max(first, 1), last, both)

    def put_grads(first, count, value_of):
        @pl.when(is_second)
        def _():
            grads_other[first : first + count, :] = value_of(1).astype(BF16)
            repeat(first // BLOCK, (first + count) // BLOCK, lambda step: grad_y(step).start())
            grads[first : first + count, :] = value_of(0).astype(BF16)

        @pl.when(is_first)
        def _():
            grads[first : first + count, :] = (value_of(0) + value_of(1)).astype(BF16)

        stream_ends(first // BLOCK, (first + count) // BLOCK)

    def set_sum(row, column, index, values):
        total = column_sum(values)
        columns = slice(column, column + total.shape[1])
        if index == 0:
            small[row : row + 1, columns] += total
        else:
            @pl.when(is_first)
            def _():
                small[row : row + 1, columns] += total

            @pl.when(is_second)
            def _():
                small_other[row : row + 1, columns] += total

    put_grads(proj_grad_at, units, lambda index: dot_tn(act[index], m_grad[set_rows(index)]))
    small[5:6, :] = column_sum(m_grad[0])

    for index in range(2):
        for number in range(length // big):
            at = big_rows(number)
            pre_grad[index, at, :] = (
                slope[index, at, :].astype(F32)
                * dot_nt(
                    m_grad[set_rows(index), at, :], weight_of(set_weights(index), proj_at, units)
                )
            ).astype(BF16)
        set_sum(6, 0, index, pre_grad[index])

    def mlp_back(index):
        at = tile_rows(index)
        n2_grad = part_sum(2, index)
        hat, rate = normed(hidden[at, :])
        small[2:3, :] += column_sum(n2_grad * hat)
        small[3:4, :] += column_sum(n2_grad)
        held = ends[ends_grad, at, :].astype(F32) + norm_backward(
            n2_grad, hat, rate, ln2_gain_ref[...]
        )
        hidden[at, :] = held
        r_grad[0, at, :] = (BRANCH_SCALE * held).astype(BF16)

        @pl.when(is_first)
        def _():
            share(2, index).start()

    def mlp_weights():
        put_grads(fc_grad_at, width, lambda index: dot_tn(n2[set_rows(index)], pre_grad[index]))
        stream_mids(0, 2)

    reduce_parts(
        2,
        lambda index, shards, at: dot_nt(pre_grad[index, at, :], weight_of(shards, fc_at, width)),
        mlp_back,
        step=big,
        between=mlp_weights,
    )
    small[4:5, :] = column_sum(r_grad[0])

    def attention_backward(index):
        shards = set_weights(index)
        head_grad[index] = dot_nt(
            r_grad[set_rows(index)], weight_of(shards, out_at, local_width)
        ).astype(BF16)
        for head in range(heads):
            columns = slice(head * HEAD_DIM, (head + 1) * HEAD_DIM)
            shares = probs[index * heads + head]
            qkv_grad[index, :, head_columns(2, head)] = dot_tn(
                shares, head_grad[index, :, columns]
            ).astype(BF16)
            share_grad = dot_nt(head_grad[index, :, columns], qkv[index, :, head_columns(2, head)])
            wide = shares.astype(F32)
            product = wide * share_grad
            score_grad = (
                product - wide * jnp.sum(product, axis=-1, keepdims=True)
            ).astype(BF16)
            qkv_grad[index, :, head_columns(0, head)] = (
                dot_nn(score_grad, qkv[index, :, head_columns(1, head)]) * scale
            ).astype(BF16)
            qkv_grad[index, :, head_columns(1, head)] = dot_tn(
                score_grad, qkv[index, :, head_columns(0, head)]
            ).astype(BF16)
        set_sum(7, 0, index, qkv_grad[index, :, 0:local_width])
        set_sum(7, 2 * local_width, index, qkv_grad[index, :, 2 * local_width :])

    attention_backward(0)
    stream_mids(2, 4)

    @pl.when(is_first)
    def _():
        for index in range(TILES):
            share_finish(2, index)

    put_grads(
        out_grad_at, local_width, lambda index: dot_tn(attended[index], r_grad[set_rows(index)])
    )
    stream_mids(4, 6)
    attention_backward(1)
    stream_mids(6, 7)

    def attention_back(index):
        at = tile_rows(index)
        n1_grad = part_sum(3, index)
        hat, rate = normed(ends[ends_in, at, :].astype(F32))
        small[0:1, :] += column_sum(n1_grad * hat)
        small[1:2, :] += column_sum(n1_grad)
        results[1, at, :] = (
            hidden[at, :] + norm_backward(n1_grad, hat, rate, ln1_gain_ref[...])
        ).astype(BF16)

        @pl.when(is_second)
        def _():
            cross(index).start()

    def attention_weights():
        put_grads(
            qkv_grad_at, qkv_rows, lambda index: dot_tn(qkv_grad[index], n1[set_rows(index)])
        )
        stream_mids(7, 10)

    reduce_parts(
        3,
        lambda index, shards, at: dot_nn(qkv_grad[index, at, :], weight_of(shards, 0, qkv_rows)),
        attention_back,
        between=attention_weights,
    )

    leave = remote(
        results.at[1 - s, token_rows(across_m)], rows_recv, leave_send.at[0], leave_recv.at[0], across
    )
    leave.start()
    small_y_copy = remote(small_other, small_y, leave_send.at[1], leave_recv.at[1], across)
    small_other[0:6, :] = small[0:6, :]
    small_y_copy.start()

    if z_line:
        stream_mids(10, blocks)

        @pl.when(jnp.logical_and(is_second, is_end))
        def _():
            def up(step):
                gather_y(step)
                grad_pair(step, grads).start()

            repeat(0, blocks, up)

        @pl.when(jnp.logical_and(is_second, is_mid))
        def _():
            gather_y(0)
            mid_up(0)

            def both(step):
                gather_y(step)
                mid_up(step)
                mid_down(step - 1)

            repeat(1, blocks, both)

        @pl.when(is_mid)
        def _():
            mid_down(blocks - 1)

        @pl.when(is_end)
        def _():
            def take(step):
                grad_pair(step, grads_mid).wait_recv()
                grad_out(step, grads_pair).start()

            repeat(0, blocks, take)

    else:
        @pl.when(is_second)
        def _():
            repeat(0, blocks, gather_y)

        repeat(0, blocks, lambda step: grad_out(step, grads).start())

    small_y_copy.wait_recv()
    small[...] += small_y[...]
    if z_line:
        small_up = remote(small, small_pair, leave_send.at[2], leave_recv.at[2], pair)
        small_across = remote(small, small_mid, leave_send.at[3], leave_recv.at[3], middle)
        small_down = remote(small_mid, small_pair, leave_send.at[2], leave_recv.at[2], pair)

        @pl.when(is_end)
        def _():
            small_up.start()
            small_down.wait_recv()
            small_out[...] = small_pair[...]
            small_up.wait_send()

        @pl.when(is_mid)
        def _():
            small_up.wait_recv()
            small[...] += small_pair[...]
            small_across.start()
            small_across.wait_recv()
            small_mid[...] += small[...]
            small_down.start()
            small_out[...] = small_mid[...]
            small_across.wait_send()
            small_down.wait_send()

    else:
        small_out[...] = small[...]

    leave.wait_recv()
    rows_out[pl.ds(chip, 1)] = results[pl.ds(1 - s, 1), token_rows(m), :].astype(F32)
    rows_out[pl.ds(1 - chip, 1)] = rows_recv[...].astype(F32)[None]
    repeat(0, blocks, lambda step: grad_out(step, grads).wait())

    entry_across(0).wait_send()
    entry_sibling(0).wait_send()
    entry_forward(0).wait_send()
    leave.wait_send()
    small_y_copy.wait_send()
    for index in range(TILES):
        cross(index).wait_send()
        cross_core(index).wait_send()
    for which in range(4):
        for index in range(TILES):
            part_copy(which, index).wait_send()

    @pl.when(is_first)
    def _():
        entry_across(1).wait_send()
        entry_sibling(1).wait_send()
        entry_forward(1).wait_send()
        for which in range(3):
            for index in range(TILES):
                share(which, index).wait_send()
                share_core(which, index).wait_send()
        for which in range(4):
            for index in range(TILES):
                far_core(which, index).wait_send()
                far(which, index).wait_send()
                far_back(which, index).wait_send()

    @pl.when(is_second)
    def _():
        bias_copy.wait_send()
        repeat(0, y_blocks, lambda step: weight_y(step).wait_send())
        if z_line:
            repeat(0, y_blocks, lambda step: weight_z(step).wait_send())
        repeat(0, blocks, lambda step: grad_y(step).wait_send())

    if z_line:
        repeat(0, blocks, lambda step: grad_pair(step, grads).wait_send())

        @pl.when(is_mid)
        def _():
            repeat(0, blocks, lambda step: grad_mid(step).wait_send())


def finish_kernel(local_width, rows_ref, small_ref, grads_ref, *outs):
    rows_out, qkv_out, out_out, fc_out, proj_out, bias_out = outs[:6]
    rows_out[...] = rows_ref[...]
    first = 0
    for target in (proj_out, fc_out, out_out, qkv_out):
        count = target.shape[0]
        target[...] = grads_ref[first : first + count, :].astype(F32)
        first += count
    bias_out[0:1, :] = small_ref[7:8, 0:local_width]
    bias_out[1:2, :] = small_ref[7:8, 2 * local_width : 3 * local_width]
    for row, target in enumerate(outs[6:]):
        target[...] = small_ref[row : row + 1, :]


def local(
    z_line,
    boundary_in,
    order,
    ln1_gain,
    ln1_bias,
    w_qkv,
    qkv_bias,
    w_out,
    out_bias,
    ln2_gain,
    ln2_bias,
    w_fc,
    fc_bias,
    w_proj,
    proj_bias,
):
    _, micro, rows, width = boundary_in.shape
    local_width = w_qkv.shape[-1]
    units = w_fc.shape[-1]
    length = rows * lax.axis_size("mp")
    heads = local_width // HEAD_DIM
    weight_rows = 4 * local_width + width + units
    blocks = weight_rows // BLOCK
    vmem = pltpu.VMEM
    dma = pltpu.SemaphoreType.DMA
    in_vmem = pl.BlockSpec(memory_space=pltpu.VMEM)
    in_any = pl.BlockSpec(memory_space=pl.ANY)
    in_smem = pl.BlockSpec(memory_space=pltpu.SMEM)
    out_rows, small, grads = pl.pallas_call(
        functools.partial(kernel, z_line),
        out_shape=(
            jax.ShapeDtypeStruct((micro, rows, width), F32),
            jax.ShapeDtypeStruct((8, width), F32),
            jax.ShapeDtypeStruct((weight_rows, width), BF16),
        ),
        in_specs=[
            in_smem,
            in_any,
            in_vmem,
            in_vmem,
            in_any,
            in_vmem,
            in_any,
            in_vmem,
            in_vmem,
            in_vmem,
            in_any,
            in_vmem,
            in_any,
            in_vmem,
        ],
        out_specs=(in_vmem, in_vmem, in_any),
        scratch_shapes=[
            vmem((micro, rows, width), BF16),
            vmem((micro, rows, width), BF16),
            vmem((2, weight_rows, width), BF16),
            vmem((2, 8, width), F32),
            vmem((3, length, width), BF16),
            vmem((2, length, width), BF16),
            vmem((rows, width), BF16),
            vmem((2, length, width), BF16),
            vmem((2, length, width), BF16),
            vmem((2, length, 3 * local_width), BF16),
            vmem((2 * heads, length, length), BF16),
            vmem((2, length, local_width), BF16),
            vmem((length, width), F32),
            vmem((2, length, units), BF16),
            vmem((2, length, units), BF16),
            vmem((2, length, units), BF16),
            vmem((2, length, width), BF16),
            vmem((2, length, width), BF16),
            vmem((2, length, local_width), BF16),
            vmem((2, length, 3 * local_width), BF16),
            vmem((4, length, width), BF16),
            vmem((4, length, width), BF16),
            vmem((4, length, width), BF16),
            vmem((weight_rows, width), BF16),
            vmem((weight_rows, width), BF16),
            vmem((weight_rows, width), BF16),
            vmem((weight_rows, width), BF16),
            vmem((weight_rows, width), BF16),
            vmem((8, width), F32),
            vmem((8, width), F32),
            vmem((8, width), F32),
            vmem((8, width), F32),
            vmem((8, width), F32),
            dma((5,)),
            dma((7,)),
            dma((7,)),
            dma((blocks,)),
            dma((blocks,)),
            dma((blocks,)),
            dma((blocks,)),
            dma((4, TILES)),
            dma((4, TILES)),
            dma((4, TILES)),
            dma((4, TILES)),
            dma((4, TILES)),
            dma((4, TILES)),
            dma((4, TILES)),
            dma((4, TILES)),
            dma((3, TILES)),
            dma((3, TILES)),
            dma((3, TILES)),
            dma((3, TILES)),
            dma((TILES,)),
            dma((TILES,)),
            dma((TILES,)),
            dma((TILES,)),
            dma((4,)),
            dma((4,)),
            dma((blocks,)),
            dma((blocks,)),
            dma((blocks,)),
            dma((blocks,)),
            dma((blocks,)),
            dma((blocks,)),
            dma((blocks,)),
        ],
        compiler_params=pltpu.CompilerParams(
            collective_id=0, has_side_effects=True, vmem_limit_bytes=63 * 2**20
        ),
        name="two_layers",
    )(
        order,
        boundary_in,
        ln1_gain,
        ln1_bias,
        jnp.swapaxes(w_qkv, 2, 3).reshape(1, 3 * local_width, width),
        qkv_bias,
        w_out,
        out_bias,
        ln2_gain,
        ln2_bias,
        w_fc,
        fc_bias,
        w_proj,
        proj_bias,
    )
    if not z_line:
        small, grads = lax.psum((small, grads), "dp")
    shapes = [
        (micro, rows, width),
        (3 * local_width, width),
        (local_width, width),
        (width, units),
        (units, width),
        (2, local_width),
    ] + [(1, width)] * 6 + [(1, units)]
    (
        out_rows,
        qkv_grad,
        out_grad,
        fc_grad,
        proj_grad,
        qkv_bias_grad,
        ln1_gain_grad,
        ln1_bias_grad,
        ln2_gain_grad,
        ln2_bias_grad,
        out_bias_grad,
        proj_bias_grad,
        fc_bias_grad,
    ) = pl.pallas_call(
        functools.partial(finish_kernel, local_width),
        out_shape=[jax.ShapeDtypeStruct(shape, F32) for shape in shapes],
        in_specs=[in_vmem] * 3,
        out_specs=[in_vmem] * len(shapes),
        compiler_params=pltpu.CompilerParams(vmem_limit_bytes=32 * 2**20),
        name="finish",
    )(out_rows, small, grads)
    return (
        out_rows[None],
        ln1_gain_grad,
        ln1_bias_grad,
        jnp.swapaxes(qkv_grad.reshape(1, 3, local_width, width), 2, 3),
        qkv_bias_grad[None],
        out_grad[None],
        out_bias_grad,
        ln2_gain_grad,
        ln2_bias_grad,
        fc_grad[None],
        fc_bias_grad,
        proj_grad[None],
        proj_bias_grad,
    )


def solution(mesh):
    return jax.shard_map(
        functools.partial(local, mesh.shape["dp"] == 4),
        mesh=mesh,
        in_specs=(
            P("section", "dp", "mp", None),
            P("dp", None),
            P("section", None),
            P("section", None),
            P("section", None, None, "mp"),
            P("section", None, "mp"),
            P("section", "mp", None),
            P("section", None),
            P("section", None),
            P("section", None),
            P("section", None, "mp"),
            P("section", "mp"),
            P("section", "mp", None),
            P("section", None),
        ),
        out_specs=(
            P("section", "dp", "mp", None),
            P("section", None),
            P("section", None),
            P("section", None, None, "mp"),
            P("section", None, "mp"),
            P("section", "mp", None),
            P("section", None),
            P("section", None),
            P("section", None),
            P("section", None, "mp"),
            P("section", "mp"),
            P("section", "mp", None),
            P("section", None),
        ),
        check_vma=False,
    )
```

```python
import functools

import jax
import jax.numpy as jnp
from jax import lax
from jax.experimental import pallas as pl
from jax.experimental.pallas import tpu as pltpu
from jax.sharding import PartitionSpec as P

HEAD_DIM = 64
BRANCH_SCALE = 0.14433756729740643
NORM_EPS = 1e-05
GELU_RATE = 0.7978845608028654
GELU_CUBE = 0.044715
NEGATIVE = -1e30
BLOCK = 96
TILES = 4
BEHIND = 3
FINISH = 192
MESH = pl.DeviceIdType.MESH
BF16 = jnp.bfloat16
F32 = jnp.float32


def dot_nn(a, b):
    return lax.dot_general(a, b, (((1,), (0,)), ((), ())), preferred_element_type=F32)


def dot_nt(a, b):
    return lax.dot_general(a, b, (((1,), (1,)), ((), ())), preferred_element_type=F32)


def dot_tn(a, b):
    return lax.dot_general(a, b, (((0,), (0,)), ((), ())), preferred_element_type=F32)


def normed(values):
    center = values - jnp.mean(values, axis=-1, keepdims=True)
    rate = lax.rsqrt(jnp.mean(center * center, axis=-1, keepdims=True) + NORM_EPS)
    return center * rate, rate


def norm_backward(grad, hat, rate, gain):
    scaled = grad * gain
    return rate * (
        scaled
        - jnp.mean(scaled, axis=-1, keepdims=True)
        - hat * jnp.mean(scaled * hat, axis=-1, keepdims=True)
    )


def column_sum(values):
    return jnp.sum(values.astype(F32), axis=0, keepdims=True)


def remote(src, dst, send_sem, recv_sem, device):
    return pltpu.make_async_remote_copy(
        src_ref=src,
        dst_ref=dst,
        send_sem=send_sem,
        recv_sem=recv_sem,
        device_id=device,
        device_id_type=MESH,
    )


def kernel(
    z_line,
    order_ref,
    boundary_ref,
    ln1_gain_ref,
    ln1_bias_ref,
    w_qkv_ref,
    qkv_bias_ref,
    w_out_ref,
    out_bias_ref,
    ln2_gain_ref,
    ln2_bias_ref,
    w_fc_ref,
    fc_bias_ref,
    w_proj_ref,
    proj_bias_ref,
    rows_out,
    small_out,
    grads_out,
    raw,
    slots,
    weights,
    biases,
    ends,
    results,
    rows_recv,
    n1,
    n2,
    qkv,
    probs,
    attended,
    hidden,
    act,
    slope,
    pre_grad,
    m_grad,
    r_grad,
    head_grad,
    qkv_grad,
    part,
    far_part,
    part_recv,
    grads,
    grads_other,
    grads_y,
    grads_pair,
    grads_mid,
    small,
    small_other,
    small_y,
    small_pair,
    small_mid,
    local_sem,
    entry_send,
    entry_recv,
    weight_y_send,
    weight_y_recv,
    weight_z_send,
    weight_z_recv,
    part_send,
    part_recv_sem,
    far_core_send,
    far_core_recv,
    far_send,
    far_recv,
    far_back_send,
    far_back_recv,
    share_send,
    share_recv,
    share_core_send,
    share_core_recv,
    cross_send,
    cross_recv,
    cross_core_send,
    cross_core_recv,
    leave_send,
    leave_recv,
    grad_y_send,
    grad_y_recv,
    grad_pair_send,
    grad_pair_recv,
    grad_mid_send,
    grad_mid_recv,
    grad_out_sem,
):
    s, d, m = lax.axis_index("section"), lax.axis_index("dp"), lax.axis_index("mp")
    core, chip = lax.rem(m, 2), lax.div(m, 2)
    half = lax.rem(d, 2)
    across_m = 2 * (1 - chip) + core
    sibling = (s, d, 2 * chip + 1 - core)
    across = (s, d, across_m)
    other_section = (1 - s, d, m)
    pair = (s, d + 1 - 2 * half, m)
    middle = (s, 3 - d, m)
    is_first, is_second = s == 0, s == 1
    is_mid = lax.div(d + 1, 2) == 1
    is_end = lax.div(d + 1, 2) != 1

    rows = boundary_ref.shape[2]
    length, width = n1.shape[1:]
    tile = length // TILES
    piece = tile // 2
    big = 2 * tile
    local_width = attended.shape[2]
    units = act.shape[2]
    heads = local_width // HEAD_DIM
    scale = HEAD_DIM ** (-0.5)
    qkv_rows = 3 * local_width
    out_at, fc_at, proj_at = qkv_rows, qkv_rows + local_width, qkv_rows + local_width + width
    weight_rows = weights.shape[1]
    blocks = weight_rows // BLOCK
    ends_in, ends_grad = 2 * s, 2 * (1 - s)

    def set_rows(index):
        return index * (1 - s)

    def set_weights(index):
        return index * s

    def tile_rows(index):
        return slice(index * tile, (index + 1) * tile)

    def big_rows(index):
        return slice(index * big, (index + 1) * big)

    def piece_rows(index, which):
        return pl.ds(pl.multiple_of(index * tile + which * piece, piece), piece)

    partners = [sibling, across, other_section]
    if z_line:
        partners += [pair, middle]
    barrier = pltpu.get_barrier_semaphore()
    for device in partners:
        pl.semaphore_signal(barrier, inc=1, device_id=device, device_id_type=MESH)

    loads = [
        pltpu.make_async_copy(boundary_ref.at[0], raw, local_sem.at[0]),
        pltpu.make_async_copy(
            w_qkv_ref.at[0], weights.at[0, pl.ds(0, qkv_rows)], local_sem.at[1]
        ),
        pltpu.make_async_copy(
            w_out_ref.at[0], weights.at[0, pl.ds(out_at, local_width)], local_sem.at[2]
        ),
        pltpu.make_async_copy(w_fc_ref.at[0], weights.at[0, pl.ds(fc_at, width)], local_sem.at[3]),
        pltpu.make_async_copy(
            w_proj_ref.at[0], weights.at[0, pl.ds(proj_at, units)], local_sem.at[4]
        ),
    ]
    for load in loads:
        load.start()

    biases[0] = jnp.zeros_like(biases[0])
    biases[0, 0:1, :] = fc_bias_ref[...]
    biases[0, 1:2, 0:local_width] = qkv_bias_ref[0, 0:1, :]
    biases[0, 2:3, 0:local_width] = qkv_bias_ref[0, 1:2, :]
    small[...] = jnp.zeros_like(small)
    small_other[...] = jnp.zeros_like(small_other)

    loads[0].wait()
    for slot in range(2):
        picked = jnp.where(is_first, order_ref[0, slot], slot).astype(F32)
        slots[slot] = (
            raw[0].astype(F32) * (1.0 - picked) + raw[1].astype(F32) * picked
        ).astype(BF16)

    pl.semaphore_wait(barrier, len(partners))

    def token_rows(index):
        return pl.ds(pl.multiple_of(index * rows, rows), rows)

    def entry_across(which):
        slot = 1 - chip if which == 0 else chip
        return remote(
            slots.at[slot],
            ends.at[which, token_rows(m)],
            entry_send.at[which],
            entry_recv.at[which],
            across,
        )

    def entry_sibling(which):
        slot = chip if which == 0 else 1 - chip
        return remote(
            slots.at[slot],
            ends.at[which, token_rows(m)],
            entry_send.at[2 + which],
            entry_recv.at[2 + which],
            sibling,
        )

    def entry_forward(which):
        at = token_rows(across_m)
        return remote(
            ends.at[which, at],
            ends.at[which, at],
            entry_send.at[4 + which],
            entry_recv.at[4 + which],
            sibling,
        )

    bias_copy = remote(biases.at[0], biases.at[1], entry_send.at[6], entry_recv.at[6], across)

    def entry_start(which):
        entry_across(which).start()
        entry_sibling(which).start()
        slot = chip if which == 0 else 1 - chip
        ends[which, token_rows(m), :] = slots[slot]

    def entry_finish(which):
        entry_across(which).wait_recv()
        entry_forward(which).start()
        entry_sibling(which).wait_recv()
        entry_forward(which).wait_recv()

    @pl.when(is_first)
    def _():
        entry_start(1)

    entry_start(0)

    y_blocks = blocks // 2 if z_line else blocks

    def weight_block(index):
        return pl.ds(pl.multiple_of(index * BLOCK, BLOCK), BLOCK)

    def near_block(step):
        return weight_block(2 * step + half if z_line else step)

    def weight_y(step):
        return remote(
            weights.at[0, near_block(step)],
            weights.at[1, near_block(step)],
            weight_y_send.at[step],
            weight_y_recv.at[step],
            across,
        )

    def weight_z(step):
        return remote(
            weights.at[1, near_block(step)],
            weights.at[1, near_block(step)],
            weight_z_send.at[step],
            weight_z_recv.at[step],
            pair,
        )

    def repeat(first, last, action):
        def step_of(step, carry):
            action(step)
            return carry

        lax.fori_loop(first, last, step_of, 0)

    def weight_pass(step):
        weight_y(step).wait_recv()
        if z_line:
            weight_z(step).start()

    for load in loads[1:]:
        load.wait()

    def cross(index):
        at = piece_rows(index, core)
        return remote(
            results.at[s, at],
            ends.at[2, at],
            cross_send.at[index],
            cross_recv.at[index],
            other_section,
        )

    def cross_core(index):
        at = piece_rows(index, core)
        return remote(
            ends.at[2, at],
            ends.at[2, at],
            cross_core_send.at[index],
            cross_core_recv.at[index],
            sibling,
        )

    shared = (n2, m_grad, r_grad)

    def share(which, index):
        at = piece_rows(index, core)
        return remote(
            shared[which].at[0, at],
            shared[which].at[1, at],
            share_send.at[which, index],
            share_recv.at[which, index],
            across,
        )

    def share_core(which, index):
        at = piece_rows(index, core)
        return remote(
            shared[which].at[1, at],
            shared[which].at[1, at],
            share_core_send.at[which, index],
            share_core_recv.at[which, index],
            sibling,
        )

    def share_finish(which, index):
        share(which, index).wait_recv()
        share_core(which, index).start()
        share_core(which, index).wait_recv()

    def part_copy(which, index):
        at = pl.ds(index * tile, tile)
        return remote(
            part.at[which, at],
            part_recv.at[which, at],
            part_send.at[which, index],
            part_recv_sem.at[which, index],
            sibling,
        )

    def spare_rows(which, index, core_of):
        return pl.ds(
            pl.multiple_of(which * length + index * tile + core_of * piece, piece), piece
        )

    def far_core(which, index):
        return remote(
            far_part.at[which, piece_rows(index, 1 - core)],
            grads_other.at[spare_rows(which, index, 1 - core)],
            far_core_send.at[which, index],
            far_core_recv.at[which, index],
            sibling,
        )

    def far(which, index):
        return remote(
            far_part.at[which, piece_rows(index, core)],
            weights.at[1, spare_rows(which, index, core)],
            far_send.at[which, index],
            far_recv.at[which, index],
            across,
        )

    def far_back(which, index):
        at = spare_rows(which, index, core)
        return remote(
            weights.at[1, at],
            weights.at[1, at],
            far_back_send.at[which, index],
            far_back_recv.at[which, index],
            sibling,
        )

    def far_pass(which, index):
        far_core(which, index).wait_recv()
        at = piece_rows(index, core)
        far_part[which, at, :] = (
            far_part[which, at, :].astype(F32)
            + grads_other[spare_rows(which, index, core), :].astype(F32)
        ).astype(BF16)
        far(which, index).start()

    def part_sum(which, index):
        at = tile_rows(index)
        near = part[which, at, :].astype(F32) + part_recv[which, at, :].astype(F32)
        first = which * length + index * tile
        other = weights[1, first : first + tile, :].astype(F32)
        return near + jnp.where(is_first, other, 0.0)

    def spans_of(step):
        return [
            (slice(first, first + step), range(first // tile, (first + step) // tile))
            for first in range(0, length, step)
        ]

    def far_parts(which, value_of, step=tile, before=None):
        for at, inside in spans_of(step):
            if before is not None:
                for index in inside:
                    before(index)
            far_part[which, at, :] = value_of(1, 0, at).astype(BF16)
            for index in inside:
                far_core(which, index).start()
                if index > 0:
                    far_pass(which, index - 1)
        far_pass(which, TILES - 1)

    def own_parts(which, value_of, step=tile):
        for at, inside in spans_of(step):
            part[which, at, :] = value_of(0, 0, at).astype(BF16)
            for index in inside:
                part_copy(which, index).start()

    def both_parts(which, value_of, step=tile):
        for at, inside in spans_of(step):
            part[which, at, :] = (value_of(0, 0, at) + value_of(1, 1, at)).astype(BF16)
            for index in inside:
                part_copy(which, index).start()

    def collect(which, finish, beside=None):
        for index in range(TILES + 1):
            if index < TILES:
                @pl.when(is_first)
                def _():
                    far(which, index).wait_recv()
                    far_back(which, index).start()

                if beside is not None:
                    beside(index)
            if index > 0:
                @pl.when(is_first)
                def _():
                    far_back(which, index - 1).wait_recv()

                part_copy(which, index - 1).wait_recv()
                finish(index - 1)

    def weight_of(shards, first, count):
        return weights[shards, first : first + count, :]

    def scale_grad(index):
        at = tile_rows(index)
        m_grad[0, at, :] = (BRANCH_SCALE * ends[ends_grad, at, :].astype(F32)).astype(BF16)

    @pl.when(is_second)
    def _():
        repeat(0, y_blocks, lambda step: weight_y(step).start())
        bias_copy.start()
        repeat(0, y_blocks, weight_pass)
        if z_line:
            repeat(0, y_blocks, lambda step: weight_z(step).wait_recv())
        bias_copy.wait_recv()
        entry_finish(0)
        for index in range(TILES):
            scale_grad(index)

    def norm_one(which, source, index):
        at = tile_rows(index)
        hat, _ = normed(ends[source, at, :].astype(F32))
        n1[which, at, :] = (hat * ln1_gain_ref[...] + ln1_bias_ref[...]).astype(BF16)

    @pl.when(is_second)
    def _():
        for index in range(TILES + 1):
            if index < TILES:
                cross(index).wait_recv()
                cross_core(index).start()
            if index > 0:
                cross_core(index - 1).wait_recv()
                norm_one(0, 2, index - 1)

    @pl.when(is_first)
    def _():
        entry_finish(1)
        for index in range(TILES):
            norm_one(1, 1, index)

    causal = lax.broadcasted_iota(jnp.int32, (length, length), 0) >= lax.broadcasted_iota(
        jnp.int32, (length, length), 1
    )

    def bias_of(shards, row, count):
        return biases[shards, row : row + 1, 0:count]

    def head_columns(kind, head):
        first = kind * local_width + head * HEAD_DIM
        return slice(first, first + HEAD_DIM)

    def attention_forward(index):
        source, shards = set_rows(index), set_weights(index)
        queries = dot_nt(n1[source], weight_of(shards, 0, local_width))
        queries = queries + bias_of(shards, 1, local_width)
        qkv[index, :, 0:local_width] = (queries.astype(BF16).astype(F32) * scale).astype(BF16)
        keys = dot_nt(n1[source], weight_of(shards, local_width, local_width))
        qkv[index, :, local_width : 2 * local_width] = keys.astype(BF16)
        values = dot_nt(n1[source], weight_of(shards, 2 * local_width, local_width))
        values = values + bias_of(shards, 2, local_width)
        qkv[index, :, 2 * local_width :] = values.astype(BF16)
        for head in range(heads):
            scores = dot_nt(
                qkv[index, :, head_columns(0, head)], qkv[index, :, head_columns(1, head)]
            )
            scores = jnp.where(causal, scores, NEGATIVE)
            raised = jnp.exp(scores - jnp.max(scores, axis=-1, keepdims=True))
            shares = raised * (1.0 / jnp.sum(raised, axis=-1, keepdims=True))
            probs[index * heads + head] = shares.astype(BF16)
            attended[index, :, head * HEAD_DIM : (head + 1) * HEAD_DIM] = dot_nn(
                probs[index * heads + head], qkv[index, :, head_columns(2, head)]
            ).astype(BF16)

    attention_forward(1)

    def attention_part(index, shards, at):
        return dot_nn(attended[index, at, :], weight_of(shards, out_at, local_width))

    @pl.when(is_first)
    def _():
        far_parts(0, attention_part)
        entry_finish(0)
        for index in range(TILES):
            norm_one(0, 0, index)

    attention_forward(0)

    @pl.when(is_first)
    def _():
        own_parts(0, attention_part)

    @pl.when(is_second)
    def _():
        both_parts(0, attention_part)

    def attention_out(index):
        at = tile_rows(index)
        held = ends[ends_in, at, :].astype(F32) + BRANCH_SCALE * (
            part_sum(0, index) + out_bias_ref[...]
        )
        hidden[at, :] = held
        hat, _ = normed(held)
        n2[0, at, :] = (hat * ln2_gain_ref[...] + ln2_bias_ref[...]).astype(BF16)

        @pl.when(is_first)
        def _():
            share(0, index).start()

    collect(0, attention_out)

    def activate(index, source, shards, at):
        u = dot_nn(n2[source, at, :], weight_of(shards, fc_at, width)) + bias_of(shards, 0, units)
        square = u * u
        bent = jnp.tanh(GELU_RATE * (u + GELU_CUBE * u * square))
        act[index, at, :] = (0.5 * u * (1.0 + bent)).astype(BF16)
        slope[index, at, :] = (
            0.5 * (1.0 + bent)
            + (0.5 * GELU_RATE) * u * (1.0 - bent * bent) * (1.0 + (3.0 * GELU_CUBE) * square)
        ).astype(BF16)

    for index in range(length // big):
        activate(0, 0, 0, big_rows(index))

    def mlp_part(index, shards, at):
        return dot_nn(act[index, at, :], weight_of(shards, proj_at, units))

    def other_activate(index):
        share_finish(0, index)
        activate(1, 1, 0, tile_rows(index))

    @pl.when(is_first)
    def _():
        own_parts(1, mlp_part)
        far_parts(1, mlp_part, before=other_activate)

    @pl.when(is_second)
    def _():
        for index in range(length // big):
            activate(1, 0, 1, big_rows(index))
        both_parts(1, mlp_part)

    proj_grad_at, fc_grad_at = 0, units
    out_grad_at = fc_grad_at + width
    qkv_grad_at = out_grad_at + local_width

    def grad_y(step):
        return remote(
            grads_other.at[weight_block(step)],
            grads_y.at[weight_block(step)],
            grad_y_send.at[step],
            grad_y_recv.at[step],
            across,
        )

    def grad_pair(step, source):
        return remote(
            source.at[weight_block(step)],
            grads_pair.at[weight_block(step)],
            grad_pair_send.at[step],
            grad_pair_recv.at[step],
            pair,
        )

    def grad_mid(step):
        return remote(
            grads.at[weight_block(step)],
            grads_mid.at[weight_block(step)],
            grad_mid_send.at[step],
            grad_mid_recv.at[step],
            middle,
        )

    def grad_out(step, source):
        at = weight_block(step)
        return pltpu.make_async_copy(source.at[at], grads_out.at[at], grad_out_sem.at[step])

    def add_into(target, source, step):
        at = weight_block(step)
        target[at, :] = (target[at, :].astype(F32) + source[at, :].astype(F32)).astype(BF16)

    def gather_y(step):
        grad_y(step).wait_recv()
        add_into(grads, grads_y, step)

    def mid_up(step):
        grad_pair(step, grads).wait_recv()
        add_into(grads, grads_pair, step)
        grad_mid(step).start()

    def mid_down(step):
        grad_mid(step).wait_recv()
        add_into(grads_mid, grads, step)
        grad_pair(step, grads_mid).start()
        grad_out(step, grads_mid).start()

    def mid_step(step, gather):
        if gather:
            gather_y(step)
        mid_up(step)

    first_ends, first_mids, second_ends, second_mids = [0], [0], [0], [0]
    first_end, second_end = jnp.logical_and(is_first, is_end), jnp.logical_and(is_second, is_end)
    first_mid, second_mid = jnp.logical_and(is_first, is_mid), jnp.logical_and(is_second, is_mid)

    def pump_ends(done, count, wanted, gather):
        first, last = done[0], done[0] + count
        done[0] = last
        if z_line:
            def up(step):
                if gather:
                    gather_y(step)
                grad_pair(step, grads).start()

            @pl.when(wanted)
            def _():
                repeat(first, last, up)

    def pump_mids(done, count, wanted, gather):
        first, last = done[0], done[0] + count
        done[0] = last
        if z_line:
            def both(step):
                mid_step(step, gather)
                mid_down(step - BEHIND)

            @pl.when(wanted)
            def _():
                if first < BEHIND:
                    repeat(first, min(BEHIND, last), lambda step: mid_step(step, gather))
                if last > BEHIND:
                    repeat(max(first, BEHIND), last, both)

    def pump_first_ends(count):
        pump_ends(first_ends, count, first_end, False)

    def pump_first(count):
        pump_mids(first_mids, count, first_mid, False)

    def pump_second_ends(count):
        pump_ends(second_ends, count, second_end, True)

    def pump_second(count):
        pump_mids(second_mids, count, second_mid, True)

    def blocks_of(first, count):
        return first // BLOCK, (first + count) // BLOCK

    def put_first(first, count, value_of):
        @pl.when(is_first)
        def _():
            grads[first : first + count, :] = (value_of(0) + value_of(1)).astype(BF16)

    def put_second_far(first, count, value_of):
        @pl.when(is_second)
        def _():
            grads_other[first : first + count, :] = value_of(1).astype(BF16)
            repeat(*blocks_of(first, count), lambda step: grad_y(step).start())

    def put_second_near(first, count, value_of):
        @pl.when(is_second)
        def _():
            grads[first : first + count, :] = value_of(0).astype(BF16)

    def set_sum(row, column, index, values):
        total = column_sum(values)
        columns = slice(column, column + total.shape[1])
        if index == 0:
            small[row : row + 1, columns] += total
        else:
            @pl.when(is_first)
            def _():
                small[row : row + 1, columns] += total

            @pl.when(is_second)
            def _():
                small_other[row : row + 1, columns] += total

    def proj_grad(index):
        return dot_tn(act[index], m_grad[set_rows(index)])

    def fc_grad(index):
        return dot_tn(n2[set_rows(index)], pre_grad[index])

    def out_grad(index):
        return dot_tn(attended[index], r_grad[set_rows(index)])

    def in_grad(index):
        return dot_tn(qkv_grad[index], n1[set_rows(index)])

    put_second_far(proj_grad_at, units, proj_grad)

    def layer_out(index):
        at = tile_rows(index)
        results[0, at, :] = (
            hidden[at, :] + BRANCH_SCALE * (part_sum(1, index) + proj_bias_ref[...])
        ).astype(BF16)

        @pl.when(is_first)
        def _():
            cross(index).start()

    collect(1, layer_out)

    @pl.when(is_first)
    def _():
        for index in range(TILES + 1):
            if index < TILES:
                cross(index).wait_recv()
                cross_core(index).start()
            if index > 0:
                cross_core(index - 1).wait_recv()
                scale_grad(index - 1)
                share(1, index - 1).start()
        grads[proj_grad_at : proj_grad_at + units, :] = proj_grad(0).astype(BF16)

    def mlp_slope(index):
        for number in range(length // big):
            at = big_rows(number)
            pre_grad[index, at, :] = (
                slope[index, at, :].astype(F32)
                * dot_nt(
                    m_grad[set_rows(index), at, :], weight_of(set_weights(index), proj_at, units)
                )
            ).astype(BF16)
        set_sum(6, 0, index, pre_grad[index])

    def mlp_back_part(index, shards, at):
        return dot_nt(pre_grad[index, at, :], weight_of(shards, fc_at, width))

    small[5:6, :] = column_sum(m_grad[0])
    mlp_slope(0)

    def share_all(which):
        for index in range(TILES):
            share(which, index).wait_recv()
            share_core(which, index).start()
        for index in range(TILES):
            share_core(which, index).wait_recv()

    @pl.when(is_first)
    def _():
        own_parts(2, mlp_back_part, step=big)
        share_all(1)
        at = slice(proj_grad_at, proj_grad_at + units)
        grads[at, :] = (grads[at, :].astype(F32) + proj_grad(1)).astype(BF16)

    pump_first_ends(units // BLOCK)

    mlp_slope(1)

    @pl.when(is_first)
    def _():
        far_parts(2, mlp_back_part, step=big)

    @pl.when(is_second)
    def _():
        both_parts(2, mlp_back_part, step=big)

    put_second_near(proj_grad_at, units, proj_grad)
    put_first(fc_grad_at, width, fc_grad)
    pump_first_ends(width // BLOCK)
    pump_first(1)

    def mlp_back(index):
        at = tile_rows(index)
        n2_grad = part_sum(2, index)
        hat, rate = normed(hidden[at, :])
        small[2:3, :] += column_sum(n2_grad * hat)
        small[3:4, :] += column_sum(n2_grad)
        held = ends[ends_grad, at, :].astype(F32) + norm_backward(
            n2_grad, hat, rate, ln2_gain_ref[...]
        )
        hidden[at, :] = held
        r_grad[0, at, :] = (BRANCH_SCALE * held).astype(BF16)

        @pl.when(is_first)
        def _():
            share(2, index).start()

    def pump_beside(index):
        if index > 0:
            pump_first(1)

    collect(2, mlp_back, pump_beside)
    small[4:5, :] = column_sum(r_grad[0])
    pump_second_ends(1)

    def attention_backward(index):
        shards = set_weights(index)
        head_grad[index] = dot_nt(
            r_grad[set_rows(index)], weight_of(shards, out_at, local_width)
        ).astype(BF16)
        for head in range(heads):
            columns = slice(head * HEAD_DIM, (head + 1) * HEAD_DIM)
            shares = probs[index * heads + head]
            qkv_grad[index, :, head_columns(2, head)] = dot_tn(
                shares, head_grad[index, :, columns]
            ).astype(BF16)
            share_grad = dot_nt(head_grad[index, :, columns], qkv[index, :, head_columns(2, head)])
            wide = shares.astype(F32)
            product = wide * share_grad
            score_grad = (
                product - wide * jnp.sum(product, axis=-1, keepdims=True)
            ).astype(BF16)
            qkv_grad[index, :, head_columns(0, head)] = (
                dot_nn(score_grad, qkv[index, :, head_columns(1, head)]) * scale
            ).astype(BF16)
            qkv_grad[index, :, head_columns(1, head)] = dot_tn(
                score_grad, qkv[index, :, head_columns(0, head)]
            ).astype(BF16)
        set_sum(7, 0, index, qkv_grad[index, :, 0:local_width])
        set_sum(7, 2 * local_width, index, qkv_grad[index, :, 2 * local_width :])

    def attention_back_part(index, shards, at):
        return dot_nn(qkv_grad[index, at, :], weight_of(shards, 0, qkv_rows))

    attention_backward(0)

    @pl.when(is_first)
    def _():
        own_parts(3, attention_back_part)

    pump_first(1)
    pump_second_ends(1)

    @pl.when(is_first)
    def _():
        share_all(2)

    put_first(out_grad_at, local_width, out_grad)
    pump_first(1)

    attention_backward(1)
    pump_first(1)
    pump_second_ends(1)
    pump_second(1)

    @pl.when(is_first)
    def _():
        far_parts(3, attention_back_part)

    @pl.when(is_second)
    def _():
        both_parts(3, attention_back_part)

    pump_first(1)
    pump_second_ends(1)

    put_first(qkv_grad_at, qkv_rows, in_grad)
    pump_first(1)

    def attention_back(index):
        at = tile_rows(index)
        n1_grad = part_sum(3, index)
        hat, rate = normed(ends[ends_in, at, :].astype(F32))
        small[0:1, :] += column_sum(n1_grad * hat)
        small[1:2, :] += column_sum(n1_grad)
        results[1, at, :] = (
            hidden[at, :] + norm_backward(n1_grad, hat, rate, ln1_gain_ref[...])
        ).astype(BF16)

        @pl.when(is_second)
        def _():
            cross(index).start()

    collect(3, attention_back, pump_beside)

    leave = remote(
        results.at[1 - s, token_rows(across_m)], rows_recv, leave_send.at[0], leave_recv.at[0], across
    )
    leave.start()
    small_y_copy = remote(small_other, small_y, leave_send.at[1], leave_recv.at[1], across)
    small_other[0:6, :] = small[0:6, :]
    small_y_copy.start()

    put_second_far(fc_grad_at, width, fc_grad)
    pump_second_ends(1)
    pump_second(1)
    put_second_near(fc_grad_at, width, fc_grad)
    pump_second_ends(1)
    pump_second(1)
    put_second_far(out_grad_at, local_width, out_grad)
    put_second_near(out_grad_at, local_width, out_grad)
    pump_second_ends(1)
    pump_second(1)
    put_second_far(qkv_grad_at, qkv_rows, in_grad)
    pump_second_ends(1)
    pump_second(1)
    put_second_near(qkv_grad_at, qkv_rows, in_grad)

    small_up = remote(small, small_pair, leave_send.at[2], leave_recv.at[2], pair)
    small_across = remote(small, small_mid, leave_send.at[3], leave_recv.at[3], middle)
    small_down = remote(small_mid, small_pair, leave_send.at[2], leave_recv.at[2], pair)

    if z_line:
        @pl.when(is_end)
        def _():
            small_y_copy.wait_recv()
            small[...] += small_y[...]
            small_up.start()

        pump_first_ends(blocks - first_ends[0])
        pump_second_ends(blocks - second_ends[0])
        near, later = blocks * 2 // 3, blocks * 5 // 6
        pump_first(near - first_mids[0])
        pump_second(near - second_mids[0])

        @pl.when(is_mid)
        def _():
            small_y_copy.wait_recv()
            small_up.wait_recv()
            small[...] += small_y[...]
            small[...] += small_pair[...]
            small_across.start()

        pump_first(later - first_mids[0])
        pump_second(later - second_mids[0])

        @pl.when(is_mid)
        def _():
            small_across.wait_recv()
            small_mid[...] += small[...]
            small_down.start()
            small_out[...] = small_mid[...]

        pump_first(blocks - first_mids[0])
        pump_second(blocks - second_mids[0])

        @pl.when(is_mid)
        def _():
            repeat(blocks - BEHIND, blocks, mid_down)

        @pl.when(is_end)
        def _():
            def take(step):
                grad_pair(step, grads_mid).wait_recv()
                grad_out(step, grads_pair).start()

            repeat(0, blocks, take)
            small_down.wait_recv()
            small_out[...] = small_pair[...]

    else:
        @pl.when(is_second)
        def _():
            repeat(0, blocks, gather_y)

        repeat(0, blocks, lambda step: grad_out(step, grads).start())
        small_y_copy.wait_recv()
        small_out[...] = small[...] + small_y[...]

    leave.wait_recv()
    rows_out[pl.ds(chip, 1)] = results[pl.ds(1 - s, 1), token_rows(m), :].astype(F32)
    rows_out[pl.ds(1 - chip, 1)] = rows_recv[...].astype(F32)[None]
    repeat(0, blocks, lambda step: grad_out(step, grads).wait())

    entry_across(0).wait_send()
    entry_sibling(0).wait_send()
    entry_forward(0).wait_send()
    leave.wait_send()
    small_y_copy.wait_send()
    for index in range(TILES):
        cross(index).wait_send()
        cross_core(index).wait_send()
    for which in range(4):
        for index in range(TILES):
            part_copy(which, index).wait_send()

    @pl.when(is_first)
    def _():
        entry_across(1).wait_send()
        entry_sibling(1).wait_send()
        entry_forward(1).wait_send()
        for which in range(3):
            for index in range(TILES):
                share(which, index).wait_send()
                share_core(which, index).wait_send()
        for which in range(4):
            for index in range(TILES):
                far_core(which, index).wait_send()
                far(which, index).wait_send()
                far_back(which, index).wait_send()

    @pl.when(is_second)
    def _():
        bias_copy.wait_send()
        repeat(0, y_blocks, lambda step: weight_y(step).wait_send())
        if z_line:
            repeat(0, y_blocks, lambda step: weight_z(step).wait_send())
        repeat(0, blocks, lambda step: grad_y(step).wait_send())

    if z_line:
        repeat(0, blocks, lambda step: grad_pair(step, grads).wait_send())

        @pl.when(is_end)
        def _():
            small_up.wait_send()

        @pl.when(is_mid)
        def _():
            repeat(0, blocks, lambda step: grad_mid(step).wait_send())
            small_across.wait_send()
            small_down.wait_send()


def finish_kernel(local_width, rows_ref, small_ref, grads_ref, *refs):
    outs, (held_rows, held, cast, in_sem, out_sem) = refs[:13], refs[13:]
    rows_out, qkv_out, out_out, fc_out, proj_out, bias_out = outs[:6]
    pieces, first = [], 0
    for target in (proj_out, fc_out, out_out, qkv_out):
        for at in range(0, target.shape[0], FINISH):
            pieces.append((first + at, min(FINISH, target.shape[0] - at), target, at))
        first += target.shape[0]
    rows_in = pltpu.make_async_copy(rows_ref, held_rows, in_sem.at[len(pieces)])
    rows_copy = pltpu.make_async_copy(held_rows, rows_out, out_sem.at[len(pieces)])

    def fetch(number):
        first, count, _, _ = pieces[number]
        at = pl.ds(first, count)
        return pltpu.make_async_copy(grads_ref.at[at], held.at[at], in_sem.at[number])

    def put(number):
        first, count, target, at = pieces[number]
        return pltpu.make_async_copy(
            cast.at[pl.ds(first, count)], target.at[pl.ds(at, count)], out_sem.at[number]
        )

    for number in range(len(pieces)):
        fetch(number).start()
    rows_in.start()
    bias_out[0:1, :] = small_ref[7:8, 0:local_width]
    bias_out[1:2, :] = small_ref[7:8, 2 * local_width : 3 * local_width]
    for row, target in enumerate(outs[6:]):
        target[...] = small_ref[row : row + 1, :]
    for number, (first, count, _, _) in enumerate(pieces):
        fetch(number).wait()
        cast[first : first + count, :] = held[first : first + count, :].astype(F32)
        put(number).start()
    rows_in.wait()
    rows_copy.start()
    for number in range(len(pieces)):
        put(number).wait()
    rows_copy.wait()


def local(
    z_line,
    boundary_in,
    order,
    ln1_gain,
    ln1_bias,
    w_qkv,
    qkv_bias,
    w_out,
    out_bias,
    ln2_gain,
    ln2_bias,
    w_fc,
    fc_bias,
    w_proj,
    proj_bias,
):
    _, micro, rows, width = boundary_in.shape
    local_width = w_qkv.shape[-1]
    units = w_fc.shape[-1]
    length = rows * lax.axis_size("mp")
    heads = local_width // HEAD_DIM
    weight_rows = 4 * local_width + width + units
    blocks = weight_rows // BLOCK
    vmem = pltpu.VMEM
    dma = pltpu.SemaphoreType.DMA
    in_vmem = pl.BlockSpec(memory_space=pltpu.VMEM)
    in_any = pl.BlockSpec(memory_space=pl.ANY)
    in_smem = pl.BlockSpec(memory_space=pltpu.SMEM)
    out_rows, small, grads = pl.pallas_call(
        functools.partial(kernel, z_line),
        out_shape=(
            jax.ShapeDtypeStruct((micro, rows, width), F32),
            jax.ShapeDtypeStruct((8, width), F32),
            jax.ShapeDtypeStruct((weight_rows, width), BF16),
        ),
        in_specs=[
            in_smem,
            in_any,
            in_vmem,
            in_vmem,
            in_any,
            in_vmem,
            in_any,
            in_vmem,
            in_vmem,
            in_vmem,
            in_any,
            in_vmem,
            in_any,
            in_vmem,
        ],
        out_specs=(in_vmem, in_vmem, in_any),
        scratch_shapes=[
            vmem((micro, rows, width), BF16),
            vmem((micro, rows, width), BF16),
            vmem((2, weight_rows, width), BF16),
            vmem((2, 8, width), F32),
            vmem((3, length, width), BF16),
            vmem((2, length, width), BF16),
            vmem((rows, width), BF16),
            vmem((2, length, width), BF16),
            vmem((2, length, width), BF16),
            vmem((2, length, 3 * local_width), BF16),
            vmem((2 * heads, length, length), BF16),
            vmem((2, length, local_width), BF16),
            vmem((length, width), F32),
            vmem((2, length, units), BF16),
            vmem((2, length, units), BF16),
            vmem((2, length, units), BF16),
            vmem((2, length, width), BF16),
            vmem((2, length, width), BF16),
            vmem((2, length, local_width), BF16),
            vmem((2, length, 3 * local_width), BF16),
            vmem((4, length, width), BF16),
            vmem((4, length, width), BF16),
            vmem((4, length, width), BF16),
            vmem((weight_rows, width), BF16),
            vmem((weight_rows, width), BF16),
            vmem((weight_rows, width), BF16),
            vmem((weight_rows, width), BF16),
            vmem((weight_rows, width), BF16),
            vmem((8, width), F32),
            vmem((8, width), F32),
            vmem((8, width), F32),
            vmem((8, width), F32),
            vmem((8, width), F32),
            dma((5,)),
            dma((7,)),
            dma((7,)),
            dma((blocks,)),
            dma((blocks,)),
            dma((blocks,)),
            dma((blocks,)),
            dma((4, TILES)),
            dma((4, TILES)),
            dma((4, TILES)),
            dma((4, TILES)),
            dma((4, TILES)),
            dma((4, TILES)),
            dma((4, TILES)),
            dma((4, TILES)),
            dma((3, TILES)),
            dma((3, TILES)),
            dma((3, TILES)),
            dma((3, TILES)),
            dma((TILES,)),
            dma((TILES,)),
            dma((TILES,)),
            dma((TILES,)),
            dma((4,)),
            dma((4,)),
            dma((blocks,)),
            dma((blocks,)),
            dma((blocks,)),
            dma((blocks,)),
            dma((blocks,)),
            dma((blocks,)),
            dma((blocks,)),
        ],
        compiler_params=pltpu.CompilerParams(
            collective_id=0, has_side_effects=True, vmem_limit_bytes=63 * 2**20
        ),
        name="two_layers",
    )(
        order,
        boundary_in,
        ln1_gain,
        ln1_bias,
        jnp.swapaxes(w_qkv, 2, 3).reshape(1, 3 * local_width, width),
        qkv_bias,
        w_out,
        out_bias,
        ln2_gain,
        ln2_bias,
        w_fc,
        fc_bias,
        w_proj,
        proj_bias,
    )
    if not z_line:
        small, grads = lax.psum((small, grads), "dp")
    shapes = [
        (micro, rows, width),
        (3 * local_width, width),
        (local_width, width),
        (width, units),
        (units, width),
        (2, local_width),
    ] + [(1, width)] * 6 + [(1, units)]
    (
        out_rows,
        qkv_grad,
        out_grad,
        fc_grad,
        proj_grad,
        qkv_bias_grad,
        ln1_gain_grad,
        ln1_bias_grad,
        ln2_gain_grad,
        ln2_bias_grad,
        out_bias_grad,
        proj_bias_grad,
        fc_bias_grad,
    ) = pl.pallas_call(
        functools.partial(finish_kernel, local_width),
        out_shape=[jax.ShapeDtypeStruct(shape, F32) for shape in shapes],
        in_specs=[in_any, in_vmem, in_any],
        out_specs=[in_any] * 5 + [in_vmem] * 8,
        scratch_shapes=[
            vmem((micro, rows, width), F32),
            vmem((weight_rows, width), BF16),
            vmem((weight_rows, width), F32),
            dma((weight_rows // FINISH + 5,)),
            dma((weight_rows // FINISH + 5,)),
        ],
        compiler_params=pltpu.CompilerParams(vmem_limit_bytes=62 * 2**20),
        name="finish",
    )(out_rows, small, grads)
    return (
        out_rows[None],
        ln1_gain_grad,
        ln1_bias_grad,
        jnp.swapaxes(qkv_grad.reshape(1, 3, local_width, width), 2, 3),
        qkv_bias_grad[None],
        out_grad[None],
        out_bias_grad,
        ln2_gain_grad,
        ln2_bias_grad,
        fc_grad[None],
        fc_bias_grad,
        proj_grad[None],
        proj_bias_grad,
    )


def solution(mesh):
    return jax.shard_map(
        functools.partial(local, mesh.shape["dp"] == 4),
        mesh=mesh,
        in_specs=(
            P("section", "dp", "mp", None),
            P("dp", None),
            P("section", None),
            P("section", None),
            P("section", None, None, "mp"),
            P("section", None, "mp"),
            P("section", "mp", None),
            P("section", None),
            P("section", None),
            P("section", None),
            P("section", None, "mp"),
            P("section", "mp"),
            P("section", "mp", None),
            P("section", None),
        ),
        out_specs=(
            P("section", "dp", "mp", None),
            P("section", None),
            P("section", None),
            P("section", None, None, "mp"),
            P("section", None, "mp"),
            P("section", "mp", None),
            P("section", None),
            P("section", None),
            P("section", None),
            P("section", None, "mp"),
            P("section", "mp"),
            P("section", "mp", None),
            P("section", None),
        ),
        check_vma=False,
    )
```

```python
import functools

import jax
import jax.numpy as jnp
from jax import lax
from jax.experimental import pallas as pl
from jax.experimental.pallas import tpu as pltpu
from jax.sharding import PartitionSpec as P

HEAD_DIM = 64
BRANCH_SCALE = 0.14433756729740643
NORM_EPS = 1e-05
GELU_RATE = 0.7978845608028654
GELU_CUBE = 0.044715
NEGATIVE = -1e30
BLOCK = 96
TILES = 4
BEHIND = 3
MESH = pl.DeviceIdType.MESH
BF16 = jnp.bfloat16
F32 = jnp.float32


def dot_nn(a, b):
    return lax.dot_general(a, b, (((1,), (0,)), ((), ())), preferred_element_type=F32)


def dot_nt(a, b):
    return lax.dot_general(a, b, (((1,), (1,)), ((), ())), preferred_element_type=F32)


def dot_tn(a, b):
    return lax.dot_general(a, b, (((0,), (0,)), ((), ())), preferred_element_type=F32)


def normed(values):
    center = values - jnp.mean(values, axis=-1, keepdims=True)
    rate = lax.rsqrt(jnp.mean(center * center, axis=-1, keepdims=True) + NORM_EPS)
    return center * rate, rate


def norm_backward(grad, hat, rate, gain):
    scaled = grad * gain
    return rate * (
        scaled
        - jnp.mean(scaled, axis=-1, keepdims=True)
        - hat * jnp.mean(scaled * hat, axis=-1, keepdims=True)
    )


def column_sum(values):
    return jnp.sum(values.astype(F32), axis=0, keepdims=True)


def remote(src, dst, send_sem, recv_sem, device):
    return pltpu.make_async_remote_copy(
        src_ref=src,
        dst_ref=dst,
        send_sem=send_sem,
        recv_sem=recv_sem,
        device_id=device,
        device_id_type=MESH,
    )


def kernel(
    z_line,
    order_ref,
    boundary_ref,
    ln1_gain_ref,
    ln1_bias_ref,
    w_qkv_ref,
    qkv_bias_ref,
    w_out_ref,
    out_bias_ref,
    ln2_gain_ref,
    ln2_bias_ref,
    w_fc_ref,
    fc_bias_ref,
    w_proj_ref,
    proj_bias_ref,
    rows_out,
    small_out,
    grads_out,
    raw,
    slots,
    weights,
    biases,
    ends,
    results,
    rows_recv,
    n1,
    n2,
    qkv,
    probs,
    attended,
    hidden,
    hidden_grad,
    act,
    slope,
    pre_grad,
    m_grad,
    r_grad,
    head_grad,
    qkv_grad,
    part,
    part_recv,
    grads,
    grads_other,
    grads_y,
    grads_pair,
    grads_mid,
    small,
    small_other,
    small_y,
    small_pair,
    small_mid,
    local_sem,
    entry_send,
    entry_recv,
    weight_y_send,
    weight_y_recv,
    weight_z_send,
    weight_z_recv,
    part_send,
    part_recv_sem,
    far_core_send,
    far_core_recv,
    far_send,
    far_recv,
    far_back_send,
    far_back_recv,
    share_send,
    share_recv,
    share_core_send,
    share_core_recv,
    cross_send,
    cross_recv,
    cross_core_send,
    cross_core_recv,
    leave_send,
    leave_recv,
    grad_y_send,
    grad_y_recv,
    grad_pair_send,
    grad_pair_recv,
    grad_mid_send,
    grad_mid_recv,
    grad_out_sem,
):
    s, d, m = lax.axis_index("section"), lax.axis_index("dp"), lax.axis_index("mp")
    core, chip = lax.rem(m, 2), lax.div(m, 2)
    half = lax.rem(d, 2)
    across_m = 2 * (1 - chip) + core
    sibling = (s, d, 2 * chip + 1 - core)
    across = (s, d, across_m)
    other_section = (1 - s, d, m)
    pair = (s, d + 1 - 2 * half, m)
    middle = (s, 3 - d, m)
    is_first, is_second = s == 0, s == 1
    is_mid = lax.div(d + 1, 2) == 1
    is_end = lax.div(d + 1, 2) != 1

    rows = boundary_ref.shape[2]
    length, width = n1.shape[1:]
    tile = length // TILES
    piece = tile // 2
    big = 2 * tile
    local_width = attended.shape[2]
    units = act.shape[2]
    heads = local_width // HEAD_DIM
    scale = HEAD_DIM ** (-0.5)
    qkv_rows = 3 * local_width
    out_at, fc_at, proj_at = qkv_rows, qkv_rows + local_width, qkv_rows + local_width + width
    weight_rows = weights.shape[1]
    blocks = weight_rows // BLOCK
    ends_in, ends_grad = 2 * s, 2 * (1 - s)

    def set_rows(index):
        return index * (1 - s)

    def set_weights(index):
        return index * s

    def tile_rows(index):
        return slice(index * tile, (index + 1) * tile)

    def big_rows(index):
        return slice(index * big, (index + 1) * big)

    def piece_rows(index, which):
        return pl.ds(pl.multiple_of(index * tile + which * piece, piece), piece)

    partners = [sibling, across, other_section]
    if z_line:
        partners += [pair, middle]
    barrier = pltpu.get_barrier_semaphore()
    for device in partners:
        pl.semaphore_signal(barrier, inc=1, device_id=device, device_id_type=MESH)

    loads = [
        pltpu.make_async_copy(boundary_ref.at[0], raw, local_sem.at[0]),
        pltpu.make_async_copy(
            w_qkv_ref.at[0], weights.at[0, pl.ds(0, qkv_rows)], local_sem.at[1]
        ),
        pltpu.make_async_copy(
            w_out_ref.at[0], weights.at[0, pl.ds(out_at, local_width)], local_sem.at[2]
        ),
        pltpu.make_async_copy(w_fc_ref.at[0], weights.at[0, pl.ds(fc_at, width)], local_sem.at[3]),
        pltpu.make_async_copy(
            w_proj_ref.at[0], weights.at[0, pl.ds(proj_at, units)], local_sem.at[4]
        ),
    ]
    for load in loads:
        load.start()

    biases[0] = jnp.zeros_like(biases[0])
    biases[0, 0:1, :] = fc_bias_ref[...]
    biases[0, 1:2, 0:local_width] = qkv_bias_ref[0, 0:1, :]
    biases[0, 2:3, 0:local_width] = qkv_bias_ref[0, 1:2, :]
    small[...] = jnp.zeros_like(small)
    small_other[...] = jnp.zeros_like(small_other)

    loads[0].wait()
    for slot in range(2):
        picked = jnp.where(is_first, order_ref[0, slot], slot).astype(F32)
        slots[slot] = (
            raw[0].astype(F32) * (1.0 - picked) + raw[1].astype(F32) * picked
        ).astype(BF16)

    pl.semaphore_wait(barrier, len(partners))

    def token_rows(index):
        return pl.ds(pl.multiple_of(index * rows, rows), rows)

    def entry_across(which):
        slot = 1 - chip if which == 0 else chip
        return remote(
            slots.at[slot],
            ends.at[which, token_rows(m)],
            entry_send.at[which],
            entry_recv.at[which],
            across,
        )

    def entry_sibling(which):
        slot = chip if which == 0 else 1 - chip
        return remote(
            slots.at[slot],
            ends.at[which, token_rows(m)],
            entry_send.at[2 + which],
            entry_recv.at[2 + which],
            sibling,
        )

    def entry_forward(which):
        at = token_rows(across_m)
        return remote(
            ends.at[which, at],
            ends.at[which, at],
            entry_send.at[4 + which],
            entry_recv.at[4 + which],
            sibling,
        )

    bias_copy = remote(biases.at[0], biases.at[1], entry_send.at[6], entry_recv.at[6], across)

    def entry_start(which):
        entry_across(which).start()
        entry_sibling(which).start()
        slot = chip if which == 0 else 1 - chip
        ends[which, token_rows(m), :] = slots[slot]

    def entry_finish(which):
        entry_across(which).wait_recv()
        entry_forward(which).start()
        entry_sibling(which).wait_recv()
        entry_forward(which).wait_recv()

    @pl.when(is_first)
    def _():
        entry_start(1)
        entry_start(0)

    y_blocks = blocks // 2 if z_line else blocks

    def weight_block(index):
        return pl.ds(pl.multiple_of(index * BLOCK, BLOCK), BLOCK)

    def near_block(step):
        return weight_block(2 * step + half if z_line else step)

    def weight_y(step):
        return remote(
            weights.at[0, near_block(step)],
            weights.at[1, near_block(step)],
            weight_y_send.at[step],
            weight_y_recv.at[step],
            across,
        )

    def weight_z(step):
        return remote(
            weights.at[1, near_block(step)],
            weights.at[1, near_block(step)],
            weight_z_send.at[step],
            weight_z_recv.at[step],
            pair,
        )

    def repeat(first, last, action):
        def step_of(step, carry):
            action(step)
            return carry

        lax.fori_loop(first, last, step_of, 0)

    y_done = [0]

    def weight_need(row):
        steps = row * y_blocks // weight_rows
        if z_line and steps > y_done[0]:
            first, y_done[0] = y_done[0], steps

            @pl.when(is_second)
            def _():
                repeat(first, steps, lambda step: weight_z(step).wait_recv())

    def weight_pass(step):
        weight_y(step).wait_recv()
        if z_line:
            weight_z(step).start()

    for load in loads[1:]:
        load.wait()

    def cross(index):
        at = piece_rows(index, core)
        return remote(
            results.at[s, at],
            ends.at[2, at],
            cross_send.at[index],
            cross_recv.at[index],
            other_section,
        )

    def cross_core(index):
        at = piece_rows(index, core)
        return remote(
            ends.at[2, at],
            ends.at[2, at],
            cross_core_send.at[index],
            cross_core_recv.at[index],
            sibling,
        )

    shared = (n2, m_grad, r_grad)

    def share(which, index):
        at = piece_rows(index, core)
        return remote(
            shared[which].at[0, at],
            shared[which].at[1, at],
            share_send.at[which, index],
            share_recv.at[which, index],
            across,
        )

    def share_core(which, index):
        at = piece_rows(index, core)
        return remote(
            shared[which].at[1, at],
            shared[which].at[1, at],
            share_core_send.at[which, index],
            share_core_recv.at[which, index],
            sibling,
        )

    def share_finish(which, index):
        share(which, index).wait_recv()
        share_core(which, index).start()
        share_core(which, index).wait_recv()

    def part_copy(which, index):
        at = pl.ds(index * tile, tile)
        return remote(
            part.at[which, at],
            part_recv.at[which, at],
            part_send.at[which, index],
            part_recv_sem.at[which, index],
            sibling,
        )

    def spare_rows(which, index, core_of):
        return pl.ds(
            pl.multiple_of(which * length + index * tile + core_of * piece, piece), piece
        )

    def far_core(which, index):
        return remote(
            grads_y.at[spare_rows(which, index, 1 - core)],
            grads_other.at[spare_rows(which, index, 1 - core)],
            far_core_send.at[which, index],
            far_core_recv.at[which, index],
            sibling,
        )

    def far(which, index):
        return remote(
            grads_y.at[spare_rows(which, index, core)],
            weights.at[1, spare_rows(which, index, core)],
            far_send.at[which, index],
            far_recv.at[which, index],
            across,
        )

    def far_back(which, index):
        at = spare_rows(which, index, core)
        return remote(
            weights.at[1, at],
            weights.at[1, at],
            far_back_send.at[which, index],
            far_back_recv.at[which, index],
            sibling,
        )

    def far_pass(which, index):
        far_core(which, index).wait_recv()
        at = spare_rows(which, index, core)
        grads_y[at, :] = (grads_y[at, :].astype(F32) + grads_other[at, :].astype(F32)).astype(BF16)
        far(which, index).start()

    def part_sum(which, index):
        at = tile_rows(index)
        near = part[which, at, :].astype(F32) + part_recv[which, at, :].astype(F32)
        first = which * length + index * tile
        other = weights[1, first : first + tile, :].astype(F32)
        return near + jnp.where(is_first, other, 0.0)

    def spans_of(step):
        return [
            (slice(first, first + step), range(first // tile, (first + step) // tile))
            for first in range(0, length, step)
        ]

    def far_parts(which, value_of, step=tile, before=None):
        for at, inside in spans_of(step):
            if before is not None:
                for index in inside:
                    before(index)
            first_row = which * length + at.start
            grads_y[first_row : first_row + step, :] = value_of(1, 0, at).astype(BF16)
            for index in inside:
                far_core(which, index).start()
                if index > 0:
                    far_pass(which, index - 1)
        far_pass(which, TILES - 1)

    def own_parts(which, value_of, step=tile):
        for at, inside in spans_of(step):
            part[which, at, :] = value_of(0, 0, at).astype(BF16)
            for index in inside:
                part_copy(which, index).start()

    def both_parts(which, value_of, step=tile):
        for at, inside in spans_of(step):
            part[which, at, :] = (value_of(0, 0, at) + value_of(1, 1, at)).astype(BF16)
            for index in inside:
                part_copy(which, index).start()

    def collect(which, finish, beside=None, first=0, last=TILES):
        for index in range(first, last + 1):
            if index < last:
                @pl.when(is_first)
                def _():
                    far(which, index).wait_recv()
                    far_back(which, index).start()

                if beside is not None:
                    beside(index)
            if index > first:
                @pl.when(is_first)
                def _():
                    far_back(which, index - 1).wait_recv()

                part_copy(which, index - 1).wait_recv()
                finish(index - 1)

    def weight_of(shards, first, count):
        return weights[shards, first : first + count, :]

    def scale_grad(index):
        at = tile_rows(index)
        m_grad[0, at, :] = (BRANCH_SCALE * ends[ends_grad, at, :].astype(F32)).astype(BF16)

    @pl.when(is_second)
    def _():
        bias_copy.start()
        repeat(0, y_blocks, lambda step: weight_y(step).start())
        entry_start(0)
        repeat(0, y_blocks, weight_pass)
        bias_copy.wait_recv()
        entry_finish(0)
        for index in range(TILES):
            scale_grad(index)

    def norm_one(which, source, index):
        at = tile_rows(index)
        hat, _ = normed(ends[source, at, :].astype(F32))
        n1[which, at, :] = (hat * ln1_gain_ref[...] + ln1_bias_ref[...]).astype(BF16)

    @pl.when(is_second)
    def _():
        for index in range(TILES + 1):
            if index < TILES:
                cross(index).wait_recv()
                cross_core(index).start()
            if index > 0:
                cross_core(index - 1).wait_recv()
                norm_one(0, 2, index - 1)

    @pl.when(is_first)
    def _():
        entry_finish(1)
        for index in range(TILES):
            norm_one(1, 1, index)

    causal = lax.broadcasted_iota(jnp.int32, (length, length), 0) >= lax.broadcasted_iota(
        jnp.int32, (length, length), 1
    )

    def bias_of(shards, row, count):
        return biases[shards, row : row + 1, 0:count]

    def head_columns(kind, head):
        first = kind * local_width + head * HEAD_DIM
        return slice(first, first + HEAD_DIM)

    def attention_forward(index):
        source, shards = set_rows(index), set_weights(index)
        queries = dot_nt(n1[source], weight_of(shards, 0, local_width))
        queries = queries + bias_of(shards, 1, local_width)
        qkv[index, :, 0:local_width] = (queries.astype(BF16).astype(F32) * scale).astype(BF16)
        keys = dot_nt(n1[source], weight_of(shards, local_width, local_width))
        qkv[index, :, local_width : 2 * local_width] = keys.astype(BF16)
        values = dot_nt(n1[source], weight_of(shards, 2 * local_width, local_width))
        values = values + bias_of(shards, 2, local_width)
        qkv[index, :, 2 * local_width :] = values.astype(BF16)
        for head in range(heads):
            scores = dot_nt(
                qkv[index, :, head_columns(0, head)], qkv[index, :, head_columns(1, head)]
            )
            scores = jnp.where(causal, scores, NEGATIVE)
            raised = jnp.exp(scores - jnp.max(scores, axis=-1, keepdims=True))
            shares = raised * (1.0 / jnp.sum(raised, axis=-1, keepdims=True))
            probs[index * heads + head] = shares.astype(BF16)
            attended[index, :, head * HEAD_DIM : (head + 1) * HEAD_DIM] = dot_nn(
                probs[index * heads + head], qkv[index, :, head_columns(2, head)]
            ).astype(BF16)

    weight_need(out_at)
    attention_forward(1)

    def attention_part(index, shards, at):
        return dot_nn(attended[index, at, :], weight_of(shards, out_at, local_width))

    @pl.when(is_first)
    def _():
        far_parts(0, attention_part)
        entry_finish(0)
        for index in range(TILES):
            norm_one(0, 0, index)

    attention_forward(0)

    weight_need(fc_at)

    @pl.when(is_first)
    def _():
        own_parts(0, attention_part)

    @pl.when(is_second)
    def _():
        both_parts(0, attention_part)

    def attention_out(index):
        at = tile_rows(index)
        held = ends[ends_in, at, :].astype(F32) + BRANCH_SCALE * (
            part_sum(0, index) + out_bias_ref[...]
        )
        hidden[at, :] = held
        hat, _ = normed(held)
        n2[0, at, :] = (hat * ln2_gain_ref[...] + ln2_bias_ref[...]).astype(BF16)

        @pl.when(is_first)
        def _():
            share(0, index).start()

    def activate(index, source, shards, at):
        u = dot_nn(n2[source, at, :], weight_of(shards, fc_at, width)) + bias_of(shards, 0, units)
        square = u * u
        bent = jnp.tanh(GELU_RATE * (u + GELU_CUBE * u * square))
        act[index, at, :] = (0.5 * u * (1.0 + bent)).astype(BF16)
        slope[index, at, :] = (
            0.5 * (1.0 + bent)
            + (0.5 * GELU_RATE) * u * (1.0 - bent * bent) * (1.0 + (3.0 * GELU_CUBE) * square)
        ).astype(BF16)

    for index in range(length // big):
        collect(0, attention_out, first=2 * index, last=2 * index + 2)
        if index == 0:
            weight_need(proj_at)
        activate(0, 0, 0, big_rows(index))

        @pl.when(is_second)
        def _():
            activate(1, 0, 1, big_rows(index))

    def mlp_part(index, shards, at):
        return dot_nn(act[index, at, :], weight_of(shards, proj_at, units))

    def other_activate(index):
        share_finish(0, index)
        activate(1, 1, 0, tile_rows(index))

    @pl.when(is_first)
    def _():
        own_parts(1, mlp_part)
        far_parts(1, mlp_part, before=other_activate)

    weight_need(weight_rows)

    proj_grad_at, fc_grad_at = 0, units
    out_grad_at = fc_grad_at + width
    qkv_grad_at = out_grad_at + local_width

    def grad_y(step):
        return remote(
            grads_other.at[weight_block(step)],
            grads_y.at[weight_block(step)],
            grad_y_send.at[step],
            grad_y_recv.at[step],
            across,
        )

    def grad_pair(step, source):
        return remote(
            source.at[weight_block(step)],
            grads_pair.at[weight_block(step)],
            grad_pair_send.at[step],
            grad_pair_recv.at[step],
            pair,
        )

    def grad_mid(step):
        return remote(
            grads.at[weight_block(step)],
            grads_mid.at[weight_block(step)],
            grad_mid_send.at[step],
            grad_mid_recv.at[step],
            middle,
        )

    def grad_out(step, source):
        at = weight_block(step)
        return pltpu.make_async_copy(source.at[at], grads_out.at[at], grad_out_sem.at[step])

    def add_into(target, source, step):
        at = weight_block(step)
        target[at, :] = (target[at, :].astype(F32) + source[at, :].astype(F32)).astype(BF16)

    def gather_y(step):
        grad_y(step).wait_recv()
        add_into(grads, grads_y, step)

    def mid_up(step):
        grad_pair(step, grads).wait_recv()
        add_into(grads, grads_pair, step)
        grad_mid(step).start()

    def mid_down(step):
        grad_mid(step).wait_recv()
        add_into(grads_mid, grads, step)
        grad_pair(step, grads_mid).start()
        grad_out(step, grads_mid).start()

    def mid_step(step, gather):
        if gather:
            gather_y(step)
        mid_up(step)

    first_ends, first_mids, second_ends, second_mids = [0], [0], [0], [0]
    first_end, second_end = jnp.logical_and(is_first, is_end), jnp.logical_and(is_second, is_end)
    first_mid, second_mid = jnp.logical_and(is_first, is_mid), jnp.logical_and(is_second, is_mid)

    def pump_ends(done, count, wanted, gather):
        first, last = done[0], done[0] + count
        done[0] = last
        if z_line:
            def up(step):
                if gather:
                    gather_y(step)
                grad_pair(step, grads).start()

            @pl.when(wanted)
            def _():
                repeat(first, last, up)

    def pump_mids(done, count, wanted, gather):
        first, last = done[0], done[0] + count
        done[0] = last
        if z_line:
            def both(step):
                mid_step(step, gather)
                mid_down(step - BEHIND)

            @pl.when(wanted)
            def _():
                if first < BEHIND:
                    repeat(first, min(BEHIND, last), lambda step: mid_step(step, gather))
                if last > BEHIND:
                    repeat(max(first, BEHIND), last, both)

    def pump_first_ends(count):
        pump_ends(first_ends, count, first_end, False)

    def pump_first(count):
        pump_mids(first_mids, count, first_mid, False)

    def pump_second_ends(count):
        pump_ends(second_ends, count, second_end, True)

    def pump_second(count):
        pump_mids(second_mids, count, second_mid, True)

    def blocks_of(first, count):
        return first // BLOCK, (first + count) // BLOCK

    def put_first(first, count, value_of):
        @pl.when(is_first)
        def _():
            grads[first : first + count, :] = (value_of(0) + value_of(1)).astype(BF16)

    def put_second_far(first, count, value_of):
        @pl.when(is_second)
        def _():
            grads_other[first : first + count, :] = value_of(1).astype(BF16)
            repeat(*blocks_of(first, count), lambda step: grad_y(step).start())

    def put_second_near(first, count, value_of):
        @pl.when(is_second)
        def _():
            grads[first : first + count, :] = value_of(0).astype(BF16)

    def set_sum(row, column, index, values):
        total = column_sum(values)
        columns = slice(column, column + total.shape[1])
        if index == 0:
            small[row : row + 1, columns] += total
        else:
            @pl.when(is_first)
            def _():
                small[row : row + 1, columns] += total

            @pl.when(is_second)
            def _():
                small_other[row : row + 1, columns] += total

    def proj_grad(index):
        return dot_tn(act[index], m_grad[set_rows(index)])

    def fc_grad(index):
        return dot_tn(n2[set_rows(index)], pre_grad[index])

    def out_grad(index):
        return dot_tn(attended[index], r_grad[set_rows(index)])

    def in_grad(index):
        return dot_tn(qkv_grad[index], n1[set_rows(index)])

    put_second_far(proj_grad_at, units, proj_grad)

    def layer_out(index):
        at = tile_rows(index)
        results[0, at, :] = (
            hidden[at, :] + BRANCH_SCALE * (part_sum(1, index) + proj_bias_ref[...])
        ).astype(BF16)

        @pl.when(is_first)
        def _():
            cross(index).start()

    @pl.when(is_first)
    def _():
        collect(1, layer_out)

    @pl.when(is_first)
    def _():
        for index in range(TILES + 1):
            if index < TILES:
                cross(index).wait_recv()
                cross_core(index).start()
            if index > 0:
                cross_core(index - 1).wait_recv()
                scale_grad(index - 1)
                share(1, index - 1).start()
        grads[proj_grad_at : proj_grad_at + units, :] = proj_grad(0).astype(BF16)

    def mlp_slope(index):
        for number in range(length // big):
            at = big_rows(number)
            pre_grad[index, at, :] = (
                slope[index, at, :].astype(F32)
                * dot_nt(
                    m_grad[set_rows(index), at, :], weight_of(set_weights(index), proj_at, units)
                )
            ).astype(BF16)
        set_sum(6, 0, index, pre_grad[index])

    def mlp_back_part(index, shards, at):
        return dot_nt(pre_grad[index, at, :], weight_of(shards, fc_at, width))

    small[5:6, :] = column_sum(m_grad[0])
    mlp_slope(0)

    def share_all(which):
        for index in range(TILES):
            share(which, index).wait_recv()
            share_core(which, index).start()
        for index in range(TILES):
            share_core(which, index).wait_recv()

    @pl.when(is_first)
    def _():
        own_parts(2, mlp_back_part, step=big)
        share_all(1)
        at = slice(proj_grad_at, proj_grad_at + units)
        grads[at, :] = (grads[at, :].astype(F32) + proj_grad(1)).astype(BF16)

    pump_first_ends(units // BLOCK)

    mlp_slope(1)

    @pl.when(is_first)
    def _():
        far_parts(2, mlp_back_part, step=big)

    @pl.when(is_second)
    def _():
        both_parts(2, mlp_back_part, step=big)

    put_second_near(proj_grad_at, units, proj_grad)
    put_first(fc_grad_at, width, fc_grad)
    pump_first_ends(width // BLOCK)
    pump_first(1)

    def mlp_back(index):
        at = tile_rows(index)
        n2_grad = part_sum(2, index)
        hat, rate = normed(hidden[at, :])
        small[2:3, :] += column_sum(n2_grad * hat)
        small[3:4, :] += column_sum(n2_grad)
        held = ends[ends_grad, at, :].astype(F32) + norm_backward(
            n2_grad, hat, rate, ln2_gain_ref[...]
        )
        hidden_grad[at, :] = held
        r_grad[0, at, :] = (BRANCH_SCALE * held).astype(BF16)

        @pl.when(is_first)
        def _():
            share(2, index).start()

    def pump_beside(index):
        if index > 0:
            pump_first(1)

    collect(2, mlp_back, pump_beside)
    small[4:5, :] = column_sum(r_grad[0])
    pump_second_ends(1)

    def attention_backward(index):
        shards = set_weights(index)
        head_grad[index] = dot_nt(
            r_grad[set_rows(index)], weight_of(shards, out_at, local_width)
        ).astype(BF16)
        for head in range(heads):
            columns = slice(head * HEAD_DIM, (head + 1) * HEAD_DIM)
            shares = probs[index * heads + head]
            qkv_grad[index, :, head_columns(2, head)] = dot_tn(
                shares, head_grad[index, :, columns]
            ).astype(BF16)
            share_grad = dot_nt(head_grad[index, :, columns], qkv[index, :, head_columns(2, head)])
            wide = shares.astype(F32)
            product = wide * share_grad
            score_grad = (
                product - wide * jnp.sum(product, axis=-1, keepdims=True)
            ).astype(BF16)
            qkv_grad[index, :, head_columns(0, head)] = (
                dot_nn(score_grad, qkv[index, :, head_columns(1, head)]) * scale
            ).astype(BF16)
            qkv_grad[index, :, head_columns(1, head)] = dot_tn(
                score_grad, qkv[index, :, head_columns(0, head)]
            ).astype(BF16)
        set_sum(7, 0, index, qkv_grad[index, :, 0:local_width])
        set_sum(7, 2 * local_width, index, qkv_grad[index, :, 2 * local_width :])

    def attention_back_part(index, shards, at):
        return dot_nn(qkv_grad[index, at, :], weight_of(shards, 0, qkv_rows))

    attention_backward(0)

    @pl.when(is_first)
    def _():
        own_parts(3, attention_back_part)

    pump_first(1)
    pump_second_ends(1)

    @pl.when(is_first)
    def _():
        share_all(2)

    put_first(out_grad_at, local_width, out_grad)
    pump_first(1)

    attention_backward(1)
    pump_first(1)
    pump_second_ends(1)
    pump_second(1)

    @pl.when(is_first)
    def _():
        far_parts(3, attention_back_part)

    @pl.when(is_second)
    def _():
        both_parts(3, attention_back_part)

    pump_first(1)
    pump_second_ends(1)

    put_first(qkv_grad_at, qkv_rows, in_grad)
    pump_first(1)

    def attention_back(index):
        at = tile_rows(index)
        n1_grad = part_sum(3, index)
        hat, rate = normed(ends[ends_in, at, :].astype(F32))
        small[0:1, :] += column_sum(n1_grad * hat)
        small[1:2, :] += column_sum(n1_grad)
        results[1, at, :] = (
            hidden_grad[at, :] + norm_backward(n1_grad, hat, rate, ln1_gain_ref[...])
        ).astype(BF16)

        @pl.when(is_second)
        def _():
            cross(index).start()

    collect(3, attention_back, pump_beside)

    leave = remote(
        results.at[1 - s, token_rows(across_m)], rows_recv, leave_send.at[0], leave_recv.at[0], across
    )
    small_y_copy = remote(small_other, small_y, leave_send.at[1], leave_recv.at[1], across)
    small_other[0:6, :] = small[0:6, :]
    small_y_copy.start()

    @pl.when(is_second)
    def _():
        both_parts(1, mlp_part)

    put_second_far(fc_grad_at, width, fc_grad)
    pump_second_ends(1)
    pump_second(1)
    put_second_near(fc_grad_at, width, fc_grad)

    @pl.when(is_second)
    def _():
        collect(1, layer_out)

    leave.start()
    pump_second_ends(1)
    pump_second(1)
    put_second_far(out_grad_at, local_width, out_grad)
    put_second_near(out_grad_at, local_width, out_grad)
    pump_second_ends(1)
    pump_second(1)
    put_second_far(qkv_grad_at, qkv_rows, in_grad)
    pump_second_ends(1)
    pump_second(1)
    put_second_near(qkv_grad_at, qkv_rows, in_grad)

    small_up = remote(small, small_pair, leave_send.at[2], leave_recv.at[2], pair)
    small_across = remote(small, small_mid, leave_send.at[3], leave_recv.at[3], middle)
    small_down = remote(small_mid, small_pair, leave_send.at[2], leave_recv.at[2], pair)

    if z_line:
        @pl.when(is_end)
        def _():
            small_y_copy.wait_recv()
            small[...] += small_y[...]
            small_up.start()

        pump_first_ends(blocks - first_ends[0])
        pump_second_ends(blocks - second_ends[0])
        near, later = blocks * 2 // 3, blocks * 5 // 6
        pump_first(near - first_mids[0])
        pump_second(near - second_mids[0])

        @pl.when(is_mid)
        def _():
            small_y_copy.wait_recv()
            small_up.wait_recv()
            small[...] += small_y[...]
            small[...] += small_pair[...]
            small_across.start()

        pump_first(later - first_mids[0])
        pump_second(later - second_mids[0])

        @pl.when(is_mid)
        def _():
            small_across.wait_recv()
            small_mid[...] += small[...]
            small_down.start()
            small_out[...] = small_mid[...]

        pump_first(blocks - first_mids[0])
        pump_second(blocks - second_mids[0])

        @pl.when(is_mid)
        def _():
            repeat(blocks - BEHIND, blocks, mid_down)

        @pl.when(is_end)
        def _():
            def take(step):
                grad_pair(step, grads_mid).wait_recv()
                grad_out(step, grads_pair).start()

            repeat(0, blocks, take)
            small_down.wait_recv()
            small_out[...] = small_pair[...]

    else:
        @pl.when(is_second)
        def _():
            repeat(0, blocks, gather_y)

        repeat(0, blocks, lambda step: grad_out(step, grads).start())
        small_y_copy.wait_recv()
        small_out[...] = small[...] + small_y[...]

    leave.wait_recv()
    rows_out[pl.ds(chip, 1)] = results[pl.ds(1 - s, 1), token_rows(m), :].astype(F32)
    rows_out[pl.ds(1 - chip, 1)] = rows_recv[...].astype(F32)[None]
    repeat(0, blocks, lambda step: grad_out(step, grads).wait())

    entry_across(0).wait_send()
    entry_sibling(0).wait_send()
    entry_forward(0).wait_send()
    leave.wait_send()
    small_y_copy.wait_send()
    for index in range(TILES):
        cross(index).wait_send()
        cross_core(index).wait_send()
    for which in range(4):
        for index in range(TILES):
            part_copy(which, index).wait_send()

    @pl.when(is_first)
    def _():
        entry_across(1).wait_send()
        entry_sibling(1).wait_send()
        entry_forward(1).wait_send()
        for which in range(3):
            for index in range(TILES):
                share(which, index).wait_send()
                share_core(which, index).wait_send()
        for which in range(4):
            for index in range(TILES):
                far_core(which, index).wait_send()
                far(which, index).wait_send()
                far_back(which, index).wait_send()

    @pl.when(is_second)
    def _():
        bias_copy.wait_send()
        repeat(0, y_blocks, lambda step: weight_y(step).wait_send())
        if z_line:
            repeat(0, y_blocks, lambda step: weight_z(step).wait_send())
        repeat(0, blocks, lambda step: grad_y(step).wait_send())

    if z_line:
        repeat(0, blocks, lambda step: grad_pair(step, grads).wait_send())

        @pl.when(is_end)
        def _():
            small_up.wait_send()

        @pl.when(is_mid)
        def _():
            repeat(0, blocks, lambda step: grad_mid(step).wait_send())
            small_across.wait_send()
            small_down.wait_send()


def local(
    z_line,
    boundary_in,
    order,
    ln1_gain,
    ln1_bias,
    w_qkv,
    qkv_bias,
    w_out,
    out_bias,
    ln2_gain,
    ln2_bias,
    w_fc,
    fc_bias,
    w_proj,
    proj_bias,
):
    _, micro, rows, width = boundary_in.shape
    local_width = w_qkv.shape[-1]
    units = w_fc.shape[-1]
    length = rows * lax.axis_size("mp")
    heads = local_width // HEAD_DIM
    weight_rows = 4 * local_width + width + units
    blocks = weight_rows // BLOCK
    vmem = pltpu.VMEM
    dma = pltpu.SemaphoreType.DMA
    in_vmem = pl.BlockSpec(memory_space=pltpu.VMEM)
    in_any = pl.BlockSpec(memory_space=pl.ANY)
    in_smem = pl.BlockSpec(memory_space=pltpu.SMEM)
    out_rows, small, grads = pl.pallas_call(
        functools.partial(kernel, z_line),
        out_shape=(
            jax.ShapeDtypeStruct((micro, rows, width), F32),
            jax.ShapeDtypeStruct((8, width), F32),
            jax.ShapeDtypeStruct((weight_rows, width), BF16),
        ),
        in_specs=[
            in_smem,
            in_any,
            in_vmem,
            in_vmem,
            in_any,
            in_vmem,
            in_any,
            in_vmem,
            in_vmem,
            in_vmem,
            in_any,
            in_vmem,
            in_any,
            in_vmem,
        ],
        out_specs=(in_vmem, in_vmem, in_any),
        scratch_shapes=[
            vmem((micro, rows, width), BF16),
            vmem((micro, rows, width), BF16),
            vmem((2, weight_rows, width), BF16),
            vmem((2, 8, width), F32),
            vmem((3, length, width), BF16),
            vmem((2, length, width), BF16),
            vmem((rows, width), BF16),
            vmem((2, length, width), BF16),
            vmem((2, length, width), BF16),
            vmem((2, length, 3 * local_width), BF16),
            vmem((2 * heads, length, length), BF16),
            vmem((2, length, local_width), BF16),
            vmem((length, width), F32),
            vmem((length, width), F32),
            vmem((2, length, units), BF16),
            vmem((2, length, units), BF16),
            vmem((2, length, units), BF16),
            vmem((2, length, width), BF16),
            vmem((2, length, width), BF16),
            vmem((2, length, local_width), BF16),
            vmem((2, length, 3 * local_width), BF16),
            vmem((4, length, width), BF16),
            vmem((4, length, width), BF16),
            vmem((weight_rows, width), BF16),
            vmem((weight_rows, width), BF16),
            vmem((weight_rows, width), BF16),
            vmem((weight_rows, width), BF16),
            vmem((weight_rows, width), BF16),
            vmem((8, width), F32),
            vmem((8, width), F32),
            vmem((8, width), F32),
            vmem((8, width), F32),
            vmem((8, width), F32),
            dma((5,)),
            dma((7,)),
            dma((7,)),
            dma((blocks,)),
            dma((blocks,)),
            dma((blocks,)),
            dma((blocks,)),
            dma((4, TILES)),
            dma((4, TILES)),
            dma((4, TILES)),
            dma((4, TILES)),
            dma((4, TILES)),
            dma((4, TILES)),
            dma((4, TILES)),
            dma((4, TILES)),
            dma((3, TILES)),
            dma((3, TILES)),
            dma((3, TILES)),
            dma((3, TILES)),
            dma((TILES,)),
            dma((TILES,)),
            dma((TILES,)),
            dma((TILES,)),
            dma((4,)),
            dma((4,)),
            dma((blocks,)),
            dma((blocks,)),
            dma((blocks,)),
            dma((blocks,)),
            dma((blocks,)),
            dma((blocks,)),
            dma((blocks,)),
        ],
        compiler_params=pltpu.CompilerParams(
            collective_id=0, has_side_effects=True, vmem_limit_bytes=63 * 2**20
        ),
        name="two_layers",
    )(
        order,
        boundary_in,
        ln1_gain,
        ln1_bias,
        jnp.swapaxes(w_qkv, 2, 3).reshape(1, 3 * local_width, width),
        qkv_bias,
        w_out,
        out_bias,
        ln2_gain,
        ln2_bias,
        w_fc,
        fc_bias,
        w_proj,
        proj_bias,
    )
    if not z_line:
        small, grads = lax.psum((small, grads), "dp")
    def weight_grad(first, count):
        return grads[first : first + count].astype(F32)[None]

    qkv_grad = weight_grad(weight_rows - 3 * local_width, 3 * local_width)
    return (
        out_rows[None],
        small[0:1],
        small[1:2],
        jnp.swapaxes(qkv_grad.reshape(1, 3, local_width, width), 2, 3),
        jnp.stack([small[7, 0:local_width], small[7, 2 * local_width : 3 * local_width]])[None],
        weight_grad(units + width, local_width),
        small[4:5],
        small[2:3],
        small[3:4],
        weight_grad(units, width),
        small[6:7, 0:units],
        weight_grad(0, units),
        small[5:6],
    )


def solution(mesh):
    return jax.shard_map(
        functools.partial(local, mesh.shape["dp"] == 4),
        mesh=mesh,
        in_specs=(
            P("section", "dp", "mp", None),
            P("dp", None),
            P("section", None),
            P("section", None),
            P("section", None, None, "mp"),
            P("section", None, "mp"),
            P("section", "mp", None),
            P("section", None),
            P("section", None),
            P("section", None),
            P("section", None, "mp"),
            P("section", "mp"),
            P("section", "mp", None),
            P("section", None),
        ),
        out_specs=(
            P("section", "dp", "mp", None),
            P("section", None),
            P("section", None),
            P("section", None, None, "mp"),
            P("section", None, "mp"),
            P("section", "mp", None),
            P("section", None),
            P("section", None),
            P("section", None),
            P("section", None, "mp"),
            P("section", "mp"),
            P("section", "mp", None),
            P("section", None),
        ),
        check_vma=False,
    )
```

```python
import functools

import jax
import jax.numpy as jnp
from jax import lax
from jax.experimental import pallas as pl
from jax.experimental.pallas import tpu as pltpu
from jax.sharding import PartitionSpec as P

HEAD_DIM = 64
BRANCH_SCALE = 0.14433756729740643
NORM_EPS = 1e-05
GELU_RATE = 0.7978845608028654
GELU_CUBE = 0.044715
NEGATIVE = -1e30
BLOCK = 96
TILES = 4
LENT = 4
BEHIND = 3
MESH = pl.DeviceIdType.MESH
BF16 = jnp.bfloat16
F32 = jnp.float32


def dot_nn(a, b):
    return lax.dot_general(a, b, (((1,), (0,)), ((), ())), preferred_element_type=F32)


def dot_nt(a, b):
    return lax.dot_general(a, b, (((1,), (1,)), ((), ())), preferred_element_type=F32)


def dot_tn(a, b):
    return lax.dot_general(a, b, (((0,), (0,)), ((), ())), preferred_element_type=F32)


def normed(values):
    center = values - jnp.mean(values, axis=-1, keepdims=True)
    rate = lax.rsqrt(jnp.mean(center * center, axis=-1, keepdims=True) + NORM_EPS)
    return center * rate, rate


def norm_backward(grad, hat, rate, gain):
    scaled = grad * gain
    return rate * (
        scaled
        - jnp.mean(scaled, axis=-1, keepdims=True)
        - hat * jnp.mean(scaled * hat, axis=-1, keepdims=True)
    )


def column_sum(values):
    return jnp.sum(values.astype(F32), axis=0, keepdims=True)


def remote(src, dst, send_sem, recv_sem, device):
    return pltpu.make_async_remote_copy(
        src_ref=src,
        dst_ref=dst,
        send_sem=send_sem,
        recv_sem=recv_sem,
        device_id=device,
        device_id_type=MESH,
    )


def kernel(
    z_line,
    order_ref,
    boundary_ref,
    ln1_gain_ref,
    ln1_bias_ref,
    w_qkv_ref,
    qkv_bias_ref,
    w_out_ref,
    out_bias_ref,
    ln2_gain_ref,
    ln2_bias_ref,
    w_fc_ref,
    fc_bias_ref,
    w_proj_ref,
    proj_bias_ref,
    rows_out,
    small_out,
    grads_out,
    raw,
    slots,
    weights,
    biases,
    ends,
    results,
    rows_recv,
    n1,
    n2,
    qkv,
    probs,
    head_rows,
    attended,
    hidden,
    hidden_grad,
    act,
    slope,
    pre_grad,
    m_grad,
    r_grad,
    qkv_head_grad,
    qkv_grad,
    part,
    part_recv,
    grads,
    grads_other,
    grads_y,
    grads_pair,
    grads_mid,
    small,
    small_other,
    small_y,
    small_pair,
    small_mid,
    local_sem,
    entry_send,
    entry_recv,
    weight_y_send,
    weight_y_recv,
    weight_z_send,
    weight_z_recv,
    part_send,
    part_recv_sem,
    far_core_send,
    far_core_recv,
    far_send,
    far_recv,
    far_back_send,
    far_back_recv,
    share_send,
    share_recv,
    share_core_send,
    share_core_recv,
    cross_send,
    cross_recv,
    cross_core_send,
    cross_core_recv,
    leave_send,
    leave_recv,
    grad_y_send,
    grad_y_recv,
    grad_pair_send,
    grad_pair_recv,
    grad_mid_send,
    grad_mid_recv,
    grad_out_sem,
    lent_send,
    lent_recv,
    back_send,
    back_recv,
):
    s, d, m = lax.axis_index("section"), lax.axis_index("dp"), lax.axis_index("mp")
    core, chip = lax.rem(m, 2), lax.div(m, 2)
    half = lax.rem(d, 2)
    across_m = 2 * (1 - chip) + core
    sibling = (s, d, 2 * chip + 1 - core)
    across = (s, d, across_m)
    other_section = (1 - s, d, m)
    pair = (s, d + 1 - 2 * half, m)
    middle = (s, 3 - d, m)
    is_first, is_second = s == 0, s == 1
    is_mid = lax.div(d + 1, 2) == 1
    is_end = lax.div(d + 1, 2) != 1

    rows = boundary_ref.shape[2]
    length, width = n1.shape[1:]
    tile = length // TILES
    piece = tile // 2
    big = 2 * tile
    local_width = attended.shape[2]
    units = act.shape[2]
    heads = local_width // HEAD_DIM
    tiles_per_big, bigs = big // tile, length // big
    scale = HEAD_DIM ** (-0.5)
    qkv_rows = 3 * local_width
    out_at, fc_at, proj_at = qkv_rows, qkv_rows + local_width, qkv_rows + local_width + width
    weight_rows = weights.shape[1]
    blocks = weight_rows // BLOCK
    ends_in, ends_grad = 2 * s, 2 * (1 - s)

    def set_rows(index):
        return index * (1 - s)

    def set_weights(index):
        return index * s

    def span(index, count):
        start = index * count
        return pl.ds(start if isinstance(start, int) else pl.multiple_of(start, count), count)

    def tile_rows(index):
        return span(index, tile)

    def big_rows(index):
        return span(index, big)

    def piece_rows(index, which):
        return pl.ds(pl.multiple_of(index * tile + which * piece, piece), piece)

    partners = [sibling, across, other_section]
    if z_line:
        partners += [pair, middle]
    barrier = pltpu.get_barrier_semaphore()
    for device in partners:
        pl.semaphore_signal(barrier, inc=1, device_id=device, device_id_type=MESH)

    loads = [
        pltpu.make_async_copy(boundary_ref.at[0], raw, local_sem.at[0]),
        pltpu.make_async_copy(
            w_qkv_ref.at[0], weights.at[0, pl.ds(0, qkv_rows)], local_sem.at[1]
        ),
        pltpu.make_async_copy(
            w_out_ref.at[0], weights.at[0, pl.ds(out_at, local_width)], local_sem.at[2]
        ),
        pltpu.make_async_copy(w_fc_ref.at[0], weights.at[0, pl.ds(fc_at, width)], local_sem.at[3]),
        pltpu.make_async_copy(
            w_proj_ref.at[0], weights.at[0, pl.ds(proj_at, units)], local_sem.at[4]
        ),
    ]
    for load in loads:
        load.start()

    biases[0] = jnp.zeros_like(biases[0])
    biases[0, 0:1, :] = fc_bias_ref[...]
    biases[0, 1:2, 0:local_width] = qkv_bias_ref[0, 0:1, :]
    biases[0, 2:3, 0:local_width] = qkv_bias_ref[0, 1:2, :]
    small[...] = jnp.zeros_like(small)
    small_other[...] = jnp.zeros_like(small_other)

    loads[0].wait()
    for slot in range(2):
        picked = jnp.where(is_first, order_ref[0, slot], slot).astype(F32)
        slots[slot] = (
            raw[0].astype(F32) * (1.0 - picked) + raw[1].astype(F32) * picked
        ).astype(BF16)

    pl.semaphore_wait(barrier, len(partners))

    def token_rows(index):
        return pl.ds(pl.multiple_of(index * rows, rows), rows)

    def entry_across(which):
        slot = 1 - chip if which == 0 else chip
        return remote(
            slots.at[slot],
            ends.at[which, token_rows(m)],
            entry_send.at[which],
            entry_recv.at[which],
            across,
        )

    def entry_sibling(which):
        slot = chip if which == 0 else 1 - chip
        return remote(
            slots.at[slot],
            ends.at[which, token_rows(m)],
            entry_send.at[2 + which],
            entry_recv.at[2 + which],
            sibling,
        )

    def entry_forward(which):
        at = token_rows(across_m)
        return remote(
            ends.at[which, at],
            ends.at[which, at],
            entry_send.at[4 + which],
            entry_recv.at[4 + which],
            sibling,
        )

    bias_copy = remote(biases.at[0], biases.at[1], entry_send.at[6], entry_recv.at[6], across)

    def entry_start(which):
        entry_across(which).start()
        entry_sibling(which).start()
        slot = chip if which == 0 else 1 - chip
        ends[which, token_rows(m), :] = slots[slot]

    def entry_finish(which):
        entry_across(which).wait_recv()
        entry_forward(which).start()
        entry_sibling(which).wait_recv()
        entry_forward(which).wait_recv()

    @pl.when(is_first)
    def _():
        entry_start(1)
        entry_start(0)

    y_blocks = blocks // 2 if z_line else blocks

    def weight_block(index):
        return pl.ds(pl.multiple_of(index * BLOCK, BLOCK), BLOCK)

    def near_block(step):
        return weight_block(2 * step + half if z_line else step)

    def weight_y(step):
        return remote(
            weights.at[0, near_block(step)],
            weights.at[1, near_block(step)],
            weight_y_send.at[step],
            weight_y_recv.at[step],
            across,
        )

    def weight_z(step):
        return remote(
            weights.at[1, near_block(step)],
            weights.at[1, near_block(step)],
            weight_z_send.at[step],
            weight_z_recv.at[step],
            pair,
        )

    def repeat(first, last, action):
        def step_of(step, carry):
            action(step)
            return carry

        lax.fori_loop(first, last, step_of, 0)

    y_done = [0]

    def weight_need(row):
        steps = row * y_blocks // weight_rows
        if z_line and steps > y_done[0]:
            first, y_done[0] = y_done[0], steps

            @pl.when(is_second)
            def _():
                repeat(first, steps, lambda step: weight_z(step).wait_recv())

    def weight_pass(step):
        weight_y(step).wait_recv()
        if z_line:
            weight_z(step).start()

    for load in loads[1:]:
        load.wait()

    def cross(index):
        at = piece_rows(index, core)
        return remote(
            results.at[s, at],
            ends.at[2, at],
            cross_send.at[index],
            cross_recv.at[index],
            other_section,
        )

    def cross_core(index):
        at = piece_rows(index, core)
        return remote(
            ends.at[2, at],
            ends.at[2, at],
            cross_core_send.at[index],
            cross_core_recv.at[index],
            sibling,
        )

    shared = (n2, m_grad, r_grad)

    def share(which, index):
        at = piece_rows(index, core)
        return remote(
            shared[which].at[0, at],
            shared[which].at[1, at],
            share_send.at[which, index],
            share_recv.at[which, index],
            across,
        )

    def share_core(which, index):
        at = piece_rows(index, core)
        return remote(
            shared[which].at[1, at],
            shared[which].at[1, at],
            share_core_send.at[which, index],
            share_core_recv.at[which, index],
            sibling,
        )

    def share_finish(which, index):
        share(which, index).wait_recv()
        share_core(which, index).start()
        share_core(which, index).wait_recv()

    def part_copy(which, index):
        at = tile_rows(index)
        return remote(
            part.at[which, at],
            part_recv.at[which, at],
            part_send.at[which, index],
            part_recv_sem.at[which, index],
            sibling,
        )

    def spare_rows(which, index, core_of):
        return pl.ds(
            pl.multiple_of(which * length + index * tile + core_of * piece, piece), piece
        )

    def far_core(which, index):
        return remote(
            grads_y.at[spare_rows(which, index, 1 - core)],
            grads_other.at[spare_rows(which, index, 1 - core)],
            far_core_send.at[which, index],
            far_core_recv.at[which, index],
            sibling,
        )

    def far(which, index):
        return remote(
            grads_y.at[spare_rows(which, index, core)],
            weights.at[1, spare_rows(which, index, core)],
            far_send.at[which, index],
            far_recv.at[which, index],
            across,
        )

    def far_back(which, index):
        at = spare_rows(which, index, core)
        return remote(
            weights.at[1, at],
            weights.at[1, at],
            far_back_send.at[which, index],
            far_back_recv.at[which, index],
            sibling,
        )

    def far_pass(which, index):
        far_core(which, index).wait_recv()
        at = spare_rows(which, index, core)
        grads_y[at, :] = (grads_y[at, :].astype(F32) + grads_other[at, :].astype(F32)).astype(BF16)
        far(which, index).start()

    def part_sum(which, index):
        at = tile_rows(index)
        near = part[which, at, :].astype(F32) + part_recv[which, at, :].astype(F32)
        other = weights[1, span(which * TILES + index, tile), :].astype(F32)
        return near + jnp.where(is_first, other, 0.0)

    def far_parts(which, value_of, per=1, before=None):
        def step(number):
            for index in range(per):
                if before is not None:
                    before(number * per + index)
            grads_y[span(which * (TILES // per) + number, per * tile), :] = value_of(
                1, 0, span(number, per * tile)
            ).astype(BF16)
            for index in range(per):
                far_core(which, number * per + index).start()

            @pl.when(number > 0)
            def _():
                for index in range(per):
                    far_pass(which, (number - 1) * per + index)

        repeat(0, TILES // per, step)
        for index in range(per):
            far_pass(which, TILES - per + index)

    def own_parts(which, value_of, per=1):
        def step(number):
            at = span(number, per * tile)
            part[which, at, :] = value_of(0, 0, at).astype(BF16)
            for index in range(per):
                part_copy(which, number * per + index).start()

        repeat(0, TILES // per, step)

    def both_parts(which, value_of, per=1):
        def step(number):
            at = span(number, per * tile)
            part[which, at, :] = (value_of(0, 0, at) + value_of(1, 1, at)).astype(BF16)
            for index in range(per):
                part_copy(which, number * per + index).start()

        repeat(0, TILES // per, step)

    def collect(which, finish, beside=None, start=0, last=TILES):
        def far_next(index):
            far(which, index).wait_recv()
            far_back(which, index).start()

        @pl.when(is_first)
        def _():
            far_next(start)

        def step(index):
            @pl.when(is_first)
            def _():
                @pl.when(index + 1 < last)
                def _():
                    far_next(index + 1)

                if beside is not None:
                    beside(index)
                far_back(which, index).wait_recv()

            part_copy(which, index).wait_recv()
            finish(index)

        repeat(start, last, step)

    def weight_of(shards, first, count):
        return weights[shards, first : first + count, :]

    def scale_grad(index):
        at = tile_rows(index)
        m_grad[0, at, :] = (BRANCH_SCALE * ends[ends_grad, at, :].astype(F32)).astype(BF16)

    @pl.when(is_second)
    def _():
        bias_copy.start()
        repeat(0, y_blocks, lambda step: weight_y(step).start())
        entry_start(0)
        repeat(0, y_blocks, weight_pass)
        bias_copy.wait_recv()
        entry_finish(0)
        repeat(0, TILES, scale_grad)

    def norm_one(which, source, index):
        at = tile_rows(index)
        hat, _ = normed(ends[source, at, :].astype(F32))
        n1[which, at, :] = (hat * ln1_gain_ref[...] + ln1_bias_ref[...]).astype(BF16)

    def cross_receive(action):
        cross(0).wait_recv()
        cross_core(0).start()

        def step(index):
            @pl.when(index + 1 < TILES)
            def _():
                cross(index + 1).wait_recv()
                cross_core(index + 1).start()

            cross_core(index).wait_recv()
            action(index)

        repeat(0, TILES, step)

    @pl.when(is_second)
    def _():
        cross_receive(lambda index: norm_one(0, 2, index))

    @pl.when(is_first)
    def _():
        entry_finish(1)
        repeat(0, TILES, lambda index: norm_one(1, 1, index))

    causal = lax.broadcasted_iota(jnp.int32, (length, length), 0) >= lax.broadcasted_iota(
        jnp.int32, (length, length), 1
    )

    def bias_of(shards, row, count):
        return biases[shards, row : row + 1, 0:count]

    def head_columns(kind, head):
        first = kind * local_width + head * HEAD_DIM
        return slice(first, first + HEAD_DIM)

    def attention_forward(index):
        source, shards = set_rows(index), set_weights(index)

        def project(number):
            at = big_rows(number)
            for kind in range(3):
                values = dot_nt(
                    n1[source, at, :], weight_of(shards, kind * local_width, local_width)
                )
                if kind == 0:
                    values = values + bias_of(shards, 1, local_width)
                if kind == 2:
                    values = values + bias_of(shards, 2, local_width)
                values = values.astype(BF16)
                if kind == 0:
                    values = (values.astype(F32) * scale).astype(BF16)
                for head in range(heads):
                    qkv[index, kind, head, at, :] = values[:, head_columns(0, head)]

        repeat(0, bigs, project)

        def attend(head):
            scores = dot_nt(qkv[index, 0, head], qkv[index, 1, head])
            scores = jnp.where(causal, scores, NEGATIVE)
            raised = jnp.exp(scores - jnp.max(scores, axis=-1, keepdims=True))
            shares = raised * (1.0 / jnp.sum(raised, axis=-1, keepdims=True))
            shares = shares.astype(BF16)
            probs[index * heads + head] = shares
            head_rows[head] = dot_nn(shares, qkv[index, 2, head]).astype(BF16)

        repeat(0, heads, attend)
        for head in range(heads):
            attended[index, :, head_columns(0, head)] = head_rows[head]

    weight_need(out_at)
    attention_forward(1)

    def attention_part(index, shards, at):
        return dot_nn(attended[index, at, :], weight_of(shards, out_at, local_width))

    @pl.when(is_first)
    def _():
        far_parts(0, attention_part)
        entry_finish(0)
        repeat(0, TILES, lambda index: norm_one(0, 0, index))

    attention_forward(0)

    weight_need(fc_at)

    @pl.when(is_first)
    def _():
        own_parts(0, attention_part)

    @pl.when(is_second)
    def _():
        both_parts(0, attention_part)

    def attention_out(index):
        at = tile_rows(index)
        held = ends[ends_in, at, :].astype(F32) + BRANCH_SCALE * (
            part_sum(0, index) + out_bias_ref[...]
        )
        hidden[at, :] = held
        hat, _ = normed(held)
        n2[0, at, :] = (hat * ln2_gain_ref[...] + ln2_bias_ref[...]).astype(BF16)

        @pl.when(is_first)
        def _():
            share(0, index).start()

    def activate(index, source, shards, at):
        u = dot_nn(n2[source, at, :], weight_of(shards, fc_at, width)) + bias_of(shards, 0, units)
        square = u * u
        bent = jnp.tanh(GELU_RATE * (u + GELU_CUBE * u * square))
        act[index, at, :] = (0.5 * u * (1.0 + bent)).astype(BF16)
        slope[index, at, :] = (
            0.5 * (1.0 + bent)
            + (0.5 * GELU_RATE) * u * (1.0 - bent * bent) * (1.0 + (3.0 * GELU_CUBE) * square)
        ).astype(BF16)

    weight_need(proj_at)

    def first_half(number):
        collect(
            0, attention_out, start=number * tiles_per_big, last=(number + 1) * tiles_per_big
        )
        activate(0, 0, 0, big_rows(number))

        @pl.when(is_second)
        def _():
            activate(1, 0, 1, big_rows(number))

    repeat(0, bigs, first_half)

    def mlp_part(index, shards, at):
        return dot_nn(act[index, at, :], weight_of(shards, proj_at, units))

    def other_activate(index):
        share_finish(0, index)
        activate(1, 1, 0, tile_rows(index))

    @pl.when(is_first)
    def _():
        own_parts(1, mlp_part)
        far_parts(1, mlp_part, before=other_activate)

    weight_need(weight_rows)

    proj_grad_at, fc_grad_at = 0, units
    out_grad_at = fc_grad_at + width
    qkv_grad_at = out_grad_at + local_width

    def grad_y(step):
        return remote(
            grads_other.at[weight_block(step)],
            grads_y.at[weight_block(step)],
            grad_y_send.at[step],
            grad_y_recv.at[step],
            across,
        )

    def grad_pair(step, source):
        return remote(
            source.at[weight_block(step)],
            grads_pair.at[weight_block(step)],
            grad_pair_send.at[step],
            grad_pair_recv.at[step],
            pair,
        )

    def grad_mid(step):
        return remote(
            grads.at[weight_block(step)],
            grads_mid.at[weight_block(step)],
            grad_mid_send.at[step],
            grad_mid_recv.at[step],
            middle,
        )

    def grad_out(step, source):
        at = weight_block(step)
        return pltpu.make_async_copy(source.at[at], grads_out.at[at], grad_out_sem.at[step])

    def add_into(target, source, step):
        at = weight_block(step)
        target[at, :] = (target[at, :].astype(F32) + source[at, :].astype(F32)).astype(BF16)

    def gather_y(step):
        grad_y(step).wait_recv()
        add_into(grads, grads_y, step)

    def mid_up(step):
        grad_pair(step, grads).wait_recv()
        add_into(grads, grads_pair, step)
        grad_mid(step).start()

    def mid_down(step, second):
        grad_mid(step).wait_recv()
        add_into(grads_mid, grads, step)
        grad_pair(step, grads_mid).start()
        deliver(step, grads_mid, second)

    def deliver(step, source, second):
        if not second:
            grad_out(step, source).start()
            return

        @pl.when(step < blocks)
        def _():
            grad_out(step, source).start()

        @pl.when(step >= blocks)
        def _():
            lent_back(step - blocks, source).start()

    def mid_step(step, gather):
        if gather:
            gather_y(step)
        mid_up(step)

    lent_from = blocks - LENT

    def lent(index):
        return remote(
            grads.at[weight_block(lent_from + index)],
            grads.at[weight_block(blocks + index)],
            lent_send.at[index],
            lent_recv.at[index],
            other_section,
        )

    def lent_back(index, source):
        return remote(
            source.at[weight_block(blocks + index)],
            source.at[weight_block(lent_from + index)],
            back_send.at[index],
            back_recv.at[index],
            other_section,
        )

    def gather(step):
        @pl.when(step < blocks)
        def _():
            gather_y(step)

        @pl.when(step >= blocks)
        def _():
            lent(step - blocks).wait_recv()

    first_ends, first_mids, second_ends, second_mids = [0], [0], [0], [0]
    first_end, second_end = jnp.logical_and(is_first, is_end), jnp.logical_and(is_second, is_end)
    first_mid, second_mid = jnp.logical_and(is_first, is_mid), jnp.logical_and(is_second, is_mid)

    def mid_step(step, second):
        if second:
            gather(step)
        mid_up(step)

        @pl.when(step >= BEHIND)
        def _():
            mid_down(step - BEHIND, second)

    def pump_ends(done, last, wanted, second):
        start, done[0] = done[0], last
        if z_line:
            def up(step):
                if second:
                    gather(step)
                grad_pair(step, grads).start()

            @pl.when(wanted)
            def _():
                repeat(start, last, up)

    def pump_mids(done, last, wanted, second):
        start, done[0] = done[0], last
        if z_line:
            @pl.when(wanted)
            def _():
                repeat(start, last, lambda step: mid_step(step, second))

    def pump_first_ends(count):
        pump_ends(first_ends, first_ends[0] + count, first_end, False)

    def pump_first(count):
        pump_mids(first_mids, first_mids[0] + count, first_mid, False)

    def pump_second_ends(count):
        pump_ends(second_ends, second_ends[0] + count, second_end, True)

    def pump_second(count):
        pump_mids(second_mids, second_mids[0] + count, second_mid, True)

    def blocks_of(first, count):
        return first // BLOCK, (first + count) // BLOCK

    def cut_columns(count):
        return (count // 256, 256) if count % 256 == 0 else (1, count)

    def put_first(first, count, value_of):
        steps, columns = cut_columns(count)

        def step(number):
            at = span(number, columns)
            grads[pl.ds(first + number * columns, columns), :] = (
                value_of(0, at) + value_of(1, at)
            ).astype(BF16)

        @pl.when(is_first)
        def _():
            repeat(0, steps, step)

    def put_second(target, index, first, count, value_of):
        steps, columns = cut_columns(count)

        def step(number):
            target[pl.ds(first + number * columns, columns), :] = value_of(
                index, span(number, columns)
            ).astype(BF16)

        @pl.when(is_second)
        def _():
            repeat(0, steps, step)

    def put_second_far(first, count, value_of):
        put_second(grads_other, 1, first, count, value_of)

        @pl.when(is_second)
        def _():
            repeat(*blocks_of(first, count), lambda step: grad_y(step).start())

    def put_second_near(first, count, value_of):
        put_second(grads, 0, first, count, value_of)

    def set_sum(row, column, index, values):
        total = column_sum(values)
        columns = slice(column, column + total.shape[1])
        if index == 0:
            small[row : row + 1, columns] += total
        else:
            @pl.when(is_first)
            def _():
                small[row : row + 1, columns] += total

            @pl.when(is_second)
            def _():
                small_other[row : row + 1, columns] += total

    def proj_grad(index, columns):
        return dot_tn(act[index, :, columns], m_grad[set_rows(index)])

    def fc_grad(index, columns):
        return dot_tn(n2[set_rows(index), :, columns], pre_grad[index])

    def out_grad(index, columns):
        return dot_tn(attended[index, :, columns], r_grad[set_rows(index)])

    def in_grad(index, columns):
        return dot_tn(qkv_grad[index, :, columns], n1[set_rows(index)])

    put_second_far(proj_grad_at, units, proj_grad)

    def layer_out(index):
        at = tile_rows(index)
        results[0, at, :] = (
            hidden[at, :] + BRANCH_SCALE * (part_sum(1, index) + proj_bias_ref[...])
        ).astype(BF16)

        @pl.when(is_first)
        def _():
            cross(index).start()

    @pl.when(is_first)
    def _():
        collect(1, layer_out)

    @pl.when(is_first)
    def _():
        def take(index):
            scale_grad(index)
            share(1, index).start()

        cross_receive(take)

        def own(number):
            columns = span(number, 256)
            grads[span(number, 256), :] = proj_grad(0, columns).astype(BF16)

        repeat(0, units // 256, own)

    def mlp_slope(index):
        def step(number):
            at = big_rows(number)
            values = (
                slope[index, at, :].astype(F32)
                * dot_nt(
                    m_grad[set_rows(index), at, :], weight_of(set_weights(index), proj_at, units)
                )
            ).astype(BF16)
            pre_grad[index, at, :] = values
            set_sum(6, 0, index, values)

        repeat(0, bigs, step)

    def mlp_back_part(index, shards, at):
        return dot_nt(pre_grad[index, at, :], weight_of(shards, fc_at, width))

    def sum_of_tiles(row, source):
        def step(index):
            small[row : row + 1, :] += column_sum(source[0, tile_rows(index), :])

        repeat(0, TILES, step)

    sum_of_tiles(5, m_grad)
    mlp_slope(0)

    def share_all(which):
        def forward(index):
            share(which, index).wait_recv()
            share_core(which, index).start()

        repeat(0, TILES, forward)
        repeat(0, TILES, lambda index: share_core(which, index).wait_recv())

    @pl.when(is_first)
    def _():
        own_parts(2, mlp_back_part, per=tiles_per_big)
        share_all(1)

        def other(number):
            columns = span(number, 256)
            grads[columns, :] = (grads[columns, :].astype(F32) + proj_grad(1, columns)).astype(
                BF16
            )

        repeat(0, units // 256, other)

    pump_first_ends(units // BLOCK)

    mlp_slope(1)

    @pl.when(is_first)
    def _():
        far_parts(2, mlp_back_part, per=tiles_per_big)

    @pl.when(is_second)
    def _():
        both_parts(2, mlp_back_part, per=tiles_per_big)

    put_second_near(proj_grad_at, units, proj_grad)
    put_first(fc_grad_at, width, fc_grad)
    pump_first_ends(width // BLOCK)
    pump_first(1)

    def mlp_back(index):
        at = tile_rows(index)
        n2_grad = part_sum(2, index)
        hat, rate = normed(hidden[at, :])
        small[2:3, :] += column_sum(n2_grad * hat)
        small[3:4, :] += column_sum(n2_grad)
        held = ends[ends_grad, at, :].astype(F32) + norm_backward(
            n2_grad, hat, rate, ln2_gain_ref[...]
        )
        hidden_grad[at, :] = held
        r_grad[0, at, :] = (BRANCH_SCALE * held).astype(BF16)

        @pl.when(is_first)
        def _():
            share(2, index).start()

    def collect_with_pump(which, finish):
        base = first_mids[0]
        first_mids[0] += TILES - 1

        def beside(index):
            if z_line:
                @pl.when(jnp.logical_and(is_mid, index > 0))
                def _():
                    mid_step(base + index - 1, False)

        collect(which, finish, beside)

    collect_with_pump(2, mlp_back)
    sum_of_tiles(4, r_grad)
    pump_second_ends(1)

    def attention_backward(index):
        shards = set_weights(index)

        def project(number):
            at = big_rows(number)
            values = dot_nt(
                r_grad[set_rows(index), at, :], weight_of(shards, out_at, local_width)
            ).astype(BF16)
            for head in range(heads):
                head_rows[head, at, :] = values[:, head_columns(0, head)]

        repeat(0, bigs, project)

        def attend(head):
            shares = probs[index * heads + head]
            rows_grad = head_rows[head]
            qkv_head_grad[2, head] = dot_tn(shares, rows_grad).astype(BF16)
            share_grad = dot_nt(rows_grad, qkv[index, 2, head])
            wide = shares.astype(F32)
            product = wide * share_grad
            score_grad = (product - wide * jnp.sum(product, axis=-1, keepdims=True)).astype(BF16)
            qkv_head_grad[0, head] = (dot_nn(score_grad, qkv[index, 1, head]) * scale).astype(BF16)
            qkv_head_grad[1, head] = dot_tn(score_grad, qkv[index, 0, head]).astype(BF16)

        repeat(0, heads, attend)
        for kind in range(3):
            for head in range(heads):
                qkv_grad[index, :, head_columns(kind, head)] = qkv_head_grad[kind, head]
        set_sum(7, 0, index, qkv_grad[index, :, 0:local_width])
        set_sum(7, 2 * local_width, index, qkv_grad[index, :, 2 * local_width :])

    def attention_back_part(index, shards, at):
        return dot_nn(qkv_grad[index, at, :], weight_of(shards, 0, qkv_rows))

    attention_backward(0)

    @pl.when(is_first)
    def _():
        own_parts(3, attention_back_part)

    pump_first(1)
    pump_second_ends(1)

    @pl.when(is_first)
    def _():
        share_all(2)

    put_first(out_grad_at, local_width, out_grad)
    pump_first(1)

    attention_backward(1)
    pump_first(1)
    pump_second_ends(1)
    pump_second(1)

    @pl.when(is_first)
    def _():
        far_parts(3, attention_back_part)

    @pl.when(is_second)
    def _():
        both_parts(3, attention_back_part)

    pump_first(1)
    pump_second_ends(1)

    put_first(qkv_grad_at, qkv_rows, in_grad)
    if z_line:
        @pl.when(is_first)
        def _():
            repeat(0, LENT, lambda index: lent(index).start())

    pump_first(1)

    def attention_back(index):
        at = tile_rows(index)
        n1_grad = part_sum(3, index)
        hat, rate = normed(ends[ends_in, at, :].astype(F32))
        small[0:1, :] += column_sum(n1_grad * hat)
        small[1:2, :] += column_sum(n1_grad)
        results[1, at, :] = (
            hidden_grad[at, :] + norm_backward(n1_grad, hat, rate, ln1_gain_ref[...])
        ).astype(BF16)

        @pl.when(is_second)
        def _():
            cross(index).start()

    collect_with_pump(3, attention_back)

    leave = remote(
        results.at[1 - s, token_rows(across_m)], rows_recv, leave_send.at[0], leave_recv.at[0], across
    )
    small_y_copy = remote(small_other, small_y, leave_send.at[1], leave_recv.at[1], across)
    small_other[0:6, :] = small[0:6, :]
    small_y_copy.start()

    @pl.when(is_second)
    def _():
        both_parts(1, mlp_part)

    put_second_far(fc_grad_at, width, fc_grad)
    pump_second_ends(1)
    pump_second(1)
    put_second_near(fc_grad_at, width, fc_grad)

    @pl.when(is_second)
    def _():
        collect(1, layer_out)

    leave.start()
    pump_second_ends(1)
    pump_second(1)
    put_second_far(out_grad_at, local_width, out_grad)
    put_second_near(out_grad_at, local_width, out_grad)
    pump_second_ends(1)
    pump_second(1)
    put_second_far(qkv_grad_at, qkv_rows, in_grad)
    pump_second_ends(1)
    pump_second(1)
    put_second_near(qkv_grad_at, qkv_rows, in_grad)

    small_up = remote(small, small_pair, leave_send.at[2], leave_recv.at[2], pair)
    small_across = remote(small, small_mid, leave_send.at[3], leave_recv.at[3], middle)
    small_down = remote(small_mid, small_pair, leave_send.at[2], leave_recv.at[2], pair)

    if z_line:
        @pl.when(is_end)
        def _():
            small_y_copy.wait_recv()
            small[...] += small_y[...]
            small_up.start()

        pump_ends(first_ends, lent_from, first_end, False)
        pump_ends(second_ends, blocks + LENT, second_end, True)
        near, later = blocks * 2 // 3, blocks * 3 // 4
        pump_mids(first_mids, near, first_mid, False)
        pump_mids(second_mids, near, second_mid, True)

        @pl.when(is_mid)
        def _():
            small_y_copy.wait_recv()
            small_up.wait_recv()
            small[...] += small_y[...]
            small[...] += small_pair[...]
            small_across.start()

        pump_mids(first_mids, later, first_mid, False)
        pump_mids(second_mids, later, second_mid, True)

        @pl.when(is_mid)
        def _():
            small_across.wait_recv()
            small_mid[...] += small[...]
            small_down.start()
            small_out[...] = small_mid[...]

        pump_mids(first_mids, lent_from, first_mid, False)
        pump_mids(second_mids, blocks + LENT, second_mid, True)

        def back(index, source):
            lent_back(index, source).wait_recv()
            grad_out(lent_from + index, source).start()

        @pl.when(first_mid)
        def _():
            repeat(lent_from - BEHIND, lent_from, lambda step: mid_down(step, False))
            repeat(0, LENT, lambda index: back(index, grads_mid))

        @pl.when(second_mid)
        def _():
            last = blocks + LENT
            repeat(last - BEHIND, last, lambda step: mid_down(step, True))

        def take(step, second):
            grad_pair(step, grads_mid).wait_recv()
            deliver(step, grads_pair, second)

        @pl.when(first_end)
        def _():
            repeat(0, lent_from, lambda step: take(step, False))
            repeat(0, LENT, lambda index: back(index, grads_pair))

        @pl.when(second_end)
        def _():
            repeat(0, blocks + LENT, lambda step: take(step, True))

        @pl.when(is_end)
        def _():
            small_down.wait_recv()
            small_out[...] = small_pair[...]

    else:
        @pl.when(is_second)
        def _():
            repeat(0, blocks, gather_y)

        repeat(0, blocks, lambda step: grad_out(step, grads).start())
        small_y_copy.wait_recv()
        small_out[...] = small[...] + small_y[...]

    leave.wait_recv()
    rows_out[pl.ds(chip, 1)] = results[pl.ds(1 - s, 1), token_rows(m), :].astype(F32)
    rows_out[pl.ds(1 - chip, 1)] = rows_recv[...].astype(F32)[None]
    repeat(0, blocks, lambda step: grad_out(step, grads).wait())

    entry_across(0).wait_send()
    entry_sibling(0).wait_send()
    entry_forward(0).wait_send()
    leave.wait_send()
    small_y_copy.wait_send()
    def tile_sends(index):
        cross(index).wait_send()
        cross_core(index).wait_send()
        for which in range(4):
            part_copy(which, index).wait_send()

    repeat(0, TILES, tile_sends)

    @pl.when(is_first)
    def _():
        entry_across(1).wait_send()
        entry_sibling(1).wait_send()
        entry_forward(1).wait_send()

        def far_sends(index):
            for which in range(3):
                share(which, index).wait_send()
                share_core(which, index).wait_send()
            for which in range(4):
                far_core(which, index).wait_send()
                far(which, index).wait_send()
                far_back(which, index).wait_send()

        repeat(0, TILES, far_sends)

    @pl.when(is_second)
    def _():
        bias_copy.wait_send()
        repeat(0, y_blocks, lambda step: weight_y(step).wait_send())
        if z_line:
            repeat(0, y_blocks, lambda step: weight_z(step).wait_send())
        repeat(0, blocks, lambda step: grad_y(step).wait_send())

    if z_line:
        sent = jnp.where(is_first, lent_from, blocks + LENT)
        repeat(0, sent, lambda step: grad_pair(step, grads).wait_send())

        @pl.when(is_first)
        def _():
            repeat(0, LENT, lambda index: lent(index).wait_send())

        @pl.when(is_second)
        def _():
            repeat(0, LENT, lambda index: lent_back(index, grads_pair).wait_send())

        @pl.when(is_end)
        def _():
            small_up.wait_send()

        @pl.when(is_mid)
        def _():
            repeat(0, sent, lambda step: grad_mid(step).wait_send())
            small_across.wait_send()
            small_down.wait_send()


def local(
    z_line,
    boundary_in,
    order,
    ln1_gain,
    ln1_bias,
    w_qkv,
    qkv_bias,
    w_out,
    out_bias,
    ln2_gain,
    ln2_bias,
    w_fc,
    fc_bias,
    w_proj,
    proj_bias,
):
    _, micro, rows, width = boundary_in.shape
    local_width = w_qkv.shape[-1]
    units = w_fc.shape[-1]
    length = rows * lax.axis_size("mp")
    heads = local_width // HEAD_DIM
    weight_rows = 4 * local_width + width + units
    blocks = weight_rows // BLOCK
    stream_rows = weight_rows + LENT * BLOCK
    vmem = pltpu.VMEM
    dma = pltpu.SemaphoreType.DMA
    in_vmem = pl.BlockSpec(memory_space=pltpu.VMEM)
    in_any = pl.BlockSpec(memory_space=pl.ANY)
    in_smem = pl.BlockSpec(memory_space=pltpu.SMEM)
    out_rows, small, grads = pl.pallas_call(
        functools.partial(kernel, z_line),
        out_shape=(
            jax.ShapeDtypeStruct((micro, rows, width), F32),
            jax.ShapeDtypeStruct((8, width), F32),
            jax.ShapeDtypeStruct((weight_rows, width), BF16),
        ),
        in_specs=[
            in_smem,
            in_any,
            in_vmem,
            in_vmem,
            in_any,
            in_vmem,
            in_any,
            in_vmem,
            in_vmem,
            in_vmem,
            in_any,
            in_vmem,
            in_any,
            in_vmem,
        ],
        out_specs=(in_vmem, in_vmem, in_any),
        scratch_shapes=[
            vmem((micro, rows, width), BF16),
            vmem((micro, rows, width), BF16),
            vmem((2, weight_rows, width), BF16),
            vmem((2, 8, width), F32),
            vmem((3, length, width), BF16),
            vmem((2, length, width), BF16),
            vmem((rows, width), BF16),
            vmem((2, length, width), BF16),
            vmem((2, length, width), BF16),
            vmem((2, 3, heads, length, HEAD_DIM), BF16),
            vmem((2 * heads, length, length), BF16),
            vmem((heads, length, HEAD_DIM), BF16),
            vmem((2, length, local_width), BF16),
            vmem((length, width), F32),
            vmem((length, width), F32),
            vmem((2, length, units), BF16),
            vmem((2, length, units), BF16),
            vmem((2, length, units), BF16),
            vmem((2, length, width), BF16),
            vmem((2, length, width), BF16),
            vmem((3, heads, length, HEAD_DIM), BF16),
            vmem((2, length, 3 * local_width), BF16),
            vmem((4, length, width), BF16),
            vmem((4, length, width), BF16),
            vmem((stream_rows, width), BF16),
            vmem((weight_rows, width), BF16),
            vmem((weight_rows, width), BF16),
            vmem((stream_rows, width), BF16),
            vmem((stream_rows, width), BF16),
            vmem((8, width), F32),
            vmem((8, width), F32),
            vmem((8, width), F32),
            vmem((8, width), F32),
            vmem((8, width), F32),
            dma((5,)),
            dma((7,)),
            dma((7,)),
            dma((blocks,)),
            dma((blocks,)),
            dma((blocks,)),
            dma((blocks,)),
            dma((4, TILES)),
            dma((4, TILES)),
            dma((4, TILES)),
            dma((4, TILES)),
            dma((4, TILES)),
            dma((4, TILES)),
            dma((4, TILES)),
            dma((4, TILES)),
            dma((3, TILES)),
            dma((3, TILES)),
            dma((3, TILES)),
            dma((3, TILES)),
            dma((TILES,)),
            dma((TILES,)),
            dma((TILES,)),
            dma((TILES,)),
            dma((4,)),
            dma((4,)),
            dma((blocks,)),
            dma((blocks,)),
            dma((blocks + LENT,)),
            dma((blocks + LENT,)),
            dma((blocks + LENT,)),
            dma((blocks + LENT,)),
            dma((blocks,)),
            dma((LENT,)),
            dma((LENT,)),
            dma((LENT,)),
            dma((LENT,)),
        ],
        compiler_params=pltpu.CompilerParams(
            collective_id=0, has_side_effects=True, vmem_limit_bytes=63 * 2**20
        ),
        name="two_layers",
    )(
        order,
        boundary_in,
        ln1_gain,
        ln1_bias,
        jnp.swapaxes(w_qkv, 2, 3).reshape(1, 3 * local_width, width),
        qkv_bias,
        w_out,
        out_bias,
        ln2_gain,
        ln2_bias,
        w_fc,
        fc_bias,
        w_proj,
        proj_bias,
    )
    if not z_line:
        small, grads = lax.psum((small, grads), "dp")
    def weight_grad(first, count):
        return grads[first : first + count].astype(F32)[None]

    qkv_grad = weight_grad(weight_rows - 3 * local_width, 3 * local_width)
    return (
        out_rows[None],
        small[0:1],
        small[1:2],
        jnp.swapaxes(qkv_grad.reshape(1, 3, local_width, width), 2, 3),
        jnp.stack([small[7, 0:local_width], small[7, 2 * local_width : 3 * local_width]])[None],
        weight_grad(units + width, local_width),
        small[4:5],
        small[2:3],
        small[3:4],
        weight_grad(units, width),
        small[6:7, 0:units],
        weight_grad(0, units),
        small[5:6],
    )


def solution(mesh):
    return jax.shard_map(
        functools.partial(local, mesh.shape["dp"] == 4),
        mesh=mesh,
        in_specs=(
            P("section", "dp", "mp", None),
            P("dp", None),
            P("section", None),
            P("section", None),
            P("section", None, None, "mp"),
            P("section", None, "mp"),
            P("section", "mp", None),
            P("section", None),
            P("section", None),
            P("section", None),
            P("section", None, "mp"),
            P("section", "mp"),
            P("section", "mp", None),
            P("section", None),
        ),
        out_specs=(
            P("section", "dp", "mp", None),
            P("section", None),
            P("section", None),
            P("section", None, None, "mp"),
            P("section", None, "mp"),
            P("section", "mp", None),
            P("section", None),
            P("section", None),
            P("section", None),
            P("section", None, "mp"),
            P("section", "mp"),
            P("section", "mp", None),
            P("section", None),
        ),
        check_vma=False,
    )
```

```python
import functools

import jax
import jax.numpy as jnp
from jax import lax
from jax.experimental import pallas as pl
from jax.experimental.pallas import tpu as pltpu
from jax.sharding import PartitionSpec as P

HEAD_DIM = 64
BRANCH_SCALE = 0.14433756729740643
NORM_EPS = 1e-05
GELU_RATE = 0.7978845608028654
GELU_CUBE = 0.044715
NEGATIVE = -1e30
BLOCK = 48
PUMP = 2
FINISH = 96
FETCH = 96
TILES = 4
LENT = 8
BEHIND = 4
MESH = pl.DeviceIdType.MESH
BF16 = jnp.bfloat16
F32 = jnp.float32


def dot_nn(a, b):
    return lax.dot_general(a, b, (((1,), (0,)), ((), ())), preferred_element_type=F32)


def dot_nt(a, b):
    return lax.dot_general(a, b, (((1,), (1,)), ((), ())), preferred_element_type=F32)


def dot_tn(a, b):
    return lax.dot_general(a, b, (((0,), (0,)), ((), ())), preferred_element_type=F32)


def normed(values):
    center = values - jnp.mean(values, axis=-1, keepdims=True)
    rate = lax.rsqrt(jnp.mean(center * center, axis=-1, keepdims=True) + NORM_EPS)
    return center * rate, rate


def norm_backward(grad, hat, rate, gain):
    scaled = grad * gain
    return rate * (
        scaled
        - jnp.mean(scaled, axis=-1, keepdims=True)
        - hat * jnp.mean(scaled * hat, axis=-1, keepdims=True)
    )


def column_sum(values):
    return jnp.sum(values.astype(F32), axis=0, keepdims=True)


def remote(src, dst, send_sem, recv_sem, device):
    return pltpu.make_async_remote_copy(
        src_ref=src,
        dst_ref=dst,
        send_sem=send_sem,
        recv_sem=recv_sem,
        device_id=device,
        device_id_type=MESH,
    )


def kernel(
    z_line,
    order_ref,
    boundary_ref,
    ln1_gain_ref,
    ln1_bias_ref,
    w_qkv_ref,
    qkv_bias_ref,
    w_out_ref,
    out_bias_ref,
    ln2_gain_ref,
    ln2_bias_ref,
    w_fc_ref,
    fc_bias_ref,
    w_proj_ref,
    proj_bias_ref,
    rows_out,
    small_out,
    grads_out,
    raw,
    slots,
    weights,
    biases,
    ends,
    results,
    rows_recv,
    n1,
    n2,
    qkv,
    probs,
    head_rows,
    attended,
    hidden,
    hidden_grad,
    act,
    slope,
    m_grad,
    r_grad,
    qkv_grad,
    part,
    part_recv,
    grads,
    grads_other,
    grads_y,
    grads_pair,
    grads_mid,
    small,
    small_other,
    small_y,
    small_pair,
    small_mid,
    local_sem,
    entry_send,
    entry_recv,
    weight_y_send,
    weight_y_recv,
    weight_z_send,
    weight_z_recv,
    part_send,
    part_recv_sem,
    far_core_send,
    far_core_recv,
    far_send,
    far_recv,
    far_back_send,
    far_back_recv,
    share_send,
    share_recv,
    share_core_send,
    share_core_recv,
    cross_send,
    cross_recv,
    cross_core_send,
    cross_core_recv,
    leave_send,
    leave_recv,
    grad_y_send,
    grad_y_recv,
    grad_pair_send,
    grad_pair_recv,
    grad_mid_send,
    grad_mid_recv,
    grad_out_sem,
    lent_send,
    lent_recv,
    back_send,
    back_recv,
):
    s, d, m = lax.axis_index("section"), lax.axis_index("dp"), lax.axis_index("mp")
    core, chip = lax.rem(m, 2), lax.div(m, 2)
    half = lax.rem(d, 2)
    across_m = 2 * (1 - chip) + core
    sibling = (s, d, 2 * chip + 1 - core)
    across = (s, d, across_m)
    other_section = (1 - s, d, m)
    pair = (s, d + 1 - 2 * half, m)
    middle = (s, 3 - d, m)
    is_first, is_second = s == 0, s == 1
    is_mid = lax.div(d + 1, 2) == 1
    is_end = lax.div(d + 1, 2) != 1

    rows = boundary_ref.shape[2]
    length, width = n1.shape[1:]
    tile = length // TILES
    piece = tile // 2
    big = 2 * tile
    local_width = attended.shape[2]
    units = act.shape[2]
    heads = local_width // HEAD_DIM
    tiles_per_big, bigs = big // tile, length // big
    scale = HEAD_DIM ** (-0.5)
    qkv_rows = 3 * local_width
    out_at, fc_at, proj_at = qkv_rows, qkv_rows + local_width, qkv_rows + local_width + width
    weight_rows = weights.shape[1]
    blocks = weight_rows // BLOCK
    ends_in, ends_grad = 2 * s, 2 * (1 - s)

    def set_rows(index):
        return index * (1 - s)

    def set_weights(index):
        return index * s

    def span(index, count):
        start = index * count
        return pl.ds(start if isinstance(start, int) else pl.multiple_of(start, count), count)

    def tile_rows(index):
        return span(index, tile)

    def big_rows(index):
        return span(index, big)

    def piece_rows(index, which):
        return pl.ds(pl.multiple_of(index * tile + which * piece, piece), piece)

    partners = [sibling, across, other_section]
    if z_line:
        partners += [pair, middle]
    barrier = pltpu.get_barrier_semaphore()
    for device in partners:
        pl.semaphore_signal(barrier, inc=1, device_id=device, device_id_type=MESH)

    loads = [
        pltpu.make_async_copy(boundary_ref.at[0], raw, local_sem.at[0]),
        pltpu.make_async_copy(
            w_qkv_ref.at[0], weights.at[0, pl.ds(0, qkv_rows)], local_sem.at[1]
        ),
        pltpu.make_async_copy(
            w_out_ref.at[0], weights.at[0, pl.ds(out_at, local_width)], local_sem.at[2]
        ),
        pltpu.make_async_copy(w_fc_ref.at[0], weights.at[0, pl.ds(fc_at, width)], local_sem.at[3]),
        pltpu.make_async_copy(
            w_proj_ref.at[0], weights.at[0, pl.ds(proj_at, units)], local_sem.at[4]
        ),
    ]
    for load in loads:
        load.start()

    biases[0] = jnp.zeros_like(biases[0])
    biases[0, 0:1, :] = fc_bias_ref[...]
    biases[0, 1:2, 0:local_width] = qkv_bias_ref[0, 0:1, :]
    biases[0, 2:3, 0:local_width] = qkv_bias_ref[0, 1:2, :]
    small[...] = jnp.zeros_like(small)
    small_other[...] = jnp.zeros_like(small_other)

    loads[0].wait()
    for slot in range(2):
        picked = jnp.where(is_first, order_ref[0, slot], slot).astype(F32)
        slots[slot] = (
            raw[0].astype(F32) * (1.0 - picked) + raw[1].astype(F32) * picked
        ).astype(BF16)

    pl.semaphore_wait(barrier, len(partners))

    def token_rows(index):
        return pl.ds(pl.multiple_of(index * rows, rows), rows)

    def entry_across(which):
        slot = 1 - chip if which == 0 else chip
        return remote(
            slots.at[slot],
            ends.at[which, token_rows(m)],
            entry_send.at[which],
            entry_recv.at[which],
            across,
        )

    def entry_sibling(which):
        slot = chip if which == 0 else 1 - chip
        return remote(
            slots.at[slot],
            ends.at[which, token_rows(m)],
            entry_send.at[2 + which],
            entry_recv.at[2 + which],
            sibling,
        )

    def entry_forward(which):
        at = token_rows(across_m)
        return remote(
            ends.at[which, at],
            ends.at[which, at],
            entry_send.at[4 + which],
            entry_recv.at[4 + which],
            sibling,
        )

    bias_copy = remote(biases.at[0], biases.at[1], entry_send.at[6], entry_recv.at[6], across)

    def entry_start(which):
        entry_across(which).start()
        entry_sibling(which).start()
        slot = chip if which == 0 else 1 - chip
        ends[which, token_rows(m), :] = slots[slot]

    def entry_pass(which):
        entry_across(which).wait_recv()
        entry_forward(which).start()

    def entry_take(which):
        entry_sibling(which).wait_recv()
        entry_forward(which).wait_recv()

    def entry_finish(which):
        entry_pass(which)
        entry_take(which)

    @pl.when(is_first)
    def _():
        entry_start(1)
        entry_start(0)

    y_blocks = weight_rows // FETCH // (2 if z_line else 1)

    def weight_block(index):
        return pl.ds(pl.multiple_of(index * BLOCK, BLOCK), BLOCK)

    def near_block(step):
        return span(2 * step + half if z_line else step, FETCH)

    def weight_y(step):
        return remote(
            weights.at[0, near_block(step)],
            weights.at[1, near_block(step)],
            weight_y_send.at[step],
            weight_y_recv.at[step],
            across,
        )

    def weight_z(step):
        return remote(
            weights.at[1, near_block(step)],
            weights.at[1, near_block(step)],
            weight_z_send.at[step],
            weight_z_recv.at[step],
            pair,
        )

    def repeat(first, last, action):
        def step_of(step, carry):
            action(step)
            return carry

        lax.fori_loop(first, last, step_of, 0)

    y_done = [0]

    def weight_need(row):
        steps = row * y_blocks // weight_rows
        if z_line and steps > y_done[0]:
            first, y_done[0] = y_done[0], steps

            @pl.when(is_second)
            def _():
                repeat(first, steps, lambda step: weight_z(step).wait_recv())

    def weight_pass(step):
        weight_y(step).wait_recv()
        if z_line:
            weight_z(step).start()

    for load in loads[1:]:
        load.wait()

    def cross(index):
        at = piece_rows(index, core)
        return remote(
            results.at[s, at],
            ends.at[2, at],
            cross_send.at[index],
            cross_recv.at[index],
            other_section,
        )

    def cross_core(index):
        at = piece_rows(index, core)
        return remote(
            ends.at[2, at],
            ends.at[2, at],
            cross_core_send.at[index],
            cross_core_recv.at[index],
            sibling,
        )

    shared = (n2, m_grad, r_grad)

    def share(which, index):
        at = piece_rows(index, core)
        return remote(
            shared[which].at[0, at],
            shared[which].at[1, at],
            share_send.at[which, index],
            share_recv.at[which, index],
            across,
        )

    def share_core(which, index):
        at = piece_rows(index, core)
        return remote(
            shared[which].at[1, at],
            shared[which].at[1, at],
            share_core_send.at[which, index],
            share_core_recv.at[which, index],
            sibling,
        )

    def share_finish(which, index):
        share(which, index).wait_recv()
        share_core(which, index).start()
        share_core(which, index).wait_recv()

    def part_copy(which, index):
        at = tile_rows(index)
        return remote(
            part.at[which, at],
            part_recv.at[which, at],
            part_send.at[which, index],
            part_recv_sem.at[which, index],
            sibling,
        )

    def spare_rows(which, index, core_of):
        return pl.ds(
            pl.multiple_of(which * length + index * tile + core_of * piece, piece), piece
        )

    def far_core(which, index):
        return remote(
            grads_y.at[spare_rows(which, index, 1 - core)],
            grads_other.at[spare_rows(which, index, 1 - core)],
            far_core_send.at[which, index],
            far_core_recv.at[which, index],
            sibling,
        )

    def far(which, index):
        return remote(
            grads_y.at[spare_rows(which, index, core)],
            weights.at[1, spare_rows(which, index, core)],
            far_send.at[which, index],
            far_recv.at[which, index],
            across,
        )

    def far_back(which, index):
        at = spare_rows(which, index, core)
        return remote(
            weights.at[1, at],
            weights.at[1, at],
            far_back_send.at[which, index],
            far_back_recv.at[which, index],
            sibling,
        )

    def far_pass(which, index):
        far_core(which, index).wait_recv()
        at = spare_rows(which, index, core)
        grads_y[at, :] = (grads_y[at, :].astype(F32) + grads_other[at, :].astype(F32)).astype(BF16)
        far(which, index).start()

    def part_sum(which, index):
        at = tile_rows(index)
        near = part[which, at, :].astype(F32) + part_recv[which, at, :].astype(F32)
        other = weights[1, span(which * TILES + index, tile), :].astype(F32)
        return near + jnp.where(is_first, other, 0.0)

    def far_parts(which, value_of, per=1, before=None):
        def step(number):
            for index in range(per):
                if before is not None:
                    before(number * per + index)
            grads_y[span(which * (TILES // per) + number, per * tile), :] = value_of(
                1, 0, span(number, per * tile)
            ).astype(BF16)
            for index in range(per):
                far_core(which, number * per + index).start()

            @pl.when(number > 0)
            def _():
                for index in range(per):
                    far_pass(which, (number - 1) * per + index)

        repeat(0, TILES // per, step)
        for index in range(per):
            far_pass(which, TILES - per + index)

    def own_parts(which, value_of, per=1):
        def step(number):
            at = span(number, per * tile)
            part[which, at, :] = value_of(0, 0, at).astype(BF16)
            for index in range(per):
                part_copy(which, number * per + index).start()

        repeat(0, TILES // per, step)

    def both_parts(which, value_of, per=1):
        def step(number):
            at = span(number, per * tile)
            part[which, at, :] = (value_of(0, 0, at) + value_of(1, 1, at)).astype(BF16)
            for index in range(per):
                part_copy(which, number * per + index).start()

        repeat(0, TILES // per, step)

    def collect(which, finish, beside=None, start=0, last=TILES):
        def far_next(index):
            far(which, index).wait_recv()
            far_back(which, index).start()

        @pl.when(is_first)
        def _():
            far_next(start)

        def step(index):
            @pl.when(is_first)
            def _():
                @pl.when(index + 1 < last)
                def _():
                    far_next(index + 1)

                if beside is not None:
                    beside(index)
                far_back(which, index).wait_recv()

            part_copy(which, index).wait_recv()
            finish(index)

        repeat(start, last, step)

    def weight_of(shards, first, count):
        return weights[shards, first : first + count, :]

    def scale_grad(index):
        at = tile_rows(index)
        m_grad[0, at, :] = (BRANCH_SCALE * ends[ends_grad, at, :].astype(F32)).astype(BF16)

    @pl.when(is_second)
    def _():
        bias_copy.start()
        repeat(0, y_blocks, lambda step: weight_y(step).start())
        entry_start(0)
        repeat(0, y_blocks, weight_pass)
        bias_copy.wait_recv()
        entry_finish(0)
        repeat(0, TILES, scale_grad)

    def norm_one(which, source, index):
        at = tile_rows(index)
        hat, _ = normed(ends[source, at, :].astype(F32))
        n1[which, at, :] = (hat * ln1_gain_ref[...] + ln1_bias_ref[...]).astype(BF16)

    def cross_receive(action):
        cross(0).wait_recv()
        cross_core(0).start()

        def step(index):
            @pl.when(index + 1 < TILES)
            def _():
                cross(index + 1).wait_recv()
                cross_core(index + 1).start()

            cross_core(index).wait_recv()
            action(index)

        repeat(0, TILES, step)

    @pl.when(is_second)
    def _():
        cross_receive(lambda index: norm_one(0, 2, index))

    @pl.when(is_first)
    def _():
        entry_finish(1)
        repeat(0, TILES, lambda index: norm_one(1, 1, index))

    causal = lax.broadcasted_iota(jnp.int32, (length, length), 1) >= lax.broadcasted_iota(
        jnp.int32, (length, length), 0
    )

    def bias_of(shards, row, count):
        return biases[shards, row : row + 1, 0:count]

    def head_columns(kind, head):
        first = kind * local_width + head * HEAD_DIM
        return slice(first, first + HEAD_DIM)

    def attention_forward(index):
        source, shards = set_rows(index), set_weights(index)

        def project(number):
            at = big_rows(number)
            for kind in range(3):
                values = dot_nt(
                    n1[source, at, :], weight_of(shards, kind * local_width, local_width)
                )
                if kind == 0:
                    values = values + bias_of(shards, 1, local_width)
                if kind == 2:
                    values = values + bias_of(shards, 2, local_width)
                values = values.astype(BF16)
                if kind == 0:
                    values = (values.astype(F32) * scale).astype(BF16)
                for head in range(heads):
                    qkv[index, kind, head, at, :] = values[:, head_columns(0, head)]

        repeat(0, bigs, project)

        for head in range(heads):
            scores = dot_nt(qkv[index, 1, head], qkv[index, 0, head])
            scores = jnp.where(causal, scores, NEGATIVE)
            raised = jnp.exp(scores - jnp.max(scores, axis=0, keepdims=True))
            shares = raised * (1.0 / jnp.sum(raised, axis=0, keepdims=True))
            shares = shares.astype(BF16)
            probs[index * heads + head] = shares
            attended[index, :, head_columns(0, head)] = dot_tn(
                shares, qkv[index, 2, head]
            ).astype(BF16)

    weight_need(out_at)
    attention_forward(1)

    def attention_part(index, shards, at):
        return dot_nn(attended[index, at, :], weight_of(shards, out_at, local_width))

    @pl.when(is_first)
    def _():
        entry_pass(0)
        far_parts(0, attention_part)
        entry_take(0)
        repeat(0, TILES, lambda index: norm_one(0, 0, index))

    attention_forward(0)

    weight_need(fc_at)

    @pl.when(is_first)
    def _():
        own_parts(0, attention_part)

    @pl.when(is_second)
    def _():
        both_parts(0, attention_part)

    def attention_out(index):
        at = tile_rows(index)
        held = ends[ends_in, at, :].astype(F32) + BRANCH_SCALE * (
            part_sum(0, index) + out_bias_ref[...]
        )
        hidden[at, :] = held
        hat, _ = normed(held)
        n2[0, at, :] = (hat * ln2_gain_ref[...] + ln2_bias_ref[...]).astype(BF16)

        @pl.when(is_first)
        def _():
            share(0, index).start()

    def activate(index, source, shards, at):
        u = dot_nn(n2[source, at, :], weight_of(shards, fc_at, width)) + bias_of(shards, 0, units)
        square = u * u
        bent = jnp.tanh(GELU_RATE * (u + GELU_CUBE * u * square))
        act[index, at, :] = (0.5 * u * (1.0 + bent)).astype(BF16)
        slope[index, at, :] = (
            0.5 * (1.0 + bent)
            + (0.5 * GELU_RATE) * u * (1.0 - bent * bent) * (1.0 + (3.0 * GELU_CUBE) * square)
        ).astype(BF16)

    weight_need(proj_at)

    def first_half(number):
        collect(
            0, attention_out, start=number * tiles_per_big, last=(number + 1) * tiles_per_big
        )
        activate(set_weights(1), 0, set_weights(1), big_rows(number))

    repeat(0, bigs, first_half)

    def mlp_part(index, shards, at):
        return dot_nn(act[index, at, :], weight_of(shards, proj_at, units))

    def other_activate(index):
        share_finish(0, index)
        activate(1, 1, 0, tile_rows(index))

    @pl.when(is_first)
    def _():
        own_parts(1, mlp_part)
        far_parts(1, mlp_part, before=other_activate)

    weight_need(weight_rows)

    proj_grad_at, fc_grad_at = 0, units
    out_grad_at = fc_grad_at + width
    qkv_grad_at = out_grad_at + local_width

    def grad_y(step):
        return remote(
            grads_other.at[weight_block(step)],
            grads_y.at[weight_block(step)],
            grad_y_send.at[step],
            grad_y_recv.at[step],
            across,
        )

    def grad_pair(step, source):
        return remote(
            source.at[weight_block(step)],
            grads_pair.at[weight_block(step)],
            grad_pair_send.at[step],
            grad_pair_recv.at[step],
            pair,
        )

    def grad_mid(step):
        return remote(
            grads.at[weight_block(step)],
            grads_mid.at[weight_block(step)],
            grad_mid_send.at[step],
            grad_mid_recv.at[step],
            middle,
        )

    def grad_out(step, source):
        at = weight_block(step)
        return pltpu.make_async_copy(source.at[at], grads_out.at[at], grad_out_sem.at[step])

    def add_into(target, source, step):
        at = weight_block(step)
        target[at, :] = (target[at, :].astype(F32) + source[at, :].astype(F32)).astype(BF16)

    def gather_y(step):
        grad_y(step).wait_recv()
        add_into(grads, grads_y, step)

    def mid_up(step):
        grad_pair(step, grads).wait_recv()
        add_into(grads, grads_pair, step)
        grad_mid(step).start()

    def mid_down(step, second):
        grad_mid(step).wait_recv()
        add_into(grads_mid, grads, step)
        grad_pair(step, grads_mid).start()
        deliver(step, grads_mid, second)

    def deliver(step, source, second):
        if not second:
            grad_out(step, source).start()
            return

        @pl.when(step < blocks)
        def _():
            grad_out(step, source).start()

        @pl.when(step >= blocks)
        def _():
            lent_back(step - blocks, source).start()

    def mid_step(step, gather):
        if gather:
            gather_y(step)
        mid_up(step)

    lent_from = blocks - LENT

    def lent(index):
        return remote(
            grads.at[weight_block(lent_from + index)],
            grads.at[weight_block(blocks + index)],
            lent_send.at[index],
            lent_recv.at[index],
            other_section,
        )

    def lent_back(index, source):
        return remote(
            source.at[weight_block(blocks + index)],
            source.at[weight_block(lent_from + index)],
            back_send.at[index],
            back_recv.at[index],
            other_section,
        )

    def gather(step):
        @pl.when(step < blocks)
        def _():
            gather_y(step)

        @pl.when(step >= blocks)
        def _():
            lent(step - blocks).wait_recv()

    first_ends, first_mids, second_ends, second_mids = [0], [0], [0], [0]
    first_end, second_end = jnp.logical_and(is_first, is_end), jnp.logical_and(is_second, is_end)
    first_mid, second_mid = jnp.logical_and(is_first, is_mid), jnp.logical_and(is_second, is_mid)

    def mid_step(step, second):
        if second:
            gather(step)
        mid_up(step)

        @pl.when(step >= BEHIND)
        def _():
            mid_down(step - BEHIND, second)

    def pump_ends(done, last, wanted, second):
        start, done[0] = done[0], last
        if z_line:
            def up(step):
                if second:
                    gather(step)
                grad_pair(step, grads).start()

            @pl.when(wanted)
            def _():
                repeat(start, last, up)

    def pump_mids(done, last, wanted, second):
        start, done[0] = done[0], last
        if z_line:
            @pl.when(wanted)
            def _():
                repeat(start, last, lambda step: mid_step(step, second))

    def pump_first_ends(count):
        pump_ends(first_ends, first_ends[0] + count, first_end, False)

    def pump_first(count):
        pump_mids(first_mids, first_mids[0] + count, first_mid, False)

    def pump_second_ends(count):
        pump_ends(second_ends, second_ends[0] + count, second_end, True)

    def pump_second(count):
        pump_mids(second_mids, second_mids[0] + count, second_mid, True)

    def blocks_of(first, count):
        return first // BLOCK, (first + count) // BLOCK

    def cut_columns(count):
        return (count // 256, 256) if count % 256 == 0 else (1, count)

    def put_first(first, count, value_of):
        steps, columns = cut_columns(count)

        def step(number):
            at = span(number, columns)
            grads[pl.ds(first + number * columns, columns), :] = (
                value_of(0, at) + value_of(1, at)
            ).astype(BF16)

        @pl.when(is_first)
        def _():
            repeat(0, steps, step)

    def put_second(target, index, first, count, value_of):
        steps, columns = cut_columns(count)

        def step(number):
            target[pl.ds(first + number * columns, columns), :] = value_of(
                index, span(number, columns)
            ).astype(BF16)

        @pl.when(is_second)
        def _():
            repeat(0, steps, step)

    def put_second_far(first, count, value_of):
        put_second(grads_other, 1, first, count, value_of)

        @pl.when(is_second)
        def _():
            repeat(*blocks_of(first, count), lambda step: grad_y(step).start())

    def put_second_near(first, count, value_of):
        put_second(grads, 0, first, count, value_of)

    def set_sum(row, column, index, values):
        total = column_sum(values)
        columns = slice(column, column + total.shape[1])
        if index == 0:
            small[row : row + 1, columns] += total
        else:
            @pl.when(is_first)
            def _():
                small[row : row + 1, columns] += total

            @pl.when(is_second)
            def _():
                small_other[row : row + 1, columns] += total

    def proj_grad(index, columns):
        return dot_tn(act[index, :, columns], m_grad[set_rows(index)])

    def fc_grad(index, columns):
        return dot_tn(n2[set_rows(index), :, columns], pre_grad[index])

    def out_grad(index, columns):
        return dot_tn(attended[index, :, columns], r_grad[set_rows(index)])

    def in_grad(index, columns):
        return dot_tn(qkv_grad[index, :, columns], n1[set_rows(index)])

    put_second_far(proj_grad_at, units, proj_grad)

    @pl.when(is_second)
    def _():
        repeat(0, bigs, lambda number: activate(0, 0, 0, big_rows(number)))

    def layer_out(index):
        at = tile_rows(index)
        results[0, at, :] = (
            hidden[at, :] + BRANCH_SCALE * (part_sum(1, index) + proj_bias_ref[...])
        ).astype(BF16)

        @pl.when(is_first)
        def _():
            cross(index).start()

    @pl.when(is_first)
    def _():
        collect(1, layer_out)

    @pl.when(is_first)
    def _():
        def take(index):
            scale_grad(index)
            share(1, index).start()

        cross_receive(take)

        def own(number):
            columns = span(number, 256)
            grads[span(number, 256), :] = proj_grad(0, columns).astype(BF16)

        repeat(0, units // 256, own)

    pre_grad = slope

    def mlp_slope(index):
        def step(number):
            at = big_rows(number)
            values = (
                slope[index, at, :].astype(F32)
                * dot_nt(
                    m_grad[set_rows(index), at, :], weight_of(set_weights(index), proj_at, units)
                )
            ).astype(BF16)
            pre_grad[index, at, :] = values
            set_sum(6, 0, index, values)

        repeat(0, bigs, step)

    def mlp_back_part(index, shards, at):
        return dot_nt(pre_grad[index, at, :], weight_of(shards, fc_at, width))

    def sum_of_tiles(row, source):
        def step(index):
            small[row : row + 1, :] += column_sum(source[0, tile_rows(index), :])

        repeat(0, TILES, step)

    sum_of_tiles(5, m_grad)
    mlp_slope(0)

    def share_all(which):
        def forward(index):
            share(which, index).wait_recv()
            share_core(which, index).start()

        repeat(0, TILES, forward)
        repeat(0, TILES, lambda index: share_core(which, index).wait_recv())

    @pl.when(is_first)
    def _():
        own_parts(2, mlp_back_part, per=tiles_per_big)
        share_all(1)

        def other(number):
            columns = span(number, 256)
            grads[columns, :] = (grads[columns, :].astype(F32) + proj_grad(1, columns)).astype(
                BF16
            )

        repeat(0, units // 256, other)

    pump_first_ends(units // BLOCK)

    mlp_slope(1)

    @pl.when(is_first)
    def _():
        far_parts(2, mlp_back_part, per=tiles_per_big)

    @pl.when(is_second)
    def _():
        both_parts(2, mlp_back_part, per=tiles_per_big)

    put_second_near(proj_grad_at, units, proj_grad)
    put_first(fc_grad_at, width, fc_grad)
    pump_first_ends(width // BLOCK)
    pump_first(PUMP)

    def mlp_back(index):
        at = tile_rows(index)
        n2_grad = part_sum(2, index)
        hat, rate = normed(hidden[at, :])
        small[2:3, :] += column_sum(n2_grad * hat)
        small[3:4, :] += column_sum(n2_grad)
        held = ends[ends_grad, at, :].astype(F32) + norm_backward(
            n2_grad, hat, rate, ln2_gain_ref[...]
        )
        hidden_grad[at, :] = held
        r_grad[0, at, :] = (BRANCH_SCALE * held).astype(BF16)

        @pl.when(is_first)
        def _():
            share(2, index).start()

    def collect_with_pump(which, finish):
        base = first_mids[0]
        first_mids[0] += (TILES - 1) * PUMP

        def beside(index):
            if z_line:
                @pl.when(jnp.logical_and(is_mid, index > 0))
                def _():
                    start = base + (index - 1) * PUMP
                    repeat(start, start + PUMP, lambda step: mid_step(step, False))

        collect(which, finish, beside)

    collect_with_pump(2, mlp_back)
    sum_of_tiles(4, r_grad)
    pump_second_ends(PUMP)

    def attention_backward(index):
        shards = set_weights(index)

        def project(number):
            at = big_rows(number)
            values = dot_nt(
                r_grad[set_rows(index), at, :], weight_of(shards, out_at, local_width)
            ).astype(BF16)
            for head in range(heads):
                head_rows[head, at, :] = values[:, head_columns(0, head)]

        repeat(0, bigs, project)

        for head in range(heads):
            shares = probs[index * heads + head]
            rows_grad = head_rows[head]
            qkv_grad[index, :, head_columns(2, head)] = dot_nn(shares, rows_grad).astype(BF16)
            share_grad = dot_nt(qkv[index, 2, head], rows_grad)
            wide = shares.astype(F32)
            product = wide * share_grad
            score_grad = (product - wide * jnp.sum(product, axis=0, keepdims=True)).astype(BF16)
            qkv_grad[index, :, head_columns(0, head)] = (
                dot_tn(score_grad, qkv[index, 1, head]) * scale
            ).astype(BF16)
            qkv_grad[index, :, head_columns(1, head)] = dot_nn(
                score_grad, qkv[index, 0, head]
            ).astype(BF16)
        set_sum(7, 0, index, qkv_grad[index, :, 0:local_width])
        set_sum(7, 2 * local_width, index, qkv_grad[index, :, 2 * local_width :])

    def attention_back_part(index, shards, at):
        return dot_nn(qkv_grad[index, at, :], weight_of(shards, 0, qkv_rows))

    attention_backward(0)

    @pl.when(is_first)
    def _():
        own_parts(3, attention_back_part)

    pump_first(PUMP)
    pump_second_ends(PUMP)

    @pl.when(is_first)
    def _():
        share_all(2)

    put_first(out_grad_at, local_width, out_grad)
    pump_first(PUMP)

    attention_backward(1)
    pump_first(PUMP)
    pump_second_ends(PUMP)
    pump_second(PUMP)

    @pl.when(is_first)
    def _():
        far_parts(3, attention_back_part)

    @pl.when(is_second)
    def _():
        both_parts(3, attention_back_part)

    pump_first(PUMP)
    pump_second_ends(PUMP)

    put_first(qkv_grad_at, qkv_rows, in_grad)
    if z_line:
        @pl.when(is_first)
        def _():
            repeat(0, LENT, lambda index: lent(index).start())

    pump_first(PUMP)

    def attention_back(index):
        at = tile_rows(index)
        n1_grad = part_sum(3, index)
        hat, rate = normed(ends[ends_in, at, :].astype(F32))
        small[0:1, :] += column_sum(n1_grad * hat)
        small[1:2, :] += column_sum(n1_grad)
        results[1, at, :] = (
            hidden_grad[at, :] + norm_backward(n1_grad, hat, rate, ln1_gain_ref[...])
        ).astype(BF16)

        @pl.when(is_second)
        def _():
            cross(index).start()

    collect_with_pump(3, attention_back)

    leave = remote(
        results.at[1 - s, token_rows(across_m)], rows_recv, leave_send.at[0], leave_recv.at[0], across
    )
    small_y_copy = remote(small_other, small_y, leave_send.at[1], leave_recv.at[1], across)
    small_other[0:6, :] = small[0:6, :]
    small_y_copy.start()

    @pl.when(is_second)
    def _():
        both_parts(1, mlp_part)

    put_second_far(fc_grad_at, width, fc_grad)
    pump_second_ends(PUMP)
    pump_second(PUMP)
    put_second_near(fc_grad_at, width, fc_grad)

    @pl.when(is_second)
    def _():
        collect(1, layer_out)

    leave.start()
    pump_second_ends(PUMP)
    pump_second(PUMP)
    put_second_far(out_grad_at, local_width, out_grad)
    put_second_near(out_grad_at, local_width, out_grad)
    pump_second_ends(PUMP)
    pump_second(PUMP)
    put_second_far(qkv_grad_at, qkv_rows, in_grad)
    pump_second_ends(PUMP)
    pump_second(PUMP)
    put_second_near(qkv_grad_at, qkv_rows, in_grad)

    small_up = remote(small, small_pair, leave_send.at[2], leave_recv.at[2], pair)
    small_across = remote(small, small_mid, leave_send.at[3], leave_recv.at[3], middle)
    small_down = remote(small_mid, small_pair, leave_send.at[2], leave_recv.at[2], pair)

    if z_line:
        @pl.when(is_end)
        def _():
            small_y_copy.wait_recv()
            small[...] += small_y[...]
            small_up.start()

        pump_ends(first_ends, lent_from, first_end, False)
        pump_ends(second_ends, blocks + LENT, second_end, True)
        near, later = blocks * 2 // 3, blocks * 3 // 4
        pump_mids(first_mids, near, first_mid, False)
        pump_mids(second_mids, near, second_mid, True)

        @pl.when(is_mid)
        def _():
            small_y_copy.wait_recv()
            small_up.wait_recv()
            small[...] += small_y[...]
            small[...] += small_pair[...]
            small_across.start()

        pump_mids(first_mids, later, first_mid, False)
        pump_mids(second_mids, later, second_mid, True)

        @pl.when(is_mid)
        def _():
            small_across.wait_recv()
            small_mid[...] += small[...]
            small_down.start()
            small_out[...] = small_mid[...]

        pump_mids(first_mids, lent_from, first_mid, False)
        pump_mids(second_mids, blocks + LENT, second_mid, True)

        def back(index, source):
            lent_back(index, source).wait_recv()
            grad_out(lent_from + index, source).start()

        @pl.when(first_mid)
        def _():
            repeat(lent_from - BEHIND, lent_from, lambda step: mid_down(step, False))
            repeat(0, LENT, lambda index: back(index, grads_mid))

        @pl.when(second_mid)
        def _():
            last = blocks + LENT
            repeat(last - BEHIND, last, lambda step: mid_down(step, True))

        def take(step, second):
            grad_pair(step, grads_mid).wait_recv()
            deliver(step, grads_pair, second)

        @pl.when(first_end)
        def _():
            repeat(0, lent_from, lambda step: take(step, False))
            repeat(0, LENT, lambda index: back(index, grads_pair))

        @pl.when(second_end)
        def _():
            repeat(0, blocks + LENT, lambda step: take(step, True))

        @pl.when(is_end)
        def _():
            small_down.wait_recv()
            small_out[...] = small_pair[...]

    else:
        @pl.when(is_second)
        def _():
            repeat(0, blocks, gather_y)

        repeat(0, blocks, lambda step: grad_out(step, grads).start())
        small_y_copy.wait_recv()
        small_out[...] = small[...] + small_y[...]

    leave.wait_recv()
    rows_out[pl.ds(chip, 1)] = results[pl.ds(1 - s, 1), token_rows(m), :].astype(F32)
    rows_out[pl.ds(1 - chip, 1)] = rows_recv[...].astype(F32)[None]
    repeat(0, blocks, lambda step: grad_out(step, grads).wait())

    entry_across(0).wait_send()
    entry_sibling(0).wait_send()
    entry_forward(0).wait_send()
    leave.wait_send()
    small_y_copy.wait_send()
    def tile_sends(index):
        cross(index).wait_send()
        cross_core(index).wait_send()
        for which in range(4):
            part_copy(which, index).wait_send()

    repeat(0, TILES, tile_sends)

    @pl.when(is_first)
    def _():
        entry_across(1).wait_send()
        entry_sibling(1).wait_send()
        entry_forward(1).wait_send()

        def far_sends(index):
            for which in range(3):
                share(which, index).wait_send()
                share_core(which, index).wait_send()
            for which in range(4):
                far_core(which, index).wait_send()
                far(which, index).wait_send()
                far_back(which, index).wait_send()

        repeat(0, TILES, far_sends)

    @pl.when(is_second)
    def _():
        bias_copy.wait_send()
        repeat(0, y_blocks, lambda step: weight_y(step).wait_send())
        if z_line:
            repeat(0, y_blocks, lambda step: weight_z(step).wait_send())
        repeat(0, blocks, lambda step: grad_y(step).wait_send())

    if z_line:
        sent = jnp.where(is_first, lent_from, blocks + LENT)
        repeat(0, sent, lambda step: grad_pair(step, grads).wait_send())

        @pl.when(is_first)
        def _():
            repeat(0, LENT, lambda index: lent(index).wait_send())

        @pl.when(is_second)
        def _():
            repeat(0, LENT, lambda index: lent_back(index, grads_pair).wait_send())

        @pl.when(is_end)
        def _():
            small_up.wait_send()

        @pl.when(is_mid)
        def _():
            repeat(0, sent, lambda step: grad_mid(step).wait_send())
            small_across.wait_send()
            small_down.wait_send()


def finish_kernel(local_width, rows_ref, small_ref, grads_ref, *refs):
    outs, (held_rows, held, cast, in_sem, out_sem, rows_sem) = refs[:13], refs[13:]
    rows_out, qkv_out, out_out, fc_out, proj_out, bias_out = outs[:6]
    rows_in = pltpu.make_async_copy(rows_ref, held_rows, rows_sem.at[0])
    rows_copy = pltpu.make_async_copy(held_rows, rows_out, rows_sem.at[1])

    def at_block(number):
        return pl.ds(pl.multiple_of(number * FINISH, FINISH), FINISH)

    def fetch(number):
        at = at_block(number)
        return pltpu.make_async_copy(grads_ref.at[at], held.at[at], in_sem.at[number])

    def repeat(start, last, action):
        def step_of(step, carry):
            action(step)
            return carry

        lax.fori_loop(start, last, step_of, 0)

    blocks = held.shape[0] // FINISH
    repeat(0, blocks, lambda number: fetch(number).start())
    rows_in.start()
    bias_out[0:1, :] = small_ref[7:8, 0:local_width]
    bias_out[1:2, :] = small_ref[7:8, 2 * local_width : 3 * local_width]
    for row, target in enumerate(outs[6:]):
        target[...] = small_ref[row : row + 1, :]
    first = 0
    puts = []
    for target in (proj_out, fc_out, out_out, qkv_out):
        count = target.shape[0] // FINISH

        def put(number, first=first, target=target):
            return pltpu.make_async_copy(
                cast.at[at_block(first + number)], target.at[at_block(number)], out_sem.at[first + number]
            )

        def step(number, first=first, put=put):
            fetch(first + number).wait()
            at = at_block(first + number)
            cast[at, :] = held[at, :].astype(F32)
            put(number).start()

        repeat(0, count, step)
        puts.append((count, put))
        first += count
    rows_in.wait()
    rows_copy.start()
    for count, put in puts:
        repeat(0, count, lambda number: put(number).wait())
    rows_copy.wait()


def local(
    z_line,
    boundary_in,
    order,
    ln1_gain,
    ln1_bias,
    w_qkv,
    qkv_bias,
    w_out,
    out_bias,
    ln2_gain,
    ln2_bias,
    w_fc,
    fc_bias,
    w_proj,
    proj_bias,
):
    _, micro, rows, width = boundary_in.shape
    local_width = w_qkv.shape[-1]
    units = w_fc.shape[-1]
    length = rows * lax.axis_size("mp")
    heads = local_width // HEAD_DIM
    weight_rows = 4 * local_width + width + units
    blocks = weight_rows // BLOCK
    stream_rows = weight_rows + LENT * BLOCK
    vmem = pltpu.VMEM
    dma = pltpu.SemaphoreType.DMA
    in_vmem = pl.BlockSpec(memory_space=pltpu.VMEM)
    in_any = pl.BlockSpec(memory_space=pl.ANY)
    in_smem = pl.BlockSpec(memory_space=pltpu.SMEM)
    out_rows, small, grads = pl.pallas_call(
        functools.partial(kernel, z_line),
        out_shape=(
            jax.ShapeDtypeStruct((micro, rows, width), F32),
            jax.ShapeDtypeStruct((8, width), F32),
            jax.ShapeDtypeStruct((weight_rows, width), BF16),
        ),
        in_specs=[
            in_smem,
            in_any,
            in_vmem,
            in_vmem,
            in_any,
            in_vmem,
            in_any,
            in_vmem,
            in_vmem,
            in_vmem,
            in_any,
            in_vmem,
            in_any,
            in_vmem,
        ],
        out_specs=(in_vmem, in_vmem, in_any),
        scratch_shapes=[
            vmem((micro, rows, width), BF16),
            vmem((micro, rows, width), BF16),
            vmem((2, weight_rows, width), BF16),
            vmem((2, 8, width), F32),
            vmem((3, length, width), BF16),
            vmem((2, length, width), BF16),
            vmem((rows, width), BF16),
            vmem((2, length, width), BF16),
            vmem((2, length, width), BF16),
            vmem((2, 3, heads, length, HEAD_DIM), BF16),
            vmem((2 * heads, length, length), BF16),
            vmem((heads, length, HEAD_DIM), BF16),
            vmem((2, length, local_width), BF16),
            vmem((length, width), F32),
            vmem((length, width), F32),
            vmem((2, length, units), BF16),
            vmem((2, length, units), BF16),
            vmem((2, length, width), BF16),
            vmem((2, length, width), BF16),
            vmem((2, length, 3 * local_width), BF16),
            vmem((4, length, width), BF16),
            vmem((4, length, width), BF16),
            vmem((stream_rows, width), BF16),
            vmem((weight_rows, width), BF16),
            vmem((weight_rows, width), BF16),
            vmem((stream_rows, width), BF16),
            vmem((stream_rows, width), BF16),
            vmem((8, width), F32),
            vmem((8, width), F32),
            vmem((8, width), F32),
            vmem((8, width), F32),
            vmem((8, width), F32),
            dma((5,)),
            dma((7,)),
            dma((7,)),
            dma((weight_rows // FETCH,)),
            dma((weight_rows // FETCH,)),
            dma((weight_rows // FETCH,)),
            dma((weight_rows // FETCH,)),
            dma((4, TILES)),
            dma((4, TILES)),
            dma((4, TILES)),
            dma((4, TILES)),
            dma((4, TILES)),
            dma((4, TILES)),
            dma((4, TILES)),
            dma((4, TILES)),
            dma((3, TILES)),
            dma((3, TILES)),
            dma((3, TILES)),
            dma((3, TILES)),
            dma((TILES,)),
            dma((TILES,)),
            dma((TILES,)),
            dma((TILES,)),
            dma((4,)),
            dma((4,)),
            dma((blocks,)),
            dma((blocks,)),
            dma((blocks + LENT,)),
            dma((blocks + LENT,)),
            dma((blocks + LENT,)),
            dma((blocks + LENT,)),
            dma((blocks,)),
            dma((LENT,)),
            dma((LENT,)),
            dma((LENT,)),
            dma((LENT,)),
        ],
        compiler_params=pltpu.CompilerParams(
            collective_id=0, has_side_effects=True, vmem_limit_bytes=63 * 2**20
        ),
        name="two_layers",
    )(
        order,
        boundary_in,
        ln1_gain,
        ln1_bias,
        jnp.swapaxes(w_qkv, 2, 3).reshape(1, 3 * local_width, width),
        qkv_bias,
        w_out,
        out_bias,
        ln2_gain,
        ln2_bias,
        w_fc,
        fc_bias,
        w_proj,
        proj_bias,
    )
    if not z_line:
        small, grads = lax.psum((small, grads), "dp")
    shapes = [
        (micro, rows, width),
        (3 * local_width, width),
        (local_width, width),
        (width, units),
        (units, width),
        (2, local_width),
    ] + [(1, width)] * 6 + [(1, units)]
    (
        out_rows,
        qkv_grad,
        out_grad,
        fc_grad,
        proj_grad,
        qkv_bias_grad,
        ln1_gain_grad,
        ln1_bias_grad,
        ln2_gain_grad,
        ln2_bias_grad,
        out_bias_grad,
        proj_bias_grad,
        fc_bias_grad,
    ) = pl.pallas_call(
        functools.partial(finish_kernel, local_width),
        out_shape=[jax.ShapeDtypeStruct(shape, F32) for shape in shapes],
        in_specs=[in_any, in_vmem, in_any],
        out_specs=[in_any] * 5 + [in_vmem] * 8,
        scratch_shapes=[
            vmem((micro, rows, width), F32),
            vmem((weight_rows, width), BF16),
            vmem((weight_rows, width), F32),
            dma((weight_rows // FINISH,)),
            dma((weight_rows // FINISH,)),
            dma((2,)),
        ],
        compiler_params=pltpu.CompilerParams(vmem_limit_bytes=62 * 2**20),
        name="finish",
    )(out_rows, small, grads)
    return (
        out_rows[None],
        ln1_gain_grad,
        ln1_bias_grad,
        jnp.swapaxes(qkv_grad.reshape(1, 3, local_width, width), 2, 3),
        qkv_bias_grad[None],
        out_grad[None],
        out_bias_grad,
        ln2_gain_grad,
        ln2_bias_grad,
        fc_grad[None],
        fc_bias_grad,
        proj_grad[None],
        proj_bias_grad,
    )


def solution(mesh):
    return jax.shard_map(
        functools.partial(local, mesh.shape["dp"] == 4),
        mesh=mesh,
        in_specs=(
            P("section", "dp", "mp", None),
            P("dp", None),
            P("section", None),
            P("section", None),
            P("section", None, None, "mp"),
            P("section", None, "mp"),
            P("section", "mp", None),
            P("section", None),
            P("section", None),
            P("section", None),
            P("section", None, "mp"),
            P("section", "mp"),
            P("section", "mp", None),
            P("section", None),
        ),
        out_specs=(
            P("section", "dp", "mp", None),
            P("section", None),
            P("section", None),
            P("section", None, None, "mp"),
            P("section", None, "mp"),
            P("section", "mp", None),
            P("section", None),
            P("section", None),
            P("section", None),
            P("section", None, "mp"),
            P("section", "mp"),
            P("section", "mp", None),
            P("section", None),
        ),
        check_vma=False,
    )
```

```python
import functools

import jax
import jax.numpy as jnp
from jax import lax
from jax.experimental import pallas as pl
from jax.experimental.pallas import tpu as pltpu
from jax.sharding import PartitionSpec as P

HEAD_DIM = 64
BRANCH_SCALE = 0.14433756729740643
NORM_EPS = 1e-05
GELU_RATE = 0.7978845608028654
GELU_CUBE = 0.044715
NEGATIVE = -1e30
BLOCK = 48
PUMP = 2
FINISH = 192
FETCH = 96
TILES = 4
PAIR = 1
LENT = 10
BEHIND = 4
MESH = pl.DeviceIdType.MESH
BF16 = jnp.bfloat16
F32 = jnp.float32


def dot_nn(a, b):
    return lax.dot_general(a, b, (((1,), (0,)), ((), ())), preferred_element_type=F32)


def dot_nt(a, b):
    return lax.dot_general(a, b, (((1,), (1,)), ((), ())), preferred_element_type=F32)


def dot_tn(a, b):
    return lax.dot_general(a, b, (((0,), (0,)), ((), ())), preferred_element_type=F32)


def normed(values):
    center = values - jnp.mean(values, axis=-1, keepdims=True)
    rate = lax.rsqrt(jnp.mean(center * center, axis=-1, keepdims=True) + NORM_EPS)
    return center * rate, rate


def norm_backward(grad, hat, rate, gain):
    scaled = grad * gain
    return rate * (
        scaled
        - jnp.mean(scaled, axis=-1, keepdims=True)
        - hat * jnp.mean(scaled * hat, axis=-1, keepdims=True)
    )


def column_sum(values):
    return jnp.sum(values.astype(F32), axis=0, keepdims=True)


def remote(src, dst, send_sem, recv_sem, device):
    return pltpu.make_async_remote_copy(
        src_ref=src,
        dst_ref=dst,
        send_sem=send_sem,
        recv_sem=recv_sem,
        device_id=device,
        device_id_type=MESH,
    )


def kernel(
    z_line,
    order_ref,
    boundary_ref,
    ln1_gain_ref,
    ln1_bias_ref,
    w_qkv_ref,
    qkv_bias_ref,
    w_out_ref,
    out_bias_ref,
    ln2_gain_ref,
    ln2_bias_ref,
    w_fc_ref,
    fc_bias_ref,
    w_proj_ref,
    proj_bias_ref,
    rows_out,
    small_out,
    grads_out,
    raw,
    slots,
    weights,
    biases,
    ends,
    results,
    rows_recv,
    n1,
    n2,
    qkv,
    probs,
    head_rows,
    attended,
    hidden,
    hidden_grad,
    act,
    slope,
    m_grad,
    r_grad,
    qkv_grad,
    part,
    part_recv,
    grads,
    grads_other,
    grads_y,
    grads_pair,
    grads_mid,
    small,
    small_other,
    small_y,
    small_pair,
    small_mid,
    local_sem,
    entry_send,
    entry_recv,
    weight_y_send,
    weight_y_recv,
    weight_z_send,
    weight_z_recv,
    part_send,
    part_recv_sem,
    far_core_send,
    far_core_recv,
    far_send,
    far_recv,
    far_back_send,
    far_back_recv,
    share_send,
    share_recv,
    share_core_send,
    share_core_recv,
    cross_send,
    cross_recv,
    cross_core_send,
    cross_core_recv,
    leave_send,
    leave_recv,
    grad_y_send,
    grad_y_recv,
    grad_pair_send,
    grad_pair_recv,
    grad_mid_send,
    grad_mid_recv,
    grad_out_sem,
    lent_send,
    lent_recv,
    back_send,
    back_recv,
):
    s, d, m = lax.axis_index("section"), lax.axis_index("dp"), lax.axis_index("mp")
    core, chip = lax.rem(m, 2), lax.div(m, 2)
    half = lax.rem(d, 2)
    across_m = 2 * (1 - chip) + core
    sibling = (s, d, 2 * chip + 1 - core)
    across = (s, d, across_m)
    other_section = (1 - s, d, m)
    pair = (s, d + 1 - 2 * half, m)
    middle = (s, 3 - d, m)
    is_first, is_second = s == 0, s == 1
    is_mid = lax.div(d + 1, 2) == 1
    is_end = lax.div(d + 1, 2) != 1

    rows = boundary_ref.shape[2]
    length, width = n1.shape[1:]
    tile = length // TILES
    piece = tile // 2
    big = length // 2
    pair_rows = PAIR * tile
    local_width = attended.shape[2]
    units = act.shape[2]
    heads = local_width // HEAD_DIM
    tiles_per_big, bigs = big // tile, length // big
    scale = HEAD_DIM ** (-0.5)
    qkv_rows = 3 * local_width
    out_at, fc_at, proj_at = qkv_rows, qkv_rows + local_width, qkv_rows + local_width + width
    weight_rows = weights.shape[1]
    blocks = weight_rows // BLOCK
    ends_in, ends_grad = 2 * s, 2 * (1 - s)

    def set_rows(index):
        return index * (1 - s)

    def set_weights(index):
        return index * s

    def span(index, count):
        start = index * count
        return pl.ds(start if isinstance(start, int) else pl.multiple_of(start, count), count)

    def tile_rows(index):
        return span(index, tile)

    def big_rows(index):
        return span(index, big)

    def piece_rows(index, which):
        return pl.ds(pl.multiple_of(index * tile + which * piece, piece), piece)

    partners = [sibling, across, other_section]
    if z_line:
        partners += [pair, middle]
    barrier = pltpu.get_barrier_semaphore()
    for device in partners:
        pl.semaphore_signal(barrier, inc=1, device_id=device, device_id_type=MESH)

    loads = [
        pltpu.make_async_copy(boundary_ref.at[0], raw, local_sem.at[0]),
        pltpu.make_async_copy(
            w_qkv_ref.at[0], weights.at[0, pl.ds(0, qkv_rows)], local_sem.at[1]
        ),
        pltpu.make_async_copy(
            w_out_ref.at[0], weights.at[0, pl.ds(out_at, local_width)], local_sem.at[2]
        ),
        pltpu.make_async_copy(w_fc_ref.at[0], weights.at[0, pl.ds(fc_at, width)], local_sem.at[3]),
        pltpu.make_async_copy(
            w_proj_ref.at[0], weights.at[0, pl.ds(proj_at, units)], local_sem.at[4]
        ),
    ]
    for load in loads:
        load.start()

    biases[0] = jnp.zeros_like(biases[0])
    biases[0, 0:1, :] = fc_bias_ref[...]
    biases[0, 1:2, 0:local_width] = qkv_bias_ref[0, 0:1, :]
    biases[0, 2:3, 0:local_width] = qkv_bias_ref[0, 1:2, :]
    small[...] = jnp.zeros_like(small)
    small_other[...] = jnp.zeros_like(small_other)

    loads[0].wait()
    for slot in range(2):
        picked = jnp.where(is_first, order_ref[0, slot], slot).astype(F32)
        slots[slot] = (
            raw[0].astype(F32) * (1.0 - picked) + raw[1].astype(F32) * picked
        ).astype(BF16)

    pl.semaphore_wait(barrier, len(partners))

    def token_rows(index):
        return pl.ds(pl.multiple_of(index * rows, rows), rows)

    def entry_across(which):
        slot = (1 - chip) * (1 - which) + chip * which
        return remote(
            slots.at[slot],
            ends.at[which, token_rows(m)],
            entry_send.at[which],
            entry_recv.at[which],
            across,
        )

    def entry_sibling(which):
        slot = chip * (1 - which) + (1 - chip) * which
        return remote(
            slots.at[slot],
            ends.at[which, token_rows(m)],
            entry_send.at[2 + which],
            entry_recv.at[2 + which],
            sibling,
        )

    def entry_forward(which):
        at = token_rows(across_m)
        return remote(
            ends.at[which, at],
            ends.at[which, at],
            entry_send.at[4 + which],
            entry_recv.at[4 + which],
            sibling,
        )

    bias_copy = remote(biases.at[0], biases.at[1], entry_send.at[6], entry_recv.at[6], across)

    def entry_start(which):
        entry_across(which).start()
        entry_sibling(which).start()
        slot = chip if which == 0 else 1 - chip
        ends[which, token_rows(m), :] = slots[slot]

    def entry_pass(which):
        entry_across(which).wait_recv()
        entry_forward(which).start()

    def entry_finish(which):
        entry_pass(which)
        entry_sibling(which).wait_recv()
        entry_forward(which).wait_recv()

    @pl.when(is_first)
    def _():
        entry_start(1)
        entry_start(0)

    y_blocks = weight_rows // FETCH // (2 if z_line else 1)

    def weight_block(index):
        return pl.ds(pl.multiple_of(index * BLOCK, BLOCK), BLOCK)

    def near_block(step):
        return span(2 * step + half if z_line else step, FETCH)

    def weight_y(step):
        return remote(
            weights.at[0, near_block(step)],
            weights.at[1, near_block(step)],
            weight_y_send.at[step],
            weight_y_recv.at[step],
            across,
        )

    def weight_z(step):
        return remote(
            weights.at[1, near_block(step)],
            weights.at[1, near_block(step)],
            weight_z_send.at[step],
            weight_z_recv.at[step],
            pair,
        )

    def repeat(first, last, action):
        def step_of(step, carry):
            action(step)
            return carry

        lax.fori_loop(first, last, step_of, 0)

    late_step = proj_at * y_blocks // weight_rows
    last_step = y_blocks - max(1, y_blocks // 12)
    y_done = [0]

    def weight_need(row):
        steps = row * y_blocks // weight_rows
        if z_line and steps > y_done[0]:
            first, y_done[0] = y_done[0], steps

            @pl.when(is_second)
            def _():
                repeat(first, steps, lambda step: weight_z(step).wait_recv())

    def weight_pass(step):
        weight_y(step).wait_recv()
        if z_line:
            weight_z(step).start()

    for load in loads[1:]:
        load.wait()

    def cross(index):
        at = piece_rows(index, core)
        return remote(
            results.at[s, at],
            ends.at[2, at],
            cross_send.at[index],
            cross_recv.at[index],
            other_section,
        )

    def cross_core(index):
        at = piece_rows(index, core)
        return remote(
            ends.at[2, at],
            ends.at[2, at],
            cross_core_send.at[index],
            cross_core_recv.at[index],
            sibling,
        )

    shared = (n2, m_grad, r_grad)

    def share(which, index):
        at = piece_rows(index, core)
        source = ends.at[2, at] if which == 1 else shared[which].at[0, at]
        return remote(
            source,
            shared[which].at[1, at],
            share_send.at[which, index],
            share_recv.at[which, index],
            across,
        )

    def share_core(which, index):
        at = piece_rows(index, core)
        return remote(
            shared[which].at[1, at],
            shared[which].at[1, at],
            share_core_send.at[which, index],
            share_core_recv.at[which, index],
            sibling,
        )

    def share_some(which, start, count):
        def forward(index):
            share(which, start + index).wait_recv()
            share_core(which, start + index).start()

        repeat(0, count, forward)
        repeat(0, count, lambda index: share_core(which, start + index).wait_recv())

    def part_copy(which, index):
        at = tile_rows(index)
        return remote(
            part.at[which, at],
            part_recv.at[which, at],
            part_send.at[which, index],
            part_recv_sem.at[which, index],
            sibling,
        )

    def spare_rows(which, index, core_of):
        return pl.ds(
            pl.multiple_of(which * length + index * tile + core_of * piece, piece), piece
        )

    def far_core(which, index):
        return remote(
            grads_y.at[spare_rows(which, index, 1 - core)],
            grads_other.at[spare_rows(which, index, 1 - core)],
            far_core_send.at[which, index],
            far_core_recv.at[which, index],
            sibling,
        )

    def far(which, index):
        return remote(
            grads_y.at[spare_rows(which, index, core)],
            weights.at[1, spare_rows(which, index, core)],
            far_send.at[which, index],
            far_recv.at[which, index],
            across,
        )

    def far_back(which, index):
        at = spare_rows(which, index, core)
        return remote(
            weights.at[1, at],
            weights.at[1, at],
            far_back_send.at[which, index],
            far_back_recv.at[which, index],
            sibling,
        )

    def far_pass(which, index):
        far_core(which, index).wait_recv()
        at = spare_rows(which, index, core)
        grads_y[at, :] = (grads_y[at, :].astype(F32) + grads_other[at, :].astype(F32)).astype(BF16)
        far(which, index).start()

    def part_sum(which, index):
        at = tile_rows(index)
        near = part[which, at, :].astype(F32) + part_recv[which, at, :].astype(F32)
        other = weights[1, span(which * TILES + index, tile), :].astype(F32)
        return near + jnp.where(is_first, other, 0.0)

    def far_parts(which, value_of, per=PAIR, before=None):
        def step(number):
            if before is not None:
                before(number)
            grads_y[span(which * (TILES // per) + number, per * tile), :] = value_of(
                1, 0, span(number, per * tile)
            ).astype(BF16)
            for index in range(per):
                far_core(which, number * per + index).start()

            @pl.when(number > 0)
            def _():
                for index in range(per):
                    far_pass(which, (number - 1) * per + index)

        repeat(0, TILES // per, step)
        for index in range(per):
            far_pass(which, TILES - per + index)

    def own_parts(which, value_of, per=PAIR):
        def step(number):
            at = span(number, per * tile)
            part[which, at, :] = value_of(0, 0, at).astype(BF16)
            for index in range(per):
                part_copy(which, number * per + index).start()

        repeat(0, TILES // per, step)

    def both_parts(which, value_of, per=PAIR):
        def step(number):
            at = span(number, per * tile)
            part[which, at, :] = (value_of(0, 0, at) + value_of(1, 1, at)).astype(BF16)
            for index in range(per):
                part_copy(which, number * per + index).start()

        repeat(0, TILES // per, step)

    def collect(which, finish, beside=None, start=0, last=TILES):
        def far_next(index):
            far(which, index).wait_recv()
            far_back(which, index).start()

        @pl.when(is_first)
        def _():
            far_next(start)

        def step(index):
            @pl.when(is_first)
            def _():
                @pl.when(index + 1 < last)
                def _():
                    far_next(index + 1)

                if beside is not None:
                    beside(index)
                far_back(which, index).wait_recv()

            part_copy(which, index).wait_recv()
            finish(index)

        repeat(start, last, step)

    def weight_of(shards, first, count):
        return weights[shards, first : first + count, :]

    def scale_grad(index):
        at = tile_rows(index)
        m_grad[0, at, :] = (BRANCH_SCALE * ends[ends_grad, at, :].astype(F32)).astype(BF16)

    @pl.when(is_second)
    def _():
        bias_copy.start()
        repeat(0, late_step, lambda step: weight_y(step).start())
        entry_start(0)
        repeat(late_step, y_blocks, lambda step: weight_y(step).start())
        repeat(0, late_step, weight_pass)
        bias_copy.wait_recv()
        entry_finish(0)
        repeat(0, TILES, scale_grad)
        repeat(late_step, last_step, weight_pass)

    def norm_big(which, source, number):
        def step(index):
            at = span(number * (big // pair_rows) + index, pair_rows)
            hat, _ = normed(ends[source, at, :].astype(F32))
            n1[which, at, :] = (hat * ln1_gain_ref[...] + ln1_bias_ref[...]).astype(BF16)

        repeat(0, big // pair_rows, step)

    def cross_receive(start, last, action, on=None):
        def pass_on(index):
            cross(index).wait_recv()
            cross_core(index).start()
            if on is not None:
                on(index)

        pass_on(start)

        def step(index):
            @pl.when(index + 1 < last)
            def _():
                pass_on(index + 1)

            cross_core(index).wait_recv()
            action(index)

        repeat(start, last, step)

    causal = lax.broadcasted_iota(jnp.int32, (length, length), 1) >= lax.broadcasted_iota(
        jnp.int32, (length, length), 0
    )

    def bias_of(shards, row, count):
        return biases[shards, row : row + 1, 0:count]

    def head_columns(kind, head):
        first = kind * local_width + head * HEAD_DIM
        return slice(first, first + HEAD_DIM)

    def project(index, number):
        source, shards = set_rows(index), set_weights(index)
        at = big_rows(number)
        for kind in range(3):
            values = dot_nt(n1[source, at, :], weight_of(shards, kind * local_width, local_width))
            if kind == 0:
                values = values + bias_of(shards, 1, local_width)
            if kind == 2:
                values = values + bias_of(shards, 2, local_width)
            values = values.astype(BF16)
            if kind == 0:
                values = (values.astype(F32) * scale).astype(BF16)
            for head in range(heads):
                qkv[index, kind, head, at, :] = values[:, head_columns(0, head)]

    def attention_forward(index):
        for head in range(heads):
            scores = dot_nt(qkv[index, 1, head], qkv[index, 0, head])
            scores = jnp.where(causal, scores, NEGATIVE)
            raised = jnp.exp(scores - jnp.max(scores, axis=0, keepdims=True))
            shares = raised * (1.0 / jnp.sum(raised, axis=0, keepdims=True))
            shares = shares.astype(BF16)
            probs[index * heads + head] = shares
            attended[index, :, head_columns(0, head)] = dot_tn(
                shares, qkv[index, 2, head]
            ).astype(BF16)

    weight_need(out_at)

    @pl.when(is_second)
    def _():
        def step(number):
            cross_receive(
                number * tiles_per_big, (number + 1) * tiles_per_big, lambda index: None
            )
            norm_big(0, 2, number)
            repeat(0, 2, lambda index: project(index, number))

        repeat(0, bigs, step)
        repeat(last_step, y_blocks, weight_pass)

    @pl.when(is_first)
    def _():
        def step(index):
            entry_sibling(index).wait_recv()
            norm_big(index, index, chip)
            project(index, chip)

        repeat(0, 2, step)
        entry_pass(1)
        entry_forward(1).wait_recv()
        norm_big(1, 1, 1 - chip)
        project(1, 1 - chip)

    attention_forward(1)

    def attention_part(index, shards, at):
        return dot_nn(attended[index, at, :], weight_of(shards, out_at, local_width))

    @pl.when(is_first)
    def _():
        far_parts(0, attention_part)
        entry_pass(0)
        entry_forward(0).wait_recv()
        norm_big(0, 0, 1 - chip)
        project(0, 1 - chip)

    attention_forward(0)

    weight_need(fc_at)

    @pl.when(is_first)
    def _():
        own_parts(0, attention_part)

    @pl.when(is_second)
    def _():
        both_parts(0, attention_part)

    def attention_out(index):
        at = tile_rows(index)
        held = ends[ends_in, at, :].astype(F32) + BRANCH_SCALE * (
            part_sum(0, index) + out_bias_ref[...]
        )
        hidden[at, :] = held
        hat, _ = normed(held)
        n2[0, at, :] = (hat * ln2_gain_ref[...] + ln2_bias_ref[...]).astype(BF16)

        @pl.when(is_first)
        def _():
            share(0, index).start()

    def activate(index, source, shards, at):
        u = dot_nn(n2[source, at, :], weight_of(shards, fc_at, width)) + bias_of(shards, 0, units)
        square = u * u
        bent = jnp.tanh(GELU_RATE * (u + GELU_CUBE * u * square))
        act[index, at, :] = (0.5 * u * (1.0 + bent)).astype(BF16)
        slope[index, at, :] = (
            0.5 * (1.0 + bent)
            + (0.5 * GELU_RATE) * u * (1.0 - bent * bent) * (1.0 + (3.0 * GELU_CUBE) * square)
        ).astype(BF16)

    weight_need(proj_at)

    def first_half(number):
        collect(
            0, attention_out, start=number * tiles_per_big, last=(number + 1) * tiles_per_big
        )
        activate(set_weights(1), 0, set_weights(1), big_rows(number))

    repeat(0, bigs, first_half)

    def mlp_part(index, shards, at):
        return dot_nn(act[index, at, :], weight_of(shards, proj_at, units))

    def other_activate(number):
        share_some(0, number * PAIR, PAIR)
        activate(1, 1, 0, span(number, pair_rows))

    @pl.when(is_first)
    def _():
        own_parts(1, mlp_part)
        far_parts(1, mlp_part, before=other_activate)

    weight_need(weight_rows)

    proj_grad_at, fc_grad_at = 0, units
    out_grad_at = fc_grad_at + width
    qkv_grad_at = out_grad_at + local_width

    def grad_y(step):
        return remote(
            grads_other.at[weight_block(step)],
            grads_y.at[weight_block(step)],
            grad_y_send.at[step],
            grad_y_recv.at[step],
            across,
        )

    def grad_pair(step, source):
        return remote(
            source.at[weight_block(step)],
            grads_pair.at[weight_block(step)],
            grad_pair_send.at[step],
            grad_pair_recv.at[step],
            pair,
        )

    def grad_mid(step):
        return remote(
            grads.at[weight_block(step)],
            grads_mid.at[weight_block(step)],
            grad_mid_send.at[step],
            grad_mid_recv.at[step],
            middle,
        )

    def grad_out(step, source):
        at = weight_block(step)
        return pltpu.make_async_copy(source.at[at], grads_out.at[at], grad_out_sem.at[step])

    def add_into(target, source, step):
        at = weight_block(step)
        target[at, :] = (target[at, :].astype(F32) + source[at, :].astype(F32)).astype(BF16)

    def gather_y(step):
        grad_y(step).wait_recv()
        add_into(grads, grads_y, step)

    def mid_up(step):
        grad_pair(step, grads).wait_recv()
        add_into(grads, grads_pair, step)
        grad_mid(step).start()

    def mid_down(step, is_lent):
        grad_mid(step).wait_recv()
        add_into(grads_mid, grads, step)
        grad_pair(step, grads_mid).start()
        deliver(step, grads_mid, is_lent)

    def deliver(step, source, is_lent):
        if is_lent:
            lent_back(step - blocks, source).start()
        else:
            grad_out(step, source).start()

    lent_from = blocks - LENT

    def lent(index):
        return remote(
            grads.at[weight_block(lent_from + index)],
            grads.at[weight_block(blocks + index)],
            lent_send.at[index],
            lent_recv.at[index],
            other_section,
        )

    def lent_back(index, source):
        return remote(
            source.at[weight_block(blocks + index)],
            source.at[weight_block(lent_from + index)],
            back_send.at[index],
            back_recv.at[index],
            other_section,
        )

    first_order = list(range(lent_from))
    turn = blocks * 7 // 8
    second_order = [*range(turn), *range(blocks, blocks + LENT), *range(turn, blocks)]

    def runs(order, start, last, behind=0):
        cuts = [start]
        for place in range(start + 1, last):
            for back in (place, place - behind):
                if back > 0 and order[back] != order[back - 1] + 1 and cuts[-1] != place:
                    cuts.append(place)
        cuts.append(last)
        return [
            (a, b, order[a] - a, order[max(a - behind, 0)] - max(a - behind, 0))
            for a, b in zip(cuts, cuts[1:])
            if b > a
        ]

    first_ends, first_mids, second_ends, second_mids = [0], [0], [0], [0]
    first_end, second_end = jnp.logical_and(is_first, is_end), jnp.logical_and(is_second, is_end)
    first_mid, second_mid = jnp.logical_and(is_first, is_mid), jnp.logical_and(is_second, is_mid)

    def gather(step, is_lent):
        if is_lent:
            lent(step - blocks).wait_recv()
        else:
            gather_y(step)

    def pump_ends(done, last, wanted, second):
        start, done[0] = done[0], last
        if z_line:
            @pl.when(wanted)
            def _():
                for a, b, offset, _ in runs(second_order if second else first_order, start, last):

                    def up(place, a=a, offset=offset):
                        if second:
                            gather(place + offset, a + offset >= blocks)
                        grad_pair(place + offset, grads).start()

                    repeat(a, b, up)

    def pump_mids(done, last, wanted, second):
        start, done[0] = done[0], last
        if z_line:
            @pl.when(wanted)
            def _():
                order = second_order if second else first_order
                for a, b, offset, old in runs(order, start, last, BEHIND):

                    def step(place, a=a, offset=offset, old=old):
                        if second:
                            gather(place + offset, a + offset >= blocks)
                        mid_up(place + offset)

                        @pl.when(place >= BEHIND)
                        def _():
                            mid_down(place - BEHIND + old, a - BEHIND + old >= blocks)

                    repeat(a, b, step)

    def pump_first_ends(count):
        pump_ends(first_ends, first_ends[0] + count, first_end, False)

    def pump_first(count):
        pump_mids(first_mids, first_mids[0] + count, first_mid, False)

    def pump_second_ends(count):
        pump_ends(second_ends, second_ends[0] + count, second_end, True)

    def pump_second(count):
        pump_mids(second_mids, second_mids[0] + count, second_mid, True)

    def cut_columns(count):
        return (2, count // 2) if count % 768 == 0 else (1, count)

    def put_first(first, count, value_of):
        steps, columns = cut_columns(count)

        def step(number):
            at = span(number, columns)
            grads[pl.ds(first + number * columns, columns), :] = (
                value_of(0, at) + value_of(1, at)
            ).astype(BF16)

        @pl.when(is_first)
        def _():
            repeat(0, steps, step)

    def put_second(target, index, first, count, value_of, after=None):
        steps, columns = cut_columns(count)

        def step(number):
            start = first + number * columns
            target[pl.ds(start, columns), :] = value_of(index, span(number, columns)).astype(BF16)
            if after is not None:
                after(first // BLOCK + number * (columns // BLOCK), columns // BLOCK)

        @pl.when(is_second)
        def _():
            repeat(0, steps, step)

    def put_second_far(first, count, value_of):
        def leave_blocks(start, number):
            repeat(start, start + number, lambda step: grad_y(step).start())

        put_second(grads_other, 1, first, count, value_of, leave_blocks)

    def put_second_near(first, count, value_of):
        put_second(grads, 0, first, count, value_of)

    def set_sum(row, column, index, values):
        total = column_sum(values)
        columns = slice(column, column + total.shape[1])
        if index == 0:
            small[row : row + 1, columns] += total
        else:
            @pl.when(is_first)
            def _():
                small[row : row + 1, columns] += total

            @pl.when(is_second)
            def _():
                small_other[row : row + 1, columns] += total

    def proj_grad(index, columns):
        return dot_tn(act[index, :, columns], m_grad[set_rows(index)])

    def fc_grad(index, columns):
        return dot_tn(n2[set_rows(index), :, columns], pre_grad[index])

    def out_grad(index, columns):
        return dot_tn(attended[index, :, columns], r_grad[set_rows(index)])

    def in_grad(index, columns):
        return dot_tn(qkv_grad[index, :, columns], n1[set_rows(index)])

    put_second_far(proj_grad_at, units, proj_grad)

    @pl.when(is_second)
    def _():
        repeat(0, bigs, lambda number: activate(0, 0, 0, big_rows(number)))

    proj_half = units // 2
    put_second_near(proj_grad_at, proj_half, proj_grad)

    def layer_out(index):
        at = tile_rows(index)
        results[0, at, :] = (
            hidden[at, :] + BRANCH_SCALE * (part_sum(1, index) + proj_bias_ref[...])
        ).astype(BF16)

        @pl.when(is_first)
        def _():
            cross(index).start()

    @pl.when(is_first)
    def _():
        collect(1, layer_out)

    @pl.when(is_first)
    def _():
        cross_receive(0, TILES, scale_grad, lambda index: share(1, index).start())

        def own(number):
            columns = span(number, units // 2)
            grads[span(number, units // 2), :] = proj_grad(0, columns).astype(BF16)

        repeat(0, 2, own)

    pre_grad = slope

    def mlp_slope(index):
        def step(number):
            at = big_rows(number)
            values = (
                slope[index, at, :].astype(F32)
                * dot_nt(
                    m_grad[set_rows(index), at, :], weight_of(set_weights(index), proj_at, units)
                )
            ).astype(BF16)
            pre_grad[index, at, :] = values

        repeat(0, bigs, step)

    def mlp_back_part(index, shards, at):
        return dot_nt(pre_grad[index, at, :], weight_of(shards, fc_at, width))

    def sum_of_rows(row, source):
        def step(number):
            small[row : row + 1, :] += column_sum(source[0, big_rows(number), :])

        repeat(0, bigs, step)

    mlp_slope(0)

    @pl.when(is_first)
    def _():
        own_parts(2, mlp_back_part, per=tiles_per_big)
        share_some(1, 0, TILES)
        repeat(0, TILES, lambda index: share_core(1, index).wait_send())

        def scale_other(number):
            at = big_rows(number)
            m_grad[1, at, :] = (BRANCH_SCALE * m_grad[1, at, :].astype(F32)).astype(BF16)

        repeat(0, bigs, scale_other)

        def other(number):
            columns = span(number, units // 2)
            grads[columns, :] = (grads[columns, :].astype(F32) + proj_grad(1, columns)).astype(
                BF16
            )
            if z_line:
                @pl.when(is_end)
                def _():
                    per = units // 2 // BLOCK
                    repeat(
                        number * per, (number + 1) * per, lambda step: grad_pair(step, grads).start()
                    )

        repeat(0, 2, other)

    first_ends[0] += units // BLOCK

    mlp_slope(1)
    pump_second_ends(1)

    @pl.when(is_first)
    def _():
        far_parts(2, mlp_back_part, per=tiles_per_big)

    @pl.when(is_second)
    def _():
        both_parts(2, mlp_back_part, per=tiles_per_big)

    put_second_near(
        proj_grad_at + proj_half,
        units - proj_half,
        lambda index, columns: proj_grad(index, pl.ds(proj_half, units - proj_half)),
    )
    put_first(fc_grad_at, width, fc_grad)
    pump_first_ends(width // BLOCK)
    pump_first(PUMP)

    pump_second_ends(1)

    def mlp_back(index):
        at = tile_rows(index)
        n2_grad = part_sum(2, index)
        hat, rate = normed(hidden[at, :])
        small[2:3, :] += column_sum(n2_grad * hat)
        small[3:4, :] += column_sum(n2_grad)
        held = ends[ends_grad, at, :].astype(F32) + norm_backward(
            n2_grad, hat, rate, ln2_gain_ref[...]
        )
        hidden_grad[at, :] = held
        r_grad[0, at, :] = (BRANCH_SCALE * held).astype(BF16)

        @pl.when(is_first)
        def _():
            share(2, index).start()

    def first_mid_step(step):
        mid_up(step)

        @pl.when(step >= BEHIND)
        def _():
            mid_down(step - BEHIND, False)

    def collect_with_pump(which, finish):
        base = first_mids[0]
        first_mids[0] += (TILES - 1) * PUMP

        def beside(index):
            if z_line:
                @pl.when(jnp.logical_and(is_mid, index > 0))
                def _():
                    start = base + (index - 1) * PUMP
                    repeat(start, start + PUMP, first_mid_step)

        collect(which, finish, beside)

    collect_with_pump(2, mlp_back)
    pump_first(1)
    pump_second_ends(1)

    def attention_backward(index):
        shards = set_weights(index)

        def project(number):
            at = big_rows(number)
            values = dot_nt(
                r_grad[set_rows(index), at, :], weight_of(shards, out_at, local_width)
            ).astype(BF16)
            for head in range(heads):
                head_rows[head, at, :] = values[:, head_columns(0, head)]

        repeat(0, bigs, project)

        for head in range(heads):
            shares = probs[index * heads + head]
            rows_grad = head_rows[head]
            qkv_grad[index, :, head_columns(2, head)] = dot_nn(shares, rows_grad).astype(BF16)
            share_grad = dot_nt(qkv[index, 2, head], rows_grad)
            wide = shares.astype(F32)
            product = wide * share_grad
            score_grad = (product - wide * jnp.sum(product, axis=0, keepdims=True)).astype(BF16)
            qkv_grad[index, :, head_columns(0, head)] = (
                dot_tn(score_grad, qkv[index, 1, head]) * scale
            ).astype(BF16)
            qkv_grad[index, :, head_columns(1, head)] = dot_nn(
                score_grad, qkv[index, 0, head]
            ).astype(BF16)
    def attention_back_part(index, shards, at):
        return dot_nn(qkv_grad[index, at, :], weight_of(shards, 0, qkv_rows))

    attention_backward(0)

    @pl.when(is_first)
    def _():
        own_parts(3, attention_back_part)

    pump_first(PUMP)
    pump_second_ends(2)
    pump_second(2)

    @pl.when(is_first)
    def _():
        share_some(2, 0, TILES)

    put_first(out_grad_at, local_width, out_grad)
    pump_first(PUMP)

    attention_backward(1)
    pump_first(PUMP)
    pump_second_ends(2)
    pump_second(1)

    @pl.when(is_first)
    def _():
        far_parts(3, attention_back_part)

    @pl.when(is_second)
    def _():
        both_parts(3, attention_back_part)

    pump_first(PUMP)
    pump_second_ends(1)
    pump_second(1)

    put_first(qkv_grad_at, qkv_rows, in_grad)
    if z_line:
        @pl.when(is_first)
        def _():
            repeat(0, LENT, lambda index: lent(index).start())

    pump_first(PUMP)

    def attention_back(index):
        at = tile_rows(index)
        n1_grad = part_sum(3, index)
        hat, rate = normed(ends[ends_in, at, :].astype(F32))
        small[0:1, :] += column_sum(n1_grad * hat)
        small[1:2, :] += column_sum(n1_grad)
        results[1, at, :] = (
            hidden_grad[at, :] + norm_backward(n1_grad, hat, rate, ln1_gain_ref[...])
        ).astype(BF16)

        @pl.when(is_second)
        def _():
            cross(index).start()

    collect_with_pump(3, attention_back)
    pump_first(1)
    pump_second_ends(1)

    leave = remote(
        results.at[1 - s, token_rows(across_m)], rows_recv, leave_send.at[0], leave_recv.at[0], across
    )
    sum_of_rows(5, m_grad)
    sum_of_rows(4, r_grad)
    for index in range(2):

        def sums(number, index=index):
            at = big_rows(number)
            set_sum(6, 0, index, pre_grad[index, at, :])
            set_sum(7, 0, index, qkv_grad[index, at, 0:local_width])
            set_sum(7, 2 * local_width, index, qkv_grad[index, at, 2 * local_width :])

        repeat(0, bigs, sums)
    small_y_copy = remote(small_other, small_y, leave_send.at[1], leave_recv.at[1], across)
    small_other[0:6, :] = small[0:6, :]
    small_y_copy.start()

    pump_first(2)
    pump_second_ends(1)
    pump_second(2)

    @pl.when(is_second)
    def _():
        both_parts(1, mlp_part)

    pump_second_ends(2)
    pump_second(2)
    put_second_far(fc_grad_at, width, fc_grad)
    pump_second_ends(2)
    pump_second(PUMP)
    put_second_near(fc_grad_at, width, fc_grad)

    @pl.when(is_second)
    def _():
        collect(1, layer_out)

    leave.start()
    pump_second_ends(2)
    pump_second(PUMP)
    put_second_far(out_grad_at, local_width, out_grad)
    put_second_near(out_grad_at, local_width, out_grad)
    pump_second_ends(2)
    pump_second(PUMP)
    put_second_far(qkv_grad_at, qkv_rows, in_grad)
    pump_second_ends(2)
    pump_second(PUMP)
    put_second_near(qkv_grad_at, qkv_rows, in_grad)

    small_up = remote(small, small_pair, leave_send.at[2], leave_recv.at[2], pair)
    small_across = remote(small, small_mid, leave_send.at[3], leave_recv.at[3], middle)
    small_down = remote(small_mid, small_pair, leave_send.at[2], leave_recv.at[2], pair)

    def rows_finish(wanted):
        @pl.when(wanted)
        def _():
            leave.wait_recv()
            rows_out[pl.ds(chip, 1)] = results[pl.ds(1 - s, 1), token_rows(m), :].astype(F32)
            rows_out[pl.ds(1 - chip, 1)] = rows_recv[...].astype(F32)[None]

    if z_line:
        @pl.when(is_end)
        def _():
            small_y_copy.wait_recv()
            small[...] += small_y[...]
            small_up.start()

        pump_ends(first_ends, lent_from, first_end, False)
        pump_ends(second_ends, blocks + LENT, second_end, True)
        near, later = blocks * 2 // 3, blocks * 3 // 4
        pump_mids(first_mids, near, first_mid, False)
        pump_mids(second_mids, near, second_mid, True)
        rows_finish(s >= 0)

        @pl.when(is_mid)
        def _():
            small_y_copy.wait_recv()
            small_up.wait_recv()
            small[...] += small_y[...]
            small[...] += small_pair[...]
            small_across.start()

        pump_mids(first_mids, later, first_mid, False)
        pump_mids(second_mids, later, second_mid, True)

        @pl.when(is_mid)
        def _():
            small_across.wait_recv()
            small_mid[...] += small[...]
            small_down.start()
            small_out[...] = small_mid[...]

        pump_mids(first_mids, lent_from, first_mid, False)
        pump_mids(second_mids, blocks + LENT, second_mid, True)

        def back(index, source):
            lent_back(index, source).wait_recv()
            grad_out(lent_from + index, source).start()

        @pl.when(first_mid)
        def _():
            repeat(lent_from - BEHIND, lent_from, lambda step: mid_down(step, False))
            repeat(0, LENT, lambda index: back(index, grads_mid))

        @pl.when(second_mid)
        def _():
            repeat(blocks - BEHIND, blocks, lambda step: mid_down(step, False))

        def take(step, is_lent):
            grad_pair(step, grads_mid).wait_recv()
            deliver(step, grads_pair, is_lent)

        @pl.when(first_end)
        def _():
            repeat(0, lent_from, lambda step: take(step, False))
            repeat(0, LENT, lambda index: back(index, grads_pair))

        @pl.when(second_end)
        def _():
            for a, b, offset, _ in runs(second_order, 0, blocks + LENT):

                def step(place, a=a, offset=offset):
                    take(place + offset, a + offset >= blocks)

                repeat(a, b, step)

        @pl.when(is_end)
        def _():
            small_down.wait_recv()
            small_out[...] = small_pair[...]

    else:
        @pl.when(is_second)
        def _():
            repeat(0, blocks, gather_y)

        repeat(0, blocks, lambda step: grad_out(step, grads).start())
        rows_finish(s >= 0)
        small_y_copy.wait_recv()
        small_out[...] = small[...] + small_y[...]

    repeat(0, blocks, lambda step: grad_out(step, grads).wait())

    entry_across(0).wait_send()
    entry_sibling(0).wait_send()
    entry_forward(0).wait_send()
    leave.wait_send()
    small_y_copy.wait_send()
    def tile_sends(index):
        cross(index).wait_send()
        cross_core(index).wait_send()
        for which in range(4):
            part_copy(which, index).wait_send()

    repeat(0, TILES, tile_sends)

    @pl.when(is_first)
    def _():
        entry_across(1).wait_send()
        entry_sibling(1).wait_send()
        entry_forward(1).wait_send()

        def far_sends(index):
            for which in range(3):
                share(which, index).wait_send()
                if which != 1:
                    share_core(which, index).wait_send()
            for which in range(4):
                far_core(which, index).wait_send()
                far(which, index).wait_send()
                far_back(which, index).wait_send()

        repeat(0, TILES, far_sends)

    @pl.when(is_second)
    def _():
        bias_copy.wait_send()
        repeat(0, y_blocks, lambda step: weight_y(step).wait_send())
        if z_line:
            repeat(0, y_blocks, lambda step: weight_z(step).wait_send())
        repeat(0, blocks, lambda step: grad_y(step).wait_send())

    if z_line:
        sent = jnp.where(is_first, lent_from, blocks + LENT)
        repeat(0, sent, lambda step: grad_pair(step, grads).wait_send())

        @pl.when(is_first)
        def _():
            repeat(0, LENT, lambda index: lent(index).wait_send())

        @pl.when(is_second)
        def _():
            repeat(0, LENT, lambda index: lent_back(index, grads_pair).wait_send())

        @pl.when(is_end)
        def _():
            small_up.wait_send()

        @pl.when(is_mid)
        def _():
            repeat(0, sent, lambda step: grad_mid(step).wait_send())
            small_across.wait_send()
            small_down.wait_send()


def finish_kernel(local_width, rows_ref, small_ref, grads_ref, *refs):
    outs, (held_rows, held, cast, in_sem, out_sem, rows_sem) = refs[:13], refs[13:]
    rows_out, qkv_out, out_out, fc_out, proj_out, bias_out = outs[:6]
    rows_in = pltpu.make_async_copy(rows_ref, held_rows, rows_sem.at[0])
    rows_copy = pltpu.make_async_copy(held_rows, rows_out, rows_sem.at[1])

    def at_block(number):
        return pl.ds(pl.multiple_of(number * FINISH, FINISH), FINISH)

    def fetch(number):
        at = at_block(number)
        return pltpu.make_async_copy(grads_ref.at[at], held.at[at], in_sem.at[number])

    def repeat(start, last, action):
        def step_of(step, carry):
            action(step)
            return carry

        lax.fori_loop(start, last, step_of, 0)

    blocks = held.shape[0] // FINISH
    repeat(0, blocks, lambda number: fetch(number).start())
    rows_in.start()
    bias_out[0:1, :] = small_ref[7:8, 0:local_width]
    bias_out[1:2, :] = small_ref[7:8, 2 * local_width : 3 * local_width]
    for row, target in enumerate(outs[6:]):
        target[...] = small_ref[row : row + 1, :]
    first = 0
    puts = []
    for target in (proj_out, fc_out, out_out, qkv_out):
        count = target.shape[0] // FINISH

        def put(number, first=first, target=target):
            return pltpu.make_async_copy(
                cast.at[at_block(first + number)], target.at[at_block(number)], out_sem.at[first + number]
            )

        def step(number, first=first, put=put):
            fetch(first + number).wait()
            at = at_block(first + number)
            cast[at, :] = held[at, :].astype(F32)
            put(number).start()

        repeat(0, count, step)
        puts.append((count, put))
        first += count
    rows_in.wait()
    rows_copy.start()
    for count, put in puts:
        repeat(0, count, lambda number: put(number).wait())
    rows_copy.wait()


def local(
    z_line,
    boundary_in,
    order,
    ln1_gain,
    ln1_bias,
    w_qkv,
    qkv_bias,
    w_out,
    out_bias,
    ln2_gain,
    ln2_bias,
    w_fc,
    fc_bias,
    w_proj,
    proj_bias,
):
    _, micro, rows, width = boundary_in.shape
    local_width = w_qkv.shape[-1]
    units = w_fc.shape[-1]
    length = rows * lax.axis_size("mp")
    heads = local_width // HEAD_DIM
    weight_rows = 4 * local_width + width + units
    blocks = weight_rows // BLOCK
    stream_rows = weight_rows + LENT * BLOCK
    vmem = pltpu.VMEM
    dma = pltpu.SemaphoreType.DMA
    in_vmem = pl.BlockSpec(memory_space=pltpu.VMEM)
    in_any = pl.BlockSpec(memory_space=pl.ANY)
    in_smem = pl.BlockSpec(memory_space=pltpu.SMEM)
    out_rows, small, grads = pl.pallas_call(
        functools.partial(kernel, z_line),
        out_shape=(
            jax.ShapeDtypeStruct((micro, rows, width), F32),
            jax.ShapeDtypeStruct((8, width), F32),
            jax.ShapeDtypeStruct((weight_rows, width), BF16),
        ),
        in_specs=[
            in_smem,
            in_any,
            in_vmem,
            in_vmem,
            in_any,
            in_vmem,
            in_any,
            in_vmem,
            in_vmem,
            in_vmem,
            in_any,
            in_vmem,
            in_any,
            in_vmem,
        ],
        out_specs=(in_vmem, in_vmem, in_any),
        scratch_shapes=[
            vmem((micro, rows, width), BF16),
            vmem((micro, rows, width), BF16),
            vmem((2, weight_rows, width), BF16),
            vmem((2, 8, width), F32),
            vmem((3, length, width), BF16),
            vmem((2, length, width), BF16),
            vmem((rows, width), BF16),
            vmem((2, length, width), BF16),
            vmem((2, length, width), BF16),
            vmem((2, 3, heads, length, HEAD_DIM), BF16),
            vmem((2 * heads, length, length), BF16),
            vmem((heads, length, HEAD_DIM), BF16),
            vmem((2, length, local_width), BF16),
            vmem((length, width), F32),
            vmem((length, width), F32),
            vmem((2, length, units), BF16),
            vmem((2, length, units), BF16),
            vmem((2, length, width), BF16),
            vmem((2, length, width), BF16),
            vmem((2, length, 3 * local_width), BF16),
            vmem((4, length, width), BF16),
            vmem((4, length, width), BF16),
            vmem((stream_rows, width), BF16),
            vmem((weight_rows, width), BF16),
            vmem((weight_rows, width), BF16),
            vmem((stream_rows, width), BF16),
            vmem((stream_rows, width), BF16),
            vmem((8, width), F32),
            vmem((8, width), F32),
            vmem((8, width), F32),
            vmem((8, width), F32),
            vmem((8, width), F32),
            dma((5,)),
            dma((7,)),
            dma((7,)),
            dma((weight_rows // FETCH,)),
            dma((weight_rows // FETCH,)),
            dma((weight_rows // FETCH,)),
            dma((weight_rows // FETCH,)),
            dma((4, TILES)),
            dma((4, TILES)),
            dma((4, TILES)),
            dma((4, TILES)),
            dma((4, TILES)),
            dma((4, TILES)),
            dma((4, TILES)),
            dma((4, TILES)),
            dma((3, TILES)),
            dma((3, TILES)),
            dma((3, TILES)),
            dma((3, TILES)),
            dma((TILES,)),
            dma((TILES,)),
            dma((TILES,)),
            dma((TILES,)),
            dma((4,)),
            dma((4,)),
            dma((blocks,)),
            dma((blocks,)),
            dma((blocks + LENT,)),
            dma((blocks + LENT,)),
            dma((blocks + LENT,)),
            dma((blocks + LENT,)),
            dma((blocks,)),
            dma((LENT,)),
            dma((LENT,)),
            dma((LENT,)),
            dma((LENT,)),
        ],
        compiler_params=pltpu.CompilerParams(
            collective_id=0, has_side_effects=True, vmem_limit_bytes=63 * 2**20
        ),
        name="two_layers",
    )(
        order,
        boundary_in,
        ln1_gain,
        ln1_bias,
        jnp.swapaxes(w_qkv, 2, 3).reshape(1, 3 * local_width, width),
        qkv_bias,
        w_out,
        out_bias,
        ln2_gain,
        ln2_bias,
        w_fc,
        fc_bias,
        w_proj,
        proj_bias,
    )
    if not z_line:
        small, grads = lax.psum((small, grads), "dp")
    shapes = [
        (micro, rows, width),
        (3 * local_width, width),
        (local_width, width),
        (width, units),
        (units, width),
        (2, local_width),
    ] + [(1, width)] * 6 + [(1, units)]
    (
        out_rows,
        qkv_grad,
        out_grad,
        fc_grad,
        proj_grad,
        qkv_bias_grad,
        ln1_gain_grad,
        ln1_bias_grad,
        ln2_gain_grad,
        ln2_bias_grad,
        out_bias_grad,
        proj_bias_grad,
        fc_bias_grad,
    ) = pl.pallas_call(
        functools.partial(finish_kernel, local_width),
        out_shape=[jax.ShapeDtypeStruct(shape, F32) for shape in shapes],
        in_specs=[in_any, in_vmem, in_any],
        out_specs=[in_any] * 5 + [in_vmem] * 8,
        scratch_shapes=[
            vmem((micro, rows, width), F32),
            vmem((weight_rows, width), BF16),
            vmem((weight_rows, width), F32),
            dma((weight_rows // FINISH,)),
            dma((weight_rows // FINISH,)),
            dma((2,)),
        ],
        compiler_params=pltpu.CompilerParams(vmem_limit_bytes=62 * 2**20),
        name="finish",
    )(out_rows, small, grads)
    return (
        out_rows[None],
        ln1_gain_grad,
        ln1_bias_grad,
        jnp.swapaxes(qkv_grad.reshape(1, 3, local_width, width), 2, 3),
        qkv_bias_grad[None],
        out_grad[None],
        out_bias_grad,
        ln2_gain_grad,
        ln2_bias_grad,
        fc_grad[None],
        fc_bias_grad,
        proj_grad[None],
        proj_bias_grad,
    )


def solution(mesh):
    return jax.shard_map(
        functools.partial(local, mesh.shape["dp"] == 4),
        mesh=mesh,
        in_specs=(
            P("section", "dp", "mp", None),
            P("dp", None),
            P("section", None),
            P("section", None),
            P("section", None, None, "mp"),
            P("section", None, "mp"),
            P("section", "mp", None),
            P("section", None),
            P("section", None),
            P("section", None),
            P("section", None, "mp"),
            P("section", "mp"),
            P("section", "mp", None),
            P("section", None),
        ),
        out_specs=(
            P("section", "dp", "mp", None),
            P("section", None),
            P("section", None),
            P("section", None, None, "mp"),
            P("section", None, "mp"),
            P("section", "mp", None),
            P("section", None),
            P("section", None),
            P("section", None),
            P("section", None, "mp"),
            P("section", "mp"),
            P("section", "mp", None),
            P("section", None),
        ),
        check_vma=False,
    )
```

```python
import functools

import jax
import jax.numpy as jnp
from jax import lax
from jax.experimental import pallas as pl
from jax.experimental.pallas import tpu as pltpu
from jax.sharding import PartitionSpec as P

HEAD_DIM = 64
BRANCH_SCALE = 0.14433756729740643
NORM_EPS = 1e-05
GELU_RATE = 0.7978845608028654
GELU_CUBE = 0.044715
NEGATIVE = -1e30
BLOCK = 48
PUMP = 2
FINISH = 192
FETCH = 96
TILES = 4
FINE = 1
SMALL = 16
LENT = 10
BEHIND = 4
MESH = pl.DeviceIdType.MESH
BF16 = jnp.bfloat16
F32 = jnp.float32


def dot_nn(a, b):
    return lax.dot_general(a, b, (((1,), (0,)), ((), ())), preferred_element_type=F32)


def dot_nt(a, b):
    return lax.dot_general(a, b, (((1,), (1,)), ((), ())), preferred_element_type=F32)


def dot_tn(a, b):
    return lax.dot_general(a, b, (((0,), (0,)), ((), ())), preferred_element_type=F32)


def normed(values):
    center = values - jnp.mean(values, axis=-1, keepdims=True)
    rate = lax.rsqrt(jnp.mean(center * center, axis=-1, keepdims=True) + NORM_EPS)
    return center * rate, rate


def norm_backward(grad, hat, rate, gain):
    scaled = grad * gain
    return rate * (
        scaled
        - jnp.mean(scaled, axis=-1, keepdims=True)
        - hat * jnp.mean(scaled * hat, axis=-1, keepdims=True)
    )


def column_sum(values):
    return jnp.sum(values.astype(F32), axis=0, keepdims=True)


def remote(src, dst, send_sem, recv_sem, device):
    return pltpu.make_async_remote_copy(
        src_ref=src,
        dst_ref=dst,
        send_sem=send_sem,
        recv_sem=recv_sem,
        device_id=device,
        device_id_type=MESH,
    )


def kernel(
    z_line,
    order_ref,
    boundary_ref,
    ln1_gain_ref,
    ln1_bias_ref,
    w_qkv_ref,
    qkv_bias_ref,
    w_out_ref,
    out_bias_ref,
    ln2_gain_ref,
    ln2_bias_ref,
    w_fc_ref,
    fc_bias_ref,
    w_proj_ref,
    proj_bias_ref,
    rows_out,
    small_out,
    grads_out,
    raw,
    slots,
    weights,
    biases,
    ends,
    results,
    rows_recv,
    n1,
    n2,
    qkv,
    probs,
    head_rows,
    attended,
    hidden,
    hidden_grad,
    act,
    slope,
    m_grad,
    r_grad,
    qkv_grad,
    part,
    part_recv,
    grads,
    grads_other,
    grads_y,
    grads_pair,
    grads_mid,
    small,
    small_other,
    small_y,
    small_pair,
    small_mid,
    local_sem,
    entry_send,
    entry_recv,
    weight_y_send,
    weight_y_recv,
    weight_z_send,
    weight_z_recv,
    part_send,
    part_recv_sem,
    far_core_send,
    far_core_recv,
    far_send,
    far_recv,
    far_back_send,
    far_back_recv,
    share_send,
    share_recv,
    share_core_send,
    share_core_recv,
    cross_send,
    cross_recv,
    cross_core_send,
    cross_core_recv,
    leave_send,
    leave_recv,
    grad_y_send,
    grad_y_recv,
    grad_pair_send,
    grad_pair_recv,
    grad_mid_send,
    grad_mid_recv,
    grad_out_sem,
    lent_send,
    lent_recv,
    back_send,
    back_recv,
):
    s, d, m = lax.axis_index("section"), lax.axis_index("dp"), lax.axis_index("mp")
    core, chip = lax.rem(m, 2), lax.div(m, 2)
    half = lax.rem(d, 2)
    across_m = 2 * (1 - chip) + core
    sibling = (s, d, 2 * chip + 1 - core)
    across = (s, d, across_m)
    other_section = (1 - s, d, m)
    pair = (s, d + 1 - 2 * half, m)
    middle = (s, 3 - d, m)
    is_first, is_second = s == 0, s == 1
    is_mid = lax.div(d + 1, 2) == 1
    is_end = lax.div(d + 1, 2) != 1

    rows = boundary_ref.shape[2]
    length, width = n1.shape[1:]
    tile = length // TILES
    piece = tile // 2
    big = length // 2
    local_width = attended.shape[2]
    units = act.shape[2]
    heads = local_width // HEAD_DIM
    tiles_per_big, bigs = big // tile, length // big
    scale = HEAD_DIM ** (-0.5)
    qkv_rows = 3 * local_width
    out_at, fc_at, proj_at = qkv_rows, qkv_rows + local_width, qkv_rows + local_width + width
    weight_rows = weights.shape[1]
    blocks = weight_rows // BLOCK
    ends_in, ends_grad = 2 * s, 2 * (1 - s)

    def set_rows(index):
        return index * (1 - s)

    def set_weights(index):
        return index * s

    def span(index, count):
        start = index * count
        return pl.ds(start if isinstance(start, int) else pl.multiple_of(start, count), count)

    def tile_rows(index):
        return span(index, tile)

    def big_rows(index):
        return span(index, big)

    def tile_of(which):
        return tile // 2 if which == FINE else tile

    def count_of(which):
        return length // tile_of(which)

    def number_of(which, index):
        return which * TILES + (TILES if which > FINE else 0) + index

    def rows_of(which, index):
        return span(index, tile_of(which))

    def piece_rows(which, index, core_of, base=0):
        size = tile_of(which) // 2
        return pl.ds(pl.multiple_of(base + (2 * index + core_of) * size, size), size)

    partners = [sibling, across, other_section]
    if z_line:
        partners += [pair, middle]
    barrier = pltpu.get_barrier_semaphore()
    for device in partners:
        pl.semaphore_signal(barrier, inc=1, device_id=device, device_id_type=MESH)

    loads = [
        pltpu.make_async_copy(boundary_ref.at[0], raw, local_sem.at[0]),
        pltpu.make_async_copy(
            w_qkv_ref.at[0], weights.at[0, pl.ds(0, qkv_rows)], local_sem.at[1]
        ),
        pltpu.make_async_copy(
            w_out_ref.at[0], weights.at[0, pl.ds(out_at, local_width)], local_sem.at[2]
        ),
        pltpu.make_async_copy(w_fc_ref.at[0], weights.at[0, pl.ds(fc_at, width)], local_sem.at[3]),
        pltpu.make_async_copy(
            w_proj_ref.at[0], weights.at[0, pl.ds(proj_at, units)], local_sem.at[4]
        ),
    ]
    for load in loads:
        load.start()

    biases[0] = jnp.zeros_like(biases[0])
    biases[0, 0:1, :] = fc_bias_ref[...]
    biases[0, 1:2, 0:local_width] = qkv_bias_ref[0, 0:1, :]
    biases[0, 2:3, 0:local_width] = qkv_bias_ref[0, 1:2, :]
    small[...] = jnp.zeros_like(small)
    small_other[...] = jnp.zeros_like(small_other)

    loads[0].wait()
    for slot in range(2):
        picked = jnp.where(is_first, order_ref[0, slot], slot).astype(F32)
        slots[slot] = (
            raw[0].astype(F32) * (1.0 - picked) + raw[1].astype(F32) * picked
        ).astype(BF16)

    pl.semaphore_wait(barrier, len(partners))

    def token_rows(index):
        return pl.ds(pl.multiple_of(index * rows, rows), rows)

    def entry_across(which):
        slot = (1 - chip) * (1 - which) + chip * which
        return remote(
            slots.at[slot],
            ends.at[which, token_rows(m)],
            entry_send.at[which],
            entry_recv.at[which],
            across,
        )

    def entry_sibling(which):
        slot = chip * (1 - which) + (1 - chip) * which
        return remote(
            slots.at[slot],
            ends.at[which, token_rows(m)],
            entry_send.at[2 + which],
            entry_recv.at[2 + which],
            sibling,
        )

    def entry_forward(which):
        at = token_rows(across_m)
        return remote(
            ends.at[which, at],
            ends.at[which, at],
            entry_send.at[4 + which],
            entry_recv.at[4 + which],
            sibling,
        )

    bias_copy = remote(biases.at[0], biases.at[1], entry_send.at[6], entry_recv.at[6], across)

    def entry_start(which):
        entry_across(which).start()
        entry_sibling(which).start()
        slot = chip if which == 0 else 1 - chip
        ends[which, token_rows(m), :] = slots[slot]

    def entry_pass(which):
        entry_across(which).wait_recv()
        entry_forward(which).start()

    def entry_finish(which):
        entry_pass(which)
        entry_sibling(which).wait_recv()
        entry_forward(which).wait_recv()

    @pl.when(is_first)
    def _():
        entry_start(1)
        entry_start(0)

    y_blocks = weight_rows // FETCH // (2 if z_line else 1)

    def weight_block(index):
        return pl.ds(pl.multiple_of(index * BLOCK, BLOCK), BLOCK)

    def near_block(step):
        return span(2 * step + half if z_line else step, FETCH)

    def weight_y(step):
        return remote(
            weights.at[0, near_block(step)],
            weights.at[1, near_block(step)],
            weight_y_send.at[0],
            weight_y_recv.at[step],
            across,
        )

    def weight_z(step):
        return remote(
            weights.at[1, near_block(step)],
            weights.at[1, near_block(step)],
            weight_z_send.at[0],
            weight_z_recv.at[step],
            pair,
        )

    def repeat(first, last, action):
        def step_of(step, carry):
            action(step)
            return carry

        lax.fori_loop(first, last, step_of, 0)

    late_step = proj_at * y_blocks // weight_rows
    y_done = [0]

    def weight_need(row):
        steps = row * y_blocks // weight_rows
        if z_line and steps > y_done[0]:
            first, y_done[0] = y_done[0], steps

            @pl.when(is_second)
            def _():
                repeat(first, steps, lambda step: weight_z(step).wait_recv())

    def weight_pass(step):
        weight_y(step).wait_recv()
        if z_line:
            weight_z(step).start()

    for load in loads[1:]:
        load.wait()

    def sent(source, sem):
        remote(source, source, sem, sem, sibling).wait_send()

    def arrived(target, sem):
        remote(target, target, sem, sem, sibling).wait_recv()

    def cross(index):
        at = piece_rows(FINE, index, core)
        return remote(
            results.at[s, at],
            ends.at[2, at],
            cross_send.at[0],
            cross_recv.at[index],
            other_section,
        )

    def cross_core(index):
        at = piece_rows(FINE, index, core)
        return remote(
            ends.at[2, at],
            ends.at[2, at],
            cross_core_send.at[0],
            cross_core_recv.at[index],
            sibling,
        )

    shared = (n2, m_grad, r_grad)

    def share(which, index):
        at = piece_rows(which, index, core)
        source = ends.at[2, at] if which == FINE else shared[which].at[0, at]
        return remote(
            source,
            shared[which].at[1, at],
            share_send.at[0],
            share_recv.at[number_of(which, index)],
            across,
        )

    def share_core(which, index):
        at = piece_rows(which, index, core)
        return remote(
            shared[which].at[1, at],
            shared[which].at[1, at],
            share_core_send.at[1 if which == FINE else 0],
            share_core_recv.at[index if which == 0 else TILES + which],
            sibling,
        )

    def share_some(which, start, count):
        def forward(index):
            share(which, start + index).wait_recv()
            share_core(which, start + index).start()

        repeat(0, count, forward)
        if which == 0:
            repeat(0, count, lambda index: share_core(which, start + index).wait_recv())
        else:
            arrived(shared[which].at[1, pl.ds(0, big)], share_core_recv.at[TILES + which])

    def part_copy(which, index):
        at = rows_of(which, index)
        return remote(
            part.at[which, at],
            part_recv.at[which, at],
            part_send.at[0],
            part_recv_sem.at[number_of(which, index)],
            sibling,
        )

    def spare_rows(which, index, core_of):
        return piece_rows(which, index, core_of, which * length)

    def far_core(which, index):
        return remote(
            grads_y.at[spare_rows(which, index, 1 - core)],
            grads_other.at[spare_rows(which, index, 1 - core)],
            far_core_send.at[0],
            far_core_recv.at[number_of(which, index)],
            sibling,
        )

    def far(which, index):
        return remote(
            grads_y.at[spare_rows(which, index, core)],
            weights.at[1, spare_rows(which, index, core)],
            far_send.at[0],
            far_recv.at[number_of(which, index)],
            across,
        )

    def far_back(which, index):
        at = spare_rows(which, index, core)
        return remote(
            weights.at[1, at],
            weights.at[1, at],
            far_back_send.at[0],
            far_back_recv.at[number_of(which, index)],
            sibling,
        )

    def far_pass(which, index):
        far_core(which, index).wait_recv()
        at = spare_rows(which, index, core)
        grads_y[at, :] = (grads_y[at, :].astype(F32) + grads_other[at, :].astype(F32)).astype(BF16)
        far(which, index).start()

    def part_sum(which, index):
        at = rows_of(which, index)
        near = part[which, at, :].astype(F32) + part_recv[which, at, :].astype(F32)
        size = tile_of(which)
        other = weights[
            1, pl.ds(pl.multiple_of(which * length + index * size, size), size), :
        ].astype(F32)
        return near + jnp.where(is_first, other, 0.0)

    def far_parts(which, value_of, per=1, before=None):
        def step(number):
            if before is not None:
                before(number)
            size = per * tile_of(which)
            grads_y[pl.ds(pl.multiple_of(which * length + number * size, size), size), :] = (
                value_of(1, 0, span(number, size)).astype(BF16)
            )
            for index in range(per):
                far_core(which, number * per + index).start()

            @pl.when(number > 0)
            def _():
                for index in range(per):
                    far_pass(which, (number - 1) * per + index)

        repeat(0, count_of(which) // per, step)
        for index in range(per):
            far_pass(which, count_of(which) - per + index)

    def own_parts(which, value_of, per=1):
        def step(number):
            at = span(number, per * tile_of(which))
            part[which, at, :] = value_of(0, 0, at).astype(BF16)
            for index in range(per):
                part_copy(which, number * per + index).start()

        repeat(0, count_of(which) // per, step)

    def both_parts(which, value_of, per=1):
        def step(number):
            at = span(number, per * tile_of(which))
            part[which, at, :] = (value_of(0, 0, at) + value_of(1, 1, at)).astype(BF16)
            for index in range(per):
                part_copy(which, number * per + index).start()

        repeat(0, count_of(which) // per, step)

    def collect(which, finish, beside=None, start=0, last=None):
        last = count_of(which) if last is None else last

        def far_next(index):
            far(which, index).wait_recv()
            far_back(which, index).start()

        @pl.when(is_first)
        def _():
            far_next(start)

        def step(index):
            @pl.when(is_first)
            def _():
                @pl.when(index + 1 < last)
                def _():
                    far_next(index + 1)

                if beside is not None:
                    beside(index)
                far_back(which, index).wait_recv()

            part_copy(which, index).wait_recv()
            finish(index)

        repeat(start, last, step)

    def weight_of(shards, first, count):
        return weights[shards, first : first + count, :]

    def scale_grad(index):
        at = rows_of(FINE, index)
        m_grad[0, at, :] = (BRANCH_SCALE * ends[ends_grad, at, :].astype(F32)).astype(BF16)

    @pl.when(is_second)
    def _():
        bias_copy.start()
        repeat(0, late_step, lambda step: weight_y(step).start())
        entry_start(0)
        repeat(late_step, y_blocks, lambda step: weight_y(step).start())
        repeat(0, late_step, weight_pass)
        bias_copy.wait_recv()
        entry_finish(0)
        repeat(0, count_of(FINE), scale_grad)
        repeat(late_step, y_blocks - bigs, weight_pass)

    def norm_big(which, source, number):
        def step(index):
            at = span(number * (big // tile) + index, tile)
            hat, _ = normed(ends[source, at, :].astype(F32))
            n1[which, at, :] = (hat * ln1_gain_ref[...] + ln1_bias_ref[...]).astype(BF16)

        repeat(0, big // tile, step)

    def cross_receive(start, last, action, on=None):
        def pass_on(index):
            cross(index).wait_recv()
            cross_core(index).start()
            if on is not None:
                on(index)

        pass_on(start)

        def step(index):
            @pl.when(index + 1 < last)
            def _():
                pass_on(index + 1)

            cross_core(index).wait_recv()
            action(index)

        repeat(start, last, step)

    causal = lax.broadcasted_iota(jnp.int32, (length, length), 1) >= lax.broadcasted_iota(
        jnp.int32, (length, length), 0
    )

    def bias_of(shards, row, count):
        return biases[shards, row : row + 1, 0:count]

    def head_columns(kind, head):
        first = kind * local_width + head * HEAD_DIM
        return slice(first, first + HEAD_DIM)

    def project(index, number):
        source, shards = set_rows(index), set_weights(index)
        at = big_rows(number)
        for kind in range(3):
            values = dot_nt(n1[source, at, :], weight_of(shards, kind * local_width, local_width))
            if kind == 0:
                values = values + bias_of(shards, 1, local_width)
            if kind == 2:
                values = values + bias_of(shards, 2, local_width)
            values = values.astype(BF16)
            if kind == 0:
                values = (values.astype(F32) * scale).astype(BF16)
            for head in range(heads):
                qkv[index, kind, head, at, :] = values[:, head_columns(0, head)]

    def attention_forward(index):
        for head in range(heads):
            scores = dot_nt(qkv[index, 1, head], qkv[index, 0, head])
            scores = jnp.where(causal, scores, NEGATIVE)
            raised = jnp.exp(scores - jnp.max(scores, axis=0, keepdims=True))
            shares = raised * (1.0 / jnp.sum(raised, axis=0, keepdims=True))
            shares = shares.astype(BF16)
            probs[index * heads + head] = shares
            attended[index, :, head_columns(0, head)] = dot_tn(
                shares, qkv[index, 2, head]
            ).astype(BF16)

    weight_need(out_at)

    @pl.when(is_second)
    def _():
        def step(number):
            def pass_on(index):
                cross(index).wait_recv()
                cross_core(index).start()

            per = count_of(FINE) // bigs
            repeat(number * per, (number + 1) * per, pass_on)
            repeat(
                number * per, (number + 1) * per, lambda index: cross_core(index).wait_recv()
            )
            norm_big(0, 2, number)
            repeat(0, 2, lambda index: project(index, number))
            weight_pass(y_blocks - bigs + number)

        repeat(0, bigs, step)

    @pl.when(is_first)
    def _():
        def step(index):
            entry_sibling(index).wait_recv()
            norm_big(index, index, chip)
            project(index, chip)

        repeat(0, 2, step)
        entry_pass(1)
        entry_forward(1).wait_recv()
        norm_big(1, 1, 1 - chip)
        project(1, 1 - chip)

    attention_forward(1)

    def attention_part(index, shards, at):
        return dot_nn(attended[index, at, :], weight_of(shards, out_at, local_width))

    @pl.when(is_first)
    def _():
        far_parts(0, attention_part)
        entry_pass(0)
        entry_forward(0).wait_recv()
        norm_big(0, 0, 1 - chip)
        project(0, 1 - chip)

    attention_forward(0)

    weight_need(fc_at)

    @pl.when(is_first)
    def _():
        own_parts(0, attention_part)

    @pl.when(is_second)
    def _():
        both_parts(0, attention_part)

    def attention_out(index):
        at = tile_rows(index)
        held = ends[ends_in, at, :].astype(F32) + BRANCH_SCALE * (
            part_sum(0, index) + out_bias_ref[...]
        )
        hidden[at, :] = held
        hat, _ = normed(held)
        n2[0, at, :] = (hat * ln2_gain_ref[...] + ln2_bias_ref[...]).astype(BF16)

        @pl.when(is_first)
        def _():
            share(0, index).start()

    def activate(index, source, shards, at):
        u = dot_nn(n2[source, at, :], weight_of(shards, fc_at, width)) + bias_of(shards, 0, units)
        square = u * u
        bent = jnp.tanh(GELU_RATE * (u + GELU_CUBE * u * square))
        act[index, at, :] = (0.5 * u * (1.0 + bent)).astype(BF16)
        slope[index, at, :] = (
            0.5 * (1.0 + bent)
            + (0.5 * GELU_RATE) * u * (1.0 - bent * bent) * (1.0 + (3.0 * GELU_CUBE) * square)
        ).astype(BF16)

    weight_need(proj_at)

    def first_half(number):
        collect(
            0, attention_out, start=number * tiles_per_big, last=(number + 1) * tiles_per_big
        )
        activate(set_weights(1), 0, set_weights(1), big_rows(number))

    repeat(0, bigs, first_half)

    def mlp_part(index, shards, at):
        return dot_nn(act[index, at, :], weight_of(shards, proj_at, units))

    def other_activate(number):
        share_some(0, number, 1)
        activate(1, 1, 0, span(number, tile))

    @pl.when(is_first)
    def _():
        own_parts(FINE, mlp_part, per=2)
        far_parts(FINE, mlp_part, per=2, before=other_activate)

    weight_need(weight_rows)

    proj_grad_at, fc_grad_at = 0, units
    out_grad_at = fc_grad_at + width
    qkv_grad_at = out_grad_at + local_width

    lent_from = blocks - LENT
    small_from, small_count = blocks + LENT, 2 * BLOCK // SMALL
    small_row = (lent_from - 2) * BLOCK

    def block_rows(step, is_small=False):
        if is_small:
            start = small_row + (step - small_from) * SMALL
            return pl.ds(start if isinstance(start, int) else pl.multiple_of(start, SMALL), SMALL)
        return weight_block(step)

    def grad_y(step, is_small=False):
        return remote(
            grads_other.at[block_rows(step, is_small)],
            grads_y.at[block_rows(step, is_small)],
            grad_y_send.at[0],
            grad_y_recv.at[step],
            across,
        )

    def grad_pair(step, source, is_small=False):
        return remote(
            source.at[block_rows(step, is_small)],
            grads_pair.at[block_rows(step, is_small)],
            grad_pair_send.at[0],
            grad_pair_recv.at[step],
            pair,
        )

    def grad_mid(step, is_small=False):
        return remote(
            grads.at[block_rows(step, is_small)],
            grads_mid.at[block_rows(step, is_small)],
            grad_mid_send.at[0],
            grad_mid_recv.at[step],
            middle,
        )

    def grad_out(step, source, is_small=False):
        at = block_rows(step, is_small)
        return pltpu.make_async_copy(source.at[at], grads_out.at[at], grad_out_sem.at[0])

    def add_into(target, source, step, is_small):
        at = block_rows(step, is_small)
        target[at, :] = (target[at, :].astype(F32) + source[at, :].astype(F32)).astype(BF16)

    def gather_y(step, is_small=False):
        grad_y(step, is_small).wait_recv()
        add_into(grads, grads_y, step, is_small)

    def mid_up(step, is_small=False):
        grad_pair(step, grads, is_small).wait_recv()
        add_into(grads, grads_pair, step, is_small)
        grad_mid(step, is_small).start()

    def kind_of(step):
        return blocks <= step < small_from, step >= small_from

    def mid_down(step, kind):
        grad_mid(step, kind[1]).wait_recv()
        add_into(grads_mid, grads, step, kind[1])
        grad_pair(step, grads_mid, kind[1]).start()
        deliver(step, grads_mid, kind)

    def deliver(step, source, kind):
        if kind[0]:
            lent_back(step - blocks, source).start()
        else:
            grad_out(step, source, kind[1]).start()

    def lent(index):
        return remote(
            grads.at[weight_block(lent_from + index)],
            grads.at[weight_block(blocks + index)],
            lent_send.at[0],
            lent_recv.at[index],
            other_section,
        )

    def lent_back(index, source):
        return remote(
            source.at[weight_block(blocks + index)],
            source.at[weight_block(lent_from + index)],
            back_send.at[0],
            back_recv.at[index],
            other_section,
        )

    small_blocks = range(small_from, small_from + small_count)
    turn = blocks - 4
    first_order = [*range(lent_from - 2), *small_blocks]
    second_order = [
        *range(lent_from - 2),
        *range(lent_from, turn),
        *range(blocks, small_from),
        *range(turn, blocks),
        *small_blocks,
    ]

    def runs(order, start, last, behind=0):
        cuts = [start]
        for place in range(start + 1, last):
            for back in (place, place - behind):
                if back > 0 and order[back] != order[back - 1] + 1 and cuts[-1] != place:
                    cuts.append(place)
        cuts.append(last)
        return [
            (a, b, order[a] - a, order[max(a - behind, 0)] - max(a - behind, 0))
            for a, b in zip(cuts, cuts[1:])
            if b > a
        ]

    first_ends, first_mids, second_ends, second_mids = [0], [0], [0], [0]
    first_end, second_end = jnp.logical_and(is_first, is_end), jnp.logical_and(is_second, is_end)
    first_mid, second_mid = jnp.logical_and(is_first, is_mid), jnp.logical_and(is_second, is_mid)

    def gather(step, kind):
        if kind[0]:
            lent(step - blocks).wait_recv()
        else:
            gather_y(step, kind[1])

    def walk(order, start, last, action):
        for a, b, offset, _ in runs(order, start, last):
            kind = kind_of(a + offset)
            repeat(a + offset, b + offset, functools.partial(action, kind=kind))

    def pump_ends(done, last, wanted, second):
        start, done[0] = done[0], last
        if z_line:
            def up(step, kind):
                if second:
                    gather(step, kind)
                grad_pair(step, grads, kind[1]).start()

            @pl.when(wanted)
            def _():
                walk(second_order if second else first_order, start, last, up)

    def pump_mids(done, last, wanted, second):
        start, done[0] = done[0], last
        if z_line:
            @pl.when(wanted)
            def _():
                order = second_order if second else first_order
                for a, b, offset, old in runs(order, start, last, BEHIND):

                    def step(place, a=a, offset=offset, old=old):
                        if second:
                            gather(place + offset, kind_of(a + offset))
                        mid_up(place + offset, kind_of(a + offset)[1])

                        @pl.when(place >= BEHIND)
                        def _():
                            mid_down(place - BEHIND + old, kind_of(max(a - BEHIND, 0) + old))

                    repeat(a, b, step)

    def pump_first_ends(count):
        pump_ends(first_ends, first_ends[0] + count, first_end, False)

    def pump_first(count):
        pump_mids(first_mids, first_mids[0] + count, first_mid, False)

    def pump_second_ends(count):
        pump_ends(second_ends, second_ends[0] + count, second_end, True)

    def pump_second(count):
        pump_mids(second_mids, second_mids[0] + count, second_mid, True)

    def cut_columns(count):
        return (2, count // 2) if count % 768 == 0 else (1, count)

    def put_first_inside(first, count, value_of):
        steps, columns = cut_columns(count)

        def step(number):
            at = span(number, columns)
            grads[pl.ds(first + number * columns, columns), :] = (
                value_of(0, at) + value_of(1, at)
            ).astype(BF16)

        repeat(0, steps, step)

    def put_first(first, count, value_of):
        @pl.when(is_first)
        def _():
            put_first_inside(first, count, value_of)

    def put_second(target, index, first, count, value_of, after=None):
        steps, columns = cut_columns(count)

        def step(number):
            start = first + number * columns
            target[pl.ds(start, columns), :] = value_of(index, span(number, columns)).astype(BF16)
            if after is not None:
                after(first // BLOCK + number * (columns // BLOCK), columns // BLOCK)

        @pl.when(is_second)
        def _():
            repeat(0, steps, step)

    def put_second_far(first, count, value_of):
        def leave_blocks(start, number):
            if z_line and first == qkv_grad_at:
                repeat(first // BLOCK, lent_from - 2, lambda step: grad_y(step).start())
                repeat(lent_from, blocks, lambda step: grad_y(step).start())
                repeat(
                    small_from, small_from + small_count, lambda step: grad_y(step, True).start()
                )
            else:
                repeat(start, start + number, lambda step: grad_y(step).start())

        put_second(grads_other, 1, first, count, value_of, leave_blocks)

    def put_second_near(first, count, value_of):
        put_second(grads, 0, first, count, value_of)

    def set_sum(row, column, index, values):
        total = column_sum(values)
        columns = slice(column, column + total.shape[1])
        if index == 0:
            small[row : row + 1, columns] += total
        else:
            @pl.when(is_first)
            def _():
                small[row : row + 1, columns] += total

            @pl.when(is_second)
            def _():
                small_other[row : row + 1, columns] += total

    def proj_grad(index, columns):
        return dot_tn(act[index, :, columns], m_grad[set_rows(index)])

    def fc_grad(index, columns):
        return dot_tn(n2[set_rows(index), :, columns], pre_grad[index])

    def out_grad(index, columns):
        return dot_tn(attended[index, :, columns], r_grad[set_rows(index)])

    def in_grad(index, columns):
        return dot_tn(qkv_grad[index, :, columns], n1[set_rows(index)])

    put_second_far(proj_grad_at, units, proj_grad)

    @pl.when(is_second)
    def _():
        repeat(0, bigs, lambda number: activate(0, 0, 0, big_rows(number)))

    proj_half = units // 2
    put_second_near(proj_grad_at, proj_half, proj_grad)

    def layer_out(index):
        at = rows_of(FINE, index)
        results[0, at, :] = (
            hidden[at, :] + BRANCH_SCALE * (part_sum(FINE, index) + proj_bias_ref[...])
        ).astype(BF16)

        @pl.when(is_first)
        def _():
            cross(index).start()

    @pl.when(is_first)
    def _():
        collect(FINE, layer_out)

    @pl.when(is_first)
    def _():
        cross_receive(0, count_of(FINE), scale_grad, lambda index: share(FINE, index).start())

        def own(number):
            columns = span(number, units // 2)
            grads[span(number, units // 2), :] = proj_grad(0, columns).astype(BF16)

        repeat(0, 2, own)

    pre_grad = slope

    def mlp_slope(index):
        def step(number):
            at = big_rows(number)
            values = (
                slope[index, at, :].astype(F32)
                * dot_nt(
                    m_grad[set_rows(index), at, :], weight_of(set_weights(index), proj_at, units)
                )
            ).astype(BF16)
            pre_grad[index, at, :] = values

        repeat(0, bigs, step)

    def mlp_back_part(index, shards, at):
        return dot_nt(pre_grad[index, at, :], weight_of(shards, fc_at, width))

    def sum_of_rows(row, source):
        def step(number):
            small[row : row + 1, :] += column_sum(source[0, big_rows(number), :])

        repeat(0, bigs, step)

    mlp_slope(0)

    @pl.when(is_first)
    def _():
        own_parts(2, mlp_back_part, per=tiles_per_big)
        share_some(FINE, 0, count_of(FINE))
        sent(m_grad.at[1, pl.ds(0, big)], share_core_send.at[1])

        def scale_other(number):
            at = big_rows(number)
            m_grad[1, at, :] = (BRANCH_SCALE * m_grad[1, at, :].astype(F32)).astype(BF16)

        repeat(0, bigs, scale_other)

        def other(number):
            columns = span(number, units // 2)
            grads[columns, :] = (grads[columns, :].astype(F32) + proj_grad(1, columns)).astype(
                BF16
            )
            if z_line:
                @pl.when(is_end)
                def _():
                    per = units // 2 // BLOCK
                    repeat(
                        number * per, (number + 1) * per, lambda step: grad_pair(step, grads).start()
                    )

        repeat(0, 2, other)

    first_ends[0] += units // BLOCK

    mlp_slope(1)
    pump_second_ends(1)

    @pl.when(is_first)
    def _():
        far_parts(2, mlp_back_part, per=tiles_per_big)

    @pl.when(is_second)
    def _():
        both_parts(2, mlp_back_part, per=tiles_per_big)

    pump_first(1)

    put_second_near(
        proj_grad_at + proj_half,
        units - proj_half,
        lambda index, columns: proj_grad(index, pl.ds(proj_half, units - proj_half)),
    )
    put_first(fc_grad_at, width, fc_grad)
    pump_first_ends(width // BLOCK)
    pump_first(1)

    pump_second_ends(1)

    def mlp_back(index):
        at = tile_rows(index)
        n2_grad = part_sum(2, index)
        hat, rate = normed(hidden[at, :])
        small[2:3, :] += column_sum(n2_grad * hat)
        small[3:4, :] += column_sum(n2_grad)
        held = ends[ends_grad, at, :].astype(F32) + norm_backward(
            n2_grad, hat, rate, ln2_gain_ref[...]
        )
        hidden_grad[at, :] = held
        r_grad[0, at, :] = (BRANCH_SCALE * held).astype(BF16)

        @pl.when(is_first)
        def _():
            share(2, index).start()

    def first_mid_step(step):
        mid_up(step)

        @pl.when(step >= BEHIND)
        def _():
            mid_down(step - BEHIND, (False, False))

    def second_end_step(step):
        gather_y(step)
        grad_pair(step, grads).start()

    def second_mid_step(step):
        gather_y(step)
        first_mid_step(step)

    def collect_with_pump(which, finish):
        base = first_mids[0]
        first_mids[0] += TILES * PUMP

        def beside(index):
            if z_line:
                @pl.when(is_mid)
                def _():
                    start = base + index * PUMP
                    repeat(start, start + PUMP, first_mid_step)

        collect(which, finish, beside)

    collect_with_pump(2, mlp_back)
    pump_first(1)
    pump_second_ends(1)

    def attention_backward(index):
        shards = set_weights(index)

        def project(number):
            at = big_rows(number)
            values = dot_nt(
                r_grad[set_rows(index), at, :], weight_of(shards, out_at, local_width)
            ).astype(BF16)
            for head in range(heads):
                head_rows[head, at, :] = values[:, head_columns(0, head)]

        repeat(0, bigs, project)

        for head in range(heads):
            shares = probs[index * heads + head]
            rows_grad = head_rows[head]
            qkv_grad[index, :, head_columns(2, head)] = dot_nn(shares, rows_grad).astype(BF16)
            share_grad = dot_nt(qkv[index, 2, head], rows_grad)
            wide = shares.astype(F32)
            product = wide * share_grad
            score_grad = (product - wide * jnp.sum(product, axis=0, keepdims=True)).astype(BF16)
            qkv_grad[index, :, head_columns(0, head)] = (
                dot_tn(score_grad, qkv[index, 1, head]) * scale
            ).astype(BF16)
            qkv_grad[index, :, head_columns(1, head)] = dot_nn(
                score_grad, qkv[index, 0, head]
            ).astype(BF16)
    def attention_back_part(index, shards, at):
        return dot_nn(qkv_grad[index, at, :], weight_of(shards, 0, qkv_rows))

    first_base, ends_base, mids_base = first_mids[0], second_ends[0], second_mids[0]
    first_mids[0] += 3 * PUMP
    second_ends[0] += 2 * PUMP
    second_mids[0] += 3

    def attention_turn(index):
        attention_backward(index)
        if z_line:
            @pl.when(first_mid)
            def _():
                start = first_base + 2 * PUMP * index
                repeat(start, start + PUMP, first_mid_step)

            @pl.when(second_end)
            def _():
                start = ends_base + PUMP * index
                repeat(start, start + PUMP, second_end_step)

            @pl.when(second_mid)
            def _():
                start = mids_base + 2 * index
                repeat(start, start + 2 - index, second_mid_step)

        @pl.when(jnp.logical_and(is_first, index == 0))
        def _():
            own_parts(3, attention_back_part)
            share_some(2, 0, TILES)
            put_first_inside(out_grad_at, local_width, out_grad)
            if z_line:
                @pl.when(is_mid)
                def _():
                    repeat(first_base + PUMP, first_base + 2 * PUMP, first_mid_step)

    repeat(0, 2, attention_turn)

    @pl.when(is_first)
    def _():
        far_parts(3, attention_back_part)

    @pl.when(is_second)
    def _():
        both_parts(3, attention_back_part)

    pump_first(PUMP)
    pump_second_ends(1)
    pump_second(1)

    put_first(qkv_grad_at, qkv_rows, in_grad)
    if z_line:
        @pl.when(is_first)
        def _():
            repeat(0, LENT, lambda index: lent(index).start())

    pump_first(PUMP)

    def attention_back(index):
        at = tile_rows(index)
        n1_grad = part_sum(3, index)
        hat, rate = normed(ends[ends_in, at, :].astype(F32))
        small[0:1, :] += column_sum(n1_grad * hat)
        small[1:2, :] += column_sum(n1_grad)
        results[1, at, :] = (
            hidden_grad[at, :] + norm_backward(n1_grad, hat, rate, ln1_gain_ref[...])
        ).astype(BF16)

        @pl.when(is_second)
        def _():
            cross(2 * index).start()
            cross(2 * index + 1).start()

    collect_with_pump(3, attention_back)
    pump_first(1)
    pump_second_ends(1)

    leave = remote(
        results.at[1 - s, token_rows(across_m)], rows_recv, leave_send.at[0], leave_recv.at[0], across
    )
    @pl.when(is_first)
    def _():
        leave.start()

    sum_of_rows(5, m_grad)
    sum_of_rows(4, r_grad)
    for index in range(2):

        def sums(number, index=index):
            at = big_rows(number)
            set_sum(6, 0, index, pre_grad[index, at, :])
            set_sum(7, 0, index, qkv_grad[index, at, 0:local_width])
            set_sum(7, 2 * local_width, index, qkv_grad[index, at, 2 * local_width :])

        repeat(0, bigs, sums)
    small_y_copy = remote(small_other, small_y, leave_send.at[1], leave_recv.at[1], across)
    small_other[0:6, :] = small[0:6, :]
    small_y_copy.start()

    pump_first(2)
    pump_second_ends(1)
    pump_second(2)

    put_second_far(fc_grad_at, width, fc_grad)
    pump_second_ends(2)
    pump_second(2)

    @pl.when(is_second)
    def _():
        both_parts(FINE, mlp_part, per=2)

    pump_second_ends(2)
    pump_second(PUMP)
    put_second_near(fc_grad_at, width, fc_grad)

    @pl.when(is_second)
    def _():
        collect(FINE, layer_out)

    pump_second_ends(2)
    pump_second(PUMP)
    put_second_far(out_grad_at, local_width, out_grad)
    put_second_near(out_grad_at, local_width, out_grad)
    pump_second_ends(2)
    pump_second(PUMP)
    put_second_far(qkv_grad_at, qkv_rows, in_grad)

    @pl.when(is_second)
    def _():
        leave.start()

    pump_second_ends(2)
    pump_second(PUMP)
    put_second_near(qkv_grad_at, qkv_rows, in_grad)

    small_up = remote(small, small_pair, leave_send.at[2], leave_recv.at[2], pair)
    small_across = remote(small, small_mid, leave_send.at[3], leave_recv.at[3], middle)
    small_down = remote(small_mid, small_pair, leave_send.at[2], leave_recv.at[2], pair)

    def rows_finish(wanted):
        @pl.when(wanted)
        def _():
            leave.wait_recv()
            rows_out[pl.ds(chip, 1)] = results[pl.ds(1 - s, 1), token_rows(m), :].astype(F32)
            rows_out[pl.ds(1 - chip, 1)] = rows_recv[...].astype(F32)[None]

    if z_line:
        @pl.when(is_end)
        def _():
            small_y_copy.wait_recv()
            small[...] += small_y[...]
            small_up.start()

        pump_ends(first_ends, len(first_order), first_end, False)
        pump_ends(second_ends, len(second_order), second_end, True)
        near, later = blocks * 2 // 3, blocks * 3 // 4
        pump_mids(first_mids, near, first_mid, False)
        pump_mids(second_mids, near, second_mid, True)

        @pl.when(is_mid)
        def _():
            small_y_copy.wait_recv()
            small_up.wait_recv()
            small[...] += small_y[...]
            small[...] += small_pair[...]
            small_across.start()

        pump_mids(first_mids, later, first_mid, False)
        pump_mids(second_mids, later, second_mid, True)
        rows_finish(is_first)

        @pl.when(is_mid)
        def _():
            small_across.wait_recv()
            small_mid[...] += small[...]
            small_down.start()
            small_out[...] = small_mid[...]

        pump_mids(first_mids, len(first_order), first_mid, False)
        pump_mids(second_mids, turn + LENT - 2, second_mid, True)
        rows_finish(is_second)
        pump_mids(second_mids, len(second_order), second_mid, True)

        def back(index, source):
            lent_back(index, source).wait_recv()
            grad_out(lent_from + index, source).start()

        @pl.when(is_mid)
        def _():
            last = small_from + small_count
            repeat(last - BEHIND, last, lambda step: mid_down(step, (False, True)))

        @pl.when(first_mid)
        def _():
            repeat(0, LENT, lambda index: back(index, grads_mid))

        def take(step, kind):
            grad_pair(step, grads_mid, kind[1]).wait_recv()
            deliver(step, grads_pair, kind)

        @pl.when(first_end)
        def _():
            walk(first_order, 0, len(first_order), take)
            repeat(0, LENT, lambda index: back(index, grads_pair))

        @pl.when(second_end)
        def _():
            walk(second_order, 0, len(second_order), take)

        @pl.when(is_end)
        def _():
            small_down.wait_recv()
            small_out[...] = small_pair[...]

    else:
        @pl.when(is_second)
        def _():
            repeat(0, blocks, gather_y)

        repeat(0, blocks, lambda step: grad_out(step, grads).start())
        rows_finish(s >= 0)
        small_y_copy.wait_recv()
        small_out[...] = small[...] + small_y[...]

    own_rows = pl.ds(0, weight_rows)
    pltpu.make_async_copy(grads.at[own_rows], grads_out, grad_out_sem.at[0]).wait()

    entry_across(0).wait_send()
    entry_sibling(0).wait_send()
    entry_forward(0).wait_send()
    leave.wait_send()
    small_y_copy.wait_send()
    sent(part, part_send.at[0])
    sent(n1.at[0, pl.ds(0, big)], cross_send.at[0])
    sent(n1.at[0, pl.ds(0, big)], cross_core_send.at[0])

    @pl.when(is_first)
    def _():
        entry_across(1).wait_send()
        entry_sibling(1).wait_send()
        entry_forward(1).wait_send()
        sent(grads.at[pl.ds(0, 3 * big)], share_send.at[0])
        sent(grads.at[pl.ds(0, 2 * big)], share_core_send.at[0])
        for sem in (far_core_send, far_send, far_back_send):
            sent(grads.at[pl.ds(0, 4 * big)], sem.at[0])

    @pl.when(is_second)
    def _():
        bias_copy.wait_send()
        sent(weights.at[0, pl.ds(0, y_blocks * FETCH)], weight_y_send.at[0])
        if z_line:
            sent(weights.at[0, pl.ds(0, y_blocks * FETCH)], weight_z_send.at[0])
        sent(grads.at[own_rows], grad_y_send.at[0])

    if z_line:

        def stream_sent(count):
            sent(grads.at[pl.ds(0, count)], grad_pair_send.at[0])

            @pl.when(is_mid)
            def _():
                sent(grads.at[pl.ds(0, count)], grad_mid_send.at[0])

        @pl.when(is_first)
        def _():
            stream_sent(lent_from * BLOCK)
            sent(grads.at[pl.ds(0, LENT * BLOCK)], lent_send.at[0])

        @pl.when(is_second)
        def _():
            stream_sent(small_from * BLOCK)
            sent(grads.at[pl.ds(0, LENT * BLOCK)], back_send.at[0])

        @pl.when(is_end)
        def _():
            small_up.wait_send()

        @pl.when(is_mid)
        def _():
            small_across.wait_send()
            small_down.wait_send()


def finish_kernel(local_width, rows_ref, small_ref, grads_ref, *refs):
    outs, (held_rows, held, cast, in_sem, out_sem, rows_sem, held_small) = refs[:13], refs[13:20]
    lines, line_sem = refs[20:28], refs[28]
    rows_out, qkv_out, out_out, fc_out, proj_out = outs[:5]
    small_in = pltpu.make_async_copy(small_ref, held_small, line_sem.at[8])
    line_copies = [
        pltpu.make_async_copy(line, target, line_sem.at[number])
        for number, (line, target) in enumerate(zip(lines, outs[5:]))
    ]
    rows_in = pltpu.make_async_copy(rows_ref, held_rows, rows_sem.at[0])
    rows_copy = pltpu.make_async_copy(held_rows, rows_out, rows_sem.at[1])

    def at_block(number):
        return pl.ds(pl.multiple_of(number * FINISH, FINISH), FINISH)

    def fetch(number):
        at = at_block(number)
        return pltpu.make_async_copy(grads_ref.at[at], held.at[at], in_sem.at[number])

    def repeat(start, last, action):
        def step_of(step, carry):
            action(step)
            return carry

        lax.fori_loop(start, last, step_of, 0)

    blocks = held.shape[0] // FINISH
    repeat(0, blocks, lambda number: fetch(number).start())
    small_in.start()
    rows_in.start()
    first = 0
    puts = []
    for target in (proj_out, fc_out, out_out, qkv_out):
        count = target.shape[0] // FINISH

        def put(number, first=first, target=target):
            return pltpu.make_async_copy(
                cast.at[at_block(first + number)], target.at[at_block(number)], out_sem.at[first + number]
            )

        def step(number, first=first, put=put):
            fetch(first + number).wait()
            at = at_block(first + number)
            cast[at, :] = held[at, :].astype(F32)
            put(number).start()

        repeat(0, count, step)
        puts.append((count, put))
        first += count
    rows_in.wait()
    rows_copy.start()
    small_in.wait()
    lines[0][0:1, :] = held_small[7:8, 0:local_width]
    lines[0][1:2, :] = held_small[7:8, 2 * local_width : 3 * local_width]
    for row, line in enumerate(lines[1:]):
        line[...] = held_small[row : row + 1, :]
    for copy in line_copies:
        copy.start()
    for copy in line_copies:
        copy.wait()
    for count, put in puts:
        repeat(0, count, lambda number: put(number).wait())
    rows_copy.wait()


def local(
    z_line,
    boundary_in,
    order,
    ln1_gain,
    ln1_bias,
    w_qkv,
    qkv_bias,
    w_out,
    out_bias,
    ln2_gain,
    ln2_bias,
    w_fc,
    fc_bias,
    w_proj,
    proj_bias,
):
    _, micro, rows, width = boundary_in.shape
    local_width = w_qkv.shape[-1]
    units = w_fc.shape[-1]
    length = rows * lax.axis_size("mp")
    heads = local_width // HEAD_DIM
    weight_rows = 4 * local_width + width + units
    blocks = weight_rows // BLOCK
    stream_rows = weight_rows + LENT * BLOCK
    numbers = blocks + LENT + 2 * BLOCK // SMALL
    vmem = pltpu.VMEM
    dma = pltpu.SemaphoreType.DMA
    in_vmem = pl.BlockSpec(memory_space=pltpu.VMEM)
    in_any = pl.BlockSpec(memory_space=pl.ANY)
    in_smem = pl.BlockSpec(memory_space=pltpu.SMEM)
    out_rows, small, grads = pl.pallas_call(
        functools.partial(kernel, z_line),
        out_shape=(
            jax.ShapeDtypeStruct((micro, rows, width), F32),
            jax.ShapeDtypeStruct((8, width), F32),
            jax.ShapeDtypeStruct((weight_rows, width), BF16),
        ),
        in_specs=[
            in_smem,
            in_any,
            in_vmem,
            in_vmem,
            in_any,
            in_vmem,
            in_any,
            in_vmem,
            in_vmem,
            in_vmem,
            in_any,
            in_vmem,
            in_any,
            in_vmem,
        ],
        out_specs=(in_vmem, in_vmem, in_any),
        scratch_shapes=[
            vmem((micro, rows, width), BF16),
            vmem((micro, rows, width), BF16),
            vmem((2, weight_rows, width), BF16),
            vmem((2, 8, width), F32),
            vmem((3, length, width), BF16),
            vmem((2, length, width), BF16),
            vmem((rows, width), BF16),
            vmem((2, length, width), BF16),
            vmem((2, length, width), BF16),
            vmem((2, 3, heads, length, HEAD_DIM), BF16),
            vmem((2 * heads, length, length), BF16),
            vmem((heads, length, HEAD_DIM), BF16),
            vmem((2, length, local_width), BF16),
            vmem((length, width), F32),
            vmem((length, width), F32),
            vmem((2, length, units), BF16),
            vmem((2, length, units), BF16),
            vmem((2, length, width), BF16),
            vmem((2, length, width), BF16),
            vmem((2, length, 3 * local_width), BF16),
            vmem((4, length, width), BF16),
            vmem((4, length, width), BF16),
            vmem((stream_rows, width), BF16),
            vmem((weight_rows, width), BF16),
            vmem((weight_rows, width), BF16),
            vmem((stream_rows, width), BF16),
            vmem((stream_rows, width), BF16),
            vmem((8, width), F32),
            vmem((8, width), F32),
            vmem((8, width), F32),
            vmem((8, width), F32),
            vmem((8, width), F32),
            dma((5,)),
            dma((7,)),
            dma((7,)),
            dma((1,)),
            dma((weight_rows // FETCH // (2 if z_line else 1),)),
            dma((1,)),
            dma((weight_rows // FETCH // (2 if z_line else 1),)),
            dma((1,)),
            dma((5 * TILES,)),
            dma((1,)),
            dma((5 * TILES,)),
            dma((1,)),
            dma((5 * TILES,)),
            dma((1,)),
            dma((5 * TILES,)),
            dma((1,)),
            dma((4 * TILES,)),
            dma((2,)),
            dma((TILES + 3,)),
            dma((1,)),
            dma((2 * TILES,)),
            dma((1,)),
            dma((2 * TILES,)),
            dma((4,)),
            dma((4,)),
            dma((1,)),
            dma((numbers,)),
            dma((1,)),
            dma((numbers,)),
            dma((1,)),
            dma((numbers,)),
            dma((1,)),
            dma((1,)),
            dma((LENT,)),
            dma((1,)),
            dma((LENT,)),
        ],
        compiler_params=pltpu.CompilerParams(
            collective_id=0, has_side_effects=True, vmem_limit_bytes=63 * 2**20
        ),
        name="two_layers",
    )(
        order,
        boundary_in,
        ln1_gain,
        ln1_bias,
        jnp.swapaxes(w_qkv, 2, 3).reshape(1, 3 * local_width, width),
        qkv_bias,
        w_out,
        out_bias,
        ln2_gain,
        ln2_bias,
        w_fc,
        fc_bias,
        w_proj,
        proj_bias,
    )
    if not z_line:
        small, grads = lax.psum((small, grads), "dp")
    shapes = [
        (micro, rows, width),
        (3 * local_width, width),
        (local_width, width),
        (width, units),
        (units, width),
        (2, local_width),
    ] + [(1, width)] * 6 + [(1, units)]
    (
        out_rows,
        qkv_grad,
        out_grad,
        fc_grad,
        proj_grad,
        qkv_bias_grad,
        ln1_gain_grad,
        ln1_bias_grad,
        ln2_gain_grad,
        ln2_bias_grad,
        out_bias_grad,
        proj_bias_grad,
        fc_bias_grad,
    ) = pl.pallas_call(
        functools.partial(finish_kernel, local_width),
        out_shape=[jax.ShapeDtypeStruct(shape, F32) for shape in shapes],
        in_specs=[in_any] * 3,
        out_specs=[in_any] * 13,
        scratch_shapes=[
            vmem((micro, rows, width), F32),
            vmem((weight_rows, width), BF16),
            vmem((weight_rows, width), F32),
            dma((weight_rows // FINISH,)),
            dma((weight_rows // FINISH,)),
            dma((2,)),
            vmem((8, width), F32),
        ]
        + [vmem(shape, F32) for shape in shapes[5:]]
        + [dma((9,))],
        compiler_params=pltpu.CompilerParams(vmem_limit_bytes=62 * 2**20),
        name="finish",
    )(out_rows, small, grads)
    return (
        out_rows[None],
        ln1_gain_grad,
        ln1_bias_grad,
        jnp.swapaxes(qkv_grad.reshape(1, 3, local_width, width), 2, 3),
        qkv_bias_grad[None],
        out_grad[None],
        out_bias_grad,
        ln2_gain_grad,
        ln2_bias_grad,
        fc_grad[None],
        fc_bias_grad,
        proj_grad[None],
        proj_bias_grad,
    )


def solution(mesh):
    return jax.shard_map(
        functools.partial(local, mesh.shape["dp"] == 4),
        mesh=mesh,
        in_specs=(
            P("section", "dp", "mp", None),
            P("dp", None),
            P("section", None),
            P("section", None),
            P("section", None, None, "mp"),
            P("section", None, "mp"),
            P("section", "mp", None),
            P("section", None),
            P("section", None),
            P("section", None),
            P("section", None, "mp"),
            P("section", "mp"),
            P("section", "mp", None),
            P("section", None),
        ),
        out_specs=(
            P("section", "dp", "mp", None),
            P("section", None),
            P("section", None),
            P("section", None, None, "mp"),
            P("section", None, "mp"),
            P("section", "mp", None),
            P("section", None),
            P("section", None),
            P("section", None),
            P("section", None, "mp"),
            P("section", "mp"),
            P("section", "mp", None),
            P("section", None),
        ),
        check_vma=False,
    )
```

```python
import functools

import jax
import jax.numpy as jnp
from jax import lax
from jax.experimental import pallas as pl
from jax.experimental.pallas import tpu as pltpu
from jax.sharding import PartitionSpec as P

HEAD_DIM = 64
BRANCH_SCALE = 0.14433756729740643
NORM_EPS = 1e-05
GELU_RATE = 0.7978845608028654
GELU_CUBE = 0.044715
NEGATIVE = -1e30
BLOCK = 48
PUMP = 2
FINISH = 192
FETCH = 96
TILES = 4
FINE = 1
SMALL = 16
LENT = 10
BEHIND = 4
MESH = pl.DeviceIdType.MESH
BF16 = jnp.bfloat16
F32 = jnp.float32


def dot_nn(a, b):
    return lax.dot_general(a, b, (((1,), (0,)), ((), ())), preferred_element_type=F32)


def dot_nt(a, b):
    return lax.dot_general(a, b, (((1,), (1,)), ((), ())), preferred_element_type=F32)


def dot_tn(a, b):
    return lax.dot_general(a, b, (((0,), (0,)), ((), ())), preferred_element_type=F32)


def normed(values):
    center = values - jnp.mean(values, axis=-1, keepdims=True)
    rate = lax.rsqrt(jnp.mean(center * center, axis=-1, keepdims=True) + NORM_EPS)
    return center * rate, rate


def norm_backward(grad, hat, rate, gain):
    scaled = grad * gain
    return rate * (
        scaled
        - jnp.mean(scaled, axis=-1, keepdims=True)
        - hat * jnp.mean(scaled * hat, axis=-1, keepdims=True)
    )


def column_sum(values):
    return jnp.sum(values.astype(F32), axis=0, keepdims=True)


def remote(src, dst, send_sem, recv_sem, device):
    return pltpu.make_async_remote_copy(
        src_ref=src,
        dst_ref=dst,
        send_sem=send_sem,
        recv_sem=recv_sem,
        device_id=device,
        device_id_type=MESH,
    )


def kernel(
    z_line,
    order_ref,
    boundary_ref,
    ln1_gain_hbm,
    ln1_bias_hbm,
    w_qkv_ref,
    qkv_bias_hbm,
    w_out_ref,
    out_bias_hbm,
    ln2_gain_hbm,
    ln2_bias_hbm,
    w_fc_ref,
    fc_bias_hbm,
    w_proj_ref,
    proj_bias_hbm,
    rows_out,
    small_out,
    grads_out,
    ln1_gain_ref,
    ln1_bias_ref,
    qkv_bias_ref,
    out_bias_ref,
    ln2_gain_ref,
    ln2_bias_ref,
    fc_bias_ref,
    proj_bias_ref,
    raw,
    slots,
    weights,
    biases,
    ends,
    results,
    rows_recv,
    rows_held,
    n1,
    n2,
    qkv,
    probs,
    head_rows,
    attended,
    hidden,
    hidden_grad,
    act,
    slope,
    m_grad,
    r_grad,
    qkv_grad,
    part,
    part_recv,
    grads,
    grads_other,
    grads_y,
    grads_pair,
    grads_mid,
    small,
    small_other,
    small_y,
    small_pair,
    small_mid,
    local_sem,
    vector_sem,
    entry_send,
    entry_recv,
    weight_y_send,
    weight_recv,
    weight_z_send,
    part_send,
    part_recv_sem,
    far_core_send,
    far_send,
    far_back_send,
    share_send,
    share_core_send,
    cross_send,
    cross_recv,
    cross_core_send,
    cross_core_recv,
    leave_send,
    leave_recv,
    grad_y_send,
    grad_y_recv,
    grad_pair_send,
    grad_pair_recv,
    grad_mid_send,
    grad_mid_recv,
    grad_out_sem,
    lent_send,
    lent_recv,
    back_send,
    back_recv,
):
    s, d, m = lax.axis_index("section"), lax.axis_index("dp"), lax.axis_index("mp")
    core, chip = lax.rem(m, 2), lax.div(m, 2)
    half = lax.rem(d, 2)
    across_m = 2 * (1 - chip) + core
    sibling = (s, d, 2 * chip + 1 - core)
    across = (s, d, across_m)
    other_section = (1 - s, d, m)
    pair = (s, d + 1 - 2 * half, m)
    middle = (s, 3 - d, m)
    is_first, is_second = s == 0, s == 1
    is_mid = lax.div(d + 1, 2) == 1
    is_end = lax.div(d + 1, 2) != 1

    rows = boundary_ref.shape[2]
    length, width = n1.shape[1:]
    tile = length // TILES
    piece = tile // 2
    big = length // 2
    local_width = attended.shape[2]
    units = act.shape[2]
    heads = local_width // HEAD_DIM
    tiles_per_big, bigs = big // tile, length // big
    scale = HEAD_DIM ** (-0.5)
    qkv_rows = 3 * local_width
    out_at, fc_at, proj_at = qkv_rows, qkv_rows + local_width, qkv_rows + local_width + width
    weight_rows = weights.shape[1]
    blocks = weight_rows // BLOCK
    ends_in, ends_grad = 2 * s, 2 * (1 - s)

    def set_rows(index):
        return index * (1 - s)

    def set_weights(index):
        return index * s

    def span(index, count):
        start = index * count
        return pl.ds(start if isinstance(start, int) else pl.multiple_of(start, count), count)

    def tile_rows(index):
        return span(index, tile)

    def big_rows(index):
        return span(index, big)

    def tile_of(which):
        return tile // 2 if which == FINE else tile

    def count_of(which):
        return length // tile_of(which)

    def number_of(which, index):
        return which * TILES + (TILES if which > FINE else 0) + index

    def rows_of(which, index):
        return span(index, tile_of(which))

    def piece_rows(which, index, core_of, base=0):
        size = tile_of(which) // 2
        return pl.ds(pl.multiple_of(base + (2 * index + core_of) * size, size), size)

    partners = [sibling, across, other_section]
    if z_line:
        partners += [pair, middle]
    barrier = pltpu.get_barrier_semaphore()
    for device in partners:
        pl.semaphore_signal(barrier, inc=1, device_id=device, device_id_type=MESH)

    loads = [
        pltpu.make_async_copy(boundary_ref.at[0], raw, local_sem.at[0]),
        pltpu.make_async_copy(
            w_qkv_ref.at[0], weights.at[0, pl.ds(0, qkv_rows)], local_sem.at[1]
        ),
        pltpu.make_async_copy(
            w_out_ref.at[0], weights.at[0, pl.ds(out_at, local_width)], local_sem.at[2]
        ),
        pltpu.make_async_copy(w_fc_ref.at[0], weights.at[0, pl.ds(fc_at, width)], local_sem.at[3]),
        pltpu.make_async_copy(
            w_proj_ref.at[0], weights.at[0, pl.ds(proj_at, units)], local_sem.at[4]
        ),
    ]
    vector_loads = [
        pltpu.make_async_copy(source, target, vector_sem.at[number])
        for number, (source, target) in enumerate(
            (
                (ln1_gain_hbm, ln1_gain_ref),
                (ln1_bias_hbm, ln1_bias_ref),
                (qkv_bias_hbm, qkv_bias_ref),
                (out_bias_hbm, out_bias_ref),
                (ln2_gain_hbm, ln2_gain_ref),
                (ln2_bias_hbm, ln2_bias_ref),
                (fc_bias_hbm, fc_bias_ref),
                (proj_bias_hbm, proj_bias_ref),
            )
        )
    ]
    for load in loads[:1] + vector_loads + loads[1:]:
        load.start()

    biases[0] = jnp.zeros_like(biases[0])
    small[...] = jnp.zeros_like(small)
    small_other[...] = jnp.zeros_like(small_other)

    loads[0].wait()
    for slot in range(2):
        picked = jnp.where(is_first, order_ref[0, slot], slot).astype(F32)
        slots[slot] = (
            raw[0].astype(F32) * (1.0 - picked) + raw[1].astype(F32) * picked
        ).astype(BF16)

    pl.semaphore_wait(barrier, len(partners))

    def token_rows(index):
        return pl.ds(pl.multiple_of(index * rows, rows), rows)

    def entry_across(which):
        slot = (1 - chip) * (1 - which) + chip * which
        return remote(
            slots.at[slot],
            ends.at[which, token_rows(m)],
            entry_send.at[which],
            entry_recv.at[which],
            across,
        )

    def entry_sibling(which):
        slot = chip * (1 - which) + (1 - chip) * which
        return remote(
            slots.at[slot],
            ends.at[which, token_rows(m)],
            entry_send.at[2 + which],
            entry_recv.at[2 + which],
            sibling,
        )

    def entry_forward(which):
        at = token_rows(across_m)
        return remote(
            ends.at[which, at],
            ends.at[which, at],
            entry_send.at[4 + which],
            entry_recv.at[4 + which],
            sibling,
        )

    bias_copy = remote(biases.at[0], biases.at[1], entry_send.at[6], entry_recv.at[6], across)

    def entry_start(which):
        entry_across(which).start()
        entry_sibling(which).start()
        slot = chip if which == 0 else 1 - chip
        ends[which, token_rows(m), :] = slots[slot]

    def entry_pass(which):
        entry_across(which).wait_recv()
        entry_forward(which).start()

    def entry_finish(which):
        entry_pass(which)
        entry_sibling(which).wait_recv()
        entry_forward(which).wait_recv()

    @pl.when(is_first)
    def _():
        entry_start(1)
        entry_start(0)

    y_blocks = weight_rows // FETCH // (2 if z_line else 1)

    def weight_block(index):
        return pl.ds(pl.multiple_of(index * BLOCK, BLOCK), BLOCK)

    def near_block(step):
        return span(2 * step + half if z_line else step, FETCH)

    def weight_y(step):
        return remote(
            weights.at[0, near_block(step)],
            weights.at[1, near_block(step)],
            weight_y_send.at[0],
            weight_recv.at[step],
            across,
        )

    def weight_z(step):
        return remote(
            weights.at[1, near_block(step)],
            weights.at[1, near_block(step)],
            weight_z_send.at[0],
            weight_recv.at[y_blocks + step],
            pair,
        )

    def repeat(first, last, action):
        def step_of(step, carry):
            action(step)
            return carry

        lax.fori_loop(first, last, step_of, 0)

    late_step = proj_at * y_blocks // weight_rows
    y_done = [0]

    def weight_need(row):
        steps = row * y_blocks // weight_rows
        if z_line and steps > y_done[0]:
            first, y_done[0] = y_done[0], steps

            @pl.when(is_second)
            def _():
                repeat(first, steps, lambda step: weight_z(step).wait_recv())

    def weight_pass(step):
        weight_y(step).wait_recv()
        if z_line:
            weight_z(step).start()

    for load in vector_loads + loads[1:]:
        load.wait()
    biases[0, 0:1, :] = fc_bias_ref[...]
    biases[0, 1:2, 0:local_width] = qkv_bias_ref[0, 0:1, :]
    biases[0, 2:3, 0:local_width] = qkv_bias_ref[0, 1:2, :]

    def sent(source, sem):
        remote(source, source, sem, sem, sibling).wait_send()

    def arrived(target, sem):
        remote(target, target, sem, sem, sibling).wait_recv()

    def cross(index):
        at = piece_rows(FINE, index, core)
        return remote(
            results.at[s, at],
            ends.at[2, at],
            cross_send.at[0],
            cross_recv.at[index],
            other_section,
        )

    def cross_core(index):
        at = piece_rows(FINE, index, core)
        return remote(
            ends.at[2, at],
            ends.at[2, at],
            cross_core_send.at[0],
            cross_core_recv.at[index],
            sibling,
        )

    shared = (n2, m_grad, r_grad)

    def share(which, index):
        at = piece_rows(which, index, core)
        source = ends.at[2, at] if which == FINE else shared[which].at[0, at]
        return remote(
            source,
            shared[which].at[1, at],
            share_send.at[0],
            weight_recv.at[number_of(which, index)],
            across,
        )

    def share_core(which, index):
        at = piece_rows(which, index, core)
        return remote(
            shared[which].at[1, at],
            shared[which].at[1, at],
            share_core_send.at[1 if which == FINE else 0],
            weight_recv.at[4 * TILES + (index if which == 0 else TILES + which)],
            sibling,
        )

    def share_some(which, start, count):
        def forward(index):
            share(which, start + index).wait_recv()
            share_core(which, start + index).start()

        repeat(0, count, forward)
        if which == 0:
            repeat(0, count, lambda index: share_core(which, start + index).wait_recv())
        else:
            arrived(shared[which].at[1, pl.ds(0, big)], weight_recv.at[5 * TILES + which])

    def part_copy(which, index):
        at = rows_of(which, index)
        return remote(
            part.at[which, at],
            part_recv.at[which, at],
            part_send.at[0],
            part_recv_sem.at[number_of(which, index)],
            sibling,
        )

    def spare_rows(which, index, core_of):
        return piece_rows(which, index, core_of, which * length)

    def far_core(which, index):
        return remote(
            grads_y.at[spare_rows(which, index, 1 - core)],
            grads_other.at[spare_rows(which, index, 1 - core)],
            far_core_send.at[0],
            grad_y_recv.at[number_of(which, index)],
            sibling,
        )

    def far(which, index):
        return remote(
            grads_y.at[spare_rows(which, index, core)],
            weights.at[1, spare_rows(which, index, core)],
            far_send.at[0],
            grad_y_recv.at[5 * TILES + number_of(which, index)],
            across,
        )

    def far_back(which, index):
        at = spare_rows(which, index, core)
        return remote(
            weights.at[1, at],
            weights.at[1, at],
            far_back_send.at[0],
            grad_y_recv.at[10 * TILES + number_of(which, index)],
            sibling,
        )

    def far_pass(which, index):
        far_core(which, index).wait_recv()
        at = spare_rows(which, index, core)
        grads_y[at, :] = (grads_y[at, :].astype(F32) + grads_other[at, :].astype(F32)).astype(BF16)
        far(which, index).start()

    def part_sum(which, index):
        at = rows_of(which, index)
        near = part[which, at, :].astype(F32) + part_recv[which, at, :].astype(F32)
        size = tile_of(which)
        other = weights[
            1, pl.ds(pl.multiple_of(which * length + index * size, size), size), :
        ].astype(F32)
        return near + jnp.where(is_first, other, 0.0)

    def far_parts(which, value_of, per=1, before=None):
        def step(number):
            if before is not None:
                before(number)
            size = per * tile_of(which)
            grads_y[pl.ds(pl.multiple_of(which * length + number * size, size), size), :] = (
                value_of(1, 0, span(number, size)).astype(BF16)
            )
            for index in range(per):
                far_core(which, number * per + index).start()

            @pl.when(number > 0)
            def _():
                for index in range(per):
                    far_pass(which, (number - 1) * per + index)

        repeat(0, count_of(which) // per, step)
        for index in range(per):
            far_pass(which, count_of(which) - per + index)

    def own_parts(which, value_of, per=1):
        def step(number):
            at = span(number, per * tile_of(which))
            part[which, at, :] = value_of(0, 0, at).astype(BF16)
            for index in range(per):
                part_copy(which, number * per + index).start()

        repeat(0, count_of(which) // per, step)

    def both_parts(which, value_of, per=1):
        def step(number):
            at = span(number, per * tile_of(which))
            part[which, at, :] = (value_of(0, 0, at) + value_of(1, 1, at)).astype(BF16)
            for index in range(per):
                part_copy(which, number * per + index).start()

        repeat(0, count_of(which) // per, step)

    def collect(which, finish, beside=None, start=0, last=None):
        last = count_of(which) if last is None else last

        def far_next(index):
            far(which, index).wait_recv()
            far_back(which, index).start()

        @pl.when(is_first)
        def _():
            far_next(start)

        def step(index):
            @pl.when(is_first)
            def _():
                @pl.when(index + 1 < last)
                def _():
                    far_next(index + 1)

                if beside is not None:
                    beside(index)
                far_back(which, index).wait_recv()

            part_copy(which, index).wait_recv()
            finish(index)

        repeat(start, last, step)

    def weight_of(shards, first, count):
        return weights[shards, first : first + count, :]

    def scale_grad(index):
        at = rows_of(FINE, index)
        m_grad[0, at, :] = (BRANCH_SCALE * ends[ends_grad, at, :].astype(F32)).astype(BF16)

    @pl.when(is_second)
    def _():
        bias_copy.start()
        repeat(0, late_step, lambda step: weight_y(step).start())
        entry_start(0)
        repeat(late_step, y_blocks, lambda step: weight_y(step).start())
        repeat(0, late_step, weight_pass)
        bias_copy.wait_recv()
        entry_finish(0)
        repeat(0, count_of(FINE), scale_grad)
        repeat(late_step, y_blocks - bigs, weight_pass)

    def norm_big(which, source, number):
        def step(index):
            at = span(number * (big // tile) + index, tile)
            hat, _ = normed(ends[source, at, :].astype(F32))
            n1[which, at, :] = (hat * ln1_gain_ref[...] + ln1_bias_ref[...]).astype(BF16)

        repeat(0, big // tile, step)

    def cross_receive(start, last, action, on=None):
        def pass_on(index):
            cross(index).wait_recv()
            cross_core(index).start()
            if on is not None:
                on(index)

        pass_on(start)

        def step(index):
            @pl.when(index + 1 < last)
            def _():
                pass_on(index + 1)

            cross_core(index).wait_recv()
            action(index)

        repeat(start, last, step)

    causal = lax.broadcasted_iota(jnp.int32, (length, length), 1) >= lax.broadcasted_iota(
        jnp.int32, (length, length), 0
    )

    def bias_of(shards, row, count):
        return biases[shards, row : row + 1, 0:count]

    def head_columns(kind, head):
        first = kind * local_width + head * HEAD_DIM
        return slice(first, first + HEAD_DIM)

    def project(index, number):
        source, shards = set_rows(index), set_weights(index)
        at = big_rows(number)
        for kind in range(3):
            values = dot_nt(n1[source, at, :], weight_of(shards, kind * local_width, local_width))
            if kind == 0:
                values = values + bias_of(shards, 1, local_width)
            if kind == 2:
                values = values + bias_of(shards, 2, local_width)
            values = values.astype(BF16)
            if kind == 0:
                values = (values.astype(F32) * scale).astype(BF16)
            for head in range(heads):
                qkv[index, kind, head, at, :] = values[:, head_columns(0, head)]

    def attention_forward(index):
        for head in range(heads):
            scores = dot_nt(qkv[index, 1, head], qkv[index, 0, head])
            scores = jnp.where(causal, scores, NEGATIVE)
            raised = jnp.exp(scores - jnp.max(scores, axis=0, keepdims=True))
            shares = raised * (1.0 / jnp.sum(raised, axis=0, keepdims=True))
            shares = shares.astype(BF16)
            probs[index * heads + head] = shares
            attended[index, :, head_columns(0, head)] = dot_tn(
                shares, qkv[index, 2, head]
            ).astype(BF16)

    weight_need(out_at)

    @pl.when(is_second)
    def _():
        def step(number):
            def pass_on(index):
                cross(index).wait_recv()
                cross_core(index).start()

            per = count_of(FINE) // bigs
            repeat(number * per, (number + 1) * per, pass_on)
            repeat(
                number * per, (number + 1) * per, lambda index: cross_core(index).wait_recv()
            )
            norm_big(0, 2, number)
            repeat(0, 2, lambda index: project(index, number))
            weight_pass(y_blocks - bigs + number)

        repeat(0, bigs, step)

    @pl.when(is_first)
    def _():
        def step(index):
            entry_sibling(index).wait_recv()
            norm_big(index, index, chip)
            project(index, chip)

        repeat(0, 2, step)
        entry_pass(1)
        entry_forward(1).wait_recv()
        norm_big(1, 1, 1 - chip)
        project(1, 1 - chip)

    attention_forward(1)

    def attention_part(index, shards, at):
        return dot_nn(attended[index, at, :], weight_of(shards, out_at, local_width))

    @pl.when(is_first)
    def _():
        far_parts(0, attention_part)
        entry_pass(0)
        entry_forward(0).wait_recv()
        norm_big(0, 0, 1 - chip)
        project(0, 1 - chip)

    attention_forward(0)

    weight_need(fc_at)

    @pl.when(is_first)
    def _():
        own_parts(0, attention_part)

    @pl.when(is_second)
    def _():
        both_parts(0, attention_part)

    def attention_out(index):
        at = tile_rows(index)
        held = ends[ends_in, at, :].astype(F32) + BRANCH_SCALE * (
            part_sum(0, index) + out_bias_ref[...]
        )
        hidden[at, :] = held
        hat, _ = normed(held)
        n2[0, at, :] = (hat * ln2_gain_ref[...] + ln2_bias_ref[...]).astype(BF16)

        @pl.when(is_first)
        def _():
            share(0, index).start()

    def activate(index, source, shards, at):
        u = dot_nn(n2[source, at, :], weight_of(shards, fc_at, width)) + bias_of(shards, 0, units)
        square = u * u
        bent = jnp.tanh(GELU_RATE * (u + GELU_CUBE * u * square))
        act[index, at, :] = (0.5 * u * (1.0 + bent)).astype(BF16)
        slope[index, at, :] = (
            0.5 * (1.0 + bent)
            + (0.5 * GELU_RATE) * u * (1.0 - bent * bent) * (1.0 + (3.0 * GELU_CUBE) * square)
        ).astype(BF16)

    weight_need(proj_at)

    def first_half(number):
        collect(
            0, attention_out, start=number * tiles_per_big, last=(number + 1) * tiles_per_big
        )
        activate(set_weights(1), 0, set_weights(1), big_rows(number))

    repeat(0, bigs, first_half)

    def mlp_part(index, shards, at):
        return dot_nn(act[index, at, :], weight_of(shards, proj_at, units))

    def other_activate(number):
        share_some(0, number, 1)
        activate(1, 1, 0, span(number, tile))

    @pl.when(is_first)
    def _():
        own_parts(FINE, mlp_part, per=2)
        far_parts(FINE, mlp_part, per=2, before=other_activate)

    weight_need(weight_rows)

    proj_grad_at, fc_grad_at = 0, units
    out_grad_at = fc_grad_at + width
    qkv_grad_at = out_grad_at + local_width

    lent_from = blocks - LENT
    small_from, small_count = blocks + LENT, 2 * BLOCK // SMALL
    small_row = (lent_from - 2) * BLOCK

    def block_rows(step, is_small=False):
        if is_small:
            start = small_row + (step - small_from) * SMALL
            return pl.ds(start if isinstance(start, int) else pl.multiple_of(start, SMALL), SMALL)
        return weight_block(step)

    def grad_y(step, is_small=False):
        return remote(
            grads_other.at[block_rows(step, is_small)],
            grads_y.at[block_rows(step, is_small)],
            grad_y_send.at[0],
            grad_y_recv.at[step - LENT if is_small else step],
            across,
        )

    def grad_pair(step, source, is_small=False):
        return remote(
            source.at[block_rows(step, is_small)],
            grads_pair.at[block_rows(step, is_small)],
            grad_pair_send.at[0],
            grad_pair_recv.at[step],
            pair,
        )

    def grad_mid(step, is_small=False):
        return remote(
            grads.at[block_rows(step, is_small)],
            grads_mid.at[block_rows(step, is_small)],
            grad_mid_send.at[0],
            grad_mid_recv.at[step],
            middle,
        )

    def grad_out(step, source, is_small=False):
        at = block_rows(step, is_small)
        return pltpu.make_async_copy(source.at[at], grads_out.at[at], grad_out_sem.at[0])

    def add_into(target, source, step, is_small):
        at = block_rows(step, is_small)
        target[at, :] = (target[at, :].astype(F32) + source[at, :].astype(F32)).astype(BF16)

    def gather_y(step, is_small=False):
        grad_y(step, is_small).wait_recv()
        add_into(grads, grads_y, step, is_small)

    def mid_up(step, is_small=False):
        grad_pair(step, grads, is_small).wait_recv()
        add_into(grads, grads_pair, step, is_small)
        grad_mid(step, is_small).start()

    def kind_of(step):
        return blocks <= step < small_from, step >= small_from

    def mid_down(step, kind):
        grad_mid(step, kind[1]).wait_recv()
        add_into(grads_mid, grads, step, kind[1])
        grad_pair(step, grads_mid, kind[1]).start()
        deliver(step, grads_mid, kind)

    def deliver(step, source, kind):
        if kind[0]:
            lent_back(step - blocks, source).start()
        else:
            grad_out(step, source, kind[1]).start()

    def lent(index):
        return remote(
            grads.at[weight_block(lent_from + index)],
            grads.at[weight_block(blocks + index)],
            lent_send.at[0],
            lent_recv.at[index],
            other_section,
        )

    def lent_back(index, source):
        return remote(
            source.at[weight_block(blocks + index)],
            source.at[weight_block(lent_from + index)],
            back_send.at[0],
            back_recv.at[index],
            other_section,
        )

    small_blocks = range(small_from, small_from + small_count)
    turn = blocks - 4
    first_order = [*range(lent_from - 2), *small_blocks]
    second_order = [
        *range(lent_from - 2),
        *range(lent_from, turn),
        *range(blocks, small_from),
        *range(turn, blocks),
        *small_blocks,
    ]

    def runs(order, start, last, behind=0):
        cuts = [start]
        for place in range(start + 1, last):
            for back in (place, place - behind):
                if back > 0 and order[back] != order[back - 1] + 1 and cuts[-1] != place:
                    cuts.append(place)
        cuts.append(last)
        return [
            (a, b, order[a] - a, order[max(a - behind, 0)] - max(a - behind, 0))
            for a, b in zip(cuts, cuts[1:])
            if b > a
        ]

    first_ends, first_mids, second_ends, second_mids = [0], [0], [0], [0]
    first_end, second_end = jnp.logical_and(is_first, is_end), jnp.logical_and(is_second, is_end)
    first_mid, second_mid = jnp.logical_and(is_first, is_mid), jnp.logical_and(is_second, is_mid)

    def gather(step, kind):
        if kind[0]:
            lent(step - blocks).wait_recv()
        else:
            gather_y(step, kind[1])

    def walk(order, start, last, action):
        for a, b, offset, _ in runs(order, start, last):
            kind = kind_of(a + offset)
            repeat(a + offset, b + offset, functools.partial(action, kind=kind))

    def pump_ends(done, last, wanted, second):
        start, done[0] = done[0], last
        if z_line:
            def up(step, kind):
                if second:
                    gather(step, kind)
                grad_pair(step, grads, kind[1]).start()

            @pl.when(wanted)
            def _():
                walk(second_order if second else first_order, start, last, up)

    def pump_mids(done, last, wanted, second):
        start, done[0] = done[0], last
        if z_line:
            @pl.when(wanted)
            def _():
                order = second_order if second else first_order
                for a, b, offset, old in runs(order, start, last, BEHIND):

                    def step(place, a=a, offset=offset, old=old):
                        if second:
                            gather(place + offset, kind_of(a + offset))
                        mid_up(place + offset, kind_of(a + offset)[1])

                        @pl.when(place >= BEHIND)
                        def _():
                            mid_down(place - BEHIND + old, kind_of(max(a - BEHIND, 0) + old))

                    repeat(a, b, step)

    def pump_first_ends(count):
        pump_ends(first_ends, first_ends[0] + count, first_end, False)

    def pump_first(count):
        pump_mids(first_mids, first_mids[0] + count, first_mid, False)

    def pump_second_ends(count):
        pump_ends(second_ends, second_ends[0] + count, second_end, True)

    def pump_second(count):
        pump_mids(second_mids, second_mids[0] + count, second_mid, True)

    def cut_columns(count):
        return (2, count // 2) if count % 768 == 0 else (1, count)

    def put_first_inside(first, count, value_of):
        steps, columns = cut_columns(count)

        def step(number):
            at = span(number, columns)
            grads[pl.ds(first + number * columns, columns), :] = (
                value_of(0, at) + value_of(1, at)
            ).astype(BF16)

        repeat(0, steps, step)

    def put_first(first, count, value_of):
        @pl.when(is_first)
        def _():
            put_first_inside(first, count, value_of)

    def put_second(target, index, first, count, value_of, after=None):
        steps, columns = cut_columns(count)

        def step(number):
            start = first + number * columns
            target[pl.ds(start, columns), :] = value_of(index, span(number, columns)).astype(BF16)
            if after is not None:
                after(first // BLOCK + number * (columns // BLOCK), columns // BLOCK)

        @pl.when(is_second)
        def _():
            repeat(0, steps, step)

    def put_second_far(first, count, value_of):
        def leave_blocks(start, number):
            if z_line and first == qkv_grad_at:
                repeat(first // BLOCK, lent_from - 2, lambda step: grad_y(step).start())
                repeat(lent_from, blocks, lambda step: grad_y(step).start())
                repeat(
                    small_from, small_from + small_count, lambda step: grad_y(step, True).start()
                )
            else:
                repeat(start, start + number, lambda step: grad_y(step).start())

        put_second(grads_other, 1, first, count, value_of, leave_blocks)

    def put_second_near(first, count, value_of):
        put_second(grads, 0, first, count, value_of)

    def set_sum(row, column, index, values):
        total = column_sum(values)
        columns = slice(column, column + total.shape[1])
        if index == 0:
            small[row : row + 1, columns] += total
        else:
            @pl.when(is_first)
            def _():
                small[row : row + 1, columns] += total

            @pl.when(is_second)
            def _():
                small_other[row : row + 1, columns] += total

    def proj_grad(index, columns):
        return dot_tn(act[index, :, columns], m_grad[set_rows(index)])

    def fc_grad(index, columns):
        return dot_tn(n2[set_rows(index), :, columns], pre_grad[index])

    def out_grad(index, columns):
        return dot_tn(attended[index, :, columns], r_grad[set_rows(index)])

    def in_grad(index, columns):
        return dot_tn(qkv_grad[index, :, columns], n1[set_rows(index)])

    put_second_far(proj_grad_at, units, proj_grad)

    @pl.when(is_second)
    def _():
        repeat(0, bigs, lambda number: activate(0, 0, 0, big_rows(number)))

    proj_half = units // 2
    put_second_near(proj_grad_at, proj_half, proj_grad)

    def layer_out(index):
        at = rows_of(FINE, index)
        results[0, at, :] = (
            hidden[at, :] + BRANCH_SCALE * (part_sum(FINE, index) + proj_bias_ref[...])
        ).astype(BF16)

        @pl.when(is_first)
        def _():
            cross(index).start()

    @pl.when(is_first)
    def _():
        collect(FINE, layer_out)

    @pl.when(is_first)
    def _():
        cross_receive(0, count_of(FINE), scale_grad, lambda index: share(FINE, index).start())

        def own(number):
            columns = span(number, units // 2)
            grads[span(number, units // 2), :] = proj_grad(0, columns).astype(BF16)

        repeat(0, 2, own)

    pre_grad = slope

    def mlp_slope(index):
        def step(number):
            at = big_rows(number)
            values = (
                slope[index, at, :].astype(F32)
                * dot_nt(
                    m_grad[set_rows(index), at, :], weight_of(set_weights(index), proj_at, units)
                )
            ).astype(BF16)
            pre_grad[index, at, :] = values

        repeat(0, bigs, step)

    def mlp_back_part(index, shards, at):
        return dot_nt(pre_grad[index, at, :], weight_of(shards, fc_at, width))

    def sum_of_rows(row, source):
        def step(number):
            small[row : row + 1, :] += column_sum(source[0, big_rows(number), :])

        repeat(0, bigs, step)

    mlp_slope(0)

    @pl.when(is_first)
    def _():
        own_parts(2, mlp_back_part, per=tiles_per_big)
        share_some(FINE, 0, count_of(FINE))
        sent(m_grad.at[1, pl.ds(0, big)], share_core_send.at[1])

        def scale_other(number):
            at = big_rows(number)
            m_grad[1, at, :] = (BRANCH_SCALE * m_grad[1, at, :].astype(F32)).astype(BF16)

        repeat(0, bigs, scale_other)

        def other(number):
            columns = span(number, units // 2)
            grads[columns, :] = (grads[columns, :].astype(F32) + proj_grad(1, columns)).astype(
                BF16
            )
            if z_line:
                @pl.when(is_end)
                def _():
                    per = units // 2 // BLOCK
                    repeat(
                        number * per, (number + 1) * per, lambda step: grad_pair(step, grads).start()
                    )

        repeat(0, 2, other)

    first_ends[0] += units // BLOCK

    mlp_slope(1)
    pump_second_ends(1)

    @pl.when(is_first)
    def _():
        far_parts(2, mlp_back_part, per=tiles_per_big)

    @pl.when(is_second)
    def _():
        both_parts(2, mlp_back_part, per=tiles_per_big)

    pump_first(1)

    put_second_near(
        proj_grad_at + proj_half,
        units - proj_half,
        lambda index, columns: proj_grad(index, pl.ds(proj_half, units - proj_half)),
    )
    put_first(fc_grad_at, width, fc_grad)
    pump_first_ends(width // BLOCK)
    pump_first(1)

    pump_second_ends(1)

    def mlp_back(index):
        at = tile_rows(index)
        n2_grad = part_sum(2, index)
        hat, rate = normed(hidden[at, :])
        small[2:3, :] += column_sum(n2_grad * hat)
        small[3:4, :] += column_sum(n2_grad)
        held = ends[ends_grad, at, :].astype(F32) + norm_backward(
            n2_grad, hat, rate, ln2_gain_ref[...]
        )
        hidden_grad[at, :] = held
        r_grad[0, at, :] = (BRANCH_SCALE * held).astype(BF16)

        @pl.when(is_first)
        def _():
            share(2, index).start()

    def first_mid_step(step):
        mid_up(step)

        @pl.when(step >= BEHIND)
        def _():
            mid_down(step - BEHIND, (False, False))

    def second_end_step(step):
        gather_y(step)
        grad_pair(step, grads).start()

    def second_mid_step(step):
        gather_y(step)
        first_mid_step(step)

    def collect_with_pump(which, finish):
        base = first_mids[0]
        first_mids[0] += TILES * PUMP

        def beside(index):
            if z_line:
                @pl.when(is_mid)
                def _():
                    start = base + index * PUMP
                    repeat(start, start + PUMP, first_mid_step)

        collect(which, finish, beside)

    collect_with_pump(2, mlp_back)
    pump_first(1)
    pump_second_ends(1)

    def attention_backward(index):
        shards = set_weights(index)

        def project(number):
            at = big_rows(number)
            values = dot_nt(
                r_grad[set_rows(index), at, :], weight_of(shards, out_at, local_width)
            ).astype(BF16)
            for head in range(heads):
                head_rows[head, at, :] = values[:, head_columns(0, head)]

        repeat(0, bigs, project)

        for head in range(heads):
            shares = probs[index * heads + head]
            rows_grad = head_rows[head]
            qkv_grad[index, :, head_columns(2, head)] = dot_nn(shares, rows_grad).astype(BF16)
            share_grad = dot_nt(qkv[index, 2, head], rows_grad)
            wide = shares.astype(F32)
            product = wide * share_grad
            score_grad = (product - wide * jnp.sum(product, axis=0, keepdims=True)).astype(BF16)
            qkv_grad[index, :, head_columns(0, head)] = (
                dot_tn(score_grad, qkv[index, 1, head]) * scale
            ).astype(BF16)
            qkv_grad[index, :, head_columns(1, head)] = dot_nn(
                score_grad, qkv[index, 0, head]
            ).astype(BF16)
    def attention_back_part(index, shards, at):
        return dot_nn(qkv_grad[index, at, :], weight_of(shards, 0, qkv_rows))

    first_base, ends_base, mids_base = first_mids[0], second_ends[0], second_mids[0]
    first_mids[0] += 3 * PUMP
    second_ends[0] += 2 * PUMP
    second_mids[0] += 3

    def attention_turn(index):
        attention_backward(index)
        if z_line:
            @pl.when(first_mid)
            def _():
                start = first_base + 2 * PUMP * index
                repeat(start, start + PUMP, first_mid_step)

            @pl.when(second_end)
            def _():
                start = ends_base + PUMP * index
                repeat(start, start + PUMP, second_end_step)

            @pl.when(second_mid)
            def _():
                start = mids_base + 2 * index
                repeat(start, start + 2 - index, second_mid_step)

        @pl.when(jnp.logical_and(is_first, index == 0))
        def _():
            own_parts(3, attention_back_part)
            share_some(2, 0, TILES)
            put_first_inside(out_grad_at, local_width, out_grad)
            if z_line:
                @pl.when(is_mid)
                def _():
                    repeat(first_base + PUMP, first_base + 2 * PUMP, first_mid_step)

    repeat(0, 2, attention_turn)

    @pl.when(is_first)
    def _():
        far_parts(3, attention_back_part)

    @pl.when(is_second)
    def _():
        both_parts(3, attention_back_part)

    pump_first(PUMP)
    pump_second_ends(1)
    pump_second(1)

    put_first(qkv_grad_at, qkv_rows, in_grad)
    if z_line:
        @pl.when(is_first)
        def _():
            repeat(0, LENT, lambda index: lent(index).start())

    pump_first(PUMP)

    def attention_back(index):
        at = tile_rows(index)
        n1_grad = part_sum(3, index)
        hat, rate = normed(ends[ends_in, at, :].astype(F32))
        small[0:1, :] += column_sum(n1_grad * hat)
        small[1:2, :] += column_sum(n1_grad)
        results[1, at, :] = (
            hidden_grad[at, :] + norm_backward(n1_grad, hat, rate, ln1_gain_ref[...])
        ).astype(BF16)

        @pl.when(is_second)
        def _():
            cross(2 * index).start()
            cross(2 * index + 1).start()

    collect_with_pump(3, attention_back)
    pump_first(1)
    pump_second_ends(1)

    leave = remote(
        results.at[1 - s, token_rows(across_m)], rows_recv, leave_send.at[0], leave_recv.at[0], across
    )
    @pl.when(is_first)
    def _():
        leave.start()

    sum_of_rows(5, m_grad)
    sum_of_rows(4, r_grad)
    for index in range(2):

        def sums(number, index=index):
            at = big_rows(number)
            set_sum(6, 0, index, pre_grad[index, at, :])
            set_sum(7, 0, index, qkv_grad[index, at, 0:local_width])
            set_sum(7, 2 * local_width, index, qkv_grad[index, at, 2 * local_width :])

        repeat(0, bigs, sums)
    small_y_copy = remote(small_other, small_y, leave_send.at[1], leave_recv.at[1], across)
    small_other[0:6, :] = small[0:6, :]
    small_y_copy.start()

    pump_first(2)
    pump_second_ends(1)
    pump_second(2)

    put_second_far(fc_grad_at, width, fc_grad)
    pump_second_ends(2)
    pump_second(2)

    @pl.when(is_second)
    def _():
        both_parts(FINE, mlp_part, per=2)

    pump_second_ends(2)
    pump_second(PUMP)
    put_second_near(fc_grad_at, width, fc_grad)

    @pl.when(is_second)
    def _():
        collect(FINE, layer_out)

    pump_second_ends(2)
    pump_second(PUMP)
    put_second_far(out_grad_at, local_width, out_grad)
    put_second_near(out_grad_at, local_width, out_grad)
    pump_second_ends(2)
    pump_second(PUMP)
    put_second_far(qkv_grad_at, qkv_rows, in_grad)

    @pl.when(is_second)
    def _():
        leave.start()

    pump_second_ends(2)
    pump_second(PUMP)
    put_second_near(qkv_grad_at, qkv_rows, in_grad)

    small_up = remote(small, small_pair, leave_send.at[2], leave_recv.at[2], pair)
    small_across = remote(small, small_mid, leave_send.at[3], leave_recv.at[3], middle)
    small_down = remote(small_mid, small_pair, leave_send.at[2], leave_recv.at[2], pair)

    rows_copy = pltpu.make_async_copy(rows_held, rows_out, local_sem.at[0])

    def small_copy(source):
        return pltpu.make_async_copy(source, small_out, local_sem.at[1])

    def rows_finish(wanted):
        @pl.when(wanted)
        def _():
            leave.wait_recv()
            rows_held[pl.ds(chip, 1)] = results[pl.ds(1 - s, 1), token_rows(m), :].astype(F32)
            rows_held[pl.ds(1 - chip, 1)] = rows_recv[...].astype(F32)[None]
            rows_copy.start()

    if z_line:
        @pl.when(is_end)
        def _():
            small_y_copy.wait_recv()
            small[...] += small_y[...]
            small_up.start()

        pump_ends(first_ends, len(first_order), first_end, False)
        pump_ends(second_ends, len(second_order), second_end, True)
        near, later = blocks * 2 // 3, blocks * 3 // 4
        pump_mids(first_mids, near, first_mid, False)
        pump_mids(second_mids, near, second_mid, True)

        @pl.when(is_mid)
        def _():
            small_y_copy.wait_recv()
            small_up.wait_recv()
            small[...] += small_y[...]
            small[...] += small_pair[...]
            small_across.start()

        pump_mids(first_mids, later, first_mid, False)
        pump_mids(second_mids, later, second_mid, True)
        rows_finish(is_first)

        @pl.when(is_mid)
        def _():
            small_across.wait_recv()
            small_mid[...] += small[...]
            small_down.start()
            small_copy(small_mid).start()

        pump_mids(first_mids, len(first_order), first_mid, False)
        pump_mids(second_mids, turn + LENT - 2, second_mid, True)
        rows_finish(is_second)
        pump_mids(second_mids, len(second_order), second_mid, True)

        def back(index, source):
            lent_back(index, source).wait_recv()
            grad_out(lent_from + index, source).start()

        @pl.when(is_mid)
        def _():
            last = small_from + small_count
            repeat(last - BEHIND, last, lambda step: mid_down(step, (False, True)))

        @pl.when(first_mid)
        def _():
            repeat(0, LENT, lambda index: back(index, grads_mid))

        def take(step, kind):
            grad_pair(step, grads_mid, kind[1]).wait_recv()
            deliver(step, grads_pair, kind)

        def small_take():
            small_down.wait_recv()
            small_copy(small_pair).start()

        @pl.when(first_end)
        def _():
            walk(first_order, 0, later, take)
            small_take()
            walk(first_order, later, len(first_order), take)
            repeat(0, LENT, lambda index: back(index, grads_pair))

        @pl.when(second_end)
        def _():
            walk(second_order, 0, turn, take)
            small_take()
            walk(second_order, turn, len(second_order), take)

    else:
        @pl.when(is_second)
        def _():
            repeat(0, blocks, gather_y)

        repeat(0, blocks, lambda step: grad_out(step, grads).start())
        rows_finish(s >= 0)
        small_y_copy.wait_recv()
        small[...] += small_y[...]
        small_copy(small).start()

    rows_copy.wait()
    small_copy(small).wait()
    own_rows = pl.ds(0, weight_rows)
    pltpu.make_async_copy(grads.at[own_rows], grads_out, grad_out_sem.at[0]).wait()

    entry_across(0).wait_send()
    entry_sibling(0).wait_send()
    entry_forward(0).wait_send()
    leave.wait_send()
    small_y_copy.wait_send()
    sent(part, part_send.at[0])
    sent(n1.at[0, pl.ds(0, big)], cross_send.at[0])
    sent(n1.at[0, pl.ds(0, big)], cross_core_send.at[0])

    @pl.when(is_first)
    def _():
        entry_across(1).wait_send()
        entry_sibling(1).wait_send()
        entry_forward(1).wait_send()
        sent(grads.at[pl.ds(0, 3 * big)], share_send.at[0])
        sent(grads.at[pl.ds(0, 2 * big)], share_core_send.at[0])
        for sem in (far_core_send, far_send, far_back_send):
            sent(grads.at[pl.ds(0, 4 * big)], sem.at[0])

    @pl.when(is_second)
    def _():
        bias_copy.wait_send()
        sent(weights.at[0, pl.ds(0, y_blocks * FETCH)], weight_y_send.at[0])
        if z_line:
            sent(weights.at[0, pl.ds(0, y_blocks * FETCH)], weight_z_send.at[0])
        sent(grads.at[own_rows], grad_y_send.at[0])

    if z_line:

        def stream_sent(count):
            sent(grads.at[pl.ds(0, count)], grad_pair_send.at[0])

            @pl.when(is_mid)
            def _():
                sent(grads.at[pl.ds(0, count)], grad_mid_send.at[0])

        @pl.when(is_first)
        def _():
            stream_sent(lent_from * BLOCK)
            sent(grads.at[pl.ds(0, LENT * BLOCK)], lent_send.at[0])

        @pl.when(is_second)
        def _():
            stream_sent(small_from * BLOCK)
            sent(grads.at[pl.ds(0, LENT * BLOCK)], back_send.at[0])

        @pl.when(is_end)
        def _():
            small_up.wait_send()

        @pl.when(is_mid)
        def _():
            small_across.wait_send()
            small_down.wait_send()


def finish_kernel(local_width, rows_ref, small_ref, grads_ref, *refs):
    outs, (held_rows, held, cast, in_sem, out_sem, rows_sem, held_small) = refs[:13], refs[13:20]
    lines, line_sem = refs[20:28], refs[28]
    rows_out, qkv_out, out_out, fc_out, proj_out = outs[:5]
    small_in = pltpu.make_async_copy(small_ref, held_small, line_sem.at[8])
    line_copies = [
        pltpu.make_async_copy(line, target, line_sem.at[number])
        for number, (line, target) in enumerate(zip(lines, outs[5:]))
    ]
    rows_in = pltpu.make_async_copy(rows_ref, held_rows, rows_sem.at[0])
    rows_copy = pltpu.make_async_copy(held_rows, rows_out, rows_sem.at[1])

    def at_block(number):
        return pl.ds(pl.multiple_of(number * FINISH, FINISH), FINISH)

    def fetch(number):
        at = at_block(number)
        return pltpu.make_async_copy(grads_ref.at[at], held.at[at], in_sem.at[number])

    def repeat(start, last, action):
        def step_of(step, carry):
            action(step)
            return carry

        lax.fori_loop(start, last, step_of, 0)

    blocks = held.shape[0] // FINISH
    repeat(0, blocks, lambda number: fetch(number).start())
    small_in.start()
    rows_in.start()
    first = 0
    puts = []
    for target in (proj_out, fc_out, out_out, qkv_out):
        count = target.shape[0] // FINISH

        def put(number, first=first, target=target):
            return pltpu.make_async_copy(
                cast.at[at_block(first + number)], target.at[at_block(number)], out_sem.at[first + number]
            )

        def step(number, first=first, put=put):
            fetch(first + number).wait()
            at = at_block(first + number)
            cast[at, :] = held[at, :].astype(F32)
            put(number).start()

        repeat(0, count, step)
        puts.append((count, put))
        first += count
    rows_in.wait()
    rows_copy.start()
    small_in.wait()
    lines[0][0:1, :] = held_small[7:8, 0:local_width]
    lines[0][1:2, :] = held_small[7:8, 2 * local_width : 3 * local_width]
    for row, line in enumerate(lines[1:]):
        line[...] = held_small[row : row + 1, :]
    for copy in line_copies:
        copy.start()
    for copy in line_copies:
        copy.wait()
    for count, put in puts:
        repeat(0, count, lambda number: put(number).wait())
    rows_copy.wait()


def local(
    z_line,
    boundary_in,
    order,
    ln1_gain,
    ln1_bias,
    w_qkv,
    qkv_bias,
    w_out,
    out_bias,
    ln2_gain,
    ln2_bias,
    w_fc,
    fc_bias,
    w_proj,
    proj_bias,
):
    _, micro, rows, width = boundary_in.shape
    local_width = w_qkv.shape[-1]
    units = w_fc.shape[-1]
    length = rows * lax.axis_size("mp")
    heads = local_width // HEAD_DIM
    weight_rows = 4 * local_width + width + units
    blocks = weight_rows // BLOCK
    stream_rows = weight_rows + LENT * BLOCK
    numbers = blocks + LENT + 2 * BLOCK // SMALL
    vmem = pltpu.VMEM
    dma = pltpu.SemaphoreType.DMA
    in_any = pl.BlockSpec(memory_space=pl.ANY)
    in_smem = pl.BlockSpec(memory_space=pltpu.SMEM)
    vectors = (ln1_gain, ln1_bias, qkv_bias, out_bias, ln2_gain, ln2_bias, fc_bias, proj_bias)
    out_rows, small, grads = pl.pallas_call(
        functools.partial(kernel, z_line),
        out_shape=(
            jax.ShapeDtypeStruct((micro, rows, width), F32),
            jax.ShapeDtypeStruct((8, width), F32),
            jax.ShapeDtypeStruct((weight_rows, width), BF16),
        ),
        in_specs=[in_smem] + [in_any] * 13,
        out_specs=(in_any,) * 3,
        scratch_shapes=[
            *(vmem(vector.shape, F32) for vector in vectors),
            vmem((micro, rows, width), BF16),
            vmem((micro, rows, width), BF16),
            vmem((2, weight_rows, width), BF16),
            vmem((2, 8, width), F32),
            vmem((3, length, width), BF16),
            vmem((2, length, width), BF16),
            vmem((rows, width), BF16),
            vmem((micro, rows, width), F32),
            vmem((2, length, width), BF16),
            vmem((2, length, width), BF16),
            vmem((2, 3, heads, length, HEAD_DIM), BF16),
            vmem((2 * heads, length, length), BF16),
            vmem((heads, length, HEAD_DIM), BF16),
            vmem((2, length, local_width), BF16),
            vmem((length, width), F32),
            vmem((length, width), F32),
            vmem((2, length, units), BF16),
            vmem((2, length, units), BF16),
            vmem((2, length, width), BF16),
            vmem((2, length, width), BF16),
            vmem((2, length, 3 * local_width), BF16),
            vmem((4, length, width), BF16),
            vmem((4, length, width), BF16),
            vmem((stream_rows, width), BF16),
            vmem((weight_rows, width), BF16),
            vmem((weight_rows, width), BF16),
            vmem((stream_rows, width), BF16),
            vmem((stream_rows, width), BF16),
            vmem((8, width), F32),
            vmem((8, width), F32),
            vmem((8, width), F32),
            vmem((8, width), F32),
            vmem((8, width), F32),
            dma((5,)),
            dma((8,)),
            dma((7,)),
            dma((7,)),
            dma((1,)),
            dma((weight_rows // FETCH,)),
            dma((1,)),
            dma((1,)),
            dma((5 * TILES,)),
            dma((1,)),
            dma((1,)),
            dma((1,)),
            dma((1,)),
            dma((2,)),
            dma((1,)),
            dma((2 * TILES,)),
            dma((1,)),
            dma((2 * TILES,)),
            dma((4,)),
            dma((4,)),
            dma((1,)),
            dma((max(numbers - LENT, 15 * TILES),)),
            dma((1,)),
            dma((numbers,)),
            dma((1,)),
            dma((numbers,)),
            dma((1,)),
            dma((1,)),
            dma((LENT,)),
            dma((1,)),
            dma((LENT,)),
        ],
        compiler_params=pltpu.CompilerParams(
            collective_id=0, has_side_effects=True, vmem_limit_bytes=63 * 2**20
        ),
        name="two_layers",
    )(
        order,
        boundary_in,
        ln1_gain,
        ln1_bias,
        jnp.swapaxes(w_qkv, 2, 3).reshape(1, 3 * local_width, width),
        qkv_bias,
        w_out,
        out_bias,
        ln2_gain,
        ln2_bias,
        w_fc,
        fc_bias,
        w_proj,
        proj_bias,
    )
    if not z_line:
        small, grads = lax.psum((small, grads), "dp")
    shapes = [
        (micro, rows, width),
        (3 * local_width, width),
        (local_width, width),
        (width, units),
        (units, width),
        (2, local_width),
    ] + [(1, width)] * 6 + [(1, units)]
    (
        out_rows,
        qkv_grad,
        out_grad,
        fc_grad,
        proj_grad,
        qkv_bias_grad,
        ln1_gain_grad,
        ln1_bias_grad,
        ln2_gain_grad,
        ln2_bias_grad,
        out_bias_grad,
        proj_bias_grad,
        fc_bias_grad,
    ) = pl.pallas_call(
        functools.partial(finish_kernel, local_width),
        out_shape=[jax.ShapeDtypeStruct(shape, F32) for shape in shapes],
        in_specs=[in_any] * 3,
        out_specs=[in_any] * 13,
        scratch_shapes=[
            vmem((micro, rows, width), F32),
            vmem((weight_rows, width), BF16),
            vmem((weight_rows, width), F32),
            dma((weight_rows // FINISH,)),
            dma((weight_rows // FINISH,)),
            dma((2,)),
            vmem((8, width), F32),
        ]
        + [vmem(shape, F32) for shape in shapes[5:]]
        + [dma((9,))],
        compiler_params=pltpu.CompilerParams(vmem_limit_bytes=62 * 2**20),
        name="finish",
    )(out_rows, small, grads)
    return (
        out_rows[None],
        ln1_gain_grad,
        ln1_bias_grad,
        jnp.swapaxes(qkv_grad.reshape(1, 3, local_width, width), 2, 3),
        qkv_bias_grad[None],
        out_grad[None],
        out_bias_grad,
        ln2_gain_grad,
        ln2_bias_grad,
        fc_grad[None],
        fc_bias_grad,
        proj_grad[None],
        proj_bias_grad,
    )


def solution(mesh):
    return jax.shard_map(
        functools.partial(local, mesh.shape["dp"] == 4),
        mesh=mesh,
        in_specs=(
            P("section", "dp", "mp", None),
            P("dp", None),
            P("section", None),
            P("section", None),
            P("section", None, None, "mp"),
            P("section", None, "mp"),
            P("section", "mp", None),
            P("section", None),
            P("section", None),
            P("section", None),
            P("section", None, "mp"),
            P("section", "mp"),
            P("section", "mp", None),
            P("section", None),
        ),
        out_specs=(
            P("section", "dp", "mp", None),
            P("section", None),
            P("section", None),
            P("section", None, None, "mp"),
            P("section", None, "mp"),
            P("section", "mp", None),
            P("section", None),
            P("section", None),
            P("section", None),
            P("section", None, "mp"),
            P("section", "mp"),
            P("section", "mp", None),
            P("section", None),
        ),
        check_vma=False,
    )
```

```python
import functools

import jax
import jax.numpy as jnp
from jax import lax
from jax.experimental import pallas as pl
from jax.experimental.pallas import tpu as pltpu
from jax.sharding import PartitionSpec as P

HEAD_DIM = 64
BRANCH_SCALE = 0.14433756729740643
NORM_EPS = 1e-05
GELU_RATE = 0.7978845608028654
GELU_CUBE = 0.044715
NEGATIVE = -1e30
BLOCK = 48
PUMP = 2
FINISH = 192
FETCH = 96
TILES = 4
FINE = 1
SMALL = 16
LENT = 10
BEHIND = 4
MESH = pl.DeviceIdType.MESH
BF16 = jnp.bfloat16
F32 = jnp.float32


def dot_nn(a, b):
    return lax.dot_general(a, b, (((1,), (0,)), ((), ())), preferred_element_type=F32)


def dot_nt(a, b):
    return lax.dot_general(a, b, (((1,), (1,)), ((), ())), preferred_element_type=F32)


def dot_tn(a, b):
    return lax.dot_general(a, b, (((0,), (0,)), ((), ())), preferred_element_type=F32)


def normed(values):
    center = values - jnp.mean(values, axis=-1, keepdims=True)
    rate = lax.rsqrt(jnp.mean(center * center, axis=-1, keepdims=True) + NORM_EPS)
    return center * rate, rate


def norm_backward(grad, hat, rate, gain):
    scaled = grad * gain
    return rate * (
        scaled
        - jnp.mean(scaled, axis=-1, keepdims=True)
        - hat * jnp.mean(scaled * hat, axis=-1, keepdims=True)
    )


def column_sum(values):
    return jnp.sum(values.astype(F32), axis=0, keepdims=True)


def remote(src, dst, send_sem, recv_sem, device):
    return pltpu.make_async_remote_copy(
        src_ref=src,
        dst_ref=dst,
        send_sem=send_sem,
        recv_sem=recv_sem,
        device_id=device,
        device_id_type=MESH,
    )


def kernel(
    z_line,
    order_hbm,
    boundary_ref,
    ln1_gain_hbm,
    ln1_bias_hbm,
    w_qkv_ref,
    qkv_bias_hbm,
    w_out_ref,
    out_bias_hbm,
    ln2_gain_hbm,
    ln2_bias_hbm,
    w_fc_ref,
    fc_bias_hbm,
    w_proj_ref,
    proj_bias_hbm,
    rows_out,
    small_out,
    grads_out,
    order_ref,
    ln1_gain_ref,
    ln1_bias_ref,
    qkv_bias_ref,
    out_bias_ref,
    ln2_gain_ref,
    ln2_bias_ref,
    fc_bias_ref,
    proj_bias_ref,
    raw,
    slots,
    weights,
    biases,
    ends,
    results,
    rows_recv,
    rows_held,
    n1,
    n2,
    qkv,
    probs,
    head_rows,
    attended,
    hidden,
    hidden_grad,
    act,
    slope,
    m_grad,
    r_grad,
    qkv_grad,
    part,
    part_recv,
    grads,
    grads_other,
    grads_y,
    grads_pair,
    grads_mid,
    small,
    small_other,
    small_y,
    small_pair,
    small_mid,
    local_sem,
    vector_sem,
    entry_send,
    entry_recv,
    weight_y_send,
    weight_recv,
    weight_z_send,
    part_send,
    part_recv_sem,
    far_core_send,
    far_send,
    far_back_send,
    share_send,
    share_core_send,
    cross_send,
    cross_recv,
    cross_core_send,
    cross_core_recv,
    leave_send,
    leave_recv,
    grad_y_send,
    grad_y_recv,
    grad_pair_send,
    grad_pair_recv,
    grad_mid_send,
    grad_mid_recv,
    grad_out_sem,
    lent_send,
    lent_recv,
    back_send,
):
    s, d, m = lax.axis_index("section"), lax.axis_index("dp"), lax.axis_index("mp")
    core, chip = lax.rem(m, 2), lax.div(m, 2)
    half = lax.rem(d, 2)
    across_m = 2 * (1 - chip) + core
    sibling = (s, d, 2 * chip + 1 - core)
    across = (s, d, across_m)
    other_section = (1 - s, d, m)
    pair = (s, d + 1 - 2 * half, m)
    middle = (s, 3 - d, m)
    is_first, is_second = s == 0, s == 1
    is_mid = lax.div(d + 1, 2) == 1
    is_end = lax.div(d + 1, 2) != 1

    rows = boundary_ref.shape[2]
    length, width = n1.shape[1:]
    tile = length // TILES
    piece = tile // 2
    big = length // 2
    local_width = attended.shape[2]
    units = act.shape[2]
    heads = local_width // HEAD_DIM
    tiles_per_big, bigs = big // tile, length // big
    scale = HEAD_DIM ** (-0.5)
    qkv_rows = 3 * local_width
    out_at, fc_at, proj_at = qkv_rows, qkv_rows + local_width, qkv_rows + local_width + width
    weight_rows = weights.shape[1]
    blocks = weight_rows // BLOCK
    ends_in, ends_grad = 2 * s, 2 * (1 - s)

    def set_rows(index):
        return index * (1 - s)

    def set_weights(index):
        return index * s

    def span(index, count):
        start = index * count
        return pl.ds(start if isinstance(start, int) else pl.multiple_of(start, count), count)

    def tile_rows(index):
        return span(index, tile)

    def big_rows(index):
        return span(index, big)

    def tile_of(which):
        return tile // 2 if which == FINE else tile

    def count_of(which):
        return length // tile_of(which)

    def number_of(which, index):
        return which * TILES + (TILES if which > FINE else 0) + index

    def rows_of(which, index):
        return span(index, tile_of(which))

    def piece_rows(which, index, core_of, base=0):
        size = tile_of(which) // 2
        return pl.ds(pl.multiple_of(base + (2 * index + core_of) * size, size), size)

    partners = [sibling, across, other_section]
    if z_line:
        partners += [pair, middle]
    barrier = pltpu.get_barrier_semaphore()
    for device in partners:
        pl.semaphore_signal(barrier, inc=1, device_id=device, device_id_type=MESH)

    loads = [
        pltpu.make_async_copy(boundary_ref.at[0], raw, local_sem.at[0]),
        pltpu.make_async_copy(
            w_qkv_ref.at[0], weights.at[0, pl.ds(0, qkv_rows)], local_sem.at[1]
        ),
        pltpu.make_async_copy(
            w_out_ref.at[0], weights.at[0, pl.ds(out_at, local_width)], local_sem.at[2]
        ),
        pltpu.make_async_copy(w_fc_ref.at[0], weights.at[0, pl.ds(fc_at, width)], local_sem.at[3]),
        pltpu.make_async_copy(
            w_proj_ref.at[0], weights.at[0, pl.ds(proj_at, units)], local_sem.at[4]
        ),
    ]
    vector_loads = [
        pltpu.make_async_copy(source, target, vector_sem.at[number])
        for number, (source, target) in enumerate(
            (
                (ln1_gain_hbm, ln1_gain_ref),
                (ln1_bias_hbm, ln1_bias_ref),
                (qkv_bias_hbm, qkv_bias_ref),
                (out_bias_hbm, out_bias_ref),
                (ln2_gain_hbm, ln2_gain_ref),
                (ln2_bias_hbm, ln2_bias_ref),
                (fc_bias_hbm, fc_bias_ref),
                (proj_bias_hbm, proj_bias_ref),
            )
        )
    ]
    order_load = pltpu.make_async_copy(order_hbm, order_ref, vector_sem.at[8])
    for load in [order_load] + loads[:1] + vector_loads + loads[1:]:
        load.start()

    biases[0] = jnp.zeros_like(biases[0])
    small[...] = jnp.zeros_like(small)
    small_other[...] = jnp.zeros_like(small_other)

    order_load.wait()
    loads[0].wait()
    for slot in range(2):
        picked = jnp.where(is_first, order_ref[0, slot], slot).astype(F32)
        slots[slot] = (
            raw[0].astype(F32) * (1.0 - picked) + raw[1].astype(F32) * picked
        ).astype(BF16)

    pl.semaphore_wait(barrier, len(partners))

    def token_rows(index):
        return pl.ds(pl.multiple_of(index * rows, rows), rows)

    def entry_across(which):
        slot = (1 - chip) * (1 - which) + chip * which
        return remote(
            slots.at[slot],
            ends.at[which, token_rows(m)],
            entry_send.at[which],
            entry_recv.at[which],
            across,
        )

    def entry_sibling(which):
        slot = chip * (1 - which) + (1 - chip) * which
        return remote(
            slots.at[slot],
            ends.at[which, token_rows(m)],
            entry_send.at[2 + which],
            entry_recv.at[2 + which],
            sibling,
        )

    def entry_forward(which):
        at = token_rows(across_m)
        return remote(
            ends.at[which, at],
            ends.at[which, at],
            entry_send.at[4 + which],
            entry_recv.at[4 + which],
            sibling,
        )

    bias_copy = remote(biases.at[0], biases.at[1], entry_send.at[6], entry_recv.at[6], across)

    def entry_start(which):
        entry_across(which).start()
        entry_sibling(which).start()
        slot = chip if which == 0 else 1 - chip
        ends[which, token_rows(m), :] = slots[slot]

    def entry_pass(which):
        entry_across(which).wait_recv()
        entry_forward(which).start()

    def entry_finish(which):
        entry_pass(which)
        entry_sibling(which).wait_recv()
        entry_forward(which).wait_recv()

    @pl.when(is_first)
    def _():
        entry_start(1)
        entry_start(0)

    y_blocks = weight_rows // FETCH // (2 if z_line else 1)

    def weight_block(index):
        return pl.ds(pl.multiple_of(index * BLOCK, BLOCK), BLOCK)

    def near_block(step):
        return span(2 * step + half if z_line else step, FETCH)

    def weight_y(step):
        return remote(
            weights.at[0, near_block(step)],
            weights.at[1, near_block(step)],
            weight_y_send.at[0],
            weight_recv.at[step],
            across,
        )

    def weight_z(step):
        return remote(
            weights.at[1, near_block(step)],
            weights.at[1, near_block(step)],
            weight_z_send.at[0],
            weight_recv.at[y_blocks + step],
            pair,
        )

    def repeat(first, last, action):
        def step_of(step, carry):
            action(step)
            return carry

        lax.fori_loop(first, last, step_of, 0)

    late_step = proj_at * y_blocks // weight_rows
    y_done = [0]

    def weight_need(row):
        steps = row * y_blocks // weight_rows
        if z_line and steps > y_done[0]:
            first, y_done[0] = y_done[0], steps

            @pl.when(is_second)
            def _():
                repeat(first, steps, lambda step: weight_z(step).wait_recv())

    def weight_pass(step):
        weight_y(step).wait_recv()
        if z_line:
            weight_z(step).start()

    for load in vector_loads + loads[1:]:
        load.wait()
    biases[0, 0:1, :] = fc_bias_ref[...]
    biases[0, 1:2, 0:local_width] = qkv_bias_ref[0, 0:1, :]
    biases[0, 2:3, 0:local_width] = qkv_bias_ref[0, 1:2, :]

    def sent(source, sem):
        remote(source, source, sem, sem, sibling).wait_send()

    def arrived(target, sem):
        remote(target, target, sem, sem, sibling).wait_recv()

    def cross(index):
        at = piece_rows(FINE, index, core)
        return remote(
            results.at[s, at],
            ends.at[2, at],
            cross_send.at[0],
            cross_recv.at[index],
            other_section,
        )

    def cross_core(index):
        at = piece_rows(FINE, index, core)
        return remote(
            ends.at[2, at],
            ends.at[2, at],
            cross_core_send.at[0],
            cross_core_recv.at[index],
            sibling,
        )

    shared = (n2, m_grad, r_grad)

    def share(which, index):
        at = piece_rows(which, index, core)
        source = ends.at[2, at] if which == FINE else shared[which].at[0, at]
        return remote(
            source,
            shared[which].at[1, at],
            share_send.at[0],
            weight_recv.at[number_of(which, index)],
            across,
        )

    def share_core(which, index):
        at = piece_rows(which, index, core)
        return remote(
            shared[which].at[1, at],
            shared[which].at[1, at],
            share_core_send.at[1 if which == FINE else 0],
            weight_recv.at[4 * TILES + (index if which == 0 else TILES + which)],
            sibling,
        )

    def share_some(which, start, count):
        def forward(index):
            share(which, start + index).wait_recv()
            share_core(which, start + index).start()

        repeat(0, count, forward)
        if which == 0:
            repeat(0, count, lambda index: share_core(which, start + index).wait_recv())
        else:
            arrived(shared[which].at[1, pl.ds(0, big)], weight_recv.at[5 * TILES + which])

    def part_copy(which, index):
        at = rows_of(which, index)
        return remote(
            part.at[which, at],
            part_recv.at[which, at],
            part_send.at[0],
            part_recv_sem.at[number_of(which, index)],
            sibling,
        )

    def spare_rows(which, index, core_of):
        return piece_rows(which, index, core_of, which * length)

    def far_core(which, index):
        return remote(
            grads_y.at[spare_rows(which, index, 1 - core)],
            grads_other.at[spare_rows(which, index, 1 - core)],
            far_core_send.at[0],
            grad_y_recv.at[number_of(which, index)],
            sibling,
        )

    def far(which, index):
        return remote(
            grads_y.at[spare_rows(which, index, core)],
            weights.at[1, spare_rows(which, index, core)],
            far_send.at[0],
            grad_y_recv.at[5 * TILES + number_of(which, index)],
            across,
        )

    def far_back(which, index):
        at = spare_rows(which, index, core)
        return remote(
            weights.at[1, at],
            weights.at[1, at],
            far_back_send.at[0],
            grad_y_recv.at[10 * TILES + number_of(which, index)],
            sibling,
        )

    def far_pass(which, index):
        far_core(which, index).wait_recv()
        at = spare_rows(which, index, core)
        grads_y[at, :] = (grads_y[at, :].astype(F32) + grads_other[at, :].astype(F32)).astype(BF16)
        far(which, index).start()

    def part_sum(which, index):
        at = rows_of(which, index)
        near = part[which, at, :].astype(F32) + part_recv[which, at, :].astype(F32)
        size = tile_of(which)
        other = weights[
            1, pl.ds(pl.multiple_of(which * length + index * size, size), size), :
        ].astype(F32)
        return near + jnp.where(is_first, other, 0.0)

    def far_parts(which, value_of, per=1, before=None):
        def step(number):
            if before is not None:
                before(number)
            size = per * tile_of(which)
            grads_y[pl.ds(pl.multiple_of(which * length + number * size, size), size), :] = (
                value_of(1, 0, span(number, size)).astype(BF16)
            )
            for index in range(per):
                far_core(which, number * per + index).start()

            @pl.when(number > 0)
            def _():
                for index in range(per):
                    far_pass(which, (number - 1) * per + index)

        repeat(0, count_of(which) // per, step)
        for index in range(per):
            far_pass(which, count_of(which) - per + index)

    def own_parts(which, value_of, per=1):
        def step(number):
            at = span(number, per * tile_of(which))
            part[which, at, :] = value_of(0, 0, at).astype(BF16)
            for index in range(per):
                part_copy(which, number * per + index).start()

        repeat(0, count_of(which) // per, step)

    def both_parts(which, value_of, per=1):
        def step(number):
            at = span(number, per * tile_of(which))
            part[which, at, :] = (value_of(0, 0, at) + value_of(1, 1, at)).astype(BF16)
            for index in range(per):
                part_copy(which, number * per + index).start()

        repeat(0, count_of(which) // per, step)

    def collect(which, finish, beside=None, start=0, last=None):
        last = count_of(which) if last is None else last

        def far_next(index):
            far(which, index).wait_recv()
            far_back(which, index).start()

        @pl.when(is_first)
        def _():
            far_next(start)

        def step(index):
            @pl.when(is_first)
            def _():
                @pl.when(index + 1 < last)
                def _():
                    far_next(index + 1)

                if beside is not None:
                    beside(index)
                far_back(which, index).wait_recv()

            part_copy(which, index).wait_recv()
            finish(index)

        repeat(start, last, step)

    def weight_of(shards, first, count):
        return weights[shards, first : first + count, :]

    def scale_grad(index):
        at = rows_of(FINE, index)
        m_grad[0, at, :] = (BRANCH_SCALE * ends[ends_grad, at, :].astype(F32)).astype(BF16)

    @pl.when(is_second)
    def _():
        bias_copy.start()
        repeat(0, late_step, lambda step: weight_y(step).start())
        entry_start(0)
        repeat(late_step, y_blocks, lambda step: weight_y(step).start())
        repeat(0, late_step, weight_pass)
        bias_copy.wait_recv()
        entry_finish(0)
        repeat(0, count_of(FINE), scale_grad)
        repeat(late_step, y_blocks - bigs, weight_pass)

    def norm_big(which, source, number):
        def step(index):
            at = span(number * (big // tile) + index, tile)
            hat, _ = normed(ends[source, at, :].astype(F32))
            n1[which, at, :] = (hat * ln1_gain_ref[...] + ln1_bias_ref[...]).astype(BF16)

        repeat(0, big // tile, step)

    def cross_receive(start, last, action, on=None):
        def pass_on(index):
            cross(index).wait_recv()
            cross_core(index).start()
            if on is not None:
                on(index)

        pass_on(start)

        def step(index):
            @pl.when(index + 1 < last)
            def _():
                pass_on(index + 1)

            cross_core(index).wait_recv()
            action(index)

        repeat(start, last, step)

    causal = lax.broadcasted_iota(jnp.int32, (length, length), 1) >= lax.broadcasted_iota(
        jnp.int32, (length, length), 0
    )

    def bias_of(shards, row, count):
        return biases[shards, row : row + 1, 0:count]

    def head_columns(kind, head):
        first = kind * local_width + head * HEAD_DIM
        return slice(first, first + HEAD_DIM)

    def project(index, number):
        source, shards = set_rows(index), set_weights(index)
        at = big_rows(number)
        for kind in range(3):
            values = dot_nt(n1[source, at, :], weight_of(shards, kind * local_width, local_width))
            if kind == 0:
                values = values + bias_of(shards, 1, local_width)
            if kind == 2:
                values = values + bias_of(shards, 2, local_width)
            values = values.astype(BF16)
            if kind == 0:
                values = (values.astype(F32) * scale).astype(BF16)
            for head in range(heads):
                qkv[index, kind, head, at, :] = values[:, head_columns(0, head)]

    def attention_forward(index):
        for head in range(heads):
            scores = dot_nt(qkv[index, 1, head], qkv[index, 0, head])
            scores = jnp.where(causal, scores, NEGATIVE)
            raised = jnp.exp(scores - jnp.max(scores, axis=0, keepdims=True))
            shares = raised * (1.0 / jnp.sum(raised, axis=0, keepdims=True))
            shares = shares.astype(BF16)
            probs[index * heads + head] = shares
            attended[index, :, head_columns(0, head)] = dot_tn(
                shares, qkv[index, 2, head]
            ).astype(BF16)

    weight_need(out_at)

    @pl.when(is_second)
    def _():
        def step(number):
            def pass_on(index):
                cross(index).wait_recv()
                cross_core(index).start()

            per = count_of(FINE) // bigs
            repeat(number * per, (number + 1) * per, pass_on)
            repeat(
                number * per, (number + 1) * per, lambda index: cross_core(index).wait_recv()
            )
            norm_big(0, 2, number)
            repeat(0, 2, lambda index: project(index, number))
            weight_pass(y_blocks - bigs + number)

        repeat(0, bigs, step)

    @pl.when(is_first)
    def _():
        def step(index):
            entry_sibling(index).wait_recv()
            norm_big(index, index, chip)
            project(index, chip)

        repeat(0, 2, step)
        entry_pass(1)
        entry_forward(1).wait_recv()
        norm_big(1, 1, 1 - chip)
        project(1, 1 - chip)

    attention_forward(1)

    def attention_part(index, shards, at):
        return dot_nn(attended[index, at, :], weight_of(shards, out_at, local_width))

    @pl.when(is_first)
    def _():
        far_parts(0, attention_part)
        entry_pass(0)
        entry_forward(0).wait_recv()
        norm_big(0, 0, 1 - chip)
        project(0, 1 - chip)

    attention_forward(0)

    weight_need(fc_at)

    @pl.when(is_first)
    def _():
        own_parts(0, attention_part)

    @pl.when(is_second)
    def _():
        both_parts(0, attention_part)

    def attention_out(index):
        at = tile_rows(index)
        held = ends[ends_in, at, :].astype(F32) + BRANCH_SCALE * (
            part_sum(0, index) + out_bias_ref[...]
        )
        hidden[at, :] = held
        hat, _ = normed(held)
        n2[0, at, :] = (hat * ln2_gain_ref[...] + ln2_bias_ref[...]).astype(BF16)

        @pl.when(is_first)
        def _():
            share(0, index).start()

    def activate(index, source, shards, at):
        u = dot_nn(n2[source, at, :], weight_of(shards, fc_at, width)) + bias_of(shards, 0, units)
        square = u * u
        bent = jnp.tanh(GELU_RATE * (u + GELU_CUBE * u * square))
        act[index, at, :] = (0.5 * u * (1.0 + bent)).astype(BF16)
        slope[index, at, :] = (
            0.5 * (1.0 + bent)
            + (0.5 * GELU_RATE) * u * (1.0 - bent * bent) * (1.0 + (3.0 * GELU_CUBE) * square)
        ).astype(BF16)

    weight_need(proj_at)

    def first_half(number):
        collect(
            0, attention_out, start=number * tiles_per_big, last=(number + 1) * tiles_per_big
        )
        activate(set_weights(1), 0, set_weights(1), big_rows(number))

    repeat(0, bigs, first_half)

    def mlp_part(index, shards, at):
        return dot_nn(act[index, at, :], weight_of(shards, proj_at, units))

    def other_activate(number):
        share_some(0, number, 1)
        activate(1, 1, 0, span(number, tile))

    @pl.when(is_first)
    def _():
        own_parts(FINE, mlp_part, per=2)
        far_parts(FINE, mlp_part, per=2, before=other_activate)

    weight_need(weight_rows)

    proj_grad_at, fc_grad_at = 0, units
    out_grad_at = fc_grad_at + width
    qkv_grad_at = out_grad_at + local_width

    lent_from = blocks - LENT
    small_from, small_count = blocks + LENT, 2 * BLOCK // SMALL
    small_row = (lent_from - 2) * BLOCK

    def block_rows(step, is_small=False):
        if is_small:
            start = small_row + (step - small_from) * SMALL
            return pl.ds(start if isinstance(start, int) else pl.multiple_of(start, SMALL), SMALL)
        return weight_block(step)

    def grad_y(step, is_small=False):
        return remote(
            grads_other.at[block_rows(step, is_small)],
            grads_y.at[block_rows(step, is_small)],
            grad_y_send.at[0],
            grad_y_recv.at[step - LENT if is_small else step],
            across,
        )

    def grad_pair(step, source, is_small=False):
        return remote(
            source.at[block_rows(step, is_small)],
            grads_pair.at[block_rows(step, is_small)],
            grad_pair_send.at[0],
            grad_pair_recv.at[step],
            pair,
        )

    def grad_mid(step, is_small=False):
        return remote(
            grads.at[block_rows(step, is_small)],
            grads_mid.at[block_rows(step, is_small)],
            grad_mid_send.at[0],
            grad_mid_recv.at[step],
            middle,
        )

    def grad_out(step, source, is_small=False):
        at = block_rows(step, is_small)
        return pltpu.make_async_copy(source.at[at], grads_out.at[at], grad_out_sem.at[0])

    def add_into(target, source, step, is_small):
        at = block_rows(step, is_small)
        target[at, :] = (target[at, :].astype(F32) + source[at, :].astype(F32)).astype(BF16)

    def gather_y(step, is_small=False):
        grad_y(step, is_small).wait_recv()
        add_into(grads, grads_y, step, is_small)

    def mid_up(step, is_small=False):
        grad_pair(step, grads, is_small).wait_recv()
        add_into(grads, grads_pair, step, is_small)
        grad_mid(step, is_small).start()

    def kind_of(step):
        return blocks <= step < small_from, step >= small_from

    def mid_down(step, kind):
        grad_mid(step, kind[1]).wait_recv()
        add_into(grads_mid, grads, step, kind[1])
        grad_pair(step, grads_mid, kind[1]).start()
        deliver(step, grads_mid, kind)

    def deliver(step, source, kind):
        if kind[0]:
            lent_back(step - blocks, source).start()
        else:
            grad_out(step, source, kind[1]).start()

    def lent(index):
        return remote(
            grads.at[weight_block(lent_from + index)],
            grads.at[weight_block(blocks + index)],
            lent_send.at[0],
            lent_recv.at[index],
            other_section,
        )

    def lent_back(index, source):
        return remote(
            source.at[weight_block(blocks + index)],
            source.at[weight_block(lent_from + index)],
            back_send.at[0],
            lent_recv.at[index],
            other_section,
        )

    small_blocks = range(small_from, small_from + small_count)
    turn = blocks - 4
    first_order = [*range(lent_from - 2), *small_blocks]
    second_order = [
        *range(lent_from - 2),
        *range(lent_from, turn),
        *range(blocks, small_from),
        *range(turn, blocks),
        *small_blocks,
    ]

    def runs(order, start, last, behind=0):
        cuts = [start]
        for place in range(start + 1, last):
            for back in (place, place - behind):
                if back > 0 and order[back] != order[back - 1] + 1 and cuts[-1] != place:
                    cuts.append(place)
        cuts.append(last)
        return [
            (a, b, order[a] - a, order[max(a - behind, 0)] - max(a - behind, 0))
            for a, b in zip(cuts, cuts[1:])
            if b > a
        ]

    first_ends, first_mids, second_ends, second_mids = [0], [0], [0], [0]
    first_end, second_end = jnp.logical_and(is_first, is_end), jnp.logical_and(is_second, is_end)
    first_mid, second_mid = jnp.logical_and(is_first, is_mid), jnp.logical_and(is_second, is_mid)

    def gather(step, kind):
        if kind[0]:
            lent(step - blocks).wait_recv()
        else:
            gather_y(step, kind[1])

    def walk(order, start, last, action):
        for a, b, offset, _ in runs(order, start, last):
            kind = kind_of(a + offset)
            repeat(a + offset, b + offset, functools.partial(action, kind=kind))

    def pump_ends(done, last, wanted, second):
        start, done[0] = done[0], last
        if z_line:
            def up(step, kind):
                if second:
                    gather(step, kind)
                grad_pair(step, grads, kind[1]).start()

            @pl.when(wanted)
            def _():
                walk(second_order if second else first_order, start, last, up)

    def pump_mids(done, last, wanted, second):
        start, done[0] = done[0], last
        if z_line:
            @pl.when(wanted)
            def _():
                order = second_order if second else first_order
                for a, b, offset, old in runs(order, start, last, BEHIND):

                    def step(place, a=a, offset=offset, old=old):
                        if second:
                            gather(place + offset, kind_of(a + offset))
                        mid_up(place + offset, kind_of(a + offset)[1])

                        @pl.when(place >= BEHIND)
                        def _():
                            mid_down(place - BEHIND + old, kind_of(max(a - BEHIND, 0) + old))

                    repeat(a, b, step)

    def pump_first_ends(count):
        pump_ends(first_ends, first_ends[0] + count, first_end, False)

    def pump_first(count):
        pump_mids(first_mids, first_mids[0] + count, first_mid, False)

    def pump_second_ends(count):
        pump_ends(second_ends, second_ends[0] + count, second_end, True)

    def pump_second(count):
        pump_mids(second_mids, second_mids[0] + count, second_mid, True)

    def cut_columns(count):
        return (2, count // 2) if count % 768 == 0 else (1, count)

    def put_first_inside(first, count, value_of):
        steps, columns = cut_columns(count)

        def step(number):
            at = span(number, columns)
            grads[pl.ds(first + number * columns, columns), :] = (
                value_of(0, at) + value_of(1, at)
            ).astype(BF16)

        repeat(0, steps, step)

    def put_first(first, count, value_of):
        @pl.when(is_first)
        def _():
            put_first_inside(first, count, value_of)

    def put_second(target, index, first, count, value_of, after=None):
        steps, columns = cut_columns(count)

        def step(number):
            start = first + number * columns
            target[pl.ds(start, columns), :] = value_of(index, span(number, columns)).astype(BF16)
            if after is not None:
                after(first // BLOCK + number * (columns // BLOCK), columns // BLOCK)

        @pl.when(is_second)
        def _():
            repeat(0, steps, step)

    def put_second_far(first, count, value_of):
        def leave_blocks(start, number):
            if z_line and first == qkv_grad_at:
                repeat(first // BLOCK, lent_from - 2, lambda step: grad_y(step).start())
                repeat(lent_from, blocks, lambda step: grad_y(step).start())
                repeat(
                    small_from, small_from + small_count, lambda step: grad_y(step, True).start()
                )
            else:
                repeat(start, start + number, lambda step: grad_y(step).start())

        put_second(grads_other, 1, first, count, value_of, leave_blocks)

    def put_second_near(first, count, value_of):
        put_second(grads, 0, first, count, value_of)

    def set_sum(row, column, index, values):
        total = column_sum(values)
        columns = slice(column, column + total.shape[1])
        if index == 0:
            small[row : row + 1, columns] += total
        else:
            @pl.when(is_first)
            def _():
                small[row : row + 1, columns] += total

            @pl.when(is_second)
            def _():
                small_other[row : row + 1, columns] += total

    def proj_grad(index, columns):
        return dot_tn(act[index, :, columns], m_grad[set_rows(index)])

    def fc_grad(index, columns):
        return dot_tn(n2[set_rows(index), :, columns], pre_grad[index])

    def out_grad(index, columns):
        return dot_tn(attended[index, :, columns], r_grad[set_rows(index)])

    def in_grad(index, columns):
        return dot_tn(qkv_grad[index, :, columns], n1[set_rows(index)])

    put_second_far(proj_grad_at, units, proj_grad)

    @pl.when(is_second)
    def _():
        repeat(0, bigs, lambda number: activate(0, 0, 0, big_rows(number)))

    proj_half = units // 2
    put_second_near(proj_grad_at, proj_half, proj_grad)

    def layer_out(index):
        at = rows_of(FINE, index)
        results[0, at, :] = (
            hidden[at, :] + BRANCH_SCALE * (part_sum(FINE, index) + proj_bias_ref[...])
        ).astype(BF16)

        @pl.when(is_first)
        def _():
            cross(index).start()

    @pl.when(is_first)
    def _():
        collect(FINE, layer_out)

    @pl.when(is_first)
    def _():
        cross_receive(0, count_of(FINE), scale_grad, lambda index: share(FINE, index).start())

        def own(number):
            columns = span(number, units // 2)
            grads[span(number, units // 2), :] = proj_grad(0, columns).astype(BF16)

        repeat(0, 2, own)

    pre_grad = slope

    def mlp_slope(index):
        def step(number):
            at = big_rows(number)
            values = (
                slope[index, at, :].astype(F32)
                * dot_nt(
                    m_grad[set_rows(index), at, :], weight_of(set_weights(index), proj_at, units)
                )
            ).astype(BF16)
            pre_grad[index, at, :] = values

        repeat(0, bigs, step)

    def mlp_back_part(index, shards, at):
        return dot_nt(pre_grad[index, at, :], weight_of(shards, fc_at, width))

    def sum_of_rows(row, source):
        def step(number):
            small[row : row + 1, :] += column_sum(source[0, big_rows(number), :])

        repeat(0, bigs, step)

    mlp_slope(0)

    @pl.when(is_first)
    def _():
        own_parts(2, mlp_back_part, per=tiles_per_big)
        share_some(FINE, 0, count_of(FINE))
        sent(m_grad.at[1, pl.ds(0, big)], share_core_send.at[1])

        def scale_other(number):
            at = big_rows(number)
            m_grad[1, at, :] = (BRANCH_SCALE * m_grad[1, at, :].astype(F32)).astype(BF16)

        repeat(0, bigs, scale_other)

        def other(number):
            columns = span(number, units // 2)
            grads[columns, :] = (grads[columns, :].astype(F32) + proj_grad(1, columns)).astype(
                BF16
            )
            if z_line:
                @pl.when(is_end)
                def _():
                    per = units // 2 // BLOCK
                    repeat(
                        number * per, (number + 1) * per, lambda step: grad_pair(step, grads).start()
                    )

        repeat(0, 2, other)

    first_ends[0] += units // BLOCK

    mlp_slope(1)
    pump_second_ends(1)

    @pl.when(is_first)
    def _():
        far_parts(2, mlp_back_part, per=tiles_per_big)

    @pl.when(is_second)
    def _():
        both_parts(2, mlp_back_part, per=tiles_per_big)

    pump_second_ends(1)

    pump_first(1)

    put_second_near(
        proj_grad_at + proj_half,
        units - proj_half,
        lambda index, columns: proj_grad(index, pl.ds(proj_half, units - proj_half)),
    )
    put_first(fc_grad_at, width, fc_grad)
    pump_first_ends(width // BLOCK)
    pump_first(1)

    pump_second_ends(1)

    def mlp_back(index):
        at = tile_rows(index)
        n2_grad = part_sum(2, index)
        hat, rate = normed(hidden[at, :])
        small[2:3, :] += column_sum(n2_grad * hat)
        small[3:4, :] += column_sum(n2_grad)
        held = ends[ends_grad, at, :].astype(F32) + norm_backward(
            n2_grad, hat, rate, ln2_gain_ref[...]
        )
        hidden_grad[at, :] = held
        r_grad[0, at, :] = (BRANCH_SCALE * held).astype(BF16)

        @pl.when(is_first)
        def _():
            share(2, index).start()

    def first_mid_step(step):
        mid_up(step)

        @pl.when(step >= BEHIND)
        def _():
            mid_down(step - BEHIND, (False, False))

    def second_end_step(step):
        gather_y(step)
        grad_pair(step, grads).start()

    def second_mid_step(step):
        gather_y(step)
        first_mid_step(step)

    def collect_with_pump(which, finish):
        base = first_mids[0]
        first_mids[0] += TILES * PUMP

        def beside(index):
            if z_line:
                @pl.when(is_mid)
                def _():
                    start = base + index * PUMP
                    repeat(start, start + PUMP, first_mid_step)

        collect(which, finish, beside)

    collect_with_pump(2, mlp_back)
    pump_first(1)
    pump_second_ends(1)

    def attention_backward(index):
        shards = set_weights(index)

        def project(number):
            at = big_rows(number)
            values = dot_nt(
                r_grad[set_rows(index), at, :], weight_of(shards, out_at, local_width)
            ).astype(BF16)
            for head in range(heads):
                head_rows[head, at, :] = values[:, head_columns(0, head)]

        repeat(0, bigs, project)

        for head in range(heads):
            shares = probs[index * heads + head]
            rows_grad = head_rows[head]
            qkv_grad[index, :, head_columns(2, head)] = dot_nn(shares, rows_grad).astype(BF16)
            share_grad = dot_nt(qkv[index, 2, head], rows_grad)
            wide = shares.astype(F32)
            product = wide * share_grad
            score_grad = (product - wide * jnp.sum(product, axis=0, keepdims=True)).astype(BF16)
            qkv_grad[index, :, head_columns(0, head)] = (
                dot_tn(score_grad, qkv[index, 1, head]) * scale
            ).astype(BF16)
            qkv_grad[index, :, head_columns(1, head)] = dot_nn(
                score_grad, qkv[index, 0, head]
            ).astype(BF16)
    def attention_back_part(index, shards, at):
        return dot_nn(qkv_grad[index, at, :], weight_of(shards, 0, qkv_rows))

    first_base, ends_base, mids_base = first_mids[0], second_ends[0], second_mids[0]
    first_mids[0] += 3 * PUMP
    second_ends[0] += 2 * PUMP
    second_mids[0] += 3

    def attention_turn(index):
        attention_backward(index)
        if z_line:
            @pl.when(first_mid)
            def _():
                start = first_base + 2 * PUMP * index
                repeat(start, start + PUMP, first_mid_step)

            @pl.when(second_end)
            def _():
                start = ends_base + PUMP * index
                repeat(start, start + PUMP, second_end_step)

            @pl.when(second_mid)
            def _():
                start = mids_base + 2 * index
                repeat(start, start + 2 - index, second_mid_step)

        @pl.when(jnp.logical_and(is_first, index == 0))
        def _():
            own_parts(3, attention_back_part)
            share_some(2, 0, TILES)
            put_first_inside(out_grad_at, local_width, out_grad)
            if z_line:
                @pl.when(is_mid)
                def _():
                    repeat(first_base + PUMP, first_base + 2 * PUMP, first_mid_step)

    repeat(0, 2, attention_turn)

    @pl.when(is_first)
    def _():
        far_parts(3, attention_back_part)

    @pl.when(is_second)
    def _():
        both_parts(3, attention_back_part)

    pump_first(PUMP)
    pump_second_ends(1)
    pump_second(1)

    put_first(qkv_grad_at, qkv_rows, in_grad)
    if z_line:
        @pl.when(is_first)
        def _():
            repeat(0, LENT, lambda index: lent(index).start())

    pump_first(PUMP)

    def attention_back(index):
        at = tile_rows(index)
        n1_grad = part_sum(3, index)
        hat, rate = normed(ends[ends_in, at, :].astype(F32))
        small[0:1, :] += column_sum(n1_grad * hat)
        small[1:2, :] += column_sum(n1_grad)
        results[1, at, :] = (
            hidden_grad[at, :] + norm_backward(n1_grad, hat, rate, ln1_gain_ref[...])
        ).astype(BF16)

        @pl.when(is_second)
        def _():
            cross(2 * index).start()
            cross(2 * index + 1).start()

    collect_with_pump(3, attention_back)
    pump_first(1)
    pump_second_ends(1)
    pump_second(1)

    leave = remote(
        results.at[1 - s, token_rows(across_m)], rows_recv, leave_send.at[0], leave_recv.at[0], across
    )
    @pl.when(is_first)
    def _():
        leave.start()

    sum_of_rows(5, m_grad)
    sum_of_rows(4, r_grad)
    for index in range(2):

        def sums(number, index=index):
            at = big_rows(number)
            set_sum(6, 0, index, pre_grad[index, at, :])
            set_sum(7, 0, index, qkv_grad[index, at, 0:local_width])
            set_sum(7, 2 * local_width, index, qkv_grad[index, at, 2 * local_width :])

        repeat(0, bigs, sums)
    small_y_copy = remote(small_other, small_y, leave_send.at[1], leave_recv.at[1], across)
    small_other[0:6, :] = small[0:6, :]
    small_y_copy.start()

    pump_first(2)
    pump_second_ends(1)
    pump_second(1)

    put_second_far(fc_grad_at, width, fc_grad)
    pump_second_ends(1)
    pump_second(1)

    @pl.when(is_second)
    def _():
        both_parts(FINE, mlp_part, per=2)

    pump_second_ends(2)
    pump_second(2)
    put_second_near(fc_grad_at, width, fc_grad)

    @pl.when(is_second)
    def _():
        collect(FINE, layer_out)

    pump_second_ends(2)
    pump_second(2)
    put_second_far(out_grad_at, local_width, out_grad)
    put_second_near(out_grad_at, local_width, out_grad)
    pump_second_ends(1)
    pump_second(1)
    put_second_far(qkv_grad_at, qkv_rows, in_grad)

    @pl.when(is_second)
    def _():
        leave.start()

    pump_second_ends(1)
    pump_second(1)
    put_second_near(qkv_grad_at, qkv_rows, in_grad)

    small_up = remote(small, small_pair, leave_send.at[2], leave_recv.at[2], pair)
    small_across = remote(small, small_mid, leave_send.at[3], leave_recv.at[3], middle)
    small_down = remote(small_mid, small_pair, leave_send.at[2], leave_recv.at[2], pair)

    rows_copy = pltpu.make_async_copy(rows_held, rows_out, local_sem.at[0])

    def small_copy(source):
        return pltpu.make_async_copy(source, small_out, local_sem.at[1])

    def rows_finish(wanted):
        @pl.when(wanted)
        def _():
            leave.wait_recv()
            rows_held[pl.ds(chip, 1)] = results[pl.ds(1 - s, 1), token_rows(m), :].astype(F32)
            rows_held[pl.ds(1 - chip, 1)] = rows_recv[...].astype(F32)[None]
            rows_copy.start()

    if z_line:
        @pl.when(is_end)
        def _():
            small_y_copy.wait_recv()
            small[...] += small_y[...]
            small_up.start()

        pump_ends(first_ends, len(first_order), first_end, False)
        pump_ends(second_ends, len(second_order), second_end, True)
        near, later = blocks * 2 // 3, blocks * 3 // 4
        pump_mids(first_mids, near, first_mid, False)
        pump_mids(second_mids, near, second_mid, True)

        @pl.when(is_mid)
        def _():
            small_y_copy.wait_recv()
            small_up.wait_recv()
            small[...] += small_y[...]
            small[...] += small_pair[...]
            small_across.start()

        pump_mids(first_mids, later, first_mid, False)
        pump_mids(second_mids, later, second_mid, True)
        rows_finish(is_first)

        @pl.when(is_mid)
        def _():
            small_across.wait_recv()
            small_mid[...] += small[...]
            small_down.start()
            small_copy(small_mid).start()

        pump_mids(first_mids, len(first_order), first_mid, False)
        pump_mids(second_mids, turn + LENT - 2, second_mid, True)
        rows_finish(is_second)
        pump_mids(second_mids, len(second_order), second_mid, True)

        def back(index, source):
            lent_back(index, source).wait_recv()
            grad_out(lent_from + index, source).start()

        @pl.when(is_mid)
        def _():
            last = small_from + small_count
            repeat(last - BEHIND, last, lambda step: mid_down(step, (False, True)))

        @pl.when(first_mid)
        def _():
            repeat(0, LENT, lambda index: back(index, grads_mid))

        def take(step, kind):
            grad_pair(step, grads_mid, kind[1]).wait_recv()
            deliver(step, grads_pair, kind)

        def small_take():
            small_down.wait_recv()
            small_copy(small_pair).start()

        @pl.when(first_end)
        def _():
            walk(first_order, 0, later, take)
            small_take()
            walk(first_order, later, len(first_order), take)
            repeat(0, LENT, lambda index: back(index, grads_pair))

        @pl.when(second_end)
        def _():
            walk(second_order, 0, turn, take)
            small_take()
            walk(second_order, turn, len(second_order), take)

    else:
        @pl.when(is_second)
        def _():
            repeat(0, blocks, gather_y)

        repeat(0, blocks, lambda step: grad_out(step, grads).start())
        rows_finish(s >= 0)
        small_y_copy.wait_recv()
        small[...] += small_y[...]
        small_copy(small).start()

    rows_copy.wait()
    small_copy(small).wait()
    own_rows = pl.ds(0, weight_rows)
    pltpu.make_async_copy(grads.at[own_rows], grads_out, grad_out_sem.at[0]).wait()

    entry_across(0).wait_send()
    entry_sibling(0).wait_send()
    entry_forward(0).wait_send()
    leave.wait_send()
    small_y_copy.wait_send()
    sent(part, part_send.at[0])
    sent(n1.at[0, pl.ds(0, big)], cross_send.at[0])
    sent(n1.at[0, pl.ds(0, big)], cross_core_send.at[0])

    @pl.when(is_first)
    def _():
        entry_across(1).wait_send()
        entry_sibling(1).wait_send()
        entry_forward(1).wait_send()
        sent(grads.at[pl.ds(0, 3 * big)], share_send.at[0])
        sent(grads.at[pl.ds(0, 2 * big)], share_core_send.at[0])
        for sem in (far_core_send, far_send, far_back_send):
            sent(grads.at[pl.ds(0, 4 * big)], sem.at[0])

    @pl.when(is_second)
    def _():
        bias_copy.wait_send()
        sent(weights.at[0, pl.ds(0, y_blocks * FETCH)], weight_y_send.at[0])
        if z_line:
            sent(weights.at[0, pl.ds(0, y_blocks * FETCH)], weight_z_send.at[0])
        sent(grads.at[own_rows], grad_y_send.at[0])

    if z_line:

        def stream_sent(count):
            sent(grads.at[pl.ds(0, count)], grad_pair_send.at[0])

            @pl.when(is_mid)
            def _():
                sent(grads.at[pl.ds(0, count)], grad_mid_send.at[0])

        @pl.when(is_first)
        def _():
            stream_sent(lent_from * BLOCK)
            sent(grads.at[pl.ds(0, LENT * BLOCK)], lent_send.at[0])

        @pl.when(is_second)
        def _():
            stream_sent(small_from * BLOCK)
            sent(grads.at[pl.ds(0, LENT * BLOCK)], back_send.at[0])

        @pl.when(is_end)
        def _():
            small_up.wait_send()

        @pl.when(is_mid)
        def _():
            small_across.wait_send()
            small_down.wait_send()


def finish_kernel(local_width, rows_ref, small_ref, grads_ref, *refs):
    outs, (held_rows, held, cast, in_sem, out_sem, rows_sem, held_small) = refs[:13], refs[13:20]
    lines, line_sem = refs[20:28], refs[28]
    rows_out, qkv_out, out_out, fc_out, proj_out = outs[:5]
    small_in = pltpu.make_async_copy(small_ref, held_small, line_sem.at[8])
    line_copies = [
        pltpu.make_async_copy(line, target, line_sem.at[number])
        for number, (line, target) in enumerate(zip(lines, outs[5:]))
    ]
    rows_in = pltpu.make_async_copy(rows_ref, held_rows, rows_sem.at[0])
    rows_copy = pltpu.make_async_copy(held_rows, rows_out, rows_sem.at[1])

    def at_block(number):
        return pl.ds(pl.multiple_of(number * FINISH, FINISH), FINISH)

    def fetch(number):
        at = at_block(number)
        return pltpu.make_async_copy(grads_ref.at[at], held.at[at], in_sem.at[number])

    def repeat(start, last, action):
        def step_of(step, carry):
            action(step)
            return carry

        lax.fori_loop(start, last, step_of, 0)

    blocks = held.shape[0] // FINISH
    repeat(0, blocks, lambda number: fetch(number).start())
    small_in.start()
    rows_in.start()
    first = 0
    puts = []
    for target in (proj_out, fc_out, out_out, qkv_out):
        count = target.shape[0] // FINISH

        def put(number, first=first, target=target):
            return pltpu.make_async_copy(
                cast.at[at_block(first + number)], target.at[at_block(number)], out_sem.at[first + number]
            )

        def step(number, first=first, put=put):
            fetch(first + number).wait()
            at = at_block(first + number)
            cast[at, :] = held[at, :].astype(F32)
            put(number).start()

        repeat(0, count, step)
        puts.append((count, put))
        first += count
    rows_in.wait()
    rows_copy.start()
    small_in.wait()
    lines[0][0:1, :] = held_small[7:8, 0:local_width]
    lines[0][1:2, :] = held_small[7:8, 2 * local_width : 3 * local_width]
    for row, line in enumerate(lines[1:]):
        line[...] = held_small[row : row + 1, :]
    for copy in line_copies:
        copy.start()
    for copy in line_copies:
        copy.wait()
    for count, put in puts:
        repeat(0, count, lambda number: put(number).wait())
    rows_copy.wait()


def local(
    z_line,
    boundary_in,
    order,
    ln1_gain,
    ln1_bias,
    w_qkv,
    qkv_bias,
    w_out,
    out_bias,
    ln2_gain,
    ln2_bias,
    w_fc,
    fc_bias,
    w_proj,
    proj_bias,
):
    _, micro, rows, width = boundary_in.shape
    local_width = w_qkv.shape[-1]
    units = w_fc.shape[-1]
    length = rows * lax.axis_size("mp")
    heads = local_width // HEAD_DIM
    weight_rows = 4 * local_width + width + units
    blocks = weight_rows // BLOCK
    stream_rows = weight_rows + LENT * BLOCK
    numbers = blocks + LENT + 2 * BLOCK // SMALL
    vmem = pltpu.VMEM
    dma = pltpu.SemaphoreType.DMA
    in_any = pl.BlockSpec(memory_space=pl.ANY)
    vectors = (ln1_gain, ln1_bias, qkv_bias, out_bias, ln2_gain, ln2_bias, fc_bias, proj_bias)
    out_rows, small, grads = pl.pallas_call(
        functools.partial(kernel, z_line),
        out_shape=(
            jax.ShapeDtypeStruct((micro, rows, width), F32),
            jax.ShapeDtypeStruct((8, width), F32),
            jax.ShapeDtypeStruct((weight_rows, width), BF16),
        ),
        in_specs=[in_any] * 14,
        out_specs=(in_any,) * 3,
        scratch_shapes=[
            pltpu.SMEM(order.shape, jnp.int32),
            *(vmem(vector.shape, F32) for vector in vectors),
            vmem((micro, rows, width), BF16),
            vmem((micro, rows, width), BF16),
            vmem((2, weight_rows, width), BF16),
            vmem((2, 8, width), F32),
            vmem((3, length, width), BF16),
            vmem((2, length, width), BF16),
            vmem((rows, width), BF16),
            vmem((micro, rows, width), F32),
            vmem((2, length, width), BF16),
            vmem((2, length, width), BF16),
            vmem((2, 3, heads, length, HEAD_DIM), BF16),
            vmem((2 * heads, length, length), BF16),
            vmem((heads, length, HEAD_DIM), BF16),
            vmem((2, length, local_width), BF16),
            vmem((length, width), F32),
            vmem((length, width), F32),
            vmem((2, length, units), BF16),
            vmem((2, length, units), BF16),
            vmem((2, length, width), BF16),
            vmem((2, length, width), BF16),
            vmem((2, length, 3 * local_width), BF16),
            vmem((4, length, width), BF16),
            vmem((4, length, width), BF16),
            vmem((stream_rows, width), BF16),
            vmem((weight_rows, width), BF16),
            vmem((weight_rows, width), BF16),
            vmem((stream_rows, width), BF16),
            vmem((stream_rows, width), BF16),
            vmem((8, width), F32),
            vmem((8, width), F32),
            vmem((8, width), F32),
            vmem((8, width), F32),
            vmem((8, width), F32),
            dma((5,)),
            dma((9,)),
            dma((7,)),
            dma((7,)),
            dma((1,)),
            dma((weight_rows // FETCH,)),
            dma((1,)),
            dma((1,)),
            dma((5 * TILES,)),
            dma((1,)),
            dma((1,)),
            dma((1,)),
            dma((1,)),
            dma((2,)),
            dma((1,)),
            dma((2 * TILES,)),
            dma((1,)),
            dma((2 * TILES,)),
            dma((4,)),
            dma((4,)),
            dma((1,)),
            dma((max(numbers - LENT, 15 * TILES),)),
            dma((1,)),
            dma((numbers,)),
            dma((1,)),
            dma((numbers,)),
            dma((1,)),
            dma((1,)),
            dma((LENT,)),
            dma((1,)),
        ],
        compiler_params=pltpu.CompilerParams(
            collective_id=0, has_side_effects=True, vmem_limit_bytes=63 * 2**20
        ),
        name="two_layers",
    )(
        order,
        boundary_in,
        ln1_gain,
        ln1_bias,
        jnp.swapaxes(w_qkv, 2, 3).reshape(1, 3 * local_width, width),
        qkv_bias,
        w_out,
        out_bias,
        ln2_gain,
        ln2_bias,
        w_fc,
        fc_bias,
        w_proj,
        proj_bias,
    )
    if not z_line:
        small, grads = lax.psum((small, grads), "dp")
    shapes = [
        (micro, rows, width),
        (3 * local_width, width),
        (local_width, width),
        (width, units),
        (units, width),
        (2, local_width),
    ] + [(1, width)] * 6 + [(1, units)]
    (
        out_rows,
        qkv_grad,
        out_grad,
        fc_grad,
        proj_grad,
        qkv_bias_grad,
        ln1_gain_grad,
        ln1_bias_grad,
        ln2_gain_grad,
        ln2_bias_grad,
        out_bias_grad,
        proj_bias_grad,
        fc_bias_grad,
    ) = pl.pallas_call(
        functools.partial(finish_kernel, local_width),
        out_shape=[jax.ShapeDtypeStruct(shape, F32) for shape in shapes],
        in_specs=[in_any] * 3,
        out_specs=[in_any] * 13,
        scratch_shapes=[
            vmem((micro, rows, width), F32),
            vmem((weight_rows, width), BF16),
            vmem((weight_rows, width), F32),
            dma((weight_rows // FINISH,)),
            dma((weight_rows // FINISH,)),
            dma((2,)),
            vmem((8, width), F32),
        ]
        + [vmem(shape, F32) for shape in shapes[5:]]
        + [dma((9,))],
        compiler_params=pltpu.CompilerParams(vmem_limit_bytes=62 * 2**20),
        name="finish",
    )(out_rows, small, grads)
    return (
        out_rows[None],
        ln1_gain_grad,
        ln1_bias_grad,
        jnp.swapaxes(qkv_grad.reshape(1, 3, local_width, width), 2, 3),
        qkv_bias_grad[None],
        out_grad[None],
        out_bias_grad,
        ln2_gain_grad,
        ln2_bias_grad,
        fc_grad[None],
        fc_bias_grad,
        proj_grad[None],
        proj_bias_grad,
    )


def solution(mesh):
    return jax.shard_map(
        functools.partial(local, mesh.shape["dp"] == 4),
        mesh=mesh,
        in_specs=(
            P("section", "dp", "mp", None),
            P("dp", None),
            P("section", None),
            P("section", None),
            P("section", None, None, "mp"),
            P("section", None, "mp"),
            P("section", "mp", None),
            P("section", None),
            P("section", None),
            P("section", None),
            P("section", None, "mp"),
            P("section", "mp"),
            P("section", "mp", None),
            P("section", None),
        ),
        out_specs=(
            P("section", "dp", "mp", None),
            P("section", None),
            P("section", None),
            P("section", None, None, "mp"),
            P("section", None, "mp"),
            P("section", "mp", None),
            P("section", None),
            P("section", None),
            P("section", None),
            P("section", None, "mp"),
            P("section", "mp"),
            P("section", "mp", None),
            P("section", None),
        ),
        check_vma=False,
    )
```

```python
import functools

import jax
import jax.numpy as jnp
from jax import lax
from jax.experimental import pallas as pl
from jax.experimental.pallas import tpu as pltpu
from jax.sharding import PartitionSpec as P

HEAD_DIM = 64
BRANCH_SCALE = 0.14433756729740643
NORM_EPS = 1e-05
GELU_RATE = 0.7978845608028654
GELU_CUBE = 0.044715
NEGATIVE = -1e30
BLOCK = 48
PUMP = 2
FINISH = 192
FETCH = 96
TILES = 4
FINE = 1
SMALL = 16
LENT = 10
BEHIND = 4
MESH = pl.DeviceIdType.MESH
BF16 = jnp.bfloat16
F32 = jnp.float32


def dot_nn(a, b):
    return lax.dot_general(a, b, (((1,), (0,)), ((), ())), preferred_element_type=F32)


def dot_nt(a, b):
    return lax.dot_general(a, b, (((1,), (1,)), ((), ())), preferred_element_type=F32)


def dot_tn(a, b):
    return lax.dot_general(a, b, (((0,), (0,)), ((), ())), preferred_element_type=F32)


def normed(values):
    center = values - jnp.mean(values, axis=-1, keepdims=True)
    rate = lax.rsqrt(jnp.mean(center * center, axis=-1, keepdims=True) + NORM_EPS)
    return center * rate, rate


def norm_backward(grad, hat, rate, gain):
    scaled = grad * gain
    return rate * (
        scaled
        - jnp.mean(scaled, axis=-1, keepdims=True)
        - hat * jnp.mean(scaled * hat, axis=-1, keepdims=True)
    )


def column_sum(values):
    return jnp.sum(values.astype(F32), axis=0, keepdims=True)


def remote(src, dst, send_sem, recv_sem, device):
    return pltpu.make_async_remote_copy(
        src_ref=src,
        dst_ref=dst,
        send_sem=send_sem,
        recv_sem=recv_sem,
        device_id=device,
        device_id_type=MESH,
    )


def kernel(
    z_line,
    order_hbm,
    boundary_ref,
    ln1_gain_hbm,
    ln1_bias_hbm,
    w_qkv_ref,
    qkv_bias_hbm,
    w_out_ref,
    out_bias_hbm,
    ln2_gain_hbm,
    ln2_bias_hbm,
    w_fc_ref,
    fc_bias_hbm,
    w_proj_ref,
    proj_bias_hbm,
    rows_out,
    small_out,
    grads_out,
    order_ref,
    ln1_gain_ref,
    ln1_bias_ref,
    qkv_bias_ref,
    out_bias_ref,
    ln2_gain_ref,
    ln2_bias_ref,
    fc_bias_ref,
    proj_bias_ref,
    raw,
    slots,
    weights,
    biases,
    ends,
    results,
    rows_recv,
    rows_held,
    n1,
    n2,
    qkv,
    probs,
    head_rows,
    attended,
    hidden,
    hidden_grad,
    act,
    slope,
    m_grad,
    r_grad,
    qkv_grad,
    part,
    part_recv,
    grads,
    grads_other,
    grads_y,
    grads_pair,
    grads_mid,
    small,
    small_other,
    small_y,
    small_pair,
    small_mid,
    local_sem,
    vector_sem,
    entry_send,
    entry_recv,
    weight_y_send,
    weight_recv,
    weight_z_send,
    part_send,
    part_recv_sem,
    far_core_send,
    far_send,
    far_back_send,
    share_send,
    share_core_send,
    cross_send,
    cross_recv,
    cross_core_send,
    cross_core_recv,
    leave_send,
    leave_recv,
    grad_y_send,
    grad_y_recv,
    grad_pair_send,
    grad_pair_recv,
    grad_mid_send,
    grad_mid_recv,
    grad_out_sem,
    lent_send,
    lent_recv,
    back_send,
):
    s, d, m = lax.axis_index("section"), lax.axis_index("dp"), lax.axis_index("mp")
    core, chip = lax.rem(m, 2), lax.div(m, 2)
    half = lax.rem(d, 2)
    across_m = 2 * (1 - chip) + core
    sibling = (s, d, 2 * chip + 1 - core)
    across = (s, d, across_m)
    other_section = (1 - s, d, m)
    pair = (s, d + 1 - 2 * half, m)
    middle = (s, 3 - d, m)
    is_first, is_second = s == 0, s == 1
    is_mid = lax.div(d + 1, 2) == 1
    is_end = lax.div(d + 1, 2) != 1

    rows = boundary_ref.shape[2]
    length, width = n1.shape[1:]
    tile = length // TILES
    piece = tile // 2
    big = length // 2
    local_width = attended.shape[2]
    units = act.shape[2]
    heads = local_width // HEAD_DIM
    tiles_per_big, bigs = big // tile, length // big
    scale = HEAD_DIM ** (-0.5)
    qkv_rows = 3 * local_width
    out_at, fc_at, proj_at = qkv_rows, qkv_rows + local_width, qkv_rows + local_width + width
    weight_rows = weights.shape[1]
    blocks = weight_rows // BLOCK
    ends_in, ends_grad = 2 * s, 2 * (1 - s)

    def set_rows(index):
        return index * (1 - s)

    def set_weights(index):
        return index * s

    def span(index, count):
        start = index * count
        return pl.ds(start if isinstance(start, int) else pl.multiple_of(start, count), count)

    def tile_rows(index):
        return span(index, tile)

    def big_rows(index):
        return span(index, big)

    def tile_of(which):
        return tile // 2 if which == FINE else tile

    def count_of(which):
        return length // tile_of(which)

    def number_of(which, index):
        return which * TILES + (TILES if which > FINE else 0) + index

    def rows_of(which, index):
        return span(index, tile_of(which))

    def piece_rows(which, index, core_of, base=0):
        size = tile_of(which) // 2
        return pl.ds(pl.multiple_of(base + (2 * index + core_of) * size, size), size)

    partners = [sibling, across, other_section]
    if z_line:
        partners += [pair, middle]
    barrier = pltpu.get_barrier_semaphore()
    for device in partners:
        pl.semaphore_signal(barrier, inc=1, device_id=device, device_id_type=MESH)

    loads = [
        pltpu.make_async_copy(boundary_ref.at[0], raw, local_sem.at[0]),
        pltpu.make_async_copy(
            w_qkv_ref.at[0], weights.at[0, pl.ds(0, qkv_rows)], local_sem.at[1]
        ),
        pltpu.make_async_copy(
            w_out_ref.at[0], weights.at[0, pl.ds(out_at, local_width)], local_sem.at[2]
        ),
        pltpu.make_async_copy(w_fc_ref.at[0], weights.at[0, pl.ds(fc_at, width)], local_sem.at[3]),
        pltpu.make_async_copy(
            w_proj_ref.at[0], weights.at[0, pl.ds(proj_at, units)], local_sem.at[4]
        ),
    ]
    vector_loads = [
        pltpu.make_async_copy(source, target, vector_sem.at[number])
        for number, (source, target) in enumerate(
            (
                (ln1_gain_hbm, ln1_gain_ref),
                (ln1_bias_hbm, ln1_bias_ref),
                (qkv_bias_hbm, qkv_bias_ref),
                (out_bias_hbm, out_bias_ref),
                (ln2_gain_hbm, ln2_gain_ref),
                (ln2_bias_hbm, ln2_bias_ref),
                (fc_bias_hbm, fc_bias_ref),
                (proj_bias_hbm, proj_bias_ref),
            )
        )
    ]
    order_load = pltpu.make_async_copy(order_hbm, order_ref, vector_sem.at[8])
    for load in [order_load] + loads[:1] + vector_loads + loads[1:]:
        load.start()

    biases[0] = jnp.zeros_like(biases[0])
    small[...] = jnp.zeros_like(small)
    small_other[...] = jnp.zeros_like(small_other)

    order_load.wait()
    loads[0].wait()
    for slot in range(2):
        picked = jnp.where(is_first, order_ref[0, slot], slot).astype(F32)
        slots[slot] = (
            raw[0].astype(F32) * (1.0 - picked) + raw[1].astype(F32) * picked
        ).astype(BF16)

    pl.semaphore_wait(barrier, len(partners))

    def token_rows(index):
        return pl.ds(pl.multiple_of(index * rows, rows), rows)

    def entry_across(which):
        slot = (1 - chip) * (1 - which) + chip * which
        return remote(
            slots.at[slot],
            ends.at[which, token_rows(m)],
            entry_send.at[which],
            entry_recv.at[which],
            across,
        )

    def entry_sibling(which):
        slot = chip * (1 - which) + (1 - chip) * which
        return remote(
            slots.at[slot],
            ends.at[which, token_rows(m)],
            entry_send.at[2 + which],
            entry_recv.at[2 + which],
            sibling,
        )

    def entry_forward(which):
        at = token_rows(across_m)
        return remote(
            ends.at[which, at],
            ends.at[which, at],
            entry_send.at[4 + which],
            entry_recv.at[4 + which],
            sibling,
        )

    bias_copy = remote(biases.at[0], biases.at[1], entry_send.at[6], entry_recv.at[6], across)

    def entry_start(which):
        entry_across(which).start()
        entry_sibling(which).start()
        slot = chip if which == 0 else 1 - chip
        ends[which, token_rows(m), :] = slots[slot]

    def entry_pass(which):
        entry_across(which).wait_recv()
        entry_forward(which).start()

    def entry_finish(which):
        entry_pass(which)
        entry_sibling(which).wait_recv()
        entry_forward(which).wait_recv()

    @pl.when(is_first)
    def _():
        entry_start(1)
        entry_start(0)

    y_blocks = weight_rows // FETCH // (2 if z_line else 1)

    def weight_block(index):
        return pl.ds(pl.multiple_of(index * BLOCK, BLOCK), BLOCK)

    def near_block(step):
        return span(2 * step + half if z_line else step, FETCH)

    def weight_y(step):
        return remote(
            weights.at[0, near_block(step)],
            weights.at[1, near_block(step)],
            weight_y_send.at[0],
            weight_recv.at[step],
            across,
        )

    def weight_z(step):
        return remote(
            weights.at[1, near_block(step)],
            weights.at[1, near_block(step)],
            weight_z_send.at[0],
            weight_recv.at[y_blocks + step],
            pair,
        )

    def repeat(first, last, action):
        def step_of(step, carry):
            action(step)
            return carry

        lax.fori_loop(first, last, step_of, 0)

    late_step = proj_at * y_blocks // weight_rows
    y_done = [0]

    def weight_need(row):
        steps = row * y_blocks // weight_rows
        if z_line and steps > y_done[0]:
            first, y_done[0] = y_done[0], steps

            @pl.when(is_second)
            def _():
                repeat(first, steps, lambda step: weight_z(step).wait_recv())

    def weight_pass(step):
        weight_y(step).wait_recv()
        if z_line:
            weight_z(step).start()

    for load in vector_loads + loads[1:]:
        load.wait()
    biases[0, 0:1, :] = fc_bias_ref[...]
    biases[0, 1:2, 0:local_width] = qkv_bias_ref[0, 0:1, :]
    biases[0, 2:3, 0:local_width] = qkv_bias_ref[0, 1:2, :]

    def sent(source, sem):
        remote(source, source, sem, sem, sibling).wait_send()

    def arrived(target, sem):
        remote(target, target, sem, sem, sibling).wait_recv()

    def cross(index):
        at = piece_rows(FINE, index, core)
        return remote(
            results.at[s, at],
            ends.at[2, at],
            cross_send.at[0],
            cross_recv.at[index],
            other_section,
        )

    def cross_core(index):
        at = piece_rows(FINE, index, core)
        return remote(
            ends.at[2, at],
            ends.at[2, at],
            cross_core_send.at[0],
            cross_core_recv.at[index],
            sibling,
        )

    shared = (n2, m_grad, r_grad)

    def share(which, index):
        at = piece_rows(which, index, core)
        source = ends.at[2, at] if which == FINE else shared[which].at[0, at]
        return remote(
            source,
            shared[which].at[1, at],
            share_send.at[0],
            weight_recv.at[number_of(which, index)],
            across,
        )

    def share_core(which, index):
        at = piece_rows(which, index, core)
        return remote(
            shared[which].at[1, at],
            shared[which].at[1, at],
            share_core_send.at[1 if which == FINE else 0],
            weight_recv.at[4 * TILES + (index if which == 0 else TILES + which)],
            sibling,
        )

    def share_some(which, start, count):
        def forward(index):
            share(which, start + index).wait_recv()
            share_core(which, start + index).start()

        repeat(0, count, forward)
        if which == 0:
            repeat(0, count, lambda index: share_core(which, start + index).wait_recv())
        else:
            arrived(shared[which].at[1, pl.ds(0, big)], weight_recv.at[5 * TILES + which])

    def part_copy(which, index):
        at = rows_of(which, index)
        return remote(
            part.at[which, at],
            part_recv.at[which, at],
            part_send.at[0],
            part_recv_sem.at[number_of(which, index)],
            sibling,
        )

    def spare_rows(which, index, core_of):
        return piece_rows(which, index, core_of, which * length)

    def far_core(which, index):
        return remote(
            grads_y.at[spare_rows(which, index, 1 - core)],
            grads_other.at[spare_rows(which, index, 1 - core)],
            far_core_send.at[0],
            grad_y_recv.at[number_of(which, index)],
            sibling,
        )

    def far(which, index):
        return remote(
            grads_y.at[spare_rows(which, index, core)],
            weights.at[1, spare_rows(which, index, core)],
            far_send.at[0],
            grad_y_recv.at[5 * TILES + number_of(which, index)],
            across,
        )

    def far_back(which, index):
        at = spare_rows(which, index, core)
        return remote(
            weights.at[1, at],
            weights.at[1, at],
            far_back_send.at[0],
            grad_y_recv.at[10 * TILES + number_of(which, index)],
            sibling,
        )

    def far_pass(which, index):
        far_core(which, index).wait_recv()
        at = spare_rows(which, index, core)
        grads_y[at, :] = (grads_y[at, :].astype(F32) + grads_other[at, :].astype(F32)).astype(BF16)
        far(which, index).start()

    def part_sum(which, index):
        at = rows_of(which, index)
        near = part[which, at, :].astype(F32) + part_recv[which, at, :].astype(F32)
        size = tile_of(which)
        other = weights[
            1, pl.ds(pl.multiple_of(which * length + index * size, size), size), :
        ].astype(F32)
        return near + jnp.where(is_first, other, 0.0)

    def far_parts(which, value_of, per=1, before=None):
        def step(number):
            if before is not None:
                before(number)
            size = per * tile_of(which)
            grads_y[pl.ds(pl.multiple_of(which * length + number * size, size), size), :] = (
                value_of(1, 0, span(number, size)).astype(BF16)
            )
            for index in range(per):
                far_core(which, number * per + index).start()

            @pl.when(number > 0)
            def _():
                for index in range(per):
                    far_pass(which, (number - 1) * per + index)

        repeat(0, count_of(which) // per, step)
        for index in range(per):
            far_pass(which, count_of(which) - per + index)

    def own_parts(which, value_of, per=1):
        def step(number):
            at = span(number, per * tile_of(which))
            part[which, at, :] = value_of(0, 0, at).astype(BF16)
            for index in range(per):
                part_copy(which, number * per + index).start()

        repeat(0, count_of(which) // per, step)

    def both_parts(which, value_of, per=1):
        def step(number):
            at = span(number, per * tile_of(which))
            part[which, at, :] = (value_of(0, 0, at) + value_of(1, 1, at)).astype(BF16)
            for index in range(per):
                part_copy(which, number * per + index).start()

        repeat(0, count_of(which) // per, step)

    def collect(which, finish, beside=None, start=0, last=None):
        last = count_of(which) if last is None else last

        def far_next(index):
            far(which, index).wait_recv()
            far_back(which, index).start()

        @pl.when(is_first)
        def _():
            far_next(start)

        def step(index):
            @pl.when(is_first)
            def _():
                @pl.when(index + 1 < last)
                def _():
                    far_next(index + 1)

                if beside is not None:
                    beside(index)
                far_back(which, index).wait_recv()

            part_copy(which, index).wait_recv()
            finish(index)

        repeat(start, last, step)

    def weight_of(shards, first, count):
        return weights[shards, first : first + count, :]

    def scale_grad(index):
        at = rows_of(FINE, index)
        m_grad[0, at, :] = (BRANCH_SCALE * ends[ends_grad, at, :].astype(F32)).astype(BF16)

    @pl.when(is_second)
    def _():
        bias_copy.start()
        repeat(0, late_step, lambda step: weight_y(step).start())
        entry_start(0)
        repeat(late_step, y_blocks, lambda step: weight_y(step).start())
        repeat(0, late_step, weight_pass)
        bias_copy.wait_recv()
        entry_finish(0)
        repeat(0, count_of(FINE), scale_grad)
        repeat(late_step, y_blocks - bigs, weight_pass)

    def norm_big(which, source, number):
        def step(index):
            at = span(number * (big // tile) + index, tile)
            hat, _ = normed(ends[source, at, :].astype(F32))
            n1[which, at, :] = (hat * ln1_gain_ref[...] + ln1_bias_ref[...]).astype(BF16)

        repeat(0, big // tile, step)

    def cross_receive(start, last, action, on=None):
        def pass_on(index):
            cross(index).wait_recv()
            cross_core(index).start()
            if on is not None:
                on(index)

        pass_on(start)

        def step(index):
            @pl.when(index + 1 < last)
            def _():
                pass_on(index + 1)

            cross_core(index).wait_recv()
            action(index)

        repeat(start, last, step)

    causal = lax.broadcasted_iota(jnp.int32, (length, length), 1) >= lax.broadcasted_iota(
        jnp.int32, (length, length), 0
    )

    def bias_of(shards, row, count):
        return biases[shards, row : row + 1, 0:count]

    def head_columns(kind, head):
        first = kind * local_width + head * HEAD_DIM
        return slice(first, first + HEAD_DIM)

    def project(index, number):
        source, shards = set_rows(index), set_weights(index)
        at = big_rows(number)
        for kind in range(3):
            values = dot_nt(n1[source, at, :], weight_of(shards, kind * local_width, local_width))
            if kind == 0:
                values = values + bias_of(shards, 1, local_width)
            if kind == 2:
                values = values + bias_of(shards, 2, local_width)
            values = values.astype(BF16)
            if kind == 0:
                values = (values.astype(F32) * scale).astype(BF16)
            for head in range(heads):
                qkv[index, kind, head, at, :] = values[:, head_columns(0, head)]

    def attention_forward(index):
        for head in range(heads):
            scores = dot_nt(qkv[index, 1, head], qkv[index, 0, head])
            scores = jnp.where(causal, scores, NEGATIVE)
            raised = jnp.exp(scores - jnp.max(scores, axis=0, keepdims=True))
            shares = raised * (1.0 / jnp.sum(raised, axis=0, keepdims=True))
            shares = shares.astype(BF16)
            probs[index * heads + head] = shares
            attended[index, :, head_columns(0, head)] = dot_tn(
                shares, qkv[index, 2, head]
            ).astype(BF16)

    weight_need(out_at)

    @pl.when(is_second)
    def _():
        def step(number):
            def pass_on(index):
                cross(index).wait_recv()
                cross_core(index).start()

            per = count_of(FINE) // bigs
            repeat(number * per, (number + 1) * per, pass_on)
            repeat(
                number * per, (number + 1) * per, lambda index: cross_core(index).wait_recv()
            )
            norm_big(0, 2, number)
            repeat(0, 2, lambda index: project(index, number))
            weight_pass(y_blocks - bigs + number)

        repeat(0, bigs, step)

    @pl.when(is_first)
    def _():
        def step(index):
            entry_sibling(index).wait_recv()
            norm_big(index, index, chip)
            project(index, chip)

        repeat(0, 2, step)
        entry_pass(1)
        entry_forward(1).wait_recv()
        norm_big(1, 1, 1 - chip)
        project(1, 1 - chip)

    attention_forward(1)

    def attention_part(index, shards, at):
        return dot_nn(attended[index, at, :], weight_of(shards, out_at, local_width))

    @pl.when(is_first)
    def _():
        far_parts(0, attention_part)
        entry_pass(0)
        entry_forward(0).wait_recv()
        norm_big(0, 0, 1 - chip)
        project(0, 1 - chip)

    attention_forward(0)

    weight_need(fc_at)

    @pl.when(is_first)
    def _():
        own_parts(0, attention_part)

    @pl.when(is_second)
    def _():
        both_parts(0, attention_part)

    def attention_out(index):
        at = tile_rows(index)
        held = ends[ends_in, at, :].astype(F32) + BRANCH_SCALE * (
            part_sum(0, index) + out_bias_ref[...]
        )
        hidden[at, :] = held
        hat, _ = normed(held)
        n2[0, at, :] = (hat * ln2_gain_ref[...] + ln2_bias_ref[...]).astype(BF16)

        @pl.when(is_first)
        def _():
            share(0, index).start()

    def activate(index, source, shards, at):
        u = dot_nn(n2[source, at, :], weight_of(shards, fc_at, width)) + bias_of(shards, 0, units)
        square = u * u
        bent = jnp.tanh(GELU_RATE * (u + GELU_CUBE * u * square))
        act[index, at, :] = (0.5 * u * (1.0 + bent)).astype(BF16)
        slope[index, at, :] = (
            0.5 * (1.0 + bent)
            + (0.5 * GELU_RATE) * u * (1.0 - bent * bent) * (1.0 + (3.0 * GELU_CUBE) * square)
        ).astype(BF16)

    weight_need(proj_at)

    def first_half(number):
        collect(
            0, attention_out, start=number * tiles_per_big, last=(number + 1) * tiles_per_big
        )
        activate(set_weights(1), 0, set_weights(1), big_rows(number))

    repeat(0, bigs, first_half)

    def mlp_part(index, shards, at):
        return dot_nn(act[index, at, :], weight_of(shards, proj_at, units))

    def other_activate(number):
        share_some(0, number, 1)
        activate(1, 1, 0, span(number, tile))

    @pl.when(is_first)
    def _():
        own_parts(FINE, mlp_part, per=2)
        far_parts(FINE, mlp_part, per=2, before=other_activate)

    weight_need(weight_rows)

    proj_grad_at, fc_grad_at = 0, units
    out_grad_at = fc_grad_at + width
    qkv_grad_at = out_grad_at + local_width

    lent_from = blocks - LENT
    small_from, small_count = blocks + LENT, 2 * BLOCK // SMALL
    small_row = (lent_from - 2) * BLOCK

    def block_rows(step, is_small=False):
        if is_small:
            start = small_row + (step - small_from) * SMALL
            return pl.ds(start if isinstance(start, int) else pl.multiple_of(start, SMALL), SMALL)
        return weight_block(step)

    def grad_y(step, is_small=False):
        return remote(
            grads_other.at[block_rows(step, is_small)],
            grads_y.at[block_rows(step, is_small)],
            grad_y_send.at[0],
            grad_y_recv.at[step - LENT if is_small else step],
            across,
        )

    def grad_pair(step, source, is_small=False):
        return remote(
            source.at[block_rows(step, is_small)],
            grads_pair.at[block_rows(step, is_small)],
            grad_pair_send.at[0],
            grad_pair_recv.at[step],
            pair,
        )

    def grad_mid(step, is_small=False):
        return remote(
            grads.at[block_rows(step, is_small)],
            grads_mid.at[block_rows(step, is_small)],
            grad_mid_send.at[0],
            grad_mid_recv.at[step],
            middle,
        )

    def grad_out(step, source, is_small=False):
        at = block_rows(step, is_small)
        return pltpu.make_async_copy(source.at[at], grads_out.at[at], grad_out_sem.at[0])

    def add_into(target, source, step, is_small):
        at = block_rows(step, is_small)
        target[at, :] = (target[at, :].astype(F32) + source[at, :].astype(F32)).astype(BF16)

    def gather_y(step, is_small=False):
        grad_y(step, is_small).wait_recv()
        add_into(grads, grads_y, step, is_small)

    def mid_up(step, is_small=False):
        grad_pair(step, grads, is_small).wait_recv()
        add_into(grads, grads_pair, step, is_small)
        grad_mid(step, is_small).start()

    def kind_of(step):
        return blocks <= step < small_from, step >= small_from

    def mid_down(step, kind):
        grad_mid(step, kind[1]).wait_recv()
        add_into(grads_mid, grads, step, kind[1])
        grad_pair(step, grads_mid, kind[1]).start()
        deliver(step, grads_mid, kind)

    def deliver(step, source, kind):
        if kind[0]:
            lent_back(step - blocks, source).start()
        else:
            grad_out(step, source, kind[1]).start()

    def lent(index):
        return remote(
            grads.at[weight_block(lent_from + index)],
            grads.at[weight_block(blocks + index)],
            lent_send.at[0],
            lent_recv.at[index],
            other_section,
        )

    def lent_back(index, source):
        return remote(
            source.at[weight_block(blocks + index)],
            source.at[weight_block(lent_from + index)],
            back_send.at[0],
            lent_recv.at[index],
            other_section,
        )

    small_blocks = range(small_from, small_from + small_count)
    turn = blocks - 4
    first_order = [*range(lent_from - 2), *small_blocks]
    second_order = [
        *range(lent_from - 2),
        *range(lent_from, turn),
        *range(blocks, small_from),
        *range(turn, blocks),
        *small_blocks,
    ]

    def runs(order, start, last, behind=0):
        cuts = [start]
        for place in range(start + 1, last):
            for back in (place, place - behind):
                if back > 0 and order[back] != order[back - 1] + 1 and cuts[-1] != place:
                    cuts.append(place)
        cuts.append(last)
        return [
            (a, b, order[a] - a, order[max(a - behind, 0)] - max(a - behind, 0))
            for a, b in zip(cuts, cuts[1:])
            if b > a
        ]

    first_ends, first_mids, second_ends, second_mids = [0], [0], [0], [0]
    first_end, second_end = jnp.logical_and(is_first, is_end), jnp.logical_and(is_second, is_end)
    first_mid, second_mid = jnp.logical_and(is_first, is_mid), jnp.logical_and(is_second, is_mid)

    def gather(step, kind):
        if kind[0]:
            lent(step - blocks).wait_recv()
        else:
            gather_y(step, kind[1])

    def walk(order, start, last, action):
        for a, b, offset, _ in runs(order, start, last):
            kind = kind_of(a + offset)
            repeat(a + offset, b + offset, functools.partial(action, kind=kind))

    def pump_ends(done, last, wanted, second):
        start, done[0] = done[0], last
        if z_line:
            def up(step, kind):
                if second:
                    gather(step, kind)
                grad_pair(step, grads, kind[1]).start()

            @pl.when(wanted)
            def _():
                walk(second_order if second else first_order, start, last, up)

    def pump_mids(done, last, wanted, second):
        start, done[0] = done[0], last
        if z_line:
            @pl.when(wanted)
            def _():
                order = second_order if second else first_order
                for a, b, offset, old in runs(order, start, last, BEHIND):

                    def step(place, a=a, offset=offset, old=old):
                        if second:
                            gather(place + offset, kind_of(a + offset))
                        mid_up(place + offset, kind_of(a + offset)[1])

                        @pl.when(place >= BEHIND)
                        def _():
                            mid_down(place - BEHIND + old, kind_of(max(a - BEHIND, 0) + old))

                    repeat(a, b, step)

    def pump_first_ends(count):
        pump_ends(first_ends, first_ends[0] + count, first_end, False)

    def pump_first(count):
        pump_mids(first_mids, first_mids[0] + count, first_mid, False)

    def pump_second_ends(count):
        pump_ends(second_ends, second_ends[0] + count, second_end, True)

    def pump_second(count):
        pump_mids(second_mids, second_mids[0] + count, second_mid, True)

    def cut_columns(count):
        return (2, count // 2) if count % 768 == 0 else (1, count)

    def put_first_inside(first, count, value_of):
        steps, columns = cut_columns(count)

        def step(number):
            at = span(number, columns)
            grads[pl.ds(first + number * columns, columns), :] = (
                value_of(0, at) + value_of(1, at)
            ).astype(BF16)

        repeat(0, steps, step)

    def put_first(first, count, value_of):
        @pl.when(is_first)
        def _():
            put_first_inside(first, count, value_of)

    def put_second(target, index, first, count, value_of, after=None):
        steps, columns = cut_columns(count)

        def step(number):
            start = first + number * columns
            target[pl.ds(start, columns), :] = value_of(index, span(number, columns)).astype(BF16)
            if after is not None:
                after(first // BLOCK + number * (columns // BLOCK), columns // BLOCK)

        @pl.when(is_second)
        def _():
            repeat(0, steps, step)

    def put_second_far(first, count, value_of):
        def leave_blocks(start, number):
            if z_line and first == qkv_grad_at:
                repeat(first // BLOCK, lent_from - 2, lambda step: grad_y(step).start())
                repeat(lent_from, blocks, lambda step: grad_y(step).start())
                repeat(
                    small_from, small_from + small_count, lambda step: grad_y(step, True).start()
                )
            else:
                repeat(start, start + number, lambda step: grad_y(step).start())

        put_second(grads_other, 1, first, count, value_of, leave_blocks)

    def put_second_near(first, count, value_of):
        put_second(grads, 0, first, count, value_of)

    def set_sum(row, column, index, values):
        total = column_sum(values)
        columns = slice(column, column + total.shape[1])
        if index == 0:
            small[row : row + 1, columns] += total
        else:
            @pl.when(is_first)
            def _():
                small[row : row + 1, columns] += total

            @pl.when(is_second)
            def _():
                small_other[row : row + 1, columns] += total

    def proj_grad(index, columns):
        return dot_tn(act[index, :, columns], m_grad[set_rows(index)])

    def fc_grad(index, columns):
        return dot_tn(n2[set_rows(index), :, columns], pre_grad[index])

    def out_grad(index, columns):
        return dot_tn(attended[index, :, columns], r_grad[set_rows(index)])

    def in_grad(index, columns):
        return dot_tn(qkv_grad[index, :, columns], n1[set_rows(index)])

    put_second_far(proj_grad_at, units, proj_grad)

    @pl.when(is_second)
    def _():
        repeat(0, bigs, lambda number: activate(0, 0, 0, big_rows(number)))

    proj_half = units // 2
    put_second_near(proj_grad_at, proj_half, proj_grad)

    def layer_out(index):
        at = rows_of(FINE, index)
        results[0, at, :] = (
            hidden[at, :] + BRANCH_SCALE * (part_sum(FINE, index) + proj_bias_ref[...])
        ).astype(BF16)

        @pl.when(is_first)
        def _():
            cross(index).start()

    @pl.when(is_first)
    def _():
        collect(FINE, layer_out)

    @pl.when(is_first)
    def _():
        cross_receive(0, count_of(FINE), scale_grad, lambda index: share(FINE, index).start())

        def own(number):
            columns = span(number, units // 2)
            grads[span(number, units // 2), :] = proj_grad(0, columns).astype(BF16)

        repeat(0, 2, own)

    pre_grad = slope

    def mlp_slope(index):
        def step(number):
            at = big_rows(number)
            values = (
                slope[index, at, :].astype(F32)
                * dot_nt(
                    m_grad[set_rows(index), at, :], weight_of(set_weights(index), proj_at, units)
                )
            ).astype(BF16)
            pre_grad[index, at, :] = values

        repeat(0, bigs, step)

    def mlp_back_part(index, shards, at):
        return dot_nt(pre_grad[index, at, :], weight_of(shards, fc_at, width))

    def sum_of_rows(row, source):
        def step(number):
            small[row : row + 1, :] += column_sum(source[0, big_rows(number), :])

        repeat(0, bigs, step)

    mlp_slope(0)

    @pl.when(is_first)
    def _():
        own_parts(2, mlp_back_part, per=tiles_per_big)
        share_some(FINE, 0, count_of(FINE))
        sent(m_grad.at[1, pl.ds(0, big)], share_core_send.at[1])

        def scale_other(number):
            at = big_rows(number)
            m_grad[1, at, :] = (BRANCH_SCALE * m_grad[1, at, :].astype(F32)).astype(BF16)

        repeat(0, bigs, scale_other)

        def other(number):
            columns = span(number, units // 2)
            grads[columns, :] = (grads[columns, :].astype(F32) + proj_grad(1, columns)).astype(
                BF16
            )
            if z_line:
                @pl.when(is_end)
                def _():
                    per = units // 2 // BLOCK
                    repeat(
                        number * per, (number + 1) * per, lambda step: grad_pair(step, grads).start()
                    )

        repeat(0, 2, other)

    first_ends[0] += units // BLOCK

    mlp_slope(1)
    pump_second_ends(1)

    @pl.when(is_first)
    def _():
        far_parts(2, mlp_back_part, per=tiles_per_big)

    @pl.when(is_second)
    def _():
        both_parts(2, mlp_back_part, per=tiles_per_big)

    pump_second_ends(1)

    pump_first(1)

    put_second_near(
        proj_grad_at + proj_half,
        units - proj_half,
        lambda index, columns: proj_grad(index, pl.ds(proj_half, units - proj_half)),
    )
    put_first(fc_grad_at, width, fc_grad)
    pump_first_ends(width // BLOCK)
    pump_first(1)

    pump_second_ends(1)

    def mlp_back(index):
        at = tile_rows(index)
        n2_grad = part_sum(2, index)
        hat, rate = normed(hidden[at, :])
        small[2:3, :] += column_sum(n2_grad * hat)
        small[3:4, :] += column_sum(n2_grad)
        held = ends[ends_grad, at, :].astype(F32) + norm_backward(
            n2_grad, hat, rate, ln2_gain_ref[...]
        )
        hidden_grad[at, :] = held
        r_grad[0, at, :] = (BRANCH_SCALE * held).astype(BF16)

        @pl.when(is_first)
        def _():
            share(2, index).start()

    def first_mid_step(step):
        mid_up(step)

        @pl.when(step >= BEHIND)
        def _():
            mid_down(step - BEHIND, (False, False))

    def second_end_step(step):
        gather_y(step)
        grad_pair(step, grads).start()

    def second_mid_step(step):
        gather_y(step)
        first_mid_step(step)

    def collect_with_pump(which, finish):
        base = first_mids[0]
        first_mids[0] += TILES * PUMP

        def beside(index):
            if z_line:
                @pl.when(is_mid)
                def _():
                    start = base + index * PUMP
                    repeat(start, start + PUMP, first_mid_step)

        collect(which, finish, beside)

    collect_with_pump(2, mlp_back)
    pump_first(1)
    pump_second_ends(1)

    def attention_backward(index):
        shards = set_weights(index)

        def project(number):
            at = big_rows(number)
            values = dot_nt(
                r_grad[set_rows(index), at, :], weight_of(shards, out_at, local_width)
            ).astype(BF16)
            for head in range(heads):
                head_rows[head, at, :] = values[:, head_columns(0, head)]

        repeat(0, bigs, project)

        for head in range(heads):
            shares = probs[index * heads + head]
            rows_grad = head_rows[head]
            qkv_grad[index, :, head_columns(2, head)] = dot_nn(shares, rows_grad).astype(BF16)
            share_grad = dot_nt(qkv[index, 2, head], rows_grad)
            wide = shares.astype(F32)
            product = wide * share_grad
            score_grad = (product - wide * jnp.sum(product, axis=0, keepdims=True)).astype(BF16)
            qkv_grad[index, :, head_columns(0, head)] = (
                dot_tn(score_grad, qkv[index, 1, head]) * scale
            ).astype(BF16)
            qkv_grad[index, :, head_columns(1, head)] = dot_nn(
                score_grad, qkv[index, 0, head]
            ).astype(BF16)
    def attention_back_part(index, shards, at):
        return dot_nn(qkv_grad[index, at, :], weight_of(shards, 0, qkv_rows))

    first_base, ends_base, mids_base = first_mids[0], second_ends[0], second_mids[0]
    first_mids[0] += 3 * PUMP
    second_ends[0] += 2 * PUMP
    second_mids[0] += 3

    def attention_turn(index):
        attention_backward(index)
        if z_line:
            @pl.when(first_mid)
            def _():
                start = first_base + 2 * PUMP * index
                repeat(start, start + PUMP, first_mid_step)

            @pl.when(second_end)
            def _():
                start = ends_base + PUMP * index
                repeat(start, start + PUMP, second_end_step)

            @pl.when(second_mid)
            def _():
                start = mids_base + 2 * index
                repeat(start, start + 2 - index, second_mid_step)

        @pl.when(jnp.logical_and(is_first, index == 0))
        def _():
            own_parts(3, attention_back_part)
            share_some(2, 0, TILES)
            put_first_inside(out_grad_at, local_width, out_grad)
            if z_line:
                @pl.when(is_mid)
                def _():
                    repeat(first_base + PUMP, first_base + 2 * PUMP, first_mid_step)

    repeat(0, 2, attention_turn)

    @pl.when(is_first)
    def _():
        far_parts(3, attention_back_part)

    pump_first(PUMP)

    put_first(qkv_grad_at, qkv_rows, in_grad)
    if z_line:
        @pl.when(is_first)
        def _():
            repeat(0, LENT, lambda index: lent(index).start())

    pump_first(PUMP)

    def attention_back(index):
        at = tile_rows(index)
        n1_grad = part_sum(3, index)
        hat, rate = normed(ends[ends_in, at, :].astype(F32))
        small[0:1, :] += column_sum(n1_grad * hat)
        small[1:2, :] += column_sum(n1_grad)
        results[1, at, :] = (
            hidden_grad[at, :] + norm_backward(n1_grad, hat, rate, ln1_gain_ref[...])
        ).astype(BF16)

        @pl.when(is_second)
        def _():
            cross(2 * index).start()
            cross(2 * index + 1).start()

    @pl.when(is_first)
    def _():
        collect_with_pump(3, attention_back)

    turn_ends, turn_mids = second_ends[0], second_mids[0]
    second_ends[0] += 1
    second_mids[0] += 1

    @pl.when(is_second)
    def _():
        def turn_of(step):
            @pl.when(step < TILES)
            def _():
                at = tile_rows(step)
                part[3, at, :] = (
                    attention_back_part(0, 0, at) + attention_back_part(1, 1, at)
                ).astype(BF16)
                part_copy(3, step).start()

            if z_line:
                @pl.when(jnp.logical_and(step == TILES, is_end))
                def _():
                    second_end_step(turn_ends)

                @pl.when(jnp.logical_and(step == TILES, is_mid))
                def _():
                    second_mid_step(turn_mids)

            @pl.when(step >= 2)
            def _():
                part_copy(3, step - 2).wait_recv()
                attention_back(step - 2)

        repeat(0, TILES + 2, turn_of)

    pump_first(1)
    pump_second_ends(1)
    pump_second(1)

    leave = remote(
        results.at[1 - s, token_rows(across_m)], rows_recv, leave_send.at[0], leave_recv.at[0], across
    )
    @pl.when(is_first)
    def _():
        leave.start()

    sum_of_rows(5, m_grad)
    sum_of_rows(4, r_grad)
    for index in range(2):

        def sums(number, index=index):
            at = big_rows(number)
            set_sum(6, 0, index, pre_grad[index, at, :])
            set_sum(7, 0, index, qkv_grad[index, at, 0:local_width])
            set_sum(7, 2 * local_width, index, qkv_grad[index, at, 2 * local_width :])

        repeat(0, bigs, sums)
    small_y_copy = remote(small_other, small_y, leave_send.at[1], leave_recv.at[1], across)
    small_other[0:6, :] = small[0:6, :]
    small_y_copy.start()

    pump_first(2)
    pump_second_ends(1)
    pump_second(1)

    put_second_far(fc_grad_at, width, fc_grad)
    pump_second_ends(1)
    pump_second(1)

    @pl.when(is_second)
    def _():
        both_parts(FINE, mlp_part, per=2)

    pump_second_ends(2)
    pump_second(2)
    put_second_near(fc_grad_at, width, fc_grad)

    @pl.when(is_second)
    def _():
        collect(FINE, layer_out)

    pump_second_ends(2)
    pump_second(2)
    put_second_far(out_grad_at, local_width, out_grad)
    put_second_near(out_grad_at, local_width, out_grad)
    pump_second_ends(1)
    pump_second(1)
    put_second_far(qkv_grad_at, qkv_rows, in_grad)

    @pl.when(is_second)
    def _():
        leave.start()

    pump_second_ends(1)
    pump_second(1)
    put_second_near(qkv_grad_at, qkv_rows, in_grad)

    small_up = remote(small, small_pair, leave_send.at[2], leave_recv.at[2], pair)
    small_across = remote(small, small_mid, leave_send.at[3], leave_recv.at[3], middle)
    small_down = remote(small_mid, small_pair, leave_send.at[2], leave_recv.at[2], pair)

    rows_copy = pltpu.make_async_copy(rows_held, rows_out, local_sem.at[0])

    def small_copy(source):
        return pltpu.make_async_copy(source, small_out, local_sem.at[1])

    def rows_finish(wanted):
        @pl.when(wanted)
        def _():
            leave.wait_recv()
            rows_held[pl.ds(chip, 1)] = results[pl.ds(1 - s, 1), token_rows(m), :].astype(F32)
            rows_held[pl.ds(1 - chip, 1)] = rows_recv[...].astype(F32)[None]
            rows_copy.start()

    if z_line:
        @pl.when(is_end)
        def _():
            small_y_copy.wait_recv()
            small[...] += small_y[...]
            small_up.start()

        pump_ends(first_ends, len(first_order), first_end, False)
        pump_ends(second_ends, len(second_order), second_end, True)
        near, later = blocks * 2 // 3, blocks * 3 // 4
        pump_mids(first_mids, near, first_mid, False)
        pump_mids(second_mids, near, second_mid, True)

        @pl.when(is_mid)
        def _():
            small_y_copy.wait_recv()
            small_up.wait_recv()
            small[...] += small_y[...]
            small[...] += small_pair[...]
            small_across.start()

        pump_mids(first_mids, later, first_mid, False)
        pump_mids(second_mids, later, second_mid, True)
        rows_finish(is_first)

        @pl.when(is_mid)
        def _():
            small_across.wait_recv()
            small_mid[...] += small[...]
            small_down.start()
            small_copy(small_mid).start()

        pump_mids(first_mids, len(first_order), first_mid, False)
        pump_mids(second_mids, turn + LENT - 2, second_mid, True)
        rows_finish(is_second)
        pump_mids(second_mids, len(second_order), second_mid, True)

        def back(index, source):
            lent_back(index, source).wait_recv()
            grad_out(lent_from + index, source).start()

        @pl.when(is_mid)
        def _():
            last = small_from + small_count
            repeat(last - BEHIND, last, lambda step: mid_down(step, (False, True)))

        @pl.when(first_mid)
        def _():
            repeat(0, LENT, lambda index: back(index, grads_mid))

        def take(step, kind):
            grad_pair(step, grads_mid, kind[1]).wait_recv()
            deliver(step, grads_pair, kind)

        def small_take():
            small_down.wait_recv()
            small_copy(small_pair).start()

        @pl.when(first_end)
        def _():
            walk(first_order, 0, later, take)
            small_take()
            walk(first_order, later, len(first_order), take)
            repeat(0, LENT, lambda index: back(index, grads_pair))

        @pl.when(second_end)
        def _():
            walk(second_order, 0, turn, take)
            small_take()
            walk(second_order, turn, len(second_order), take)

    else:
        @pl.when(is_second)
        def _():
            repeat(0, blocks, gather_y)

        repeat(0, blocks, lambda step: grad_out(step, grads).start())
        rows_finish(s >= 0)
        small_y_copy.wait_recv()
        small[...] += small_y[...]
        small_copy(small).start()

    rows_copy.wait()
    small_copy(small).wait()
    own_rows = pl.ds(0, weight_rows)
    pltpu.make_async_copy(grads.at[own_rows], grads_out, grad_out_sem.at[0]).wait()

    entry_across(0).wait_send()
    entry_sibling(0).wait_send()
    entry_forward(0).wait_send()
    leave.wait_send()
    small_y_copy.wait_send()
    sent(part, part_send.at[0])
    sent(n1.at[0, pl.ds(0, big)], cross_send.at[0])
    sent(n1.at[0, pl.ds(0, big)], cross_core_send.at[0])

    @pl.when(is_first)
    def _():
        entry_across(1).wait_send()
        entry_sibling(1).wait_send()
        entry_forward(1).wait_send()
        sent(grads.at[pl.ds(0, 3 * big)], share_send.at[0])
        sent(grads.at[pl.ds(0, 2 * big)], share_core_send.at[0])
        for sem in (far_core_send, far_send, far_back_send):
            sent(grads.at[pl.ds(0, 4 * big)], sem.at[0])

    @pl.when(is_second)
    def _():
        bias_copy.wait_send()
        sent(weights.at[0, pl.ds(0, y_blocks * FETCH)], weight_y_send.at[0])
        if z_line:
            sent(weights.at[0, pl.ds(0, y_blocks * FETCH)], weight_z_send.at[0])
        sent(grads.at[own_rows], grad_y_send.at[0])

    if z_line:

        def stream_sent(count):
            sent(grads.at[pl.ds(0, count)], grad_pair_send.at[0])

            @pl.when(is_mid)
            def _():
                sent(grads.at[pl.ds(0, count)], grad_mid_send.at[0])

        @pl.when(is_first)
        def _():
            stream_sent(lent_from * BLOCK)
            sent(grads.at[pl.ds(0, LENT * BLOCK)], lent_send.at[0])

        @pl.when(is_second)
        def _():
            stream_sent(small_from * BLOCK)
            sent(grads.at[pl.ds(0, LENT * BLOCK)], back_send.at[0])

        @pl.when(is_end)
        def _():
            small_up.wait_send()

        @pl.when(is_mid)
        def _():
            small_across.wait_send()
            small_down.wait_send()


def finish_kernel(local_width, rows_ref, small_ref, grads_ref, *refs):
    outs, (held_rows, held, cast, in_sem, out_sem, rows_sem, held_small) = refs[:13], refs[13:20]
    lines, line_sem = refs[20:28], refs[28]
    rows_out, qkv_out, out_out, fc_out, proj_out = outs[:5]
    small_in = pltpu.make_async_copy(small_ref, held_small, line_sem.at[8])
    line_copies = [
        pltpu.make_async_copy(line, target, line_sem.at[number])
        for number, (line, target) in enumerate(zip(lines, outs[5:]))
    ]
    rows_in = pltpu.make_async_copy(rows_ref, held_rows, rows_sem.at[0])
    rows_copy = pltpu.make_async_copy(held_rows, rows_out, rows_sem.at[1])

    def at_block(number):
        return pl.ds(pl.multiple_of(number * FINISH, FINISH), FINISH)

    def fetch(number):
        at = at_block(number)
        return pltpu.make_async_copy(grads_ref.at[at], held.at[at], in_sem.at[number])

    def repeat(start, last, action):
        def step_of(step, carry):
            action(step)
            return carry

        lax.fori_loop(start, last, step_of, 0)

    blocks = held.shape[0] // FINISH
    repeat(0, blocks, lambda number: fetch(number).start())
    small_in.start()
    rows_in.start()
    first = 0
    puts = []
    for target in (proj_out, fc_out, out_out, qkv_out):
        count = target.shape[0] // FINISH

        def put(number, first=first, target=target):
            return pltpu.make_async_copy(
                cast.at[at_block(first + number)], target.at[at_block(number)], out_sem.at[first + number]
            )

        def step(number, first=first, put=put):
            fetch(first + number).wait()
            at = at_block(first + number)
            cast[at, :] = held[at, :].astype(F32)
            put(number).start()

        repeat(0, count, step)
        puts.append((count, put))
        first += count
    rows_in.wait()
    rows_copy.start()
    small_in.wait()
    lines[0][0:1, :] = held_small[7:8, 0:local_width]
    lines[0][1:2, :] = held_small[7:8, 2 * local_width : 3 * local_width]
    for row, line in enumerate(lines[1:]):
        line[...] = held_small[row : row + 1, :]
    for copy in line_copies:
        copy.start()
    for copy in line_copies:
        copy.wait()
    for count, put in puts:
        repeat(0, count, lambda number: put(number).wait())
    rows_copy.wait()


def local(
    z_line,
    boundary_in,
    order,
    ln1_gain,
    ln1_bias,
    w_qkv,
    qkv_bias,
    w_out,
    out_bias,
    ln2_gain,
    ln2_bias,
    w_fc,
    fc_bias,
    w_proj,
    proj_bias,
):
    _, micro, rows, width = boundary_in.shape
    local_width = w_qkv.shape[-1]
    units = w_fc.shape[-1]
    length = rows * lax.axis_size("mp")
    heads = local_width // HEAD_DIM
    weight_rows = 4 * local_width + width + units
    blocks = weight_rows // BLOCK
    stream_rows = weight_rows + LENT * BLOCK
    numbers = blocks + LENT + 2 * BLOCK // SMALL
    vmem = pltpu.VMEM
    dma = pltpu.SemaphoreType.DMA
    in_any = pl.BlockSpec(memory_space=pl.ANY)
    vectors = (ln1_gain, ln1_bias, qkv_bias, out_bias, ln2_gain, ln2_bias, fc_bias, proj_bias)
    out_rows, small, grads = pl.pallas_call(
        functools.partial(kernel, z_line),
        out_shape=(
            jax.ShapeDtypeStruct((micro, rows, width), F32),
            jax.ShapeDtypeStruct((8, width), F32),
            jax.ShapeDtypeStruct((weight_rows, width), BF16),
        ),
        in_specs=[in_any] * 14,
        out_specs=(in_any,) * 3,
        scratch_shapes=[
            pltpu.SMEM(order.shape, jnp.int32),
            *(vmem(vector.shape, F32) for vector in vectors),
            vmem((micro, rows, width), BF16),
            vmem((micro, rows, width), BF16),
            vmem((2, weight_rows, width), BF16),
            vmem((2, 8, width), F32),
            vmem((3, length, width), BF16),
            vmem((2, length, width), BF16),
            vmem((rows, width), BF16),
            vmem((micro, rows, width), F32),
            vmem((2, length, width), BF16),
            vmem((2, length, width), BF16),
            vmem((2, 3, heads, length, HEAD_DIM), BF16),
            vmem((2 * heads, length, length), BF16),
            vmem((heads, length, HEAD_DIM), BF16),
            vmem((2, length, local_width), BF16),
            vmem((length, width), F32),
            vmem((length, width), F32),
            vmem((2, length, units), BF16),
            vmem((2, length, units), BF16),
            vmem((2, length, width), BF16),
            vmem((2, length, width), BF16),
            vmem((2, length, 3 * local_width), BF16),
            vmem((4, length, width), BF16),
            vmem((4, length, width), BF16),
            vmem((stream_rows, width), BF16),
            vmem((weight_rows, width), BF16),
            vmem((weight_rows, width), BF16),
            vmem((stream_rows, width), BF16),
            vmem((stream_rows, width), BF16),
            vmem((8, width), F32),
            vmem((8, width), F32),
            vmem((8, width), F32),
            vmem((8, width), F32),
            vmem((8, width), F32),
            dma((5,)),
            dma((9,)),
            dma((7,)),
            dma((7,)),
            dma((1,)),
            dma((weight_rows // FETCH,)),
            dma((1,)),
            dma((1,)),
            dma((5 * TILES,)),
            dma((1,)),
            dma((1,)),
            dma((1,)),
            dma((1,)),
            dma((2,)),
            dma((1,)),
            dma((2 * TILES,)),
            dma((1,)),
            dma((2 * TILES,)),
            dma((4,)),
            dma((4,)),
            dma((1,)),
            dma((max(numbers - LENT, 15 * TILES),)),
            dma((1,)),
            dma((numbers,)),
            dma((1,)),
            dma((numbers,)),
            dma((1,)),
            dma((1,)),
            dma((LENT,)),
            dma((1,)),
        ],
        compiler_params=pltpu.CompilerParams(
            collective_id=0, has_side_effects=True, vmem_limit_bytes=63 * 2**20
        ),
        name="two_layers",
    )(
        order,
        boundary_in,
        ln1_gain,
        ln1_bias,
        jnp.swapaxes(w_qkv, 2, 3).reshape(1, 3 * local_width, width),
        qkv_bias,
        w_out,
        out_bias,
        ln2_gain,
        ln2_bias,
        w_fc,
        fc_bias,
        w_proj,
        proj_bias,
    )
    if not z_line:
        small, grads = lax.psum((small, grads), "dp")
    shapes = [
        (micro, rows, width),
        (3 * local_width, width),
        (local_width, width),
        (width, units),
        (units, width),
        (2, local_width),
    ] + [(1, width)] * 6 + [(1, units)]
    (
        out_rows,
        qkv_grad,
        out_grad,
        fc_grad,
        proj_grad,
        qkv_bias_grad,
        ln1_gain_grad,
        ln1_bias_grad,
        ln2_gain_grad,
        ln2_bias_grad,
        out_bias_grad,
        proj_bias_grad,
        fc_bias_grad,
    ) = pl.pallas_call(
        functools.partial(finish_kernel, local_width),
        out_shape=[jax.ShapeDtypeStruct(shape, F32) for shape in shapes],
        in_specs=[in_any] * 3,
        out_specs=[in_any] * 13,
        scratch_shapes=[
            vmem((micro, rows, width), F32),
            vmem((weight_rows, width), BF16),
            vmem((weight_rows, width), F32),
            dma((weight_rows // FINISH,)),
            dma((weight_rows // FINISH,)),
            dma((2,)),
            vmem((8, width), F32),
        ]
        + [vmem(shape, F32) for shape in shapes[5:]]
        + [dma((9,))],
        compiler_params=pltpu.CompilerParams(vmem_limit_bytes=62 * 2**20),
        name="finish",
    )(out_rows, small, grads)
    return (
        out_rows[None],
        ln1_gain_grad,
        ln1_bias_grad,
        jnp.swapaxes(qkv_grad.reshape(1, 3, local_width, width), 2, 3),
        qkv_bias_grad[None],
        out_grad[None],
        out_bias_grad,
        ln2_gain_grad,
        ln2_bias_grad,
        fc_grad[None],
        fc_bias_grad,
        proj_grad[None],
        proj_bias_grad,
    )


def solution(mesh):
    return jax.shard_map(
        functools.partial(local, mesh.shape["dp"] == 4),
        mesh=mesh,
        in_specs=(
            P("section", "dp", "mp", None),
            P("dp", None),
            P("section", None),
            P("section", None),
            P("section", None, None, "mp"),
            P("section", None, "mp"),
            P("section", "mp", None),
            P("section", None),
            P("section", None),
            P("section", None),
            P("section", None, "mp"),
            P("section", "mp"),
            P("section", "mp", None),
            P("section", None),
        ),
        out_specs=(
            P("section", "dp", "mp", None),
            P("section", None),
            P("section", None),
            P("section", None, None, "mp"),
            P("section", None, "mp"),
            P("section", "mp", None),
            P("section", None),
            P("section", None),
            P("section", None),
            P("section", None, "mp"),
            P("section", "mp"),
            P("section", "mp", None),
            P("section", None),
        ),
        check_vma=False,
    )
```
